32 devices in a mesh: lon: 16 (over z, y, x), lat: 2 (over core).
Axes of the slice: x: 2, y: 2, z: 4, core: 2. Of those that a mesh axis runs over, the one named last changes fastest.
Arguments:
- tokens: bfloat16 [384, 48, 2, 512], P('lon', 'lat'), may hold values from -6 to 6
- qkv_weight: bfloat16 [2, 512, 1536], P(None, 'lon'), may hold values from -0.25 to 0.25
- out_weight: bfloat16 [2, 512, 512], P(None, 'lon'), may hold values from -0.25 to 0.25
- up_weight: bfloat16 [2, 512, 2048], P(None, 'lon'), may hold values from -0.25 to 0.25
- down_weight: bfloat16 [2, 512, 2048], P(None, 'lon'), may hold values from -0.125 to 0.125
- norm_gain: float32 [2, 2, 512], replicated, may hold values from 0.25 to 1.75
- logit_scale: float32 [2, 16], replicated, may hold values from 2 to 20
Outputs:
- mixed: bfloat16 [384, 48, 2, 512], P('lon', 'lat')
The draws below stay inside these ranges and needn't reach their ends.
All inputs are finite; a program needn't handle non-finite values.
Results may differ from the reference program's by a relative error of at most 0.014.
Values may be sent and summed in bfloat16 or wider, within the bound.
No kernel may reach another device: no remote copies, remote signals or barrier semaphores. Data moves between devices by JAX's collectives and lax.ppermute only.
A program may use at most 128 MiB of HBM per device.

```python
import math
import jax
import jax.numpy as jnp
from jax import lax

D = 512
HEADS = 16
HID = 2048
WLON = 12
WLAT = 6
LEVELS = 2
NLON = 384
NLAT = 48


def steps_of(key, dims, split, least, top_value):
    def one(position, shards_of):
        heights = jax.random.uniform(jax.random.fold_in(jax.random.fold_in(key, 6), position), (shards_of,), jnp.float32, least / len(split), top_value / len(split))
        return jnp.repeat(jnp.exp(heights), dims[position] // shards_of).reshape((-1,) + (1,) * (len(dims) - position - 1))

    level = one(*split[0])
    for cut in split[1:]:
        level = level * one(*cut)
    return level


def normal_values(own_key, dims, width, bound, shards=(), kind=jnp.bfloat16):
    values = width * jax.random.normal(own_key, dims, jnp.float32)
    if shards:
        values = values * steps_of(own_key, dims, shards, -0.22, 0.18)
    return jnp.clip(values, -bound, bound).astype(kind)


def setup_inputs(seed: int = 0) -> dict:
    splits = jax.random.split(jax.random.key(seed), 8)
    tokens = normal_values(splits[0], (NLON, NLAT, LEVELS, D), 1.0, 6.0, ((0, 16), (1, 2)))
    qkv_weight = normal_values(splits[1], (2, D, 3 * D), D ** -0.5, 0.25, ((1, 16),))
    out_weight = normal_values(splits[2], (2, D, D), D ** -0.5, 0.25, ((1, 16),))
    up_weight = normal_values(splits[3], (2, D, HID), D ** -0.5, 0.25, ((1, 16),))
    down_weight = normal_values(splits[4], (2, D, HID), HID ** -0.5, 0.125, ((1, 16),))
    norm_gain = jnp.clip(1.0 + 0.15 * jax.random.normal(splits[5], (2, 2, D), jnp.float32), 0.25, 1.75)
    logit_scale = jnp.clip(jnp.exp(jax.random.uniform(splits[6], (2, HEADS), jnp.float32, math.log(2.0), math.log(20.0))), 2.0, 20.0)
    return dict(tokens=tokens, qkv_weight=qkv_weight, out_weight=out_weight, up_weight=up_weight, down_weight=down_weight, norm_gain=norm_gain, logit_scale=logit_scale)


def layer_norm(value, gain_row):
    averaged = lax.optimization_barrier(jnp.mean(value, -1, keepdims=True))
    centred = value - averaged
    variance = lax.optimization_barrier(jnp.mean(centred * centred, -1, keepdims=True))
    return centred / jnp.sqrt(variance + 1e-05) * gain_row

def to_windows(local_cells):
    col_count, row_count, levels, features = local_cells.shape
    arranged = local_cells.reshape(col_count // WLON, WLON, row_count // WLAT, WLAT, levels, features)
    arranged = arranged.transpose(0, 2, 1, 3, 4, 5)
    return arranged.reshape(-1, WLON * WLAT * levels, features)

def from_windows(windows, col_count, row_count):
    features = windows.shape[-1]
    arranged = windows.reshape(col_count // WLON, row_count // WLAT, WLON, WLAT, LEVELS, features)
    arranged = arranged.transpose(0, 2, 1, 3, 4, 5)
    return arranged.reshape(col_count, row_count, LEVELS, features)

def window_groups(col_count, row_count, row_start, total_rows):
    lat_rows = row_start + jnp.arange(row_count, dtype=jnp.int32)
    wrapped = (lat_rows >= total_rows - WLAT // 2).astype(jnp.float32)
    flags = jnp.broadcast_to(wrapped[None, :, None], (col_count, row_count, LEVELS))
    flags = flags.reshape(col_count // WLON, WLON, row_count // WLAT, WLAT, LEVELS).transpose(0, 2, 1, 3, 4)
    return flags.reshape(-1, WLON * WLAT * LEVELS)

def unit_rows(vectors):
    length = jnp.sqrt(lax.optimization_barrier(jnp.sum(vectors * vectors, -1, keepdims=True)))
    return vectors / jnp.maximum(length, 0.5 * math.sqrt(vectors.shape[-1]))

def attend(triples, window_count, window_cells, sharpness_all, allowed):
    features = triples.shape[-1] // 3
    head_dim = features // HEADS
    head_split = triples.reshape(window_count, window_cells, 3, HEADS, head_dim).transpose(2, 3, 0, 1, 4)

    def one_head(inputs):
        queries, key_rows, values, sharpness = inputs
        query_unit = unit_rows(queries.astype(jnp.float32))
        key_unit = unit_rows(key_rows.astype(jnp.float32))
        scores = jnp.einsum('wqd,wkd->wqk', query_unit, key_unit, precision=lax.Precision.HIGHEST) * sharpness
        weights = jnp.exp(scores)
        if allowed is not None:
            weights = weights * allowed
        weights = (weights / lax.optimization_barrier(jnp.sum(weights, -1, keepdims=True))).astype(jnp.bfloat16)
        return jnp.einsum('wqk,wkd->wqd', weights.astype(jnp.float32), values.astype(jnp.float32)).astype(jnp.bfloat16)
    attended = lax.map(one_head, (head_split[0], head_split[1], head_split[2], sharpness_all))
    return attended.transpose(1, 2, 0, 3).reshape(window_count * window_cells, features)

def block_pass(local_cells, qkv_w, out_w, up_w, down_w, gain_pair, sharpness_all, row_start, total_rows, shifted):
    col_count, row_count = (local_cells.shape[0], local_cells.shape[1])
    windows = to_windows(local_cells)
    window_count, window_cells, features = windows.shape
    token_rows = windows.reshape(window_count * window_cells, features)
    allowed = None
    if shifted:
        groups = window_groups(col_count, row_count, row_start, total_rows)
        allowed = (groups[:, :, None] == groups[:, None, :]).astype(jnp.float32)
    triples = jnp.dot(token_rows, qkv_w, preferred_element_type=jnp.float32).astype(jnp.bfloat16)
    attended = attend(triples, window_count, window_cells, sharpness_all, allowed)
    projected = jnp.dot(attended, out_w, preferred_element_type=jnp.float32)
    middle = (token_rows.astype(jnp.float32) + layer_norm(projected, gain_pair[0])).astype(jnp.bfloat16)
    hidden = jax.nn.gelu(jnp.dot(middle, up_w, preferred_element_type=jnp.float32)).astype(jnp.bfloat16)
    down_sum = lax.dot_general(hidden, down_w, (((1,), (1,)), ((), ())), preferred_element_type=jnp.float32)
    result = (middle.astype(jnp.float32) + layer_norm(down_sum, gain_pair[1])).astype(jnp.bfloat16)
    return from_windows(result.reshape(window_count, window_cells, features), col_count, row_count)

def reference(tokens, qkv_weight, out_weight, up_weight, down_weight, norm_gain, logit_scale):
    total_rows = tokens.shape[1]
    column_shape = (tokens.shape[0] // WLON, WLON) + tokens.shape[1:]

    def plain_block(column_cells):
        return block_pass(column_cells, qkv_weight[0], out_weight[0], up_weight[0], down_weight[0], norm_gain[0], logit_scale[0], 0, total_rows, False)

    def shifted_block(column_cells):
        return block_pass(column_cells, qkv_weight[1], out_weight[1], up_weight[1], down_weight[1], norm_gain[1], logit_scale[1], 0, total_rows, True)
    plain_out = lax.map(plain_block, tokens.reshape(column_shape)).reshape(tokens.shape)
    rolled = jnp.roll(plain_out, (-(WLON // 2), -(WLAT // 2)), axis=(0, 1))
    second = lax.map(shifted_block, rolled.reshape(column_shape)).reshape(tokens.shape)
    return jnp.roll(second, (WLON // 2, WLAT // 2), axis=(0, 1))
```

```python
import functools
import math

import numpy as np

import jax
import jax.numpy as jnp
from jax import lax
from jax.experimental import pallas as pl
from jax.experimental.pallas import tpu as pltpu
from jax.sharding import PartitionSpec as P

HEADS = 16
HEAD = 32
WLON = 12
WLAT = 6
LEVELS = 2
CELLS = WLON * WLAT * LEVELS
MAIN = 128
REST = CELLS - MAIN
GROUP = 8
WIDE = GROUP * HEAD
ANY = pl.BlockSpec(memory_space=pl.ANY)
NT = (((1,), (1,)), ((), ()))


def dot(a, b, dims=(((1,), (0,)), ((), ()))):
    return lax.dot_general(a, b, dims, preferred_element_type=jnp.float32)


def layer_norm(value, gain_row):
    averaged = jnp.mean(value, -1, keepdims=True)
    centred = value - averaged
    variance = jnp.mean(centred * centred, -1, keepdims=True)
    return centred * lax.rsqrt(variance + 1e-05) * gain_row


def relayed(rows, lat_size):
    return lat_size == 2 and rows % 32 == 0


def cut_kernel(half, qkv_ref, out_ref, up_ref, down_ref, *refs):
    chunks, sems = refs[:-1], refs[-1]
    first = pl.multiple_of(lax.axis_index("lat") * half, 16)
    copies = []
    for index, target in enumerate(chunks):
        block, part = divmod(index, 2)
        place = 0
        for source in ((qkv_ref, out_ref), (up_ref, down_ref))[part]:
            width = source.shape[2]
            copies.append(
                pltpu.make_async_copy(
                    source.at[block, pl.ds(first, half), :],
                    target.at[0, :, pl.ds(place, width)],
                    sems.at[len(copies)],
                )
            )
            place += width
    for copy in copies:
        copy.start()
    for copy in copies:
        copy.wait()


def cut_chunks(qkv_weight, out_weight, up_weight, down_weight):
    blocks, rows, _ = qkv_weight.shape
    widths = (
        qkv_weight.shape[2] + out_weight.shape[2],
        up_weight.shape[2] + down_weight.shape[2],
    )
    return pl.pallas_call(
        functools.partial(cut_kernel, rows // 2),
        out_shape=[
            jax.ShapeDtypeStruct((1, rows // 2, width), jnp.bfloat16) for width in widths * blocks
        ],
        in_specs=[ANY] * 4,
        out_specs=[ANY] * (2 * blocks),
        scratch_shapes=[pltpu.SemaphoreType.DMA((4 * blocks,))],
    )(qkv_weight, out_weight, up_weight, down_weight)


def send(block, lon_size, move):
    pairs = []
    for lon in range(lon_size):
        for core in range(2):
            z, y, x, core_to = move(lon // 4, lon // 2 % 2, lon % 2, core)
            pairs.append((lon * 2 + core, (z * 4 + y * 2 + x) * 2 + core_to))
    return lax.ppermute(block, ("lon", "lat"), pairs)


def relay(own, lon_size):
    depth = lon_size // 4
    column = [own] + [
        send(own, lon_size, lambda z, y, x, c, step=step: ((z + step) % depth, y, x, c))
        for step in range(1, depth)
    ]
    column = jnp.concatenate(column, 0)
    beside = send(
        column, lon_size, lambda z, y, x, c: (z, y, 1 - x, c) if c == 0 else (z, 1 - y, x, c)
    )
    first = jnp.concatenate([column, beside], 0)
    second = send(
        first, lon_size, lambda z, y, x, c: (z, 1 - y, x, c) if c == 0 else (z, y, 1 - x, c)
    )
    swap = lambda z, y, x, c: (z, y, x, 1 - c)
    return [first, second, send(first, lon_size, swap), send(second, lon_size, swap)]


def load_pieces(pieces, w_ref, sem):
    if len(pieces) == 1:
        copy = pltpu.make_async_copy(pieces[0].at[0], w_ref, sem)
        copy.start()
        copy.wait()
        return
    depth = pieces[0].shape[0] // 2
    half = pieces[0].shape[1]
    lon, lat = lax.axis_index("lon"), lax.axis_index("lat")
    z, y, x = lon // 4, lon // 2 % 2, lon % 2
    for index, piece in enumerate(pieces):
        core = lat if index < 2 else 1 - lat
        if index % 2 == 0:
            squares = (y * 2 + x, jnp.where(core == 0, y * 2 + 1 - x, (1 - y) * 2 + x))
        else:
            squares = (
                jnp.where(core == 0, (1 - y) * 2 + x, y * 2 + 1 - x),
                (1 - y) * 2 + 1 - x,
            )
        for j in range(2 * depth):
            shard = (z + depth - j % depth) % depth * 4 + squares[j // depth]
            row = pl.multiple_of((shard * 2 + core) * half, 16)
            pltpu.make_async_copy(piece.at[j], w_ref.at[pl.ds(row, half), :], sem).start()
    pltpu.make_async_copy(w_ref, w_ref, sem).wait()


def attend_kernel(shifted, row_windows, count, *refs):
    x_ref, pieces = refs[0], refs[1 : 1 + count]
    gain_ref, sharp_ref = refs[1 + count : 3 + count]
    allow_ref = refs[3 + count] if shifted else None
    out_ref, w_ref, vt_ref, sem = refs[-4:]
    features = x_ref.shape[-1]

    @pl.when(pl.program_id(0) == 0)
    def _():
        load_pieces(pieces, w_ref, sem)
        vt_ref[...] = w_ref[:, 2 * features : 3 * features].T

    tokens = x_ref[0]
    queries = dot(tokens, w_ref[:, :features]).astype(jnp.bfloat16).astype(jnp.float32)
    keys = dot(tokens, w_ref[:, features : 2 * features]).astype(jnp.bfloat16).astype(jnp.float32)
    values = dot(vt_ref[...], tokens, NT).astype(jnp.bfloat16)

    channel = lax.broadcasted_iota(jnp.int32, (WIDE, WIDE), 0) // HEAD
    same_head = jnp.where(
        channel == lax.broadcasted_iota(jnp.int32, (WIDE, WIDE), 1) // HEAD, 1.0, 0.0
    ).astype(jnp.bfloat16)
    lane_head = lax.broadcasted_iota(jnp.int32, (1, WIDE), 1) // HEAD
    diagonal = (
        lax.broadcasted_iota(jnp.int32, (WIDE, MAIN), 0) // HEAD
        == lax.broadcasted_iota(jnp.int32, (WIDE, MAIN), 1) // REST
    )
    if shifted:
        last = jnp.logical_and(
            pl.program_id(0) % row_windows == row_windows - 1,
            lax.axis_index("lat") == lax.axis_size("lat") - 1,
        )
        allow = jnp.where(last, allow_ref[...], 1.0)
        allow_main = jnp.concatenate([allow[:, :MAIN]] * 2, 1)
        allow_rest = allow[:, MAIN:]

    def units(part):
        squares = (part * part).astype(jnp.bfloat16)
        length2 = dot(squares, same_head)
        return part * lax.rsqrt(jnp.maximum(length2, 0.25 * HEAD))

    main_rows, rest_rows = [], []
    for group in range(HEADS // GROUP):
        lanes = slice(group * WIDE, (group + 1) * WIDE)
        query = (units(queries[:, lanes]) * sharp_ref[:, lanes]).astype(jnp.bfloat16)
        key = units(keys[:, lanes]).astype(jnp.bfloat16)
        value = values[lanes]

        def masked(rows, head):
            return jnp.where(lane_head == head, rows, jnp.zeros_like(rows))

        def weights(stacked, allowed):
            scores = dot(key, stacked, NT)
            powers = jnp.exp2(scores)
            if shifted:
                powers = powers * allowed
            return powers.astype(jnp.bfloat16), 1.0 / jnp.sum(powers, 0, keepdims=True)

        for pair in range(GROUP // 2):
            stacked = jnp.concatenate(
                [masked(query[:MAIN], 2 * pair), masked(query[:MAIN], 2 * pair + 1)], 0
            )
            weight, inverse = weights(stacked, allow_main if shifted else None)
            both = dot(value[2 * pair * HEAD : 2 * (pair + 1) * HEAD], weight) * inverse
            main_rows += [both[:HEAD, :MAIN], both[HEAD:, MAIN:]]
        stacked = jnp.concatenate([masked(query[MAIN:], head) for head in range(GROUP)], 0)
        weight, inverse = weights(stacked, allow_rest if shifted else None)
        rest = dot(value, weight) * inverse
        rest_rows.append(jnp.where(diagonal, rest, 0.0))
    attended = jnp.concatenate(
        [jnp.concatenate(main_rows, 0).T, jnp.concatenate(rest_rows, 0).T], 0
    ).astype(jnp.bfloat16)
    projected = dot(attended, w_ref[:, 3 * features :])
    rest = projected[MAIN : MAIN + REST]
    for head in range(1, GROUP):
        rest = rest + projected[MAIN + head * REST : MAIN + (head + 1) * REST]
    projected = jnp.concatenate([projected[:MAIN], rest], 0)
    middle = tokens.astype(jnp.float32) + layer_norm(projected, gain_ref[...])
    out_ref[0] = middle.astype(jnp.bfloat16)


def allowed_pairs():
    token = np.arange(CELLS)
    side = token // LEVELS % WLAT >= WLAT // 2
    rest = np.tile(side[MAIN:], GROUP)
    return (side[:, None] == np.concatenate([side[:MAIN], rest])[None, :]).astype(np.float32)


def attend(windows, pieces, gain, sharp, shifted, row_windows):
    count, cells, features = windows.shape
    whole = lambda shape: pl.BlockSpec(shape, lambda i: (0,) * len(shape))
    block = pl.BlockSpec((1, cells, features), lambda i: (i, 0, 0))
    extra = (jnp.asarray(allowed_pairs()),) if shifted else ()
    return pl.pallas_call(
        functools.partial(attend_kernel, shifted, row_windows, len(pieces)),
        grid=(count,),
        out_shape=jax.ShapeDtypeStruct(windows.shape, jnp.bfloat16),
        in_specs=[block]
        + [ANY] * len(pieces)
        + [whole((1, features))] * 2
        + [whole(e.shape) for e in extra],
        out_specs=block,
        scratch_shapes=[
            pltpu.VMEM((features, 4 * features), jnp.bfloat16),
            pltpu.VMEM((features, features), jnp.bfloat16),
            pltpu.SemaphoreType.DMA,
        ],
        compiler_params=pltpu.CompilerParams(vmem_limit_bytes=40 * 2**20),
        cost_estimate=pl.CostEstimate(
            flops=count * 11_000_000_00, bytes_accessed=6_000_000, transcendentals=0
        ),
    )(windows, *pieces, gain, sharp, *extra)


def feed_kernel(count, hidden_size, chunk, *refs):
    x_ref, pieces = refs[0], refs[1 : 1 + count]
    gain_ref, out_ref, w_ref, sem = refs[1 + count :]

    @pl.when(pl.program_id(0) == 0)
    def _():
        load_pieces(pieces, w_ref, sem)

    tokens = x_ref[...]
    total = jnp.zeros(tokens.shape, jnp.float32)
    for start in range(0, hidden_size, chunk):
        grown = dot(tokens, w_ref[:, start : start + chunk])
        hidden = jax.nn.gelu(grown).astype(jnp.bfloat16)
        total = total + dot(
            hidden, w_ref[:, hidden_size + start : hidden_size + start + chunk], NT
        )
    result = tokens.astype(jnp.float32) + layer_norm(total, gain_ref[...])
    out_ref[...] = result.astype(jnp.bfloat16)


def feed(rows, pieces, gain, hidden_size):
    count, features = rows.shape
    tile = 2 * CELLS
    block = pl.BlockSpec((tile, features), lambda i: (i, 0))
    return pl.pallas_call(
        functools.partial(feed_kernel, len(pieces), hidden_size, 512),
        grid=(count // tile,),
        out_shape=jax.ShapeDtypeStruct(rows.shape, jnp.bfloat16),
        in_specs=[block]
        + [ANY] * len(pieces)
        + [pl.BlockSpec((1, features), lambda i: (0, 0))],
        out_specs=block,
        scratch_shapes=[
            pltpu.VMEM((features, 2 * hidden_size), jnp.bfloat16),
            pltpu.SemaphoreType.DMA,
        ],
        compiler_params=pltpu.CompilerParams(vmem_limit_bytes=40 * 2**20),
        cost_estimate=pl.CostEstimate(
            flops=4 * count * features * hidden_size, bytes_accessed=8_000_000, transcendentals=0
        ),
    )(rows, *pieces, gain)


def to_windows(cells):
    cols, rows, levels, features = cells.shape
    arranged = cells.reshape(cols // WLON, WLON, rows // WLAT, WLAT, levels, features)
    return arranged.transpose(0, 2, 1, 3, 4, 5).reshape(-1, CELLS, features)


def from_windows(windows, cols, rows):
    features = windows.shape[-1]
    arranged = windows.reshape(cols // WLON, rows // WLAT, WLON, WLAT, LEVELS, features)
    return arranged.transpose(0, 2, 1, 3, 4, 5).reshape(cols, rows, LEVELS, features)


def shift_from(block, lon_step, lat_step):
    lons, lats = lax.axis_size("lon"), lax.axis_size("lat")
    pairs = []
    for lon in range(lons):
        for lat in range(lats):
            source = (lon + lon_step) % lons * lats + (lat + lat_step) % lats
            pairs.append((source, lon * lats + lat))
    return lax.ppermute(block, ("lon", "lat"), pairs)


def roll_on(cells):
    c, r = WLON // 2, WLAT // 2
    ahead = shift_from(cells[:c, r:], 1, 0)
    above = shift_from(cells[c:, :r], 0, 1)
    corner = shift_from(cells[:c, :r], 1, 1)
    return jnp.concatenate(
        [
            jnp.concatenate([cells[c:, r:], ahead], 0),
            jnp.concatenate([above, corner], 0),
        ],
        1,
    )


def roll_back(cells):
    c, r = WLON // 2, WLAT // 2
    behind = shift_from(cells[-c:, :-r], -1, 0)
    below = shift_from(cells[:-c, -r:], 0, -1)
    corner = shift_from(cells[-c:, -r:], -1, -1)
    return jnp.concatenate(
        [
            jnp.concatenate([corner, below], 0),
            jnp.concatenate([behind, cells[:-c, :-r]], 0),
        ],
        1,
    )


def per_device(tokens, qkv_weight, out_weight, up_weight, down_weight, norm_gain, logit_scale):
    cols, rows, _, features = tokens.shape
    hidden_size = up_weight.shape[-1]
    lon_size = lax.axis_size("lon")
    if relayed(qkv_weight.shape[1], lax.axis_size("lat")):
        chunks = cut_chunks(qkv_weight, out_weight, up_weight, down_weight)
        gathered = [relay(chunk, lon_size) for chunk in chunks]
    else:
        gathered = []
        for block in range(2):
            for pair in ((qkv_weight, out_weight), (up_weight, down_weight)):
                joined = jnp.concatenate([weight[block] for weight in pair], 1)
                gathered.append([lax.all_gather(joined, "lon", axis=0, tiled=True)[None]])
    sharp = jnp.repeat(logit_scale * math.log2(math.e), HEAD, axis=1)

    def block_pass(cells, block, shifted):
        windows = to_windows(cells)
        middle = attend(
            windows,
            gathered[2 * block],
            norm_gain[block, :1],
            sharp[block : block + 1],
            shifted,
            rows // WLAT,
        )
        result = feed(
            middle.reshape(-1, features), gathered[2 * block + 1], norm_gain[block, 1:], hidden_size
        )
        return from_windows(result.reshape(windows.shape), cols, rows)

    rolled = roll_on(block_pass(tokens, 0, False))
    return roll_back(block_pass(rolled, 1, True))


def solution(mesh):
    placed = (
        P("lon", "lat", None, None),
        P(None, "lon", None),
        P(None, "lon", None),
        P(None, "lon", None),
        P(None, "lon", None),
        P(),
        P(),
    )
    return jax.shard_map(
        per_device,
        mesh=mesh,
        in_specs=placed,
        out_specs=P("lon", "lat", None, None),
        check_vma=False,
    )
```

```python
import functools
import math

import numpy as np

import jax
import jax.numpy as jnp
from jax import lax
from jax.experimental import pallas as pl
from jax.experimental.pallas import tpu as pltpu
from jax.sharding import PartitionSpec as P

HEADS = 16
HEAD = 32
WLON = 12
WLAT = 6
LEVELS = 2
CELLS = WLON * WLAT * LEVELS
MAIN = 128
REST = CELLS - MAIN
GROUP = 8
WIDE = GROUP * HEAD
ANY = pl.BlockSpec(memory_space=pl.ANY)
NT = (((1,), (1,)), ((), ()))


def dot(a, b, dims=(((1,), (0,)), ((), ()))):
    return lax.dot_general(a, b, dims, preferred_element_type=jnp.float32)


def layer_norm(value, gain_row):
    averaged = jnp.mean(value, -1, keepdims=True)
    centred = value - averaged
    variance = jnp.mean(centred * centred, -1, keepdims=True)
    return centred * lax.rsqrt(variance + 1e-05) * gain_row


def relayed(rows, lat_size):
    return lat_size == 2 and rows % 32 == 0


def cut_kernel(half, qkv_ref, out_ref, up_ref, down_ref, *chunks):
    first = pl.multiple_of(lax.axis_index("lat") * half, 16)
    for block, target in enumerate(chunks):
        place = 0
        for source in (qkv_ref, out_ref, up_ref, down_ref):
            width = source.shape[2]
            target[:, place : place + width] = source[block, pl.ds(first, half), :]
            place += width


def cut_chunks(qkv_weight, out_weight, up_weight, down_weight):
    weights = (qkv_weight, out_weight, up_weight, down_weight)
    blocks, rows, _ = qkv_weight.shape
    width = sum(weight.shape[2] for weight in weights)
    return pl.pallas_call(
        functools.partial(cut_kernel, rows // 2),
        out_shape=[jax.ShapeDtypeStruct((rows // 2, width), jnp.bfloat16)] * blocks,
    )(*weights)


def load_pieces(pieces, w_ref, sem, first):
    if len(pieces) == 1:
        copy = pltpu.make_async_copy(pieces[0].at[:, pl.ds(first, w_ref.shape[1])], w_ref, sem)
        copy.start()
        copy.wait()
        return
    depth = pieces[0].shape[0] // 2
    half = pieces[0].shape[1]
    lon, lat = lax.axis_index("lon"), lax.axis_index("lat")
    z, y, x = lon // 4, lon // 2 % 2, lon % 2
    for index, piece in enumerate(pieces):
        core = lat if index < 2 else 1 - lat
        if index % 2 == 0:
            squares = (y * 2 + x, jnp.where(core == 0, y * 2 + 1 - x, (1 - y) * 2 + x))
        else:
            squares = (
                jnp.where(core == 0, (1 - y) * 2 + x, y * 2 + 1 - x),
                (1 - y) * 2 + 1 - x,
            )
        for j in range(2 * depth):
            shard = (z + depth - j % depth) % depth * 4 + squares[j // depth]
            row = pl.multiple_of((shard * 2 + core) * half, 16)
            pltpu.make_async_copy(piece.at[j], w_ref.at[pl.ds(row, half), :], sem).start()
    pltpu.make_async_copy(w_ref, w_ref, sem).wait()


def attend_kernel(shifted, row_windows, count, *refs):
    x_ref, pieces = refs[0], refs[1 : 1 + count]
    gain_ref, sharp_ref = refs[1 + count : 3 + count]
    allow_ref = refs[3 + count] if shifted else None
    out_ref, w_ref, vt_ref, sem = refs[-4:]
    features = x_ref.shape[-1]

    @pl.when(pl.program_id(0) == 0)
    def _():
        load_pieces(pieces, w_ref, sem, 0)
        vt_ref[...] = w_ref[:, 2 * features : 3 * features].T

    tokens = x_ref[0]
    queries = dot(tokens, w_ref[:, :features]).astype(jnp.bfloat16).astype(jnp.float32)
    keys = dot(tokens, w_ref[:, features : 2 * features]).astype(jnp.bfloat16).astype(jnp.float32)
    values = dot(vt_ref[...], tokens, NT).astype(jnp.bfloat16)

    channel = lax.broadcasted_iota(jnp.int32, (WIDE, WIDE), 0) // HEAD
    same_head = jnp.where(
        channel == lax.broadcasted_iota(jnp.int32, (WIDE, WIDE), 1) // HEAD, 1.0, 0.0
    ).astype(jnp.bfloat16)
    lane_head = lax.broadcasted_iota(jnp.int32, (1, WIDE), 1) // HEAD
    diagonal = (
        lax.broadcasted_iota(jnp.int32, (WIDE, MAIN), 0) // HEAD
        == lax.broadcasted_iota(jnp.int32, (WIDE, MAIN), 1) // REST
    )
    if shifted:
        last = jnp.logical_and(
            pl.program_id(0) % row_windows == row_windows - 1,
            lax.axis_index("lat") == lax.axis_size("lat") - 1,
        )
        allow = jnp.where(last, allow_ref[...], 1.0)
        allow_main = jnp.concatenate([allow[:, :MAIN]] * 2, 1)
        allow_rest = allow[:, MAIN:]

    def units(part):
        squares = (part * part).astype(jnp.bfloat16)
        length2 = dot(squares, same_head)
        return part * lax.rsqrt(jnp.maximum(length2, 0.25 * HEAD))

    main_rows, rest_rows = [], []
    for group in range(HEADS // GROUP):
        lanes = slice(group * WIDE, (group + 1) * WIDE)
        query = (units(queries[:, lanes]) * sharp_ref[:, lanes]).astype(jnp.bfloat16)
        key = units(keys[:, lanes]).astype(jnp.bfloat16)
        value = values[lanes]

        def masked(rows, head):
            return jnp.where(lane_head == head, rows, jnp.zeros_like(rows))

        def weights(stacked, allowed):
            scores = dot(key, stacked, NT)
            powers = jnp.exp2(scores)
            if shifted:
                powers = powers * allowed
            return powers.astype(jnp.bfloat16), 1.0 / jnp.sum(powers, 0, keepdims=True)

        for pair in range(GROUP // 2):
            stacked = jnp.concatenate(
                [masked(query[:MAIN], 2 * pair), masked(query[:MAIN], 2 * pair + 1)], 0
            )
            weight, inverse = weights(stacked, allow_main if shifted else None)
            both = dot(value[2 * pair * HEAD : 2 * (pair + 1) * HEAD], weight) * inverse
            main_rows += [both[:HEAD, :MAIN], both[HEAD:, MAIN:]]
        stacked = jnp.concatenate([masked(query[MAIN:], head) for head in range(GROUP)], 0)
        weight, inverse = weights(stacked, allow_rest if shifted else None)
        rest = dot(value, weight) * inverse
        rest_rows.append(jnp.where(diagonal, rest, 0.0))
    attended = jnp.concatenate(
        [jnp.concatenate(main_rows, 0).T, jnp.concatenate(rest_rows, 0).T], 0
    ).astype(jnp.bfloat16)
    projected = dot(attended, w_ref[:, 3 * features :])
    rest = projected[MAIN : MAIN + REST]
    for head in range(1, GROUP):
        rest = rest + projected[MAIN + head * REST : MAIN + (head + 1) * REST]
    projected = jnp.concatenate([projected[:MAIN], rest], 0)
    middle = tokens.astype(jnp.float32) + layer_norm(projected, gain_ref[...])
    out_ref[0] = middle.astype(jnp.bfloat16)


def allowed_pairs():
    token = np.arange(CELLS)
    side = token // LEVELS % WLAT >= WLAT // 2
    rest = np.tile(side[MAIN:], GROUP)
    return (side[:, None] == np.concatenate([side[:MAIN], rest])[None, :]).astype(np.float32)


def attend(windows, pieces, gain, sharp, shifted, row_windows):
    count, cells, features = windows.shape
    whole = lambda shape: pl.BlockSpec(shape, lambda i: (0,) * len(shape))
    block = pl.BlockSpec((1, cells, features), lambda i: (i, 0, 0))
    extra = (jnp.asarray(allowed_pairs()),) if shifted else ()
    return pl.pallas_call(
        functools.partial(attend_kernel, shifted, row_windows, len(pieces)),
        grid=(count,),
        out_shape=jax.ShapeDtypeStruct(windows.shape, jnp.bfloat16),
        in_specs=[block]
        + [ANY] * len(pieces)
        + [whole((1, features))] * 2
        + [whole(e.shape) for e in extra],
        out_specs=block,
        scratch_shapes=[
            pltpu.VMEM((features, 4 * features), jnp.bfloat16),
            pltpu.VMEM((features, features), jnp.bfloat16),
            pltpu.SemaphoreType.DMA,
        ],
        compiler_params=pltpu.CompilerParams(vmem_limit_bytes=40 * 2**20),
        cost_estimate=pl.CostEstimate(
            flops=count * 11_000_000_00, bytes_accessed=6_000_000, transcendentals=0
        ),
    )(windows, *pieces, gain, sharp, *extra)


def feed_kernel(count, hidden_size, chunk, *refs):
    x_ref, pieces = refs[0], refs[1 : 1 + count]
    gain_ref, out_ref, w_ref, sem = refs[1 + count :]

    @pl.when(pl.program_id(0) == 0)
    def _():
        load_pieces(pieces, w_ref, sem, 4 * w_ref.shape[0])

    tokens = x_ref[...]
    total = jnp.zeros(tokens.shape, jnp.float32)
    for start in range(0, hidden_size, chunk):
        grown = dot(tokens, w_ref[:, start : start + chunk])
        hidden = jax.nn.gelu(grown).astype(jnp.bfloat16)
        total = total + dot(
            hidden, w_ref[:, hidden_size + start : hidden_size + start + chunk], NT
        )
    result = tokens.astype(jnp.float32) + layer_norm(total, gain_ref[...])
    out_ref[...] = result.astype(jnp.bfloat16)


def feed(rows, pieces, gain, hidden_size):
    count, features = rows.shape
    tile = 2 * CELLS
    block = pl.BlockSpec((tile, features), lambda i: (i, 0))
    return pl.pallas_call(
        functools.partial(feed_kernel, len(pieces), hidden_size, 512),
        grid=(count // tile,),
        out_shape=jax.ShapeDtypeStruct(rows.shape, jnp.bfloat16),
        in_specs=[block]
        + [ANY] * len(pieces)
        + [pl.BlockSpec((1, features), lambda i: (0, 0))],
        out_specs=block,
        scratch_shapes=[
            pltpu.VMEM((features, 2 * hidden_size), jnp.bfloat16),
            pltpu.SemaphoreType.DMA,
        ],
        compiler_params=pltpu.CompilerParams(vmem_limit_bytes=40 * 2**20),
        cost_estimate=pl.CostEstimate(
            flops=4 * count * features * hidden_size, bytes_accessed=8_000_000, transcendentals=0
        ),
    )(rows, *pieces, gain)


def to_windows(cells):
    cols, rows, levels, features = cells.shape
    arranged = cells.reshape(cols // WLON, WLON, rows // WLAT, WLAT, levels, features)
    return arranged.transpose(0, 2, 1, 3, 4, 5).reshape(-1, CELLS, features)


def from_windows(windows, cols, rows):
    features = windows.shape[-1]
    arranged = windows.reshape(cols // WLON, rows // WLAT, WLON, WLAT, LEVELS, features)
    return arranged.transpose(0, 2, 1, 3, 4, 5).reshape(cols, rows, LEVELS, features)


def shift_from(block, lon_step, lat_step):
    lons, lats = lax.axis_size("lon"), lax.axis_size("lat")
    pairs = []
    for lon in range(lons):
        for lat in range(lats):
            source = (lon + lon_step) % lons * lats + (lat + lat_step) % lats
            pairs.append((source, lon * lats + lat))
    return lax.ppermute(block, ("lon", "lat"), pairs)


def roll_on(cells):
    c, r = WLON // 2, WLAT // 2
    ahead = shift_from(cells[:c, r:], 1, 0)
    above = shift_from(cells[c:, :r], 0, 1)
    corner = shift_from(cells[:c, :r], 1, 1)
    return jnp.concatenate(
        [
            jnp.concatenate([cells[c:, r:], ahead], 0),
            jnp.concatenate([above, corner], 0),
        ],
        1,
    )


def roll_back(cells):
    c, r = WLON // 2, WLAT // 2
    behind = shift_from(cells[-c:, :-r], -1, 0)
    below = shift_from(cells[:-c, -r:], 0, -1)
    corner = shift_from(cells[-c:, -r:], -1, -1)
    return jnp.concatenate(
        [
            jnp.concatenate([corner, below], 0),
            jnp.concatenate([behind, cells[:-c, :-r]], 0),
        ],
        1,
    )


def per_device(tokens, qkv_weight, out_weight, up_weight, down_weight, norm_gain, logit_scale):
    cols, rows, _, features = tokens.shape
    hidden_size = up_weight.shape[-1]
    lon_size = lax.axis_size("lon")
    if relayed(qkv_weight.shape[1], lax.axis_size("lat")):
        chunks = cut_chunks(qkv_weight, out_weight, up_weight, down_weight)
        gathered = [lax.all_gather(chunk, ("lon", "lat"), axis=0, tiled=True) for chunk in chunks]
    else:
        weights = (qkv_weight, out_weight, up_weight, down_weight)
        chunks = [jnp.concatenate([weight[block] for weight in weights], 1) for block in range(2)]
        gathered = [lax.all_gather(chunk, "lon", axis=0, tiled=True) for chunk in chunks]
    sharp = jnp.repeat(logit_scale * math.log2(math.e), HEAD, axis=1)

    def block_pass(cells, block, shifted):
        windows = to_windows(cells)
        middle = attend(
            windows,
            [gathered[block]],
            norm_gain[block, :1],
            sharp[block : block + 1],
            shifted,
            rows // WLAT,
        )
        result = feed(
            middle.reshape(-1, features), [gathered[block]], norm_gain[block, 1:], hidden_size
        )
        return from_windows(result.reshape(windows.shape), cols, rows)

    rolled = roll_on(block_pass(tokens, 0, False))
    return roll_back(block_pass(rolled, 1, True))


def solution(mesh):
    placed = (
        P("lon", "lat", None, None),
        P(None, "lon", None),
        P(None, "lon", None),
        P(None, "lon", None),
        P(None, "lon", None),
        P(),
        P(),
    )
    return jax.shard_map(
        per_device,
        mesh=mesh,
        in_specs=placed,
        out_specs=P("lon", "lat", None, None),
        check_vma=False,
    )
```

```python
import functools
import math

import numpy as np

import jax
import jax.numpy as jnp
from jax import lax
from jax.experimental import pallas as pl
from jax.experimental.pallas import tpu as pltpu
from jax.sharding import PartitionSpec as P

HEADS = 16
HEAD = 32
WLON = 12
WLAT = 6
LEVELS = 2
CELLS = WLON * WLAT * LEVELS
MAIN = 128
REST = CELLS - MAIN
GROUP = 8
WIDE = GROUP * HEAD
ANY = pl.BlockSpec(memory_space=pl.ANY)
NT = (((1,), (1,)), ((), ()))


def dot(a, b, dims=(((1,), (0,)), ((), ()))):
    return lax.dot_general(a, b, dims, preferred_element_type=jnp.float32)


def layer_norm(value, gain_row):
    averaged = jnp.mean(value, -1, keepdims=True)
    centred = value - averaged
    variance = jnp.mean(centred * centred, -1, keepdims=True)
    return centred * lax.rsqrt(variance + 1e-05) * gain_row


def relayed(rows, lat_size):
    return lat_size == 2 and rows % 32 == 0


def cut_kernel(half, qkv_ref, out_ref, up_ref, down_ref, *chunks):
    first = pl.multiple_of(lax.axis_index("lat") * half, 16)
    for block, target in enumerate(chunks):
        place = 0
        for source in (qkv_ref, out_ref, up_ref, down_ref):
            width = source.shape[2]
            target[:, place : place + width] = source[block, pl.ds(first, half), :]
            place += width


def cut_chunks(qkv_weight, out_weight, up_weight, down_weight):
    weights = (qkv_weight, out_weight, up_weight, down_weight)
    blocks, rows, _ = qkv_weight.shape
    width = sum(weight.shape[2] for weight in weights)
    return pl.pallas_call(
        functools.partial(cut_kernel, rows // 2),
        out_shape=[jax.ShapeDtypeStruct((rows // 2, width), jnp.bfloat16)] * blocks,
    )(*weights)


def load_pieces(pieces, w_ref, sem, first):
    if len(pieces) == 1:
        copy = pltpu.make_async_copy(pieces[0].at[:, pl.ds(first, w_ref.shape[1])], w_ref, sem)
        copy.start()
        copy.wait()
        return
    depth = pieces[0].shape[0] // 2
    half = pieces[0].shape[1]
    lon, lat = lax.axis_index("lon"), lax.axis_index("lat")
    z, y, x = lon // 4, lon // 2 % 2, lon % 2
    for index, piece in enumerate(pieces):
        core = lat if index < 2 else 1 - lat
        if index % 2 == 0:
            squares = (y * 2 + x, jnp.where(core == 0, y * 2 + 1 - x, (1 - y) * 2 + x))
        else:
            squares = (
                jnp.where(core == 0, (1 - y) * 2 + x, y * 2 + 1 - x),
                (1 - y) * 2 + 1 - x,
            )
        for j in range(2 * depth):
            shard = (z + depth - j % depth) % depth * 4 + squares[j // depth]
            row = pl.multiple_of((shard * 2 + core) * half, 16)
            pltpu.make_async_copy(piece.at[j], w_ref.at[pl.ds(row, half), :], sem).start()
    pltpu.make_async_copy(w_ref, w_ref, sem).wait()


def attend_kernel(shifted, row_windows, count, *refs):
    x_ref, pieces = refs[0], refs[1 : 1 + count]
    gain_ref, sharp_ref, ones_ref = refs[1 + count : 4 + count]
    allow_ref = refs[4 + count] if shifted else None
    out_ref, w_ref, sem = refs[-3:]
    held, _, features = x_ref.shape

    @pl.when(pl.program_id(0) == 0)
    def _():
        load_pieces(pieces, w_ref, sem, 0)

    tokens = x_ref[...].reshape(held * CELLS, features)
    channel = lax.broadcasted_iota(jnp.int32, (WIDE, WIDE), 0) // HEAD
    same_head = jnp.where(
        channel == lax.broadcasted_iota(jnp.int32, (WIDE, WIDE), 1) // HEAD, 1.0, 0.0
    ).astype(jnp.bfloat16)
    lane_head = lax.broadcasted_iota(jnp.int32, (1, WIDE), 1) // HEAD
    masks = [jnp.where(lane_head == head, 1.0, 0.0).astype(jnp.bfloat16) for head in range(GROUP)]

    def units(part):
        rounded = part.astype(jnp.bfloat16)
        length2 = dot(rounded * rounded, same_head)
        return part * lax.rsqrt(jnp.maximum(length2, 0.25 * HEAD))

    attended = [[] for _ in range(held)]
    for group in range(HEADS // GROUP):
        lanes = [slice(n * features + group * WIDE, n * features + (group + 1) * WIDE) for n in range(3)]
        queries = (units(dot(tokens, w_ref[:, lanes[0]])) * sharp_ref[:, lanes[0]]).astype(jnp.bfloat16)
        keys = units(dot(tokens, w_ref[:, lanes[1]])).astype(jnp.bfloat16)
        values = dot(tokens, w_ref[:, lanes[2]]).astype(jnp.bfloat16)
        for window in range(held):
            own = slice(window * CELLS, (window + 1) * CELLS)
            query, key, value = queries[own], keys[own], values[own]
            stacked = jnp.concatenate([query * mask for mask in masks], 0)
            main = jnp.exp2(dot(stacked, key[:MAIN], NT)).astype(jnp.bfloat16)
            rest_keys = jnp.concatenate([key[MAIN:] * mask for mask in masks], 0)
            rest = jnp.exp2(dot(query, rest_keys, NT)).astype(jnp.bfloat16)
            parts = [main[head * CELLS : (head + 1) * CELLS] for head in range(GROUP)] + [rest]
            if shifted:
                last = jnp.logical_and(
                    (pl.program_id(0) * held + window) % row_windows == row_windows - 1,
                    lax.axis_index("lat") == lax.axis_size("lat") - 1,
                )
                allow = jnp.where(last, allow_ref[...], 1.0).astype(jnp.bfloat16)
                parts = [part * allow[:, :MAIN] for part in parts[:-1]] + [rest * allow[:, MAIN:]]
            weights = jnp.concatenate(parts, 1)
            stacked = jnp.concatenate(
                [value[:MAIN] * mask for mask in masks] + [value[MAIN:] * mask for mask in masks], 0
            )
            total = dot(weights, ones_ref[...])
            attended[window].append((dot(weights, stacked) / total).astype(jnp.bfloat16))
    attended = jnp.concatenate([jnp.concatenate(parts, 1) for parts in attended], 0)
    projected = dot(attended, w_ref[:, 3 * features :])
    middle = tokens.astype(jnp.float32) + layer_norm(projected, gain_ref[...])
    out_ref[...] = middle.astype(jnp.bfloat16).reshape(out_ref.shape)


def allowed_pairs():
    token = np.arange(CELLS)
    side = token // LEVELS % WLAT >= WLAT // 2
    rest = np.tile(side[MAIN:], GROUP)
    return (side[:, None] == np.concatenate([side[:MAIN], rest])[None, :]).astype(np.float32)


def head_columns():
    rows = np.concatenate([np.repeat(np.arange(GROUP), MAIN), np.repeat(np.arange(GROUP), REST)])
    return (rows[:, None] == np.arange(WIDE)[None, :] // HEAD).astype(np.float32)


def attend(windows, pieces, gain, sharp, shifted, row_windows, held=2):
    count, cells, features = windows.shape
    whole = lambda shape: pl.BlockSpec(shape, lambda i: (0,) * len(shape))
    block = pl.BlockSpec((held, cells, features), lambda i: (i, 0, 0))
    ones = jnp.asarray(head_columns(), jnp.bfloat16)
    extra = (jnp.asarray(allowed_pairs()),) if shifted else ()
    return pl.pallas_call(
        functools.partial(attend_kernel, shifted, row_windows, len(pieces)),
        grid=(count // held,),
        out_shape=jax.ShapeDtypeStruct(windows.shape, jnp.bfloat16),
        in_specs=[block]
        + [ANY] * len(pieces)
        + [whole((1, features))] * 2
        + [whole(ones.shape)]
        + [whole(e.shape) for e in extra],
        out_specs=block,
        scratch_shapes=[
            pltpu.VMEM((features, 4 * features), jnp.bfloat16),
            pltpu.SemaphoreType.DMA,
        ],
        compiler_params=pltpu.CompilerParams(vmem_limit_bytes=40 * 2**20),
        cost_estimate=pl.CostEstimate(
            flops=count * 1_000_000_000, bytes_accessed=6_000_000, transcendentals=0
        ),
    )(windows, *pieces, gain, sharp, ones, *extra)


def feed_kernel(count, hidden_size, chunk, *refs):
    x_ref, pieces = refs[0], refs[1 : 1 + count]
    gain_ref, out_ref, w_ref, sem = refs[1 + count :]

    @pl.when(pl.program_id(0) == 0)
    def _():
        load_pieces(pieces, w_ref, sem, 4 * w_ref.shape[0])

    tokens = x_ref[...]
    total = jnp.zeros(tokens.shape, jnp.float32)
    for start in range(0, hidden_size, chunk):
        grown = dot(tokens, w_ref[:, start : start + chunk])
        slope = math.sqrt(2.0 / math.pi)
        bent = jnp.tanh(grown * (grown * grown * (0.044715 * slope) + slope))
        hidden = (grown + grown * bent).astype(jnp.bfloat16)
        total = total + dot(
            hidden, w_ref[:, hidden_size + start : hidden_size + start + chunk], NT
        )
    result = tokens.astype(jnp.float32) + layer_norm(0.5 * total, gain_ref[...])
    out_ref[...] = result.astype(jnp.bfloat16)


def feed(rows, pieces, gain, hidden_size):
    count, features = rows.shape
    tile = 2 * CELLS
    block = pl.BlockSpec((tile, features), lambda i: (i, 0))
    return pl.pallas_call(
        functools.partial(feed_kernel, len(pieces), hidden_size, 512),
        grid=(count // tile,),
        out_shape=jax.ShapeDtypeStruct(rows.shape, jnp.bfloat16),
        in_specs=[block]
        + [ANY] * len(pieces)
        + [pl.BlockSpec((1, features), lambda i: (0, 0))],
        out_specs=block,
        scratch_shapes=[
            pltpu.VMEM((features, 2 * hidden_size), jnp.bfloat16),
            pltpu.SemaphoreType.DMA,
        ],
        compiler_params=pltpu.CompilerParams(vmem_limit_bytes=40 * 2**20),
        cost_estimate=pl.CostEstimate(
            flops=4 * count * features * hidden_size, bytes_accessed=8_000_000, transcendentals=0
        ),
    )(rows, *pieces, gain)


def to_windows(cells):
    cols, rows, levels, features = cells.shape
    arranged = cells.reshape(cols // WLON, WLON, rows // WLAT, WLAT, levels, features)
    return arranged.transpose(0, 2, 1, 3, 4, 5).reshape(-1, CELLS, features)


def from_windows(windows, cols, rows):
    features = windows.shape[-1]
    arranged = windows.reshape(cols // WLON, rows // WLAT, WLON, WLAT, LEVELS, features)
    return arranged.transpose(0, 2, 1, 3, 4, 5).reshape(cols, rows, LEVELS, features)


def shift_from(block, lon_step, lat_step):
    lons, lats = lax.axis_size("lon"), lax.axis_size("lat")
    pairs = []
    for lon in range(lons):
        for lat in range(lats):
            source = (lon + lon_step) % lons * lats + (lat + lat_step) % lats
            pairs.append((source, lon * lats + lat))
    return lax.ppermute(block, ("lon", "lat"), pairs)


def roll_on(cells):
    c, r = WLON // 2, WLAT // 2
    ahead = shift_from(cells[:c, r:], 1, 0)
    above = shift_from(cells[c:, :r], 0, 1)
    corner = shift_from(cells[:c, :r], 1, 1)
    return jnp.concatenate(
        [
            jnp.concatenate([cells[c:, r:], ahead], 0),
            jnp.concatenate([above, corner], 0),
        ],
        1,
    )


def roll_back(cells):
    c, r = WLON // 2, WLAT // 2
    behind = shift_from(cells[-c:, :-r], -1, 0)
    below = shift_from(cells[:-c, -r:], 0, -1)
    corner = shift_from(cells[-c:, -r:], -1, -1)
    return jnp.concatenate(
        [
            jnp.concatenate([corner, below], 0),
            jnp.concatenate([behind, cells[:-c, :-r]], 0),
        ],
        1,
    )


def per_device(tokens, qkv_weight, out_weight, up_weight, down_weight, norm_gain, logit_scale):
    cols, rows, _, features = tokens.shape
    hidden_size = up_weight.shape[-1]
    lon_size = lax.axis_size("lon")
    if relayed(qkv_weight.shape[1], lax.axis_size("lat")):
        chunks = cut_chunks(qkv_weight, out_weight, up_weight, down_weight)
        gathered = [lax.all_gather(chunk, ("lon", "lat"), axis=0, tiled=True) for chunk in chunks]
    else:
        weights = (qkv_weight, out_weight, up_weight, down_weight)
        chunks = [jnp.concatenate([weight[block] for weight in weights], 1) for block in range(2)]
        gathered = [lax.all_gather(chunk, "lon", axis=0, tiled=True) for chunk in chunks]
    sharp = jnp.repeat(logit_scale * math.log2(math.e), HEAD, axis=1)

    def block_pass(cells, block, shifted):
        windows = to_windows(cells)
        middle = attend(
            windows,
            [gathered[block]],
            norm_gain[block, :1],
            sharp[block : block + 1],
            shifted,
            rows // WLAT,
        )
        result = feed(
            middle.reshape(-1, features), [gathered[block]], norm_gain[block, 1:], hidden_size
        )
        return from_windows(result.reshape(windows.shape), cols, rows)

    rolled = roll_on(block_pass(tokens, 0, False))
    return roll_back(block_pass(rolled, 1, True))


def solution(mesh):
    placed = (
        P("lon", "lat", None, None),
        P(None, "lon", None),
        P(None, "lon", None),
        P(None, "lon", None),
        P(None, "lon", None),
        P(),
        P(),
    )
    return jax.shard_map(
        per_device,
        mesh=mesh,
        in_specs=placed,
        out_specs=P("lon", "lat", None, None),
        check_vma=False,
    )
```

```python
import functools
import math

import numpy as np

import jax
import jax.numpy as jnp
from jax import lax
from jax.experimental import pallas as pl
from jax.experimental.pallas import tpu as pltpu
from jax.sharding import PartitionSpec as P

HEADS = 16
HEAD = 32
WLON = 12
WLAT = 6
LEVELS = 2
CELLS = WLON * WLAT * LEVELS
MAIN = 128
REST = CELLS - MAIN
GROUP = 8
WIDE = GROUP * HEAD
ANY = pl.BlockSpec(memory_space=pl.ANY)
NT = (((1,), (1,)), ((), ()))


def dot(a, b, dims=(((1,), (0,)), ((), ()))):
    return lax.dot_general(a, b, dims, preferred_element_type=jnp.float32)


def layer_norm(value, gain_row):
    averaged = jnp.mean(value, -1, keepdims=True)
    centred = value - averaged
    variance = jnp.mean(centred * centred, -1, keepdims=True)
    return centred * lax.rsqrt(variance + 1e-05) * gain_row


def relayed(rows, lat_size):
    return lat_size == 2 and rows % 32 == 0


def cut_rows(half, sources, block, target):
    first = pl.multiple_of(lax.axis_index("lat") * half, 16)
    place = 0
    for source in sources:
        width = source.shape[2]
        target[:, place : place + width] = source[block, pl.ds(first, half), :]
        place += width


def first_kernel(half, qkv_ref, out_ref, up_ref, down_ref, early_ref, late_ref):
    cut_rows(half, (qkv_ref, out_ref), 0, early_ref)
    cut_rows(half, (up_ref, down_ref), 1, late_ref)


def first_cut(qkv_weight, out_weight, up_weight, down_weight):
    half = qkv_weight.shape[1] // 2
    widths = (
        qkv_weight.shape[2] + out_weight.shape[2],
        up_weight.shape[2] + down_weight.shape[2],
    )
    return pl.pallas_call(
        functools.partial(first_kernel, half),
        out_shape=[jax.ShapeDtypeStruct((half, width), jnp.bfloat16) for width in widths],
    )(qkv_weight, out_weight, up_weight, down_weight)


def join_kernel(count, block, *refs):
    pieces, sources, column_ref = refs[:count], refs[count:-2], refs[-2]
    for index, piece in enumerate(pieces):
        column_ref[index] = piece[...]
    cut_rows(pieces[0].shape[0], sources, block, refs[-1])


def last_join_kernel(*refs):
    for index, piece in enumerate(refs[:-1]):
        refs[-1][index] = piece[...]


def join(pieces, weights=(), block=0):
    half = pieces[0].shape[0]
    column = jax.ShapeDtypeStruct((len(pieces),) + pieces[0].shape, jnp.bfloat16)
    if not weights:
        return pl.pallas_call(last_join_kernel, out_shape=column)(*pieces), None
    width = sum(weight.shape[2] for weight in weights)
    return pl.pallas_call(
        functools.partial(join_kernel, len(pieces), block),
        out_shape=[column, jax.ShapeDtypeStruct((half, width), jnp.bfloat16)],
    )(*pieces, *weights)


def send(block, lon_size, move):
    pairs = []
    for lon in range(lon_size):
        for core in range(2):
            z, y, x, core_to = move(lon // 4, lon // 2 % 2, lon % 2, core)
            pairs.append((lon * 2 + core, (z * 4 + y * 2 + x) * 2 + core_to))
    return lax.ppermute(block, ("lon", "lat"), pairs)


def along_z(own, lon_size):
    depth = lon_size // 4
    return [own] + [
        send(own, lon_size, lambda z, y, x, c, step=step: ((z + step) % depth, y, x, c))
        for step in range(1, depth)
    ]


def spread(column, lon_size):
    one = lambda z, y, x, c: (z, y, 1 - x, c) if c == 0 else (z, 1 - y, x, c)
    other = lambda z, y, x, c: (z, 1 - y, x, c) if c == 0 else (z, y, 1 - x, c)
    beside = send(column, lon_size, one)
    across = send(column, lon_size, other)
    corner = send(beside, lon_size, other)
    own = [column, beside, across, corner]
    return own + [send(part, lon_size, lambda z, y, x, c: (z, y, x, 1 - c)) for part in own]


def load_pieces(pieces, w_ref, sem, first):
    if len(pieces) == 1:
        copy = pltpu.make_async_copy(pieces[0].at[:, pl.ds(first, w_ref.shape[1])], w_ref, sem)
        copy.start()
        copy.wait()
        return
    depth, half, _ = pieces[0].shape
    lon, lat = lax.axis_index("lon"), lax.axis_index("lat")
    z, y, x = lon // 4, lon // 2 % 2, lon % 2
    by_x, by_y = y * 2 + 1 - x, (1 - y) * 2 + x
    for index, piece in enumerate(pieces):
        core = lat if index < 4 else 1 - lat
        square = (
            y * 2 + x,
            jnp.where(core == 0, by_x, by_y),
            jnp.where(core == 0, by_y, by_x),
            (1 - y) * 2 + 1 - x,
        )[index % 4]
        for step in range(depth):
            shard = (z + depth - step) % depth * 4 + square
            row = pl.multiple_of((shard * 2 + core) * half, 16)
            pltpu.make_async_copy(piece.at[step], w_ref.at[pl.ds(row, half), :], sem).start()
    pltpu.make_async_copy(w_ref, w_ref, sem).wait()


def attend_kernel(shifted, row_windows, count, *refs):
    x_ref, pieces = refs[0], refs[1 : 1 + count]
    gain_ref, sharp_ref, ones_ref = refs[1 + count : 4 + count]
    allow_ref = refs[4 + count] if shifted else None
    out_ref, w_ref, sem = refs[-3:]
    held, _, features = x_ref.shape

    @pl.when(pl.program_id(0) == 0)
    def _():
        load_pieces(pieces, w_ref, sem, 0)

    tokens = x_ref[...].reshape(held * CELLS, features)
    channel = lax.broadcasted_iota(jnp.int32, (WIDE, WIDE), 0) // HEAD
    same_head = jnp.where(
        channel == lax.broadcasted_iota(jnp.int32, (WIDE, WIDE), 1) // HEAD, 1.0, 0.0
    ).astype(jnp.bfloat16)
    lane_head = lax.broadcasted_iota(jnp.int32, (1, WIDE), 1) // HEAD
    masks = [jnp.where(lane_head == head, 1.0, 0.0).astype(jnp.bfloat16) for head in range(GROUP)]

    def units(part):
        rounded = part.astype(jnp.bfloat16)
        length2 = dot(rounded * rounded, same_head)
        return part * lax.rsqrt(jnp.maximum(length2, 0.25 * HEAD))

    attended = [[] for _ in range(held)]
    for group in range(HEADS // GROUP):
        lanes = [slice(n * features + group * WIDE, n * features + (group + 1) * WIDE) for n in range(3)]
        queries = (units(dot(tokens, w_ref[:, lanes[0]])) * sharp_ref[:, lanes[0]]).astype(jnp.bfloat16)
        keys = units(dot(tokens, w_ref[:, lanes[1]])).astype(jnp.bfloat16)
        values = dot(tokens, w_ref[:, lanes[2]]).astype(jnp.bfloat16)
        for window in range(held):
            own = slice(window * CELLS, (window + 1) * CELLS)
            query, key, value = queries[own], keys[own], values[own]
            stacked = jnp.concatenate([query * mask for mask in masks], 0)
            main = jnp.exp2(dot(stacked, key[:MAIN], NT)).astype(jnp.bfloat16)
            rest_keys = jnp.concatenate([key[MAIN:] * mask for mask in masks], 0)
            rest = jnp.exp2(dot(query, rest_keys, NT)).astype(jnp.bfloat16)
            parts = [main[head * CELLS : (head + 1) * CELLS] for head in range(GROUP)] + [rest]
            if shifted:
                last = jnp.logical_and(
                    (pl.program_id(0) * held + window) % row_windows == row_windows - 1,
                    lax.axis_index("lat") == lax.axis_size("lat") - 1,
                )
                allow = jnp.where(last, allow_ref[...], 1.0).astype(jnp.bfloat16)
                parts = [part * allow[:, :MAIN] for part in parts[:-1]] + [rest * allow[:, MAIN:]]
            weights = jnp.concatenate(parts, 1)
            stacked = jnp.concatenate(
                [value[:MAIN] * mask for mask in masks] + [value[MAIN:] * mask for mask in masks], 0
            )
            total = dot(weights, ones_ref[...])
            attended[window].append((dot(weights, stacked) / total).astype(jnp.bfloat16))
    attended = jnp.concatenate([jnp.concatenate(parts, 1) for parts in attended], 0)
    projected = dot(attended, w_ref[:, 3 * features :])
    middle = tokens.astype(jnp.float32) + layer_norm(projected, gain_ref[...])
    out_ref[...] = middle.astype(jnp.bfloat16).reshape(out_ref.shape)


def allowed_pairs():
    token = np.arange(CELLS)
    side = token // LEVELS % WLAT >= WLAT // 2
    rest = np.tile(side[MAIN:], GROUP)
    return (side[:, None] == np.concatenate([side[:MAIN], rest])[None, :]).astype(np.float32)


def head_columns():
    rows = np.concatenate([np.repeat(np.arange(GROUP), MAIN), np.repeat(np.arange(GROUP), REST)])
    return (rows[:, None] == np.arange(WIDE)[None, :] // HEAD).astype(np.float32)


def attend(windows, pieces, gain, sharp, shifted, row_windows, held=2):
    count, cells, features = windows.shape
    whole = lambda shape: pl.BlockSpec(shape, lambda i: (0,) * len(shape))
    block = pl.BlockSpec((held, cells, features), lambda i: (i, 0, 0))
    ones = jnp.asarray(head_columns(), jnp.bfloat16)
    extra = (jnp.asarray(allowed_pairs()),) if shifted else ()
    return pl.pallas_call(
        functools.partial(attend_kernel, shifted, row_windows, len(pieces)),
        grid=(count // held,),
        out_shape=jax.ShapeDtypeStruct(windows.shape, jnp.bfloat16),
        in_specs=[block]
        + [ANY] * len(pieces)
        + [whole((1, features))] * 2
        + [whole(ones.shape)]
        + [whole(e.shape) for e in extra],
        out_specs=block,
        scratch_shapes=[
            pltpu.VMEM((features, 4 * features), jnp.bfloat16),
            pltpu.SemaphoreType.DMA,
        ],
        compiler_params=pltpu.CompilerParams(vmem_limit_bytes=40 * 2**20),
        cost_estimate=pl.CostEstimate(
            flops=count * 1_000_000_000, bytes_accessed=6_000_000, transcendentals=0
        ),
    )(windows, *pieces, gain, sharp, ones, *extra)


def feed_kernel(count, hidden_size, chunk, *refs):
    x_ref, pieces = refs[0], refs[1 : 1 + count]
    gain_ref, out_ref, w_ref, sem = refs[1 + count :]

    @pl.when(pl.program_id(0) == 0)
    def _():
        load_pieces(pieces, w_ref, sem, 0)

    tokens = x_ref[...]
    total = jnp.zeros(tokens.shape, jnp.float32)
    for start in range(0, hidden_size, chunk):
        grown = dot(tokens, w_ref[:, start : start + chunk])
        slope = math.sqrt(2.0 / math.pi)
        bent = jnp.tanh(grown * (grown * grown * (0.044715 * slope) + slope))
        hidden = (grown + grown * bent).astype(jnp.bfloat16)
        total = total + dot(
            hidden, w_ref[:, hidden_size + start : hidden_size + start + chunk], NT
        )
    result = tokens.astype(jnp.float32) + layer_norm(0.5 * total, gain_ref[...])
    out_ref[...] = result.astype(jnp.bfloat16)


def feed(rows, pieces, gain, hidden_size):
    count, features = rows.shape
    tile = 2 * CELLS
    block = pl.BlockSpec((tile, features), lambda i: (i, 0))
    return pl.pallas_call(
        functools.partial(feed_kernel, len(pieces), hidden_size, 512),
        grid=(count // tile,),
        out_shape=jax.ShapeDtypeStruct(rows.shape, jnp.bfloat16),
        in_specs=[block]
        + [ANY] * len(pieces)
        + [pl.BlockSpec((1, features), lambda i: (0, 0))],
        out_specs=block,
        scratch_shapes=[
            pltpu.VMEM((features, 2 * hidden_size), jnp.bfloat16),
            pltpu.SemaphoreType.DMA,
        ],
        compiler_params=pltpu.CompilerParams(vmem_limit_bytes=40 * 2**20),
        cost_estimate=pl.CostEstimate(
            flops=4 * count * features * hidden_size, bytes_accessed=8_000_000, transcendentals=0
        ),
    )(rows, *pieces, gain)


def to_windows(cells):
    cols, rows, levels, features = cells.shape
    arranged = cells.reshape(cols // WLON, WLON, rows // WLAT, WLAT, levels, features)
    return arranged.transpose(0, 2, 1, 3, 4, 5).reshape(-1, CELLS, features)


def from_windows(windows, cols, rows):
    features = windows.shape[-1]
    arranged = windows.reshape(cols // WLON, rows // WLAT, WLON, WLAT, LEVELS, features)
    return arranged.transpose(0, 2, 1, 3, 4, 5).reshape(cols, rows, LEVELS, features)


def shift_from(block, lon_step, lat_step):
    lons, lats = lax.axis_size("lon"), lax.axis_size("lat")
    pairs = []
    for lon in range(lons):
        for lat in range(lats):
            source = (lon + lon_step) % lons * lats + (lat + lat_step) % lats
            pairs.append((source, lon * lats + lat))
    return lax.ppermute(block, ("lon", "lat"), pairs)


def roll_on(cells):
    c, r = WLON // 2, WLAT // 2
    ahead = shift_from(cells[:c, r:], 1, 0)
    above = shift_from(cells[c:, :r], 0, 1)
    corner = shift_from(cells[:c, :r], 1, 1)
    return jnp.concatenate(
        [
            jnp.concatenate([cells[c:, r:], ahead], 0),
            jnp.concatenate([above, corner], 0),
        ],
        1,
    )


def roll_back(cells):
    c, r = WLON // 2, WLAT // 2
    behind = shift_from(cells[-c:, :-r], -1, 0)
    below = shift_from(cells[:-c, -r:], 0, -1)
    corner = shift_from(cells[-c:, -r:], -1, -1)
    return jnp.concatenate(
        [
            jnp.concatenate([corner, below], 0),
            jnp.concatenate([behind, cells[:-c, :-r]], 0),
        ],
        1,
    )


def per_device(tokens, qkv_weight, out_weight, up_weight, down_weight, norm_gain, logit_scale):
    cols, rows, _, features = tokens.shape
    hidden_size = up_weight.shape[-1]
    lon_size = lax.axis_size("lon")
    weights = (qkv_weight, out_weight, up_weight, down_weight)
    if relayed(qkv_weight.shape[1], lax.axis_size("lat")):
        own, late = first_cut(*weights)
        late = [lax.all_gather(late, ("lon", "lat"), axis=0, tiled=True)]
        gathered = []
        for cut, block in ((weights[2:], 0), (weights[:2], 1), ((), 0)):
            column, own = join(along_z(own, lon_size), cut, block)
            gathered.append(spread(column, lon_size))
        gathered.append(late)
    else:
        gathered = []
        for block in range(2):
            for pair in (weights[:2], weights[2:]):
                chunk = jnp.concatenate([weight[block] for weight in pair], 1)
                gathered.append([lax.all_gather(chunk, "lon", axis=0, tiled=True)])
    sharp = jnp.repeat(logit_scale * math.log2(math.e), HEAD, axis=1)

    def block_pass(cells, block, shifted):
        windows = to_windows(cells)
        middle = attend(
            windows,
            gathered[2 * block],
            norm_gain[block, :1],
            sharp[block : block + 1],
            shifted,
            rows // WLAT,
        )
        result = feed(
            middle.reshape(-1, features), gathered[2 * block + 1], norm_gain[block, 1:], hidden_size
        )
        return from_windows(result.reshape(windows.shape), cols, rows)

    rolled = roll_on(block_pass(tokens, 0, False))
    return roll_back(block_pass(rolled, 1, True))


def solution(mesh):
    placed = (
        P("lon", "lat", None, None),
        P(None, "lon", None),
        P(None, "lon", None),
        P(None, "lon", None),
        P(None, "lon", None),
        P(),
        P(),
    )
    return jax.shard_map(
        per_device,
        mesh=mesh,
        in_specs=placed,
        out_specs=P("lon", "lat", None, None),
        check_vma=False,
    )
```

```python
import functools
import math

import numpy as np

import jax
import jax.numpy as jnp
from jax import lax
from jax.experimental import pallas as pl
from jax.experimental.pallas import tpu as pltpu
from jax.sharding import PartitionSpec as P

HEADS = 16
HEAD = 32
WLON = 12
WLAT = 6
LEVELS = 2
CELLS = WLON * WLAT * LEVELS
MAIN = 128
REST = CELLS - MAIN
QUARTER = CELLS // 4
GROUP = 8
WIDE = GROUP * HEAD
ANY = pl.BlockSpec(memory_space=pl.ANY)
NT = (((1,), (1,)), ((), ()))


def dot(a, b, dims=(((1,), (0,)), ((), ()))):
    return lax.dot_general(a, b, dims, preferred_element_type=jnp.float32)


def layer_norm(value, gain_row):
    averaged = jnp.mean(value, -1, keepdims=True)
    centred = value - averaged
    variance = jnp.mean(centred * centred, -1, keepdims=True)
    return centred * lax.rsqrt(variance + 1e-05) * gain_row


def relayed(rows, lat_size):
    return lat_size == 2 and rows % 32 == 0


def join_kernel(count, block, waits, *refs):
    pieces, sources, outs = refs[:count], refs[count:-2], refs[-2:]
    if not count:
        outs = (None, refs[-1])
        sources = refs[:-1]
    sources = sources[: len(sources) - waits]
    for index, piece in enumerate(pieces):
        outs[0][index] = piece[...]
    half = outs[1].shape[0]
    first = pl.multiple_of(lax.axis_index("lat") * half, 16)
    place = 0
    for source in sources:
        width = source.shape[2]
        outs[1][:, place : place + width] = source[block, pl.ds(first, half), :]
        place += width


def last_join_kernel(count, *refs):
    for index, piece in enumerate(refs[:count]):
        refs[-1][index] = piece[...]


def join(pieces, weights=(), block=0, after=()):
    count = len(pieces)
    column = [jax.ShapeDtypeStruct((count,) + piece.shape, jnp.bfloat16) for piece in pieces[:1]]
    held = [pl.BlockSpec(memory_space=pltpu.VMEM)] * (count + len(weights))
    specs = held + [ANY] * len(after)
    if not weights:
        kernel, out_shape = functools.partial(last_join_kernel, count), column
    else:
        kernel = functools.partial(join_kernel, count, block, len(after))
        width = sum(weight.shape[2] for weight in weights)
        chunk = jax.ShapeDtypeStruct((weights[0].shape[1] // 2, width), jnp.bfloat16)
        out_shape = column + [chunk]
    outs = pl.pallas_call(kernel, out_shape=out_shape, in_specs=specs)(*pieces, *weights, *after)
    outs = list(outs)
    return (outs + [None])[:2] if pieces else [None, outs[0]]


def send(block, move):
    pairs = []
    for lon in range(lax.axis_size("lon")):
        for core in range(2):
            z, y, x, core_to = move(lon // 4, lon // 2 % 2, lon % 2, core)
            pairs.append((lon * 2 + core, (z * 4 + y * 2 + x) * 2 + core_to))
    return lax.ppermute(block, ("lon", "lat"), pairs)


def along_z(own):
    depth = lax.axis_size("lon") // 4
    return [own] + [
        send(own, lambda z, y, x, c, step=step: ((z + step) % depth, y, x, c))
        for step in range(1, depth)
    ]


def one_way(z, y, x, c):
    return (z, y, 1 - x, c) if c == 0 else (z, 1 - y, x, c)


def other_way(z, y, x, c):
    return (z, 1 - y, x, c) if c == 0 else (z, y, 1 - x, c)


def swap(z, y, x, c):
    return z, y, x, 1 - c


def tied(array, after):
    return lax.optimization_barrier((array, after))[0]


def whole_pieces(column, beside, across, corner, after=()):
    own = [column, beside, across, corner]
    return own + [send(part, swap) for part in own[:-1]] + [send(tied(corner, after), swap)]


def load_pieces(pieces, w_ref, sem, first):
    if len(pieces) == 1:
        copy = pltpu.make_async_copy(pieces[0].at[:, pl.ds(first, w_ref.shape[1])], w_ref, sem)
        copy.start()
        copy.wait()
        return
    depth, half, _ = pieces[0].shape
    lon, lat = lax.axis_index("lon"), lax.axis_index("lat")
    z, y, x = lon // 4, lon // 2 % 2, lon % 2
    by_x, by_y = y * 2 + 1 - x, (1 - y) * 2 + x
    for index, piece in enumerate(pieces):
        core = lat if index < 4 else 1 - lat
        square = (
            y * 2 + x,
            jnp.where(core == 0, by_x, by_y),
            jnp.where(core == 0, by_y, by_x),
            (1 - y) * 2 + 1 - x,
        )[index % 4]
        for step in range(depth):
            shard = (z + depth - step) % depth * 4 + square
            row = pl.multiple_of((shard * 2 + core) * half, 16)
            pltpu.make_async_copy(piece.at[step], w_ref.at[pl.ds(row, half), :], sem).start()
    pltpu.make_async_copy(w_ref, w_ref, sem).wait()


def rolled_window(left_ref, right_ref, left_low, right_low, place, last):
    quarters = []
    for side, low in ((left_ref, left_low), (right_ref, right_low)):
        quarters.append(side[place, 1].astype(jnp.float32))
        following = side[jnp.minimum(place + 1, last), 0].astype(jnp.float32)
        quarters.append(jnp.where(place == last, low.astype(jnp.float32), following))
    return jnp.concatenate(quarters, 0).astype(jnp.bfloat16)


def attend_kernel(shifted, row_windows, count, lows, *refs):
    sources = 4 if shifted else 1
    x_refs, pieces = refs[:sources], refs[sources : sources + count]
    gain_ref, sharp_ref, ones_ref = refs[sources + count : sources + count + 3]
    allow_ref = refs[sources + count + 3] if shifted else None
    out_ref, w_ref, sem = refs[-3:]
    held, _, features = out_ref.shape

    @pl.when(pl.program_id(0) == 0)
    def _():
        load_pieces(pieces, w_ref, sem, 0)

    if shifted:
        left_ref, right_ref, left_low, right_low = x_refs
        tokens = jnp.concatenate(
            [
                rolled_window(
                    left_ref,
                    right_ref,
                    left_low[lows[0]],
                    right_low[lows[1]],
                    pl.program_id(0) * held + window,
                    row_windows - 1,
                )
                for window in range(held)
            ],
            0,
        )
    else:
        tokens = x_refs[0][...].reshape(held * CELLS, features)
    channel = lax.broadcasted_iota(jnp.int32, (WIDE, WIDE), 0) // HEAD
    same_head = jnp.where(
        channel == lax.broadcasted_iota(jnp.int32, (WIDE, WIDE), 1) // HEAD, 1.0, 0.0
    ).astype(jnp.bfloat16)
    lane_head = lax.broadcasted_iota(jnp.int32, (1, WIDE), 1) // HEAD
    masks = [jnp.where(lane_head == head, 1.0, 0.0).astype(jnp.bfloat16) for head in range(GROUP)]

    def units(part):
        rounded = part.astype(jnp.bfloat16)
        length2 = dot(rounded * rounded, same_head)
        return part * lax.rsqrt(jnp.maximum(length2, 0.25 * HEAD))

    attended = [[] for _ in range(held)]
    for group in range(HEADS // GROUP):
        lanes = [slice(n * features + group * WIDE, n * features + (group + 1) * WIDE) for n in range(3)]
        queries = (units(dot(tokens, w_ref[:, lanes[0]])) * sharp_ref[:, lanes[0]]).astype(jnp.bfloat16)
        keys = units(dot(tokens, w_ref[:, lanes[1]])).astype(jnp.bfloat16)
        values = dot(tokens, w_ref[:, lanes[2]]).astype(jnp.bfloat16)
        for window in range(held):
            own = slice(window * CELLS, (window + 1) * CELLS)
            query, key, value = queries[own], keys[own], values[own]
            stacked = jnp.concatenate([query * mask for mask in masks], 0)
            main = jnp.exp2(dot(stacked, key[:MAIN], NT)).astype(jnp.bfloat16)
            rest_keys = jnp.concatenate([key[MAIN:] * mask for mask in masks], 0)
            rest = jnp.exp2(dot(query, rest_keys, NT)).astype(jnp.bfloat16)
            parts = [main[head * CELLS : (head + 1) * CELLS] for head in range(GROUP)] + [rest]
            if shifted:
                last = jnp.logical_and(
                    (pl.program_id(0) * held + window) % row_windows == row_windows - 1,
                    lax.axis_index("lat") == lax.axis_size("lat") - 1,
                )
                allow = jnp.where(last, allow_ref[...], 1.0).astype(jnp.bfloat16)
                parts = [part * allow[:, :MAIN] for part in parts[:-1]] + [rest * allow[:, MAIN:]]
            weights = jnp.concatenate(parts, 1)
            stacked = jnp.concatenate(
                [value[:MAIN] * mask for mask in masks] + [value[MAIN:] * mask for mask in masks], 0
            )
            total = dot(weights, ones_ref[...])
            attended[window].append((dot(weights, stacked) / total).astype(jnp.bfloat16))
    attended = jnp.concatenate([jnp.concatenate(parts, 1) for parts in attended], 0)
    projected = dot(attended, w_ref[:, 3 * features :])
    middle = tokens.astype(jnp.float32) + layer_norm(projected, gain_ref[...])
    out_ref[...] = middle.astype(jnp.bfloat16).reshape(out_ref.shape)


def allowed_pairs():
    side = np.arange(CELLS) // QUARTER % 2
    rest = np.tile(side[MAIN:], GROUP)
    return (side[:, None] == np.concatenate([side[:MAIN], rest])[None, :]).astype(np.float32)


def head_columns():
    rows = np.concatenate([np.repeat(np.arange(GROUP), MAIN), np.repeat(np.arange(GROUP), REST)])
    return (rows[:, None] == np.arange(WIDE)[None, :] // HEAD).astype(np.float32)


def attend(sources, lows, pieces, gain, sharp, row_windows, after=(), held=2):
    shifted = len(sources) > 1
    features = sources[0].shape[-1]
    whole = lambda shape: pl.BlockSpec(shape, lambda i: (0,) * len(shape))
    block = pl.BlockSpec((held, CELLS, features), lambda i: (i, 0, 0))
    ones = jnp.asarray(head_columns(), jnp.bfloat16)
    extra = (jnp.asarray(allowed_pairs()),) if shifted else ()
    return pl.pallas_call(
        functools.partial(attend_kernel, shifted, row_windows, len(pieces), lows),
        grid=(row_windows // held,),
        out_shape=jax.ShapeDtypeStruct((row_windows, CELLS, features), jnp.bfloat16),
        in_specs=([whole(source.shape) for source in sources] if shifted else [block])
        + [ANY] * len(pieces)
        + [whole((1, features))] * 2
        + [whole(ones.shape)]
        + [whole(e.shape) for e in extra]
        + [ANY] * len(after),
        out_specs=block,
        scratch_shapes=[
            pltpu.VMEM((features, 4 * features), jnp.bfloat16),
            pltpu.SemaphoreType.DMA,
        ],
        compiler_params=pltpu.CompilerParams(vmem_limit_bytes=24 * 2**20),
        cost_estimate=pl.CostEstimate(
            flops=row_windows * 2_000_000_000, bytes_accessed=6_000_000, transcendentals=0
        ),
    )(*sources, *pieces, gain, sharp, ones, *extra, *after)


def feed_kernel(count, hidden_size, chunk, edge, *refs):
    x_ref, pieces, gain_ref = refs[0], refs[1 : 1 + count], refs[1 + count]
    left_ref, right_ref, edge_ref, w_ref, sem = refs[-5:]
    held, _, features = x_ref.shape

    @pl.when(pl.program_id(0) == 0)
    def _():
        load_pieces(pieces, w_ref, sem, 0)

    tokens = x_ref[...].reshape(held * CELLS, features)
    total = jnp.zeros(tokens.shape, jnp.float32)
    for start in range(0, hidden_size, chunk):
        grown = dot(tokens, w_ref[:, start : start + chunk])
        slope = math.sqrt(2.0 / math.pi)
        bent = jnp.tanh(grown * (grown * grown * (0.044715 * slope) + slope))
        hidden = (grown + grown * bent).astype(jnp.bfloat16)
        total = total + dot(
            hidden, w_ref[:, hidden_size + start : hidden_size + start + chunk], NT
        )
    result = tokens.astype(jnp.float32) + layer_norm(0.5 * total, gain_ref[...])
    edge_window, edge_half = edge
    for window in range(held):
        for side, target in enumerate((left_ref, right_ref)):
            for half in range(2):
                start = window * CELLS + (side * 2 + half) * QUARTER
                quarter = result[start : start + QUARTER].astype(jnp.bfloat16)
                target[window, half] = quarter
                if half == edge_half and window == edge_window % held:

                    @pl.when(pl.program_id(0) == edge_window // held)
                    def _(quarter=quarter, side=side):
                        edge_ref[side] = quarter


def feed(windows, pieces, gain, hidden_size, edge, after=(), held=2):
    count, cells, features = windows.shape
    block = pl.BlockSpec((held, cells, features), lambda i: (i, 0, 0))
    side = pl.BlockSpec((held, 2, QUARTER, features), lambda i: (i, 0, 0, 0))
    return pl.pallas_call(
        functools.partial(feed_kernel, len(pieces), hidden_size, 512, edge),
        grid=(count // held,),
        out_shape=[jax.ShapeDtypeStruct((count, 2, QUARTER, features), jnp.bfloat16)] * 2
        + [jax.ShapeDtypeStruct((2, QUARTER, features), jnp.bfloat16)],
        in_specs=[block]
        + [ANY] * len(pieces)
        + [pl.BlockSpec((1, features), lambda i: (0, 0))]
        + [ANY] * len(after),
        out_specs=[side, side, pl.BlockSpec((2, QUARTER, features), lambda i: (0, 0, 0))],
        scratch_shapes=[
            pltpu.VMEM((features, 2 * hidden_size), jnp.bfloat16),
            pltpu.SemaphoreType.DMA,
        ],
        compiler_params=pltpu.CompilerParams(vmem_limit_bytes=24 * 2**20),
        cost_estimate=pl.CostEstimate(
            flops=6 * count * cells * features * hidden_size,
            bytes_accessed=8_000_000,
            transcendentals=0,
        ),
    )(windows, *pieces, gain, *after)


def shift_from(block, lon_step, lat_step):
    lons, lats = lax.axis_size("lon"), lax.axis_size("lat")
    pairs = []
    for lon in range(lons):
        for lat in range(lats):
            source = (lon + lon_step) % lons * lats + (lat + lat_step) % lats
            pairs.append((source, lon * lats + lat))
    return lax.ppermute(block, ("lon", "lat"), pairs)


def to_windows(cells):
    cols, rows, levels, features = cells.shape
    c, r = WLON // 2, WLAT // 2
    arranged = cells.reshape(cols // WLON, 2, c, rows // WLAT, 2, r, levels, features)
    arranged = arranged.transpose(0, 3, 1, 4, 2, 5, 6, 7)
    return arranged.reshape(cols // WLON, rows // WLAT, CELLS, features)


def strip(quarters):
    features = quarters.shape[-1]
    c, r = WLON // 2, WLAT // 2
    arranged = quarters.reshape(-1, c, r, LEVELS, features).transpose(1, 0, 2, 3, 4)
    return arranged.reshape(c, -1, LEVELS, features)


def back_in_place(sides, behind, below, corner):
    features = behind.shape[-1]
    flat = lambda side: side.reshape(-1, QUARTER, features)[:-1]
    c, r = WLON // 2, WLAT // 2
    own = jnp.concatenate([strip(flat(side)) for side in sides[:-1]], 0)
    tops = jnp.concatenate([strip(low[None]) for low in below], 0)
    first = jnp.concatenate([strip(corner[None]), strip(flat(behind))], 1)
    return jnp.concatenate([first, jnp.concatenate([tops, own], 1)], 0)


def per_device(tokens, qkv_weight, out_weight, up_weight, down_weight, norm_gain, logit_scale):
    cols, rows, _, features = tokens.shape
    hidden_size = up_weight.shape[-1]
    row_windows = rows // WLAT
    weights = (qkv_weight, out_weight, up_weight, down_weight)
    relay = relayed(qkv_weight.shape[1], lax.axis_size("lat"))
    sharp = jnp.repeat(logit_scale * math.log2(math.e), HEAD, axis=1)
    windows = to_windows(tokens)

    def attention(block, sources, lows, pieces, after=()):
        return attend(
            sources,
            lows,
            pieces,
            norm_gain[block, :1],
            sharp[block : block + 1],
            row_windows,
            after,
        )

    def forward(block, middle, pieces, edge, after=()):
        return feed(middle, pieces, norm_gain[block, 1:], hidden_size, edge, after)

    low_edge, high_edge = (0, 0), (row_windows - 1, 1)
    if relay:
        _, own = join([], weights[:2], 0)
        column, own = join(along_z(own), weights[2:], 0, (windows,))
        beside, across = send(column, one_way), send(column, other_way)
        corner = send(beside, other_way)
        pieces = whole_pieces(column, beside, across, corner)
        column, own = join(along_z(own), weights[:2], 1, (beside, across))
        beside, across = send(column, one_way), send(column, other_way)
        middle_0 = attention(0, [windows[0]], None, pieces)
        corner = send(tied(beside, middle_0), other_way)
        middle_1 = attention(0, [windows[1]], None, pieces, (middle_0,))
        feed_pieces = whole_pieces(column, beside, across, corner, middle_1)
        column, own = join(along_z(own), weights[2:], 1, (middle_1, beside, across))
        beside, across = send(column, one_way), send(column, other_way)
        left, right, low_0 = forward(0, middle_0, feed_pieces, low_edge)
        corner = send(tied(beside, low_0), other_way)
        last_column, _ = join(along_z(own), (), 0, (low_0, beside, across))
        last_beside, last_across = send(last_column, one_way), send(last_column, other_way)
        left_1, right_1, low_1 = forward(0, middle_1, feed_pieces, low_edge, (low_0,))
        pieces = whole_pieces(column, beside, across, corner, low_1)
        last_corner = send(tied(last_beside, low_1), other_way)
    else:
        gathered = []
        for block in range(2):
            for pair in (weights[:2], weights[2:]):
                chunk = jnp.concatenate([weight[block] for weight in pair], 1)
                gathered.append([lax.all_gather(chunk, "lon", axis=0, tiled=True)])
        first_pieces, feed_pieces, pieces, last_pieces = gathered
        middle_0 = attention(0, [windows[0]], None, first_pieces)
        middle_1 = attention(0, [windows[1]], None, first_pieces)
        left, right, low_0 = forward(0, middle_0, feed_pieces, low_edge)
        left_1, right_1, low_1 = forward(0, middle_1, feed_pieces, low_edge)
    ahead = shift_from(left, 1, 0)
    ahead_low = shift_from(low_0, 1, 1)
    below_0 = shift_from(low_0, 0, 1)
    below_1 = shift_from(low_1, 0, 1)

    middle_0 = attention(1, [right, left_1, below_0, below_1], (1, 0), pieces)
    if relay:
        last_pieces = whole_pieces(last_column, last_beside, last_across, last_corner, middle_0)
    middle_1 = attention(1, [right_1, ahead, below_1, ahead_low], (1, 0), pieces, (middle_0,))
    left_1, right_1, high_1 = forward(1, middle_1, last_pieces, high_edge)
    behind = shift_from(right_1, -1, 0)
    corner = shift_from(high_1, -1, -1)
    above_1 = shift_from(high_1, 0, -1)
    left, right, high_0 = forward(1, middle_0, last_pieces, high_edge, (high_1,))
    above_0 = shift_from(high_0, 0, -1)
    return back_in_place(
        (left, right, left_1, right_1), behind, (above_0[0], above_0[1], above_1[0]), corner[1]
    )


def solution(mesh):
    placed = (
        P("lon", "lat", None, None),
        P(None, "lon", None),
        P(None, "lon", None),
        P(None, "lon", None),
        P(None, "lon", None),
        P(),
        P(),
    )
    return jax.shard_map(
        per_device,
        mesh=mesh,
        in_specs=placed,
        out_specs=P("lon", "lat", None, None),
        check_vma=False,
    )
```

```python
import functools
import math

import numpy as np

import jax
import jax.numpy as jnp
from jax import lax
from jax.experimental import pallas as pl
from jax.experimental.pallas import tpu as pltpu
from jax.sharding import PartitionSpec as P

HEADS = 16
HEAD = 32
WLON = 12
WLAT = 6
LEVELS = 2
CELLS = WLON * WLAT * LEVELS
MAIN = 128
REST = CELLS - MAIN
QUARTER = CELLS // 4
GROUP = 8
WIDE = GROUP * HEAD
ANY = pl.BlockSpec(memory_space=pl.ANY)
NT = (((1,), (1,)), ((), ()))


def dot(a, b, dims=(((1,), (0,)), ((), ()))):
    return lax.dot_general(a, b, dims, preferred_element_type=jnp.float32)


def layer_norm(value, gain_row):
    averaged = jnp.mean(value, -1, keepdims=True)
    centred = value - averaged
    variance = jnp.mean(centred * centred, -1, keepdims=True)
    return centred * lax.rsqrt(variance + 1e-05) * gain_row


def relayed(rows, lat_size):
    return lat_size == 2 and rows % 32 == 0


def join_kernel(sizes, cuts, waits, *refs):
    outs = refs[len(refs) - len(sizes) - len(cuts) :]
    place = 0
    for size, column_ref in zip(sizes, outs):
        for index in range(size):
            column_ref[index] = refs[place + index][...]
        place += size
    for (block, count), chunk_ref in zip(cuts, outs[len(sizes) :]):
        half = chunk_ref.shape[0]
        first = pl.multiple_of(lax.axis_index("lat") * half, 16)
        start = 0
        for source in refs[place : place + count]:
            width = source.shape[2]
            chunk_ref[:, start : start + width] = source[block, pl.ds(first, half), :]
            start += width
        place += count


def join(columns, cuts=(), after=()):
    pieces = [piece for column in columns for piece in column]
    sources = [weight for _, weights in cuts for weight in weights]
    out_shape = [
        jax.ShapeDtypeStruct((len(column),) + column[0].shape, jnp.bfloat16) for column in columns
    ]
    for _, weights in cuts:
        width = sum(weight.shape[2] for weight in weights)
        out_shape.append(jax.ShapeDtypeStruct((weights[0].shape[1] // 2, width), jnp.bfloat16))
    kernel = functools.partial(
        join_kernel,
        [len(column) for column in columns],
        [(block, len(weights)) for block, weights in cuts],
        len(after),
    )
    held = pl.BlockSpec(memory_space=pltpu.VMEM)
    return pl.pallas_call(
        kernel,
        out_shape=out_shape,
        in_specs=[held] * (len(pieces) + len(sources)) + [ANY] * len(after),
        compiler_params=pltpu.CompilerParams(vmem_limit_bytes=8 * 2**20),
    )(*pieces, *sources, *after)


def send(block, move):
    pairs = []
    for lon in range(lax.axis_size("lon")):
        for core in range(2):
            z, y, x, core_to = move(lon // 4, lon // 2 % 2, lon % 2, core)
            pairs.append((lon * 2 + core, (z * 4 + y * 2 + x) * 2 + core_to))
    return lax.ppermute(block, ("lon", "lat"), pairs)


def along_z(own):
    depth = lax.axis_size("lon") // 4
    return [own] + [
        send(own, lambda z, y, x, c, step=step: ((z + step) % depth, y, x, c))
        for step in range(1, depth)
    ]


def swap(z, y, x, c):
    return z, y, x, 1 - c


def tied(array, after):
    return lax.optimization_barrier((array, after))[0]


def to_neighbours(column):
    return [
        send(column, lambda z, y, x, c: (z, y, 1 - x, c)),
        send(column, lambda z, y, x, c: (z, 1 - y, x, c)),
        send(column, lambda z, y, x, c: (z, 1 - y, 1 - x, c)),
    ]


def whole_pieces(column, received, after=None):
    sent = received if after is None else [tied(part, after) for part in received]
    return [column] + received + [send(part, swap) for part in [column] + sent]


def load_pieces(pieces, w_ref, stage_ref, sem):
    if len(pieces) == 1:
        copy = pltpu.make_async_copy(pieces[0], w_ref, sem.at[0])
        copy.start()
        copy.wait()
        return
    depth, half, _ = pieces[0].shape
    copies = [
        pltpu.make_async_copy(piece, stage_ref.at[index], sem.at[index])
        for index, piece in enumerate(pieces)
    ]
    for copy in copies:
        copy.start()
    lon, lat = lax.axis_index("lon"), lax.axis_index("lat")
    z, y, x = lon // 4, lon // 2 % 2, lon % 2
    squares = (y * 2 + x, y * 2 + 1 - x, (1 - y) * 2 + x, (1 - y) * 2 + 1 - x)
    for index, copy in enumerate(copies):
        core = lat if index < 4 else 1 - lat
        copy.wait()
        for step in range(depth):
            shard = (z + depth - step) % depth * 4 + squares[index % 4]
            row = pl.multiple_of((shard * 2 + core) * half, 16)
            w_ref[pl.ds(row, half), :] = stage_ref[index, step]


def load_scratch(pieces, rows, width):
    stage = (len(pieces),) + pieces[0].shape if len(pieces) > 1 else (1, 1, 16, 128)
    return [
        pltpu.VMEM((rows, width), jnp.bfloat16),
        pltpu.VMEM(stage, jnp.bfloat16),
        pltpu.SemaphoreType.DMA((len(pieces),)),
    ]


def rolled_window(place, row_windows, sides, ahead_ref, low_ref, ahead_low_ref):
    (left_0, right_0), (left_1, right_1) = sides
    first = place < row_windows
    row = place % row_windows
    following = jnp.minimum(row + 1, row_windows - 1)
    wide = lambda quarter: quarter.astype(jnp.float32)
    pick = lambda a, b: jnp.where(first, wide(a), wide(b))
    low = lambda quarter, value: jnp.where(row == row_windows - 1, quarter, value)
    quarters = [
        pick(right_0[row, 1], right_1[row, 1]),
        low(pick(low_ref[1], low_ref[3]), pick(right_0[following, 0], right_1[following, 0])),
        pick(left_1[row, 1], ahead_ref[row, 1]),
        low(pick(low_ref[2], ahead_low_ref[0]), pick(left_1[following, 0], ahead_ref[following, 0])),
    ]
    return jnp.concatenate(quarters, 0).astype(jnp.bfloat16)


def attend_kernel(shifted, row_windows, count, *refs):
    sources = 7 if shifted else 1
    x_refs, pieces = refs[:sources], refs[sources : sources + count]
    gain_ref, sharp_ref, ones_ref = refs[sources + count : sources + count + 3]
    allow_ref = refs[sources + count + 3] if shifted else None
    out_ref, w_ref, stage_ref, sem = refs[-4:]
    held, _, features = out_ref.shape

    @pl.when(pl.program_id(0) == 0)
    def _():
        load_pieces(pieces, w_ref, stage_ref, sem)

    if shifted:
        sides = (x_refs[0:2], x_refs[2:4])
        tokens = jnp.concatenate(
            [
                rolled_window(pl.program_id(0) * held + window, row_windows, sides, *x_refs[4:])
                for window in range(held)
            ],
            0,
        )
    else:
        tokens = x_refs[0][...].reshape(held * CELLS, features)
    channel = lax.broadcasted_iota(jnp.int32, (WIDE, WIDE), 0) // HEAD
    same_head = jnp.where(
        channel == lax.broadcasted_iota(jnp.int32, (WIDE, WIDE), 1) // HEAD, 1.0, 0.0
    ).astype(jnp.bfloat16)
    lane_head = lax.broadcasted_iota(jnp.int32, (1, WIDE), 1) // HEAD
    masks = [jnp.where(lane_head == head, 1.0, 0.0).astype(jnp.bfloat16) for head in range(GROUP)]

    def units(part):
        rounded = part.astype(jnp.bfloat16)
        length2 = dot(rounded * rounded, same_head)
        return part * lax.rsqrt(jnp.maximum(length2, 0.25 * HEAD))

    attended = [[] for _ in range(held)]
    for group in range(HEADS // GROUP):
        lanes = [slice(n * features + group * WIDE, n * features + (group + 1) * WIDE) for n in range(3)]
        queries = (units(dot(tokens, w_ref[:, lanes[0]])) * sharp_ref[:, lanes[0]]).astype(jnp.bfloat16)
        keys = units(dot(tokens, w_ref[:, lanes[1]])).astype(jnp.bfloat16)
        values = dot(tokens, w_ref[:, lanes[2]]).astype(jnp.bfloat16)
        for window in range(held):
            own = slice(window * CELLS, (window + 1) * CELLS)
            query, key, value = queries[own], keys[own], values[own]
            stacked = jnp.concatenate([query * mask for mask in masks], 0)
            main = jnp.exp2(dot(stacked, key[:MAIN], NT)).astype(jnp.bfloat16)
            rest_keys = jnp.concatenate([key[MAIN:] * mask for mask in masks], 0)
            rest = jnp.exp2(dot(query, rest_keys, NT)).astype(jnp.bfloat16)
            parts = [main[head * CELLS : (head + 1) * CELLS] for head in range(GROUP)] + [rest]
            if shifted:
                last = jnp.logical_and(
                    (pl.program_id(0) * held + window) % row_windows == row_windows - 1,
                    lax.axis_index("lat") == lax.axis_size("lat") - 1,
                )
                allow = jnp.where(last, allow_ref[...], 1.0).astype(jnp.bfloat16)
                parts = [part * allow[:, :MAIN] for part in parts[:-1]] + [rest * allow[:, MAIN:]]
            weights = jnp.concatenate(parts, 1)
            stacked = jnp.concatenate(
                [value[:MAIN] * mask for mask in masks] + [value[MAIN:] * mask for mask in masks], 0
            )
            total = dot(weights, ones_ref[...])
            attended[window].append((dot(weights, stacked) / total).astype(jnp.bfloat16))
    attended = jnp.concatenate([jnp.concatenate(parts, 1) for parts in attended], 0)
    projected = dot(attended, w_ref[:, 3 * features :])
    middle = tokens.astype(jnp.float32) + layer_norm(projected, gain_ref[...])
    out_ref[...] = middle.astype(jnp.bfloat16).reshape(out_ref.shape)


def allowed_pairs():
    side = np.arange(CELLS) // QUARTER % 2
    rest = np.tile(side[MAIN:], GROUP)
    return (side[:, None] == np.concatenate([side[:MAIN], rest])[None, :]).astype(np.float32)


def head_columns():
    rows = np.concatenate([np.repeat(np.arange(GROUP), MAIN), np.repeat(np.arange(GROUP), REST)])
    return (rows[:, None] == np.arange(WIDE)[None, :] // HEAD).astype(np.float32)


def attend(sources, pieces, gain, sharp, row_windows, after=(), held=2):
    shifted = len(sources) > 1
    features = sources[0].shape[-1]
    count = 2 * row_windows
    whole = lambda shape: pl.BlockSpec(shape, lambda i: (0,) * len(shape))
    block = pl.BlockSpec((held, CELLS, features), lambda i: (i, 0, 0))
    ones = jnp.asarray(head_columns(), jnp.bfloat16)
    extra = (jnp.asarray(allowed_pairs()),) if shifted else ()
    return pl.pallas_call(
        functools.partial(attend_kernel, shifted, row_windows, len(pieces)),
        grid=(count // held,),
        out_shape=jax.ShapeDtypeStruct((count, CELLS, features), jnp.bfloat16),
        in_specs=([whole(source.shape) for source in sources] if shifted else [block])
        + [ANY] * len(pieces)
        + [whole((1, features))] * 2
        + [whole(ones.shape)]
        + [whole(e.shape) for e in extra]
        + [ANY] * len(after),
        out_specs=block,
        scratch_shapes=load_scratch(pieces, features, 4 * features),
        compiler_params=pltpu.CompilerParams(vmem_limit_bytes=24 * 2**20),
        cost_estimate=pl.CostEstimate(
            flops=count * 2_000_000_000, bytes_accessed=6_000_000, transcendentals=0
        ),
    )(*sources, *pieces, gain, sharp, ones, *extra, *after)


def feed_kernel(count, hidden_size, chunk, edge, *refs):
    x_ref, pieces, gain_ref = refs[0], refs[1 : 1 + count], refs[1 + count]
    left_ref, right_ref, edge_ref, w_ref, stage_ref, sem = refs[-6:]
    held, _, features = x_ref.shape

    @pl.when(pl.program_id(0) == 0)
    def _():
        load_pieces(pieces, w_ref, stage_ref, sem)

    tokens = x_ref[...].reshape(held * CELLS, features)
    total = jnp.zeros(tokens.shape, jnp.float32)
    for start in range(0, hidden_size, chunk):
        grown = dot(tokens, w_ref[:, start : start + chunk])
        slope = math.sqrt(2.0 / math.pi)
        bent = jnp.tanh(grown * (grown * grown * (0.044715 * slope) + slope))
        hidden = (grown + grown * bent).astype(jnp.bfloat16)
        total = total + dot(
            hidden, w_ref[:, hidden_size + start : hidden_size + start + chunk], NT
        )
    result = tokens.astype(jnp.float32) + layer_norm(0.5 * total, gain_ref[...])
    edge_window, edge_half = edge
    for window in range(held):
        for side, target in enumerate((left_ref, right_ref)):
            for half in range(2):
                start = window * CELLS + (side * 2 + half) * QUARTER
                quarter = result[start : start + QUARTER].astype(jnp.bfloat16)
                target[window, half] = quarter
                if half == edge_half and window == edge_window % held:

                    @pl.when(pl.program_id(0) == edge_window // held)
                    def _(quarter=quarter, side=side):
                        edge_ref[side] = quarter


def feed(windows, column, pieces, gain, hidden_size, edge, after=(), held=2):
    count, cells, features = windows.shape
    count = count // 2
    block = pl.BlockSpec((held, cells, features), lambda i: (i + column * count // held, 0, 0))
    side = pl.BlockSpec((held, 2, QUARTER, features), lambda i: (i, 0, 0, 0))
    return pl.pallas_call(
        functools.partial(feed_kernel, len(pieces), hidden_size, 512, edge),
        grid=(count // held,),
        out_shape=[jax.ShapeDtypeStruct((count, 2, QUARTER, features), jnp.bfloat16)] * 2
        + [jax.ShapeDtypeStruct((2, QUARTER, features), jnp.bfloat16)],
        in_specs=[block]
        + [ANY] * len(pieces)
        + [pl.BlockSpec((1, features), lambda i: (0, 0))]
        + [ANY] * len(after),
        out_specs=[side, side, pl.BlockSpec((2, QUARTER, features), lambda i: (0, 0, 0))],
        scratch_shapes=load_scratch(pieces, features, 2 * hidden_size),
        compiler_params=pltpu.CompilerParams(vmem_limit_bytes=24 * 2**20),
        cost_estimate=pl.CostEstimate(
            flops=8 * count * cells * features * hidden_size,
            bytes_accessed=8_000_000,
            transcendentals=0,
        ),
    )(windows, *pieces, gain, *after)


def shift_from(block, lon_step, lat_step):
    lons, lats = lax.axis_size("lon"), lax.axis_size("lat")
    pairs = []
    for lon in range(lons):
        for lat in range(lats):
            source = (lon + lon_step) % lons * lats + (lat + lat_step) % lats
            pairs.append((source, lon * lats + lat))
    return lax.ppermute(block, ("lon", "lat"), pairs)


def to_windows(cells):
    cols, rows, levels, features = cells.shape
    c, r = WLON // 2, WLAT // 2
    arranged = cells.reshape(cols // WLON, 2, c, rows // WLAT, 2, r, levels, features)
    arranged = arranged.transpose(0, 3, 1, 4, 2, 5, 6, 7)
    return arranged.reshape(-1, CELLS, features)


def strip(quarters):
    features = quarters.shape[-1]
    c, r = WLON // 2, WLAT // 2
    arranged = quarters.reshape(-1, c, r, LEVELS, features).transpose(1, 0, 2, 3, 4)
    return arranged.reshape(c, -1, LEVELS, features)


def back_in_place(sides, behind, below, corner):
    features = behind.shape[-1]
    flat = lambda side: side.reshape(-1, QUARTER, features)[:-1]
    c, r = WLON // 2, WLAT // 2
    own = jnp.concatenate([strip(flat(side)) for side in sides[:-1]], 0)
    tops = jnp.concatenate([strip(low[None]) for low in below], 0)
    first = jnp.concatenate([strip(corner[None]), strip(flat(behind))], 1)
    return jnp.concatenate([first, jnp.concatenate([tops, own], 1)], 0)


def per_device(tokens, qkv_weight, out_weight, up_weight, down_weight, norm_gain, logit_scale):
    cols, rows, _, features = tokens.shape
    hidden_size = up_weight.shape[-1]
    row_windows = rows // WLAT
    weights = (qkv_weight, out_weight, up_weight, down_weight)
    relay = relayed(qkv_weight.shape[1], lax.axis_size("lat"))
    spread = np.arange(HEADS)[:, None] == np.arange(features)[None, :] // HEAD
    sharp = logit_scale[:, :, None] * jnp.asarray(spread * math.log2(math.e), jnp.float32)[None]
    sharp = jnp.sum(sharp, 1)
    windows = to_windows(tokens)

    def attention(block, sources, pieces, after=()):
        return attend(
            sources, pieces, norm_gain[block, :1], sharp[block : block + 1], row_windows, after
        )

    def forward(block, middle, column, pieces, edge, after=()):
        return feed(middle, column, pieces, norm_gain[block, 1:], hidden_size, edge, after)

    low_edge, high_edge = (0, 0), (row_windows - 1, 1)
    if relay:
        attend_weights, feed_weights = weights[:2], weights[2:]
        (own,) = join([], [(0, attend_weights)])
        column, feed_own, own = join(
            [along_z(own)], [(0, feed_weights), (1, attend_weights)], (windows,)
        )
        pieces = whole_pieces(column, to_neighbours(column))
        feed_column, column, last_own = join(
            [along_z(feed_own), along_z(own)], [(1, feed_weights)]
        )
        feed_received = to_neighbours(feed_column)
        middle = attention(0, [windows], pieces, (feed_column,))
        feed_pieces = whole_pieces(feed_column, feed_received, middle)
        received = to_neighbours(tied(column, middle))
        left_0, right_0, low_0 = forward(0, middle, 0, feed_pieces, low_edge)
        left_1, right_1, low_1 = forward(0, middle, 1, feed_pieces, low_edge, (low_0,))
        pieces = whole_pieces(column, received, low_1)
        (last_column,) = join([along_z(last_own)], (), (low_1,))
        received = to_neighbours(last_column)
        after = (last_column,)
    else:
        gathered = []
        for block in range(2):
            for pair in (weights[:2], weights[2:]):
                chunk = jnp.concatenate([weight[block] for weight in pair], 1)
                gathered.append([lax.all_gather(chunk, "lon", axis=0, tiled=True)])
        first_pieces, feed_pieces, pieces, last_pieces = gathered
        middle = attention(0, [windows], first_pieces)
        left_0, right_0, low_0 = forward(0, middle, 0, feed_pieces, low_edge)
        left_1, right_1, low_1 = forward(0, middle, 1, feed_pieces, low_edge)
        after = ()
    ahead = shift_from(left_0, 1, 0)
    low = jnp.concatenate([low_0, low_1], 0)
    ahead_low = shift_from(low_0, 1, 1)
    below = shift_from(low, 0, 1)
    sources = [left_0, right_0, left_1, right_1, ahead, below, ahead_low]
    middle = attention(1, sources, pieces, after)
    if relay:
        last_pieces = whole_pieces(last_column, received, middle)
    left_1, right_1, high_1 = forward(1, middle, 1, last_pieces, high_edge)
    behind = shift_from(right_1, -1, 0)
    corner = shift_from(high_1, -1, -1)
    left_0, right_0, high_0 = forward(1, middle, 0, last_pieces, high_edge, (high_1,))
    above = shift_from(jnp.concatenate([high_0, high_1], 0), 0, -1)
    return back_in_place(
        (left_0, right_0, left_1, right_1), behind, (above[0], above[1], above[2]), corner[1]
    )


def solution(mesh):
    placed = (
        P("lon", "lat", None, None),
        P(None, "lon", None),
        P(None, "lon", None),
        P(None, "lon", None),
        P(None, "lon", None),
        P(),
        P(),
    )
    return jax.shard_map(
        per_device,
        mesh=mesh,
        in_specs=placed,
        out_specs=P("lon", "lat", None, None),
        check_vma=False,
    )
```

```python
import functools
import math

import numpy as np

import jax
import jax.numpy as jnp
from jax import lax
from jax.experimental import pallas as pl
from jax.experimental.pallas import tpu as pltpu
from jax.sharding import PartitionSpec as P

HEADS = 16
HEAD = 32
WLON = 12
WLAT = 6
LEVELS = 2
CELLS = WLON * WLAT * LEVELS
MAIN = 128
REST = CELLS - MAIN
QUARTER = CELLS // 4
GROUP = 8
PART = 4
WIDE = GROUP * HEAD
ANY = pl.BlockSpec(memory_space=pl.ANY)
NT = (((1,), (1,)), ((), ()))


def dot(a, b, dims=(((1,), (0,)), ((), ()))):
    return lax.dot_general(a, b, dims, preferred_element_type=jnp.float32)


def layer_norm(value, gain_row):
    averaged = jnp.mean(value, -1, keepdims=True)
    centred = value - averaged
    variance = jnp.mean(centred * centred, -1, keepdims=True)
    return centred * lax.rsqrt(variance + 1e-05) * gain_row


def relayed(rows, lon_size, lat_size):
    return lat_size == 2 and rows % 32 == 0 and lon_size == 16


def join_kernel(columns, cuts, *refs):
    outs = refs[len(refs) - sum(len(widths) for _, widths in columns) - len(cuts) :]
    place, out = 0, 0
    for count, widths in columns:
        row = 0
        for piece in refs[place : place + count]:
            start = 0
            for target, width in zip(outs[out : out + len(widths)], widths):
                target[row : row + piece.shape[0]] = piece[:, :, start : start + width]
                start += width
            row += piece.shape[0]
        place, out = place + count, out + len(widths)
    for blocks, chunk_ref in zip(cuts, outs[out:]):
        half = chunk_ref.shape[1]
        first = pl.multiple_of(lax.axis_index("lat") * half, 16)
        start = 0
        for block, source in zip(blocks, refs[place : place + len(blocks)]):
            width = source.shape[2]
            chunk_ref[0, :, start : start + width] = source[block, pl.ds(first, half), :]
            start += width
        place += len(blocks)


def join(columns, cuts=(), after=(), widths=None):
    pieces = [piece for column in columns for piece in column]
    sources = [weight for cut in cuts for _, weight in cut]
    out_shape, sizes = [], []
    for column in columns:
        count, half, width = column[0].shape
        count = sum(piece.shape[0] for piece in column)
        sizes.append((len(column), widths or (width,)))
        for part in widths or (width,):
            out_shape.append(jax.ShapeDtypeStruct((count, half, part), jnp.bfloat16))
    for cut in cuts:
        width = sum(weight.shape[2] for _, weight in cut)
        out_shape.append(jax.ShapeDtypeStruct((1, cut[0][1].shape[1] // 2, width), jnp.bfloat16))
    held = pl.BlockSpec(memory_space=pltpu.VMEM)
    return pl.pallas_call(
        functools.partial(join_kernel, sizes, [[block for block, _ in cut] for cut in cuts]),
        out_shape=out_shape,
        in_specs=[held] * (len(pieces) + len(sources)) + [ANY] * len(after),
        compiler_params=pltpu.CompilerParams(vmem_limit_bytes=10 * 2**20),
    )(*pieces, *sources, *after)


def send(block, move):
    pairs = []
    for lon in range(lax.axis_size("lon")):
        for core in range(2):
            z, y, x, core_to = move(lon // 4, lon // 2 % 2, lon % 2, core)
            pairs.append((lon * 2 + core, (z * 4 + y * 2 + x) * 2 + core_to))
    return lax.ppermute(block, ("lon", "lat"), pairs)


def across_z(block, bit):
    return send(block, lambda z, y, x, c: (z ^ bit, y, x, c))


def along_z(block, after=()):
    bit = 2
    while bit < lax.axis_size("lon") // 4:
        (block,) = join([[block, across_z(block, bit)]], (), after)
        bit *= 2
    return block


def swap(z, y, x, c):
    return z, y, x, 1 - c


def tied(array, after):
    return lax.optimization_barrier((array, after))[0]


def to_neighbours(column):
    return [
        send(column, lambda z, y, x, c: (z, y, 1 - x, c)),
        send(column, lambda z, y, x, c: (z, 1 - y, x, c)),
        send(column, lambda z, y, x, c: (z, 1 - y, 1 - x, c)),
    ]


def whole_pieces(column, received, after=None):
    sent = received if after is None else [tied(part, after) for part in received]
    return [column] + received + [send(part, swap) for part in [column] + sent]


def load_pieces(pieces, w_ref, stage_ref, sem):
    if len(pieces) == 1:
        copy = pltpu.make_async_copy(pieces[0], w_ref, sem.at[0])
        copy.start()
        copy.wait()
        return
    half = pieces[0].shape[-2]
    lon_size = lax.axis_size("lon")
    copies = [
        pltpu.make_async_copy(piece, stage_ref.at[index], sem.at[index])
        for index, piece in enumerate(pieces)
    ]
    for copy in copies:
        copy.start()
    lon, lat = lax.axis_index("lon"), lax.axis_index("lat")
    z, y, x = lon // 4, lon // 2 % 2, lon % 2
    squares = (y * 2 + x, y * 2 + 1 - x, (1 - y) * 2 + x, (1 - y) * 2 + 1 - x)
    joined = len(pieces) == 2
    for index, copy in enumerate(copies):
        core = lat if index < len(pieces) // 2 else 1 - lat
        copy.wait()
        for column in range(4) if joined else (index % 4,):
            for step in range(lon_size // 4):
                shard = (z ^ step) * 4 + squares[column]
                row = pl.multiple_of((shard * 2 + core) * half, 16)
                place = column * (lon_size // 4) + step if joined else step
                w_ref[pl.ds(row, half), :] = stage_ref[index, place]


def load_scratch(pieces, rows, width):
    stage = (len(pieces),) + pieces[0].shape if len(pieces) > 1 else (1, 1, 16, 128)
    return [
        pltpu.VMEM((rows, width), jnp.bfloat16),
        pltpu.VMEM(stage, jnp.bfloat16),
        pltpu.SemaphoreType.DMA((len(pieces),)),
    ]


def rolled_window(place, row_windows, sides, ahead_ref, low_ref, ahead_low_ref):
    (left_0, right_0), (left_1, right_1) = sides
    first = place < row_windows
    row = place % row_windows
    following = jnp.minimum(row + 1, row_windows - 1)
    wide = lambda quarter: quarter.astype(jnp.float32)
    pick = lambda a, b: jnp.where(first, wide(a), wide(b))
    low = lambda quarter, value: jnp.where(row == row_windows - 1, quarter, value)
    quarters = [
        pick(right_0[row, 1], right_1[row, 1]),
        low(pick(low_ref[1], low_ref[3]), pick(right_0[following, 0], right_1[following, 0])),
        pick(left_1[row, 1], ahead_ref[row, 1]),
        low(pick(low_ref[2], ahead_low_ref[0]), pick(left_1[following, 0], ahead_ref[following, 0])),
    ]
    return jnp.concatenate(quarters, 0).astype(jnp.bfloat16)


def attend_kernel(shifted, row_windows, count, *refs):
    sources = 7 if shifted else 1
    x_refs, pieces = refs[:sources], refs[sources : sources + count]
    gain_ref, sharp_ref, ones_ref = refs[sources + count : sources + count + 3]
    allow_ref = refs[sources + count + 3] if shifted else None
    out_ref, w_ref, stage_ref, sem = refs[-4:]
    held, _, features = out_ref.shape

    @pl.when(pl.program_id(0) == 0)
    def _():
        load_pieces(pieces, w_ref, stage_ref, sem)

    if shifted:
        sides = (x_refs[0:2], x_refs[2:4])
        tokens = jnp.concatenate(
            [
                rolled_window(pl.program_id(0) * held + window, row_windows, sides, *x_refs[4:])
                for window in range(held)
            ],
            0,
        )
    else:
        tokens = x_refs[0][...].reshape(held * CELLS, features)
    channel = lax.broadcasted_iota(jnp.int32, (WIDE, WIDE), 0) // HEAD
    same_head = jnp.where(
        channel == lax.broadcasted_iota(jnp.int32, (WIDE, WIDE), 1) // HEAD, 1.0, 0.0
    ).astype(jnp.bfloat16)
    lane_head = lax.broadcasted_iota(jnp.int32, (1, WIDE), 1) // HEAD
    ones = lambda condition: jnp.where(condition, 1.0, 0.0).astype(jnp.bfloat16)
    pairs = [ones(lane_head % PART == head) for head in range(PART)]
    halves = [ones(lane_head // PART == part) for part in range(2)]
    masks = [ones(lane_head == head) for head in range(GROUP)]
    narrow = [ones(lane_head[:, :MAIN] == head) for head in range(PART)]

    def units(part):
        rounded = part.astype(jnp.bfloat16)
        length2 = dot(rounded * rounded, same_head)
        return part * lax.rsqrt(jnp.maximum(length2, 0.25 * HEAD))

    attended = [[] for _ in range(held)]
    for group in range(HEADS // GROUP):
        lanes = [slice(n * features + group * WIDE, n * features + (group + 1) * WIDE) for n in range(3)]
        queries = (units(dot(tokens, w_ref[:, lanes[0]])) * sharp_ref[:, lanes[0]]).astype(jnp.bfloat16)
        keys = units(dot(tokens, w_ref[:, lanes[1]])).astype(jnp.bfloat16)
        values = dot(tokens, w_ref[:, lanes[2]]).astype(jnp.bfloat16)
        for window in range(held):
            own = slice(window * CELLS, (window + 1) * CELLS)
            query, key, value = queries[own], keys[own], values[own]
            stacked = jnp.concatenate([query * pair for pair in pairs], 0)
            main_keys = jnp.concatenate([key[:MAIN] * half for half in halves], 0)
            main = jnp.exp2(dot(stacked, main_keys, NT)).astype(jnp.bfloat16)
            rest_keys = jnp.concatenate([key[MAIN:] * mask for mask in masks], 0)
            rest = jnp.exp2(dot(query, rest_keys, NT)).astype(jnp.bfloat16)
            if shifted:
                last = jnp.logical_and(
                    (pl.program_id(0) * held + window) % row_windows == row_windows - 1,
                    lax.axis_index("lat") == lax.axis_size("lat") - 1,
                )
                allow = jnp.where(last, allow_ref[...], 1.0).astype(jnp.bfloat16)
                rest = rest * allow[:, MAIN:]
            for part in range(2):
                lanes = slice(part * MAIN, (part + 1) * MAIN)
                parts = [main[head * CELLS : (head + 1) * CELLS, lanes] for head in range(PART)]
                if shifted:
                    parts = [one * allow[:, :MAIN] for one in parts]
                own_value = value[:, lanes]
                none = jnp.zeros((REST, MAIN), jnp.bfloat16)
                own_rest = [own_value[MAIN:] * mask for mask in narrow]
                other_rest = [none] * PART
                stacked = jnp.concatenate(
                    [own_value[:MAIN] * mask for mask in narrow]
                    + (own_rest + other_rest if part == 0 else other_rest + own_rest),
                    0,
                )
                both = jnp.concatenate([stacked, ones_ref[:, lanes]], 1)
                summed = dot(jnp.concatenate(parts + [rest], 1), both)
                attended[window].append(
                    (summed[:, :MAIN] / summed[:, MAIN:]).astype(jnp.bfloat16)
                )
    attended = jnp.concatenate([jnp.concatenate(parts, 1) for parts in attended], 0)
    projected = dot(attended, w_ref[:, 3 * features :])
    middle = tokens.astype(jnp.float32) + layer_norm(projected, gain_ref[...])
    out_ref[...] = middle.astype(jnp.bfloat16).reshape(out_ref.shape)


def allowed_pairs():
    side = np.arange(CELLS) // QUARTER % 2
    rest = np.tile(side[MAIN:], GROUP)
    return (side[:, None] == np.concatenate([side[:MAIN], rest])[None, :]).astype(np.float32)


def head_columns():
    halves = []
    for part in range(2):
        own = np.arange(part * PART, (part + 1) * PART)
        rows = np.concatenate([np.repeat(own, MAIN), np.repeat(np.arange(GROUP), REST)])
        halves.append(rows[:, None] == np.repeat(own, HEAD)[None, :])
    return np.concatenate(halves, 1).astype(np.float32)


def attend(sources, pieces, gain, sharp, row_windows, after=(), held=2):
    shifted = len(sources) > 1
    features = sources[0].shape[-1]
    count = 2 * row_windows
    whole = lambda shape: pl.BlockSpec(shape, lambda i: (0,) * len(shape))
    block = pl.BlockSpec((held, CELLS, features), lambda i: (i, 0, 0))
    ones = jnp.asarray(head_columns(), jnp.bfloat16)
    extra = (jnp.asarray(allowed_pairs()),) if shifted else ()
    return pl.pallas_call(
        functools.partial(attend_kernel, shifted, row_windows, len(pieces)),
        grid=(count // held,),
        out_shape=jax.ShapeDtypeStruct((count, CELLS, features), jnp.bfloat16),
        in_specs=([whole(source.shape) for source in sources] if shifted else [block])
        + [ANY] * len(pieces)
        + [whole((1, features))] * 2
        + [whole(ones.shape)]
        + [whole(e.shape) for e in extra]
        + [ANY] * len(after),
        out_specs=block,
        scratch_shapes=load_scratch(pieces, features, 4 * features),
        compiler_params=pltpu.CompilerParams(vmem_limit_bytes=24 * 2**20),
        cost_estimate=pl.CostEstimate(
            flops=count * 2_000_000_000, bytes_accessed=6_000_000, transcendentals=0
        ),
    )(*sources, *pieces, gain, sharp, ones, *extra, *after)


def feed_kernel(count, hidden_size, chunk, edge, *refs):
    x_ref, pieces, gain_ref = refs[0], refs[1 : 1 + count], refs[1 + count]
    left_ref, right_ref, edge_ref, w_ref, stage_ref, sem = refs[-6:]
    held, _, features = x_ref.shape

    @pl.when(pl.program_id(0) == 0)
    def _():
        load_pieces(pieces, w_ref, stage_ref, sem)

    tokens = x_ref[...].reshape(held * CELLS, features)
    total = jnp.zeros(tokens.shape, jnp.float32)
    for start in range(0, hidden_size, chunk):
        grown = dot(tokens, w_ref[:, start : start + chunk])
        slope = math.sqrt(2.0 / math.pi)
        bent = jnp.tanh(grown * (grown * grown * (0.044715 * slope) + slope))
        hidden = (grown + grown * bent).astype(jnp.bfloat16)
        total = total + dot(
            hidden, w_ref[:, hidden_size + start : hidden_size + start + chunk], NT
        )
    result = tokens.astype(jnp.float32) + layer_norm(0.5 * total, gain_ref[...])
    edge_window, edge_half = edge
    for window in range(held):
        for side, target in enumerate((left_ref, right_ref)):
            for half in range(2):
                start = window * CELLS + (side * 2 + half) * QUARTER
                quarter = result[start : start + QUARTER].astype(jnp.bfloat16)
                target[window, half] = quarter
                if half == edge_half and window == edge_window % held:

                    @pl.when(pl.program_id(0) == edge_window // held)
                    def _(quarter=quarter, side=side):
                        edge_ref[side] = quarter


def feed(windows, column, pieces, gain, hidden_size, edge, after=(), held=2):
    count, cells, features = windows.shape
    count = count // 2
    block = pl.BlockSpec((held, cells, features), lambda i: (i + column * count // held, 0, 0))
    side = pl.BlockSpec((held, 2, QUARTER, features), lambda i: (i, 0, 0, 0))
    return pl.pallas_call(
        functools.partial(feed_kernel, len(pieces), hidden_size, 512, edge),
        grid=(count // held,),
        out_shape=[jax.ShapeDtypeStruct((count, 2, QUARTER, features), jnp.bfloat16)] * 2
        + [jax.ShapeDtypeStruct((2, QUARTER, features), jnp.bfloat16)],
        in_specs=[block]
        + [ANY] * len(pieces)
        + [pl.BlockSpec((1, features), lambda i: (0, 0))]
        + [ANY] * len(after),
        out_specs=[side, side, pl.BlockSpec((2, QUARTER, features), lambda i: (0, 0, 0))],
        scratch_shapes=load_scratch(pieces, features, 2 * hidden_size),
        compiler_params=pltpu.CompilerParams(vmem_limit_bytes=24 * 2**20),
        cost_estimate=pl.CostEstimate(
            flops=8 * count * cells * features * hidden_size,
            bytes_accessed=8_000_000,
            transcendentals=0,
        ),
    )(windows, *pieces, gain, *after)


def shift_from(block, lon_step, lat_step):
    lons, lats = lax.axis_size("lon"), lax.axis_size("lat")
    pairs = []
    for lon in range(lons):
        for lat in range(lats):
            source = (lon + lon_step) % lons * lats + (lat + lat_step) % lats
            pairs.append((source, lon * lats + lat))
    return lax.ppermute(block, ("lon", "lat"), pairs)


def to_windows(cells):
    cols, rows, levels, features = cells.shape
    c, r = WLON // 2, WLAT // 2
    arranged = cells.reshape(cols // WLON, 2, c, rows // WLAT, 2, r, levels, features)
    arranged = arranged.transpose(0, 3, 1, 4, 2, 5, 6, 7)
    return arranged.reshape(-1, CELLS, features)


def strip(quarters):
    features = quarters.shape[-1]
    c, r = WLON // 2, WLAT // 2
    arranged = quarters.reshape(-1, c, r, LEVELS, features).transpose(1, 0, 2, 3, 4)
    return arranged.reshape(c, -1, LEVELS, features)


def back_in_place(sides, behind, below, corner):
    features = behind.shape[-1]
    flat = lambda side: side.reshape(-1, QUARTER, features)[:-1]
    c, r = WLON // 2, WLAT // 2
    own = jnp.concatenate([strip(flat(side)) for side in sides], 0)
    tops = jnp.concatenate([strip(low[None]) for low in below], 0)
    first = jnp.concatenate([strip(corner[None]), strip(flat(behind))], 1)
    return jnp.concatenate([first, jnp.concatenate([tops, own], 1)], 0)


def per_device(tokens, qkv_weight, out_weight, up_weight, down_weight, norm_gain, logit_scale):
    cols, rows, _, features = tokens.shape
    hidden_size = up_weight.shape[-1]
    row_windows = rows // WLAT
    weights = (qkv_weight, out_weight, up_weight, down_weight)
    relay = relayed(qkv_weight.shape[1], lax.axis_size("lon"), lax.axis_size("lat"))
    spread = np.arange(HEADS)[:, None] == np.arange(features)[None, :] // HEAD
    sharp = logit_scale[:, :, None] * jnp.asarray(spread * math.log2(math.e), jnp.float32)[None]
    sharp = jnp.sum(sharp, 1)
    windows = to_windows(tokens)

    def attention(block, sources, pieces, after=()):
        return attend(
            sources, pieces, norm_gain[block, :1], sharp[block : block + 1], row_windows, after
        )

    def forward(block, middle, column, pieces, edge, after=()):
        return feed(middle, column, pieces, norm_gain[block, 1:], hidden_size, edge, after)

    low_edge, high_edge = (0, 0), (row_windows - 1, 1)
    if relay:
        (own,) = join([], [[(0, weight) for weight in weights[:2]]])
        later = [(0, weight) for weight in weights[2:]] + [(1, weight) for weight in weights]
        (later_own,) = join([], [later])
        attend_width, feed_width = (
            sum(weight.shape[2] for weight in pair) for pair in (weights[:2], weights[2:])
        )
        (pair,) = join([[own, across_z(own, 1)]], (), (windows,))
        column = along_z(pair)
        pieces = whole_pieces(column, to_neighbours(column))
        feed_pair, last_pair = join(
            [[later_own, across_z(later_own, 1)]], widths=(feed_width, attend_width + feed_width)
        )
        feed_column = along_z(feed_pair)
        feed_received = to_neighbours(feed_column)
        last_pair = tied(last_pair, feed_column)
        last_other = across_z(last_pair, 2)
        middle = attention(0, [windows], pieces, (feed_column,))
        feed_pieces = whole_pieces(feed_column, feed_received, (middle, last_other))
        column, last_column = join(
            [[last_pair, last_other]], (), tuple(feed_pieces[4:]), (attend_width, feed_width)
        )
        received = to_neighbours(column)
        left_0, right_0, low_0 = forward(0, middle, 0, feed_pieces, low_edge, (column,))
        (joined,) = join([[column] + [tied(part, low_0) for part in received]])
        pieces = [joined, send(joined, swap)]
        last_received = to_neighbours(tied(last_column, joined))
        left_1, right_1, low_1 = forward(0, middle, 1, feed_pieces, low_edge, (joined,))
    else:
        gathered = []
        for block in range(2):
            for pair in (weights[:2], weights[2:]):
                chunk = jnp.concatenate([weight[block] for weight in pair], 1)
                gathered.append([lax.all_gather(chunk, "lon", axis=0, tiled=True)])
        first_pieces, feed_pieces, pieces, last_pieces = gathered
        middle = attention(0, [windows], first_pieces)
        left_0, right_0, low_0 = forward(0, middle, 0, feed_pieces, low_edge)
        left_1, right_1, low_1 = forward(0, middle, 1, feed_pieces, low_edge)
    ahead = shift_from(left_0, 1, 0)
    low = jnp.concatenate([low_0, low_1], 0)
    ahead_low = shift_from(low_0, 1, 1)
    below = shift_from(low, 0, 1)
    sources = [left_0, right_0, left_1, right_1, ahead, below, ahead_low]
    middle = attention(1, sources, pieces)
    if relay:
        last_pieces = whole_pieces(last_column, last_received, middle)
    left_1, right_1, high_1 = forward(1, middle, 1, last_pieces, high_edge)
    behind = shift_from(right_1, -1, 0)
    corner = shift_from(high_1, -1, -1)
    left_0, right_0, high_0 = forward(1, middle, 0, last_pieces, high_edge, (high_1,))
    above = shift_from(jnp.concatenate([high_0, high_1], 0), 0, -1)
    sides, above, corner = tied(((left_0, right_0, left_1), above, corner), behind)
    return back_in_place(
        sides, behind, (above[0], above[1], above[2]), corner[1]
    )


def solution(mesh):
    placed = (
        P("lon", "lat", None, None),
        P(None, "lon", None),
        P(None, "lon", None),
        P(None, "lon", None),
        P(None, "lon", None),
        P(),
        P(),
    )
    return jax.shard_map(
        per_device,
        mesh=mesh,
        in_specs=placed,
        out_specs=P("lon", "lat", None, None),
        check_vma=False,
    )
```

```python
import functools
import math

import numpy as np

import jax
import jax.numpy as jnp
from jax import lax
from jax.experimental import pallas as pl
from jax.experimental.pallas import tpu as pltpu
from jax.sharding import PartitionSpec as P

HEADS = 16
HEAD = 32
WLON = 12
WLAT = 6
LEVELS = 2
CELLS = WLON * WLAT * LEVELS
MAIN = 128
REST = CELLS - MAIN
QUARTER = CELLS // 4
GROUP = 8
PART = 4
WIDE = GROUP * HEAD
ANY = pl.BlockSpec(memory_space=pl.ANY)
NT = (((1,), (1,)), ((), ()))


def dot(a, b, dims=(((1,), (0,)), ((), ()))):
    return lax.dot_general(a, b, dims, preferred_element_type=jnp.float32)


def layer_norm(value, gain_row):
    averaged = jnp.mean(value, -1, keepdims=True)
    centred = value - averaged
    variance = jnp.mean(centred * centred, -1, keepdims=True)
    return centred * lax.rsqrt(variance + 1e-05) * gain_row


def relayed(rows, lon_size, lat_size):
    return lat_size == 2 and rows % 32 == 0 and lon_size == 16


def join_kernel(columns, cuts, *refs):
    outs = refs[len(refs) - sum(len(widths) for _, widths in columns) - len(cuts) :]
    place, out = 0, 0
    for count, widths in columns:
        row = 0
        for piece in refs[place : place + count]:
            start = 0
            for target, width in zip(outs[out : out + len(widths)], widths):
                target[row : row + piece.shape[0]] = piece[:, :, start : start + width]
                start += width
            row += piece.shape[0]
        place, out = place + count, out + len(widths)
    for blocks, chunk_ref in zip(cuts, outs[out:]):
        half = chunk_ref.shape[1]
        first = pl.multiple_of(lax.axis_index("lat") * half, 16)
        start = 0
        for block, source in zip(blocks, refs[place : place + len(blocks)]):
            width = source.shape[2]
            chunk_ref[0, :, start : start + width] = source[block, pl.ds(first, half), :]
            start += width
        place += len(blocks)


def join(columns, cuts=(), after=(), widths=None):
    pieces = [piece for column in columns for piece in column]
    sources = [weight for cut in cuts for _, weight in cut]
    out_shape, sizes = [], []
    for column in columns:
        count, half, width = column[0].shape
        count = sum(piece.shape[0] for piece in column)
        sizes.append((len(column), widths or (width,)))
        for part in widths or (width,):
            out_shape.append(jax.ShapeDtypeStruct((count, half, part), jnp.bfloat16))
    for cut in cuts:
        width = sum(weight.shape[2] for _, weight in cut)
        out_shape.append(jax.ShapeDtypeStruct((1, cut[0][1].shape[1] // 2, width), jnp.bfloat16))
    held = pl.BlockSpec(memory_space=pltpu.VMEM)
    return pl.pallas_call(
        functools.partial(join_kernel, sizes, [[block for block, _ in cut] for cut in cuts]),
        out_shape=out_shape,
        in_specs=[held] * (len(pieces) + len(sources)) + [ANY] * len(after),
        compiler_params=pltpu.CompilerParams(vmem_limit_bytes=10 * 2**20),
    )(*pieces, *sources, *after)


def send(block, move):
    pairs = []
    for lon in range(lax.axis_size("lon")):
        for core in range(2):
            z, y, x, core_to = move(lon // 4, lon // 2 % 2, lon % 2, core)
            pairs.append((lon * 2 + core, (z * 4 + y * 2 + x) * 2 + core_to))
    return lax.ppermute(block, ("lon", "lat"), pairs)


def across_z(block, bit):
    return send(block, lambda z, y, x, c: (z ^ bit, y, x, c))


def along_z(block, after=()):
    bit = 2
    while bit < lax.axis_size("lon") // 4:
        (block,) = join([[block, across_z(block, bit)]], (), after)
        bit *= 2
    return block


def swap(z, y, x, c):
    return z, y, x, 1 - c


def tied(array, after):
    return lax.optimization_barrier((array, after))[0]


def beside(z, y, x, c):
    return (z, y, 1 - x, c) if c == 0 else (z, 1 - y, x, c)


def across(z, y, x, c):
    return (z, 1 - y, x, c) if c == 0 else (z, y, 1 - x, c)


def corner(z, y, x, c):
    return z, 1 - y, 1 - x, c


def whole_pieces(column, received, after=None):
    sent = received if after is None else [tied(part, after) for part in received]
    return [column] + received + [send(part, swap) for part in [column] + sent]


def load_pieces(pieces, w_ref, stage_ref, sem):
    if len(pieces) == 1:
        copy = pltpu.make_async_copy(pieces[0], w_ref, sem.at[0])
        copy.start()
        copy.wait()
        return
    half = pieces[0].shape[-2]
    lon_size = lax.axis_size("lon")
    copies = [
        pltpu.make_async_copy(piece, stage_ref.at[index], sem.at[index])
        for index, piece in enumerate(pieces)
    ]
    for copy in copies:
        copy.start()
    lon, lat = lax.axis_index("lon"), lax.axis_index("lat")
    z, y, x = lon // 4, lon // 2 % 2, lon % 2
    by_x, by_y = y * 2 + 1 - x, (1 - y) * 2 + x
    joined = len(pieces) == 2
    for index, copy in enumerate(copies):
        core = lat if index < len(pieces) // 2 else 1 - lat
        squares = (
            y * 2 + x,
            jnp.where(core == 0, by_x, by_y),
            jnp.where(core == 0, by_y, by_x),
            (1 - y) * 2 + 1 - x,
        )
        copy.wait()
        for column in range(4) if joined else (index % 4,):
            for step in range(lon_size // 4):
                shard = (z ^ step) * 4 + squares[column]
                row = pl.multiple_of((shard * 2 + core) * half, 16)
                place = column * (lon_size // 4) + step if joined else step
                w_ref[pl.ds(row, half), :] = stage_ref[index, place]


def load_scratch(pieces, rows, width):
    stage = (len(pieces),) + pieces[0].shape if len(pieces) > 1 else (1, 1, 16, 128)
    return [
        pltpu.VMEM((rows, width), jnp.bfloat16),
        pltpu.VMEM(stage, jnp.bfloat16),
        pltpu.SemaphoreType.DMA((len(pieces),)),
    ]


def rolled_window(place, row_windows, sides, ahead_ref, low_ref, ahead_low_ref):
    (left_0, right_0), (left_1, right_1) = sides
    first = place < row_windows
    row = place % row_windows
    following = jnp.minimum(row + 1, row_windows - 1)
    wide = lambda quarter: quarter.astype(jnp.float32)
    pick = lambda a, b: jnp.where(first, wide(a), wide(b))
    low = lambda quarter, value: jnp.where(row == row_windows - 1, quarter, value)
    quarters = [
        pick(right_0[row, 1], right_1[row, 1]),
        low(pick(low_ref[1], low_ref[3]), pick(right_0[following, 0], right_1[following, 0])),
        pick(left_1[row, 1], ahead_ref[row, 1]),
        low(pick(low_ref[2], ahead_low_ref[0]), pick(left_1[following, 0], ahead_ref[following, 0])),
    ]
    return jnp.concatenate(quarters, 0).astype(jnp.bfloat16)


def attend_kernel(shifted, row_windows, count, *refs):
    sources = 7 if shifted else 1
    x_refs, pieces = refs[:sources], refs[sources : sources + count]
    gain_ref, sharp_ref, ones_ref = refs[sources + count : sources + count + 3]
    allow_ref = refs[sources + count + 3] if shifted else None
    out_ref, w_ref, stage_ref, sem = refs[-4:]
    held, _, features = out_ref.shape

    @pl.when(pl.program_id(0) == 0)
    def _():
        load_pieces(pieces, w_ref, stage_ref, sem)

    if shifted:
        sides = (x_refs[0:2], x_refs[2:4])
        tokens = jnp.concatenate(
            [
                rolled_window(pl.program_id(0) * held + window, row_windows, sides, *x_refs[4:])
                for window in range(held)
            ],
            0,
        )
    else:
        tokens = x_refs[0][...].reshape(held * CELLS, features)
    channel = lax.broadcasted_iota(jnp.int32, (WIDE, WIDE), 0) // HEAD
    same_head = jnp.where(
        channel == lax.broadcasted_iota(jnp.int32, (WIDE, WIDE), 1) // HEAD, 1.0, 0.0
    ).astype(jnp.bfloat16)
    lane_head = lax.broadcasted_iota(jnp.int32, (1, WIDE), 1) // HEAD
    ones = lambda condition: jnp.where(condition, 1.0, 0.0).astype(jnp.bfloat16)
    pairs = [ones(lane_head % PART == head) for head in range(PART)]
    halves = [ones(lane_head // PART == part) for part in range(2)]
    masks = [ones(lane_head == head) for head in range(GROUP)]
    narrow = [ones(lane_head[:, :MAIN] == head) for head in range(PART)]

    def units(part):
        rounded = part.astype(jnp.bfloat16)
        length2 = dot(rounded * rounded, same_head)
        return part * lax.rsqrt(jnp.maximum(length2, 0.25 * HEAD))

    attended = [[] for _ in range(held)]
    for group in range(HEADS // GROUP):
        lanes = [slice(n * features + group * WIDE, n * features + (group + 1) * WIDE) for n in range(3)]
        queries = (units(dot(tokens, w_ref[:, lanes[0]])) * sharp_ref[:, lanes[0]]).astype(jnp.bfloat16)
        keys = units(dot(tokens, w_ref[:, lanes[1]])).astype(jnp.bfloat16)
        values = dot(tokens, w_ref[:, lanes[2]]).astype(jnp.bfloat16)
        for window in range(held):
            own = slice(window * CELLS, (window + 1) * CELLS)
            query, key, value = queries[own], keys[own], values[own]
            stacked = jnp.concatenate([query * pair for pair in pairs], 0)
            main_keys = jnp.concatenate([key[:MAIN] * half for half in halves], 0)
            main = jnp.exp2(dot(stacked, main_keys, NT)).astype(jnp.bfloat16)
            rest_keys = jnp.concatenate([key[MAIN:] * mask for mask in masks], 0)
            rest = jnp.exp2(dot(query, rest_keys, NT)).astype(jnp.bfloat16)
            if shifted:
                last = jnp.logical_and(
                    (pl.program_id(0) * held + window) % row_windows == row_windows - 1,
                    lax.axis_index("lat") == lax.axis_size("lat") - 1,
                )
                allow = jnp.where(last, allow_ref[...], 1.0).astype(jnp.bfloat16)
                rest = rest * allow[:, MAIN:]
            for part in range(2):
                lanes = slice(part * MAIN, (part + 1) * MAIN)
                parts = [main[head * CELLS : (head + 1) * CELLS, lanes] for head in range(PART)]
                if shifted:
                    parts = [one * allow[:, :MAIN] for one in parts]
                own_value = value[:, lanes]
                none = jnp.zeros((REST, MAIN), jnp.bfloat16)
                own_rest = [own_value[MAIN:] * mask for mask in narrow]
                other_rest = [none] * PART
                stacked = jnp.concatenate(
                    [own_value[:MAIN] * mask for mask in narrow]
                    + (own_rest + other_rest if part == 0 else other_rest + own_rest),
                    0,
                )
                both = jnp.concatenate([stacked, ones_ref[:, lanes]], 1)
                summed = dot(jnp.concatenate(parts + [rest], 1), both)
                attended[window].append(
                    (summed[:, :MAIN] / summed[:, MAIN:]).astype(jnp.bfloat16)
                )
    attended = jnp.concatenate([jnp.concatenate(parts, 1) for parts in attended], 0)
    projected = dot(attended, w_ref[:, 3 * features :])
    middle = tokens.astype(jnp.float32) + layer_norm(projected, gain_ref[...])
    out_ref[...] = middle.astype(jnp.bfloat16).reshape(out_ref.shape)


def allowed_pairs():
    side = np.arange(CELLS) // QUARTER % 2
    rest = np.tile(side[MAIN:], GROUP)
    return (side[:, None] == np.concatenate([side[:MAIN], rest])[None, :]).astype(np.float32)


def head_columns():
    halves = []
    for part in range(2):
        own = np.arange(part * PART, (part + 1) * PART)
        rows = np.concatenate([np.repeat(own, MAIN), np.repeat(np.arange(GROUP), REST)])
        halves.append(rows[:, None] == np.repeat(own, HEAD)[None, :])
    return np.concatenate(halves, 1).astype(np.float32)


def attend(sources, pieces, gain, sharp, row_windows, after=(), held=2):
    shifted = len(sources) > 1
    features = sources[0].shape[-1]
    count = 2 * row_windows
    whole = lambda shape: pl.BlockSpec(shape, lambda i: (0,) * len(shape))
    block = pl.BlockSpec((held, CELLS, features), lambda i: (i, 0, 0))
    ones = jnp.asarray(head_columns(), jnp.bfloat16)
    extra = (jnp.asarray(allowed_pairs()),) if shifted else ()
    return pl.pallas_call(
        functools.partial(attend_kernel, shifted, row_windows, len(pieces)),
        grid=(count // held,),
        out_shape=jax.ShapeDtypeStruct((count, CELLS, features), jnp.bfloat16),
        in_specs=([whole(source.shape) for source in sources] if shifted else [block])
        + [ANY] * len(pieces)
        + [whole((1, features))] * 2
        + [whole(ones.shape)]
        + [whole(e.shape) for e in extra]
        + [ANY] * len(after),
        out_specs=block,
        scratch_shapes=load_scratch(pieces, features, 4 * features),
        compiler_params=pltpu.CompilerParams(vmem_limit_bytes=24 * 2**20),
        cost_estimate=pl.CostEstimate(
            flops=count * 2_000_000_000, bytes_accessed=6_000_000, transcendentals=0
        ),
    )(*sources, *pieces, gain, sharp, ones, *extra, *after)


def feed_kernel(count, hidden_size, chunk, edge, *refs):
    x_ref, pieces, gain_ref = refs[0], refs[1 : 1 + count], refs[1 + count]
    left_ref, right_ref, edge_ref, w_ref, stage_ref, sem = refs[-6:]
    held, _, features = x_ref.shape

    @pl.when(pl.program_id(0) == 0)
    def _():
        load_pieces(pieces, w_ref, stage_ref, sem)

    tokens = x_ref[...].reshape(held * CELLS, features)
    total = jnp.zeros(tokens.shape, jnp.float32)
    for start in range(0, hidden_size, chunk):
        grown = dot(tokens, w_ref[:, start : start + chunk])
        slope = math.sqrt(2.0 / math.pi)
        bent = jnp.tanh(grown * (grown * grown * (0.044715 * slope) + slope))
        hidden = (grown + grown * bent).astype(jnp.bfloat16)
        total = total + dot(
            hidden, w_ref[:, hidden_size + start : hidden_size + start + chunk], NT
        )
    result = tokens.astype(jnp.float32) + layer_norm(0.5 * total, gain_ref[...])
    edge_window, edge_half = edge
    for window in range(held):
        for side, target in enumerate((left_ref, right_ref)):
            for half in range(2):
                start = window * CELLS + (side * 2 + half) * QUARTER
                quarter = result[start : start + QUARTER].astype(jnp.bfloat16)
                target[window, half] = quarter
                if half == edge_half and window == edge_window % held:

                    @pl.when(pl.program_id(0) == edge_window // held)
                    def _(quarter=quarter, side=side):
                        edge_ref[side] = quarter


def feed(windows, column, pieces, gain, hidden_size, edge, after=(), held=2):
    count, cells, features = windows.shape
    count = count // 2
    block = pl.BlockSpec((held, cells, features), lambda i: (i + column * count // held, 0, 0))
    side = pl.BlockSpec((held, 2, QUARTER, features), lambda i: (i, 0, 0, 0))
    return pl.pallas_call(
        functools.partial(feed_kernel, len(pieces), hidden_size, 512, edge),
        grid=(count // held,),
        out_shape=[jax.ShapeDtypeStruct((count, 2, QUARTER, features), jnp.bfloat16)] * 2
        + [jax.ShapeDtypeStruct((2, QUARTER, features), jnp.bfloat16)],
        in_specs=[block]
        + [ANY] * len(pieces)
        + [pl.BlockSpec((1, features), lambda i: (0, 0))]
        + [ANY] * len(after),
        out_specs=[side, side, pl.BlockSpec((2, QUARTER, features), lambda i: (0, 0, 0))],
        scratch_shapes=load_scratch(pieces, features, 2 * hidden_size),
        compiler_params=pltpu.CompilerParams(vmem_limit_bytes=24 * 2**20),
        cost_estimate=pl.CostEstimate(
            flops=8 * count * cells * features * hidden_size,
            bytes_accessed=8_000_000,
            transcendentals=0,
        ),
    )(windows, *pieces, gain, *after)


def shift_from(block, lon_step, lat_step):
    lons, lats = lax.axis_size("lon"), lax.axis_size("lat")
    pairs = []
    for lon in range(lons):
        for lat in range(lats):
            source = (lon + lon_step) % lons * lats + (lat + lat_step) % lats
            pairs.append((source, lon * lats + lat))
    return lax.ppermute(block, ("lon", "lat"), pairs)


def to_windows(cells):
    cols, rows, levels, features = cells.shape
    c, r = WLON // 2, WLAT // 2
    arranged = cells.reshape(cols // WLON, 2, c, rows // WLAT, 2, r, levels, features)
    arranged = arranged.transpose(0, 3, 1, 4, 2, 5, 6, 7)
    return arranged.reshape(-1, CELLS, features)


def strip(quarters):
    features = quarters.shape[-1]
    c, r = WLON // 2, WLAT // 2
    arranged = quarters.reshape(-1, c, r, LEVELS, features).transpose(1, 0, 2, 3, 4)
    return arranged.reshape(c, -1, LEVELS, features)


def back_in_place(sides, behind, above, high):
    features = behind.shape[-1]
    flat = lambda side: side.reshape(-1, QUARTER, features)[:-1]
    c, r = WLON // 2, WLAT // 2
    own = jnp.concatenate([strip(flat(side)) for side in sides], 0)
    tops = jnp.concatenate([strip(low[None]) for low in above], 0)
    first = jnp.concatenate([strip(high[None]), strip(flat(behind))], 1)
    return jnp.concatenate([first, jnp.concatenate([tops, own], 1)], 0)


def per_device(tokens, qkv_weight, out_weight, up_weight, down_weight, norm_gain, logit_scale):
    cols, rows, _, features = tokens.shape
    hidden_size = up_weight.shape[-1]
    row_windows = rows // WLAT
    weights = (qkv_weight, out_weight, up_weight, down_weight)
    relay = relayed(qkv_weight.shape[1], lax.axis_size("lon"), lax.axis_size("lat"))
    spread = np.arange(HEADS)[:, None] == np.arange(features)[None, :] // HEAD
    sharp = logit_scale[:, :, None] * jnp.asarray(spread * math.log2(math.e), jnp.float32)[None]
    sharp = jnp.sum(sharp, 1)
    windows = to_windows(tokens)

    def attention(block, sources, pieces, after=()):
        return attend(
            sources, pieces, norm_gain[block, :1], sharp[block : block + 1], row_windows, after
        )

    def forward(block, middle, column, pieces, edge, after=()):
        return feed(middle, column, pieces, norm_gain[block, 1:], hidden_size, edge, after)

    low_edge, high_edge = (0, 0), (row_windows - 1, 1)
    if relay:
        (own,) = join([], [[(0, weight) for weight in weights[:2]]])
        later = [(0, weight) for weight in weights[2:]] + [(1, weight) for weight in weights]
        (later_own,) = join([], [later])
        attend_width, feed_width = (
            sum(weight.shape[2] for weight in pair) for pair in (weights[:2], weights[2:])
        )
        (pair,) = join([[own, across_z(own, 1)]], (), (windows,))
        column = along_z(pair)
        pieces = whole_pieces(column, [send(column, way) for way in (beside, across, corner)])
        feed_pair, last_pair = join(
            [[later_own, across_z(later_own, 1)]], widths=(feed_width, attend_width + feed_width)
        )
        feed_column = along_z(feed_pair)
        received = [send(feed_column, way) for way in (beside, across)]
        last_pair = tied(last_pair, feed_column)
        last_other = across_z(last_pair, 2)
        middle = attention(0, [windows], pieces, (feed_column,))
        received.append(send(tied(received[0], (middle, last_other)), across))
        feed_pieces = whole_pieces(feed_column, received, middle)
        column, last_column = join(
            [[last_pair, last_other]], (), (received[2],), (attend_width, feed_width)
        )
        received = [send(column, way) for way in (beside, across)]
        left_0, right_0, low_0 = forward(0, middle, 0, feed_pieces, low_edge, (column,))
        received.append(send(tied(received[0], low_0), across))
        last_column = tied(last_column, (low_0, received[1]))
        last_received = [send(last_column, way) for way in (beside, across, corner)]
        ahead, ahead_low = shift_from(left_0, 1, 0), shift_from(low_0, 1, 1)
        left_1, right_1, low_1 = forward(0, middle, 1, feed_pieces, low_edge, (low_0, received[1]))
        (joined,) = join([[column] + [tied(part, (low_1, ahead, ahead_low)) for part in received]])
        pieces = [joined, send(joined, swap)]
    else:
        gathered = []
        for block in range(2):
            for pair in (weights[:2], weights[2:]):
                chunk = jnp.concatenate([weight[block] for weight in pair], 1)
                gathered.append([lax.all_gather(chunk, "lon", axis=0, tiled=True)])
        first_pieces, feed_pieces, pieces, last_pieces = gathered
        middle = attention(0, [windows], first_pieces)
        left_0, right_0, low_0 = forward(0, middle, 0, feed_pieces, low_edge)
        left_1, right_1, low_1 = forward(0, middle, 1, feed_pieces, low_edge)
        ahead, ahead_low = shift_from(left_0, 1, 0), shift_from(low_0, 1, 1)
    below = shift_from(tied(jnp.concatenate([low_0, low_1], 0), ahead_low), 0, 1)
    sources = [left_0, right_0, left_1, right_1, ahead, below, ahead_low]
    middle = attention(1, sources, pieces)
    if relay:
        last_pieces = whole_pieces(last_column, last_received, middle)
    left_1, right_1, high_1 = forward(1, middle, 1, last_pieces, high_edge)
    behind = shift_from(right_1, -1, 0)
    behind_high = shift_from(high_1, -1, -1)
    left_0, right_0, high_0 = forward(1, middle, 0, last_pieces, high_edge, (high_1,))
    above = shift_from(tied(jnp.concatenate([high_0, high_1], 0), behind_high), 0, -1)
    sides, above, behind_high = tied(((left_0, right_0, left_1), above, behind_high), behind)
    return back_in_place(sides, behind, (above[0], above[1], above[2]), behind_high[1])


def solution(mesh):
    placed = (
        P("lon", "lat", None, None),
        P(None, "lon", None),
        P(None, "lon", None),
        P(None, "lon", None),
        P(None, "lon", None),
        P(),
        P(),
    )
    return jax.shard_map(
        per_device,
        mesh=mesh,
        in_specs=placed,
        out_specs=P("lon", "lat", None, None),
        check_vma=False,
    )
```

```python
import functools
import math

import numpy as np

import jax
import jax.numpy as jnp
from jax import lax
from jax.experimental import pallas as pl
from jax.experimental.pallas import tpu as pltpu
from jax.sharding import PartitionSpec as P

HEADS = 16
HEAD = 32
WLON = 12
WLAT = 6
LEVELS = 2
CELLS = WLON * WLAT * LEVELS
MAIN = 128
REST = CELLS - MAIN
QUARTER = CELLS // 4
GROUP = 8
PART = 4
WIDE = GROUP * HEAD
Z_ORDER = (0, 2, 1, 3)
ANY = pl.BlockSpec(memory_space=pl.ANY)
NT = (((1,), (1,)), ((), ()))


def dot(a, b, dims=(((1,), (0,)), ((), ()))):
    return lax.dot_general(a, b, dims, preferred_element_type=jnp.float32)


def layer_norm(value, gain_row):
    averaged = jnp.mean(value, -1, keepdims=True)
    centred = value - averaged
    variance = jnp.mean(centred * centred, -1, keepdims=True)
    return centred * lax.rsqrt(variance + 1e-05) * gain_row


def relayed(rows, lon_size, lat_size):
    return lat_size == 2 and rows % 32 == 0 and lon_size == 16


def join_kernel(columns, cuts, *refs):
    outs = refs[len(refs) - sum(len(widths) for _, widths in columns) - len(cuts) :]
    place, out = 0, 0
    for count, widths in columns:
        row = 0
        for piece in refs[place : place + count]:
            start = 0
            for target, width in zip(outs[out : out + len(widths)], widths):
                target[row : row + piece.shape[0]] = piece[:, :, start : start + width]
                start += width
            row += piece.shape[0]
        place, out = place + count, out + len(widths)
    for blocks, chunk_ref in zip(cuts, outs[out:]):
        half = chunk_ref.shape[1]
        first = pl.multiple_of(lax.axis_index("lat") * half, 16)
        start = 0
        for block, source in zip(blocks, refs[place : place + len(blocks)]):
            width = source.shape[2]
            chunk_ref[0, :, start : start + width] = source[block, pl.ds(first, half), :]
            start += width
        place += len(blocks)


def join(columns, cuts=(), after=(), widths=None):
    pieces = [piece for column in columns for piece in column]
    sources = [weight for cut in cuts for _, weight in cut]
    out_shape, sizes = [], []
    for column in columns:
        count, half, width = column[0].shape
        count = sum(piece.shape[0] for piece in column)
        sizes.append((len(column), widths or (width,)))
        for part in widths or (width,):
            out_shape.append(jax.ShapeDtypeStruct((count, half, part), jnp.bfloat16))
    for cut in cuts:
        width = sum(weight.shape[2] for _, weight in cut)
        out_shape.append(jax.ShapeDtypeStruct((1, cut[0][1].shape[1] // 2, width), jnp.bfloat16))
    held = pl.BlockSpec(memory_space=pltpu.VMEM)
    return pl.pallas_call(
        functools.partial(join_kernel, sizes, [[block for block, _ in cut] for cut in cuts]),
        out_shape=out_shape,
        in_specs=[held] * (len(pieces) + len(sources)) + [ANY] * len(after),
        compiler_params=pltpu.CompilerParams(vmem_limit_bytes=10 * 2**20),
    )(*pieces, *sources, *after)


def send(block, move):
    pairs = []
    for lon in range(lax.axis_size("lon")):
        for core in range(2):
            z, y, x, core_to = move(lon // 4, lon // 2 % 2, lon % 2, core)
            pairs.append((lon * 2 + core, (z * 4 + y * 2 + x) * 2 + core_to))
    return lax.ppermute(block, ("lon", "lat"), pairs)


def across_z(block, bit):
    return send(block, lambda z, y, x, c: (z ^ bit, y, x, c))


def swap(z, y, x, c):
    return z, y, x, 1 - c


def tied(array, after):
    return lax.optimization_barrier((array, after))[0]


def beside(z, y, x, c):
    return (z, y, 1 - x, c) if c == 0 else (z, 1 - y, x, c)


def across(z, y, x, c):
    return (z, 1 - y, x, c) if c == 0 else (z, y, 1 - x, c)


def corner(z, y, x, c):
    return z, 1 - y, 1 - x, c


def whole_pieces(column, received, after=None):
    sent = received if after is None else [tied(part, after) for part in received]
    return [column] + received + [send(part, swap) for part in [column] + sent]


def load_pieces(pieces, w_ref, stage_ref, sem):
    if len(pieces) == 1:
        copy = pltpu.make_async_copy(pieces[0], w_ref, sem.at[0])
        copy.start()
        copy.wait()
        return
    half = pieces[0].shape[-2]
    copies = [
        pltpu.make_async_copy(piece, stage_ref.at[index], sem.at[index])
        for index, piece in enumerate(pieces)
    ]
    for copy in copies:
        copy.start()
    lon, lat = lax.axis_index("lon"), lax.axis_index("lat")
    z, y, x = lon // 4, lon // 2 % 2, lon % 2
    by_x, by_y = y * 2 + 1 - x, (1 - y) * 2 + x
    joined = len(pieces) == 2
    for index, copy in enumerate(copies):
        core = lat if index < len(pieces) // 2 else 1 - lat
        squares = (
            y * 2 + x,
            jnp.where(core == 0, by_x, by_y),
            jnp.where(core == 0, by_y, by_x),
            (1 - y) * 2 + 1 - x,
        )
        copy.wait()
        for column in range(4) if joined else (index % 4,):
            for step in range(len(Z_ORDER)):
                shard = (z ^ Z_ORDER[step]) * 4 + squares[column]
                row = pl.multiple_of((shard * 2 + core) * half, 16)
                place = column * len(Z_ORDER) + step if joined else step
                w_ref[pl.ds(row, half), :] = stage_ref[index, place]


def load_scratch(pieces, rows, width):
    stage = (len(pieces),) + pieces[0].shape if len(pieces) > 1 else (1, 1, 16, 128)
    return [
        pltpu.VMEM((rows, width), jnp.bfloat16),
        pltpu.VMEM(stage, jnp.bfloat16),
        pltpu.SemaphoreType.DMA((len(pieces),)),
    ]


def rolled_window(place, row_windows, sides, ahead_ref, low_ref, ahead_low_ref):
    (left_0, right_0), (left_1, right_1) = sides
    first = place < row_windows
    row = place % row_windows
    following = jnp.minimum(row + 1, row_windows - 1)
    wide = lambda quarter: quarter.astype(jnp.float32)
    pick = lambda a, b: jnp.where(first, wide(a), wide(b))
    low = lambda quarter, value: jnp.where(row == row_windows - 1, quarter, value)
    quarters = [
        pick(right_0[row, 1], right_1[row, 1]),
        low(pick(low_ref[1], low_ref[3]), pick(right_0[following, 0], right_1[following, 0])),
        pick(left_1[row, 1], ahead_ref[row, 1]),
        low(pick(low_ref[2], ahead_low_ref[0]), pick(left_1[following, 0], ahead_ref[following, 0])),
    ]
    return jnp.concatenate(quarters, 0).astype(jnp.bfloat16)


def attend_kernel(shifted, row_windows, count, *refs):
    sources = 7 if shifted else 1
    x_refs, pieces = refs[:sources], refs[sources : sources + count]
    gain_ref, sharp_ref, ones_ref = refs[sources + count : sources + count + 3]
    allow_ref = refs[sources + count + 3] if shifted else None
    out_ref, w_ref, stage_ref, sem = refs[-4:]
    held, _, features = out_ref.shape

    @pl.when(pl.program_id(0) == 0)
    def _():
        load_pieces(pieces, w_ref, stage_ref, sem)

    if shifted:
        sides = (x_refs[0:2], x_refs[2:4])
        tokens = jnp.concatenate(
            [
                rolled_window(pl.program_id(0) * held + window, row_windows, sides, *x_refs[4:])
                for window in range(held)
            ],
            0,
        )
    else:
        tokens = x_refs[0][...].reshape(held * CELLS, features)
    channel = lax.broadcasted_iota(jnp.int32, (WIDE, WIDE), 0) // HEAD
    same_head = jnp.where(
        channel == lax.broadcasted_iota(jnp.int32, (WIDE, WIDE), 1) // HEAD, 1.0, 0.0
    ).astype(jnp.bfloat16)
    lane_head = lax.broadcasted_iota(jnp.int32, (1, WIDE), 1) // HEAD
    ones = lambda condition: jnp.where(condition, 1.0, 0.0).astype(jnp.bfloat16)
    pairs = [ones(lane_head % PART == head) for head in range(PART)]
    halves = [ones(lane_head // PART == part) for part in range(2)]
    masks = [ones(lane_head == head) for head in range(GROUP)]
    narrow = [ones(lane_head[:, :MAIN] == head) for head in range(PART)]

    def units(part):
        rounded = part.astype(jnp.bfloat16)
        length2 = dot(rounded * rounded, same_head)
        return part * lax.rsqrt(jnp.maximum(length2, 0.25 * HEAD))

    attended = [[] for _ in range(held)]
    for group in range(HEADS // GROUP):
        lanes = [slice(n * features + group * WIDE, n * features + (group + 1) * WIDE) for n in range(3)]
        queries = (units(dot(tokens, w_ref[:, lanes[0]])) * sharp_ref[:, lanes[0]]).astype(jnp.bfloat16)
        keys = units(dot(tokens, w_ref[:, lanes[1]])).astype(jnp.bfloat16)
        values = dot(tokens, w_ref[:, lanes[2]]).astype(jnp.bfloat16)
        for window in range(held):
            own = slice(window * CELLS, (window + 1) * CELLS)
            query, key, value = queries[own], keys[own], values[own]
            stacked = jnp.concatenate([query * pair for pair in pairs], 0)
            main_keys = jnp.concatenate([key[:MAIN] * half for half in halves], 0)
            main = jnp.exp2(dot(stacked, main_keys, NT)).astype(jnp.bfloat16)
            rest_keys = jnp.concatenate([key[MAIN:] * mask for mask in masks], 0)
            rest = jnp.exp2(dot(query, rest_keys, NT)).astype(jnp.bfloat16)
            if shifted:
                last = jnp.logical_and(
                    (pl.program_id(0) * held + window) % row_windows == row_windows - 1,
                    lax.axis_index("lat") == lax.axis_size("lat") - 1,
                )
                allow = jnp.where(last, allow_ref[...], 1.0).astype(jnp.bfloat16)
                rest = rest * allow[:, MAIN:]
            for part in range(2):
                lanes = slice(part * MAIN, (part + 1) * MAIN)
                parts = [main[head * CELLS : (head + 1) * CELLS, lanes] for head in range(PART)]
                if shifted:
                    parts = [one * allow[:, :MAIN] for one in parts]
                own_value = value[:, lanes]
                none = jnp.zeros((REST, MAIN), jnp.bfloat16)
                own_rest = [own_value[MAIN:] * mask for mask in narrow]
                other_rest = [none] * PART
                stacked = jnp.concatenate(
                    [own_value[:MAIN] * mask for mask in narrow]
                    + (own_rest + other_rest if part == 0 else other_rest + own_rest),
                    0,
                )
                both = jnp.concatenate([stacked, ones_ref[:, lanes]], 1)
                summed = dot(jnp.concatenate(parts + [rest], 1), both)
                attended[window].append(
                    (summed[:, :MAIN] / summed[:, MAIN:]).astype(jnp.bfloat16)
                )
    attended = jnp.concatenate([jnp.concatenate(parts, 1) for parts in attended], 0)
    projected = dot(attended, w_ref[:, 3 * features :])
    middle = tokens.astype(jnp.float32) + layer_norm(projected, gain_ref[...])
    out_ref[...] = middle.astype(jnp.bfloat16).reshape(out_ref.shape)


def allowed_pairs():
    side = np.arange(CELLS) // QUARTER % 2
    rest = np.tile(side[MAIN:], GROUP)
    return (side[:, None] == np.concatenate([side[:MAIN], rest])[None, :]).astype(np.float32)


def head_columns():
    halves = []
    for part in range(2):
        own = np.arange(part * PART, (part + 1) * PART)
        rows = np.concatenate([np.repeat(own, MAIN), np.repeat(np.arange(GROUP), REST)])
        halves.append(rows[:, None] == np.repeat(own, HEAD)[None, :])
    return np.concatenate(halves, 1).astype(np.float32)


def attend(sources, pieces, gain, sharp, row_windows, after=(), held=2):
    shifted = len(sources) > 1
    features = sources[0].shape[-1]
    count = 2 * row_windows
    whole = lambda shape: pl.BlockSpec(shape, lambda i: (0,) * len(shape))
    block = pl.BlockSpec((held, CELLS, features), lambda i: (i, 0, 0))
    ones = jnp.asarray(head_columns(), jnp.bfloat16)
    extra = (jnp.asarray(allowed_pairs()),) if shifted else ()
    return pl.pallas_call(
        functools.partial(attend_kernel, shifted, row_windows, len(pieces)),
        grid=(count // held,),
        out_shape=jax.ShapeDtypeStruct((count, CELLS, features), jnp.bfloat16),
        in_specs=([whole(source.shape) for source in sources] if shifted else [block])
        + [ANY] * len(pieces)
        + [whole((1, features))] * 2
        + [whole(ones.shape)]
        + [whole(e.shape) for e in extra]
        + [ANY] * len(after),
        out_specs=block,
        scratch_shapes=load_scratch(pieces, features, 4 * features),
        compiler_params=pltpu.CompilerParams(vmem_limit_bytes=24 * 2**20),
        cost_estimate=pl.CostEstimate(
            flops=count * 2_000_000_000, bytes_accessed=6_000_000, transcendentals=0
        ),
    )(*sources, *pieces, gain, sharp, ones, *extra, *after)


def feed_kernel(count, hidden_size, chunk, edge, *refs):
    x_ref, pieces, gain_ref = refs[0], refs[1 : 1 + count], refs[1 + count]
    left_ref, right_ref, edge_ref, w_ref, stage_ref, sem = refs[-6:]
    held, _, features = x_ref.shape

    @pl.when(pl.program_id(0) == 0)
    def _():
        load_pieces(pieces, w_ref, stage_ref, sem)

    tokens = x_ref[...].reshape(held * CELLS, features)
    total = jnp.zeros(tokens.shape, jnp.float32)
    for start in range(0, hidden_size, chunk):
        grown = dot(tokens, w_ref[:, start : start + chunk])
        slope = math.sqrt(2.0 / math.pi)
        bent = jnp.tanh(grown * (grown * grown * (0.044715 * slope) + slope))
        hidden = (grown + grown * bent).astype(jnp.bfloat16)
        total = total + dot(
            hidden, w_ref[:, hidden_size + start : hidden_size + start + chunk], NT
        )
    result = tokens.astype(jnp.float32) + layer_norm(0.5 * total, gain_ref[...])
    edge_window, edge_half = edge
    for window in range(held):
        for side, target in enumerate((left_ref, right_ref)):
            for half in range(2):
                start = window * CELLS + (side * 2 + half) * QUARTER
                quarter = result[start : start + QUARTER].astype(jnp.bfloat16)
                target[window, half] = quarter
                if half == edge_half and window == edge_window % held:

                    @pl.when(pl.program_id(0) == edge_window // held)
                    def _(quarter=quarter, side=side):
                        edge_ref[side] = quarter


def feed(windows, column, pieces, gain, hidden_size, edge, after=(), held=2):
    count, cells, features = windows.shape
    count = count // 2
    block = pl.BlockSpec((held, cells, features), lambda i: (i + column * count // held, 0, 0))
    side = pl.BlockSpec((held, 2, QUARTER, features), lambda i: (i, 0, 0, 0))
    return pl.pallas_call(
        functools.partial(feed_kernel, len(pieces), hidden_size, 512, edge),
        grid=(count // held,),
        out_shape=[jax.ShapeDtypeStruct((count, 2, QUARTER, features), jnp.bfloat16)] * 2
        + [jax.ShapeDtypeStruct((2, QUARTER, features), jnp.bfloat16)],
        in_specs=[block]
        + [ANY] * len(pieces)
        + [pl.BlockSpec((1, features), lambda i: (0, 0))]
        + [ANY] * len(after),
        out_specs=[side, side, pl.BlockSpec((2, QUARTER, features), lambda i: (0, 0, 0))],
        scratch_shapes=load_scratch(pieces, features, 2 * hidden_size),
        compiler_params=pltpu.CompilerParams(vmem_limit_bytes=24 * 2**20),
        cost_estimate=pl.CostEstimate(
            flops=8 * count * cells * features * hidden_size,
            bytes_accessed=8_000_000,
            transcendentals=0,
        ),
    )(windows, *pieces, gain, *after)


def shift_from(block, lon_step, lat_step):
    lons, lats = lax.axis_size("lon"), lax.axis_size("lat")
    pairs = []
    for lon in range(lons):
        for lat in range(lats):
            source = (lon + lon_step) % lons * lats + (lat + lat_step) % lats
            pairs.append((source, lon * lats + lat))
    return lax.ppermute(block, ("lon", "lat"), pairs)


def to_windows(cells):
    cols, rows, levels, features = cells.shape
    c, r = WLON // 2, WLAT // 2
    arranged = cells.reshape(cols // WLON, 2, c, rows // WLAT, 2, r, levels, features)
    arranged = arranged.transpose(0, 3, 1, 4, 2, 5, 6, 7)
    return arranged.reshape(-1, CELLS, features)


def strip(quarters):
    features = quarters.shape[-1]
    c, r = WLON // 2, WLAT // 2
    arranged = quarters.reshape(-1, c, r, LEVELS, features).transpose(1, 0, 2, 3, 4)
    return arranged.reshape(c, -1, LEVELS, features)


def back_in_place(sides, behind, above, high):
    features = behind.shape[-1]
    flat = lambda side: side.reshape(-1, QUARTER, features)[:-1]
    c, r = WLON // 2, WLAT // 2
    own = jnp.concatenate([strip(flat(side)) for side in sides], 0)
    tops = jnp.concatenate([strip(low[None]) for low in above], 0)
    first = jnp.concatenate([strip(high[None]), strip(flat(behind))], 1)
    return jnp.concatenate([first, jnp.concatenate([tops, own], 1)], 0)


def per_device(tokens, qkv_weight, out_weight, up_weight, down_weight, norm_gain, logit_scale):
    cols, rows, _, features = tokens.shape
    hidden_size = up_weight.shape[-1]
    row_windows = rows // WLAT
    weights = (qkv_weight, out_weight, up_weight, down_weight)
    relay = relayed(qkv_weight.shape[1], lax.axis_size("lon"), lax.axis_size("lat"))
    spread = np.arange(HEADS)[:, None] == np.arange(features)[None, :] // HEAD
    sharp = logit_scale[:, :, None] * jnp.asarray(spread * math.log2(math.e), jnp.float32)[None]
    sharp = jnp.sum(sharp, 1)
    windows = to_windows(tokens)

    def attention(block, sources, pieces, after=()):
        return attend(
            sources, pieces, norm_gain[block, :1], sharp[block : block + 1], row_windows, after
        )

    def forward(block, middle, column, pieces, edge, after=()):
        return feed(middle, column, pieces, norm_gain[block, 1:], hidden_size, edge, after)

    low_edge, high_edge = (0, 0), (row_windows - 1, 1)
    if relay:
        (own,) = join([], [[(0, weight) for weight in weights[:2]]])
        feed_own, last_own = join(
            [], [[(0, weight) for weight in weights[2:]], [(1, weight) for weight in weights]]
        )
        widths = tuple(sum(weight.shape[2] for weight in pair) for pair in (weights[:2], weights[2:]))
        (pair,) = join([[own, across_z(own, 2)]], (), (windows,))
        (feed_pair,) = join([[feed_own, across_z(feed_own, 2)]])
        (column,) = join([[pair, across_z(pair, 1)]], (), (feed_pair,))
        pieces = whole_pieces(column, [send(column, way) for way in (beside, across, corner)])
        (last_pair,) = join([[last_own, across_z(last_own, 2)]])
        (feed_column,) = join([[feed_pair, across_z(feed_pair, 1)]], (), (last_pair,))
        received = [send(feed_column, way) for way in (beside, across, corner)]
        last_pair = tied(last_pair, feed_column)
        last_other = across_z(last_pair, 1)
        middle = attention(0, [windows], pieces, (feed_column,))
        feed_pieces = whole_pieces(feed_column, received, (middle, last_other))
        column, last_column = join([[last_pair, last_other]], (), (middle,), widths)
        received = [send(column, way) for way in (beside, across, corner)]
        left_0, right_0, low_0 = forward(0, middle, 0, feed_pieces, low_edge, (column,))
        last_column = tied(last_column, low_0)
        last_received = [send(last_column, way) for way in (beside, across, corner)]
        ahead, ahead_low = shift_from(left_0, 1, 0), shift_from(low_0, 1, 1)
        left_1, right_1, low_1 = forward(0, middle, 1, feed_pieces, low_edge, (low_0,))
        (joined,) = join([[column] + [tied(part, (low_1, ahead, ahead_low)) for part in received]])
        pieces = [joined, send(joined, swap)]
    else:
        gathered = []
        for block in range(2):
            for pair in (weights[:2], weights[2:]):
                chunk = jnp.concatenate([weight[block] for weight in pair], 1)
                gathered.append([lax.all_gather(chunk, "lon", axis=0, tiled=True)])
        first_pieces, feed_pieces, pieces, last_pieces = gathered
        middle = attention(0, [windows], first_pieces)
        left_0, right_0, low_0 = forward(0, middle, 0, feed_pieces, low_edge)
        left_1, right_1, low_1 = forward(0, middle, 1, feed_pieces, low_edge)
        ahead, ahead_low = shift_from(left_0, 1, 0), shift_from(low_0, 1, 1)
    below = shift_from(tied(jnp.concatenate([low_0, low_1], 0), ahead_low), 0, 1)
    sources = [left_0, right_0, left_1, right_1, ahead, below, ahead_low]
    middle = attention(1, sources, pieces)
    if relay:
        last_pieces = whole_pieces(last_column, last_received, middle)
    left_1, right_1, high_1 = forward(1, middle, 1, last_pieces, high_edge)
    behind = shift_from(right_1, -1, 0)
    behind_high = shift_from(high_1, -1, -1)
    left_0, right_0, high_0 = forward(1, middle, 0, last_pieces, high_edge, (high_1,))
    above = shift_from(tied(jnp.concatenate([high_0, high_1], 0), behind_high), 0, -1)
    sides, above, behind_high = tied(((left_0, right_0, left_1), above, behind_high), behind)
    return back_in_place(sides, behind, (above[0], above[1], above[2]), behind_high[1])


def solution(mesh):
    placed = (
        P("lon", "lat", None, None),
        P(None, "lon", None),
        P(None, "lon", None),
        P(None, "lon", None),
        P(None, "lon", None),
        P(),
        P(),
    )
    return jax.shard_map(
        per_device,
        mesh=mesh,
        in_specs=placed,
        out_specs=P("lon", "lat", None, None),
        check_vma=False,
    )
```

```python
import functools
import math

import numpy as np

import jax
import jax.numpy as jnp
from jax import lax
from jax.experimental import pallas as pl
from jax.experimental.pallas import tpu as pltpu
from jax.sharding import PartitionSpec as P

HEADS = 16
HEAD = 32
WLON = 12
WLAT = 6
LEVELS = 2
CELLS = WLON * WLAT * LEVELS
MAIN = 128
REST = CELLS - MAIN
QUARTER = CELLS // 4
GROUP = 8
PART = 4
WIDE = GROUP * HEAD
Z_ORDER = (0, 2, 1, 3)
ANY = pl.BlockSpec(memory_space=pl.ANY)
NT = (((1,), (1,)), ((), ()))


def dot(a, b, dims=(((1,), (0,)), ((), ()))):
    return lax.dot_general(a, b, dims, preferred_element_type=jnp.float32)


def layer_norm(value, gain_row):
    averaged = jnp.mean(value, -1, keepdims=True)
    centred = value - averaged
    variance = jnp.mean(centred * centred, -1, keepdims=True)
    return centred * lax.rsqrt(variance + 1e-05) * gain_row


def relayed(rows, lon_size, lat_size):
    return lat_size == 2 and rows % 32 == 0 and lon_size == 16


def join_kernel(columns, cuts, *refs):
    outs = refs[len(refs) - sum(len(widths) for _, widths in columns) - len(cuts) :]
    place, out = 0, 0
    for count, widths in columns:
        row = 0
        for piece in refs[place : place + count]:
            start = 0
            for target, width in zip(outs[out : out + len(widths)], widths):
                target[row : row + piece.shape[0]] = piece[:, :, start : start + width]
                start += width
            row += piece.shape[0]
        place, out = place + count, out + len(widths)
    for blocks, chunk_ref in zip(cuts, outs[out:]):
        half = chunk_ref.shape[1]
        first = pl.multiple_of(lax.axis_index("lat") * half, 16)
        start = 0
        for block, source in zip(blocks, refs[place : place + len(blocks)]):
            width = source.shape[2]
            chunk_ref[0, :, start : start + width] = source[block, pl.ds(first, half), :]
            start += width
        place += len(blocks)


def join(columns, cuts=(), after=(), widths=None):
    pieces = [piece for column in columns for piece in column]
    sources = [weight for cut in cuts for _, weight in cut]
    out_shape, sizes = [], []
    for column in columns:
        count, half, width = column[0].shape
        count = sum(piece.shape[0] for piece in column)
        sizes.append((len(column), widths or (width,)))
        for part in widths or (width,):
            out_shape.append(jax.ShapeDtypeStruct((count, half, part), jnp.bfloat16))
    for cut in cuts:
        width = sum(weight.shape[2] for _, weight in cut)
        out_shape.append(jax.ShapeDtypeStruct((1, cut[0][1].shape[1] // 2, width), jnp.bfloat16))
    held = pl.BlockSpec(memory_space=pltpu.VMEM)
    return pl.pallas_call(
        functools.partial(join_kernel, sizes, [[block for block, _ in cut] for cut in cuts]),
        out_shape=out_shape,
        in_specs=[held] * (len(pieces) + len(sources)) + [ANY] * len(after),
        compiler_params=pltpu.CompilerParams(vmem_limit_bytes=10 * 2**20),
    )(*pieces, *sources, *after)


def send(block, move):
    pairs = []
    for lon in range(lax.axis_size("lon")):
        for core in range(2):
            z, y, x, core_to = move(lon // 4, lon // 2 % 2, lon % 2, core)
            pairs.append((lon * 2 + core, (z * 4 + y * 2 + x) * 2 + core_to))
    return lax.ppermute(block, ("lon", "lat"), pairs)


def across_z(block, bit):
    return send(block, lambda z, y, x, c: (z ^ bit, y, x, c))


def swap(z, y, x, c):
    return z, y, x, 1 - c


def tied(array, after):
    return lax.optimization_barrier((array, after))[0]


def beside(z, y, x, c):
    return (z, y, 1 - x, c) if c == 0 else (z, 1 - y, x, c)


def across(z, y, x, c):
    return (z, 1 - y, x, c) if c == 0 else (z, y, 1 - x, c)


def corner(z, y, x, c):
    return z, 1 - y, 1 - x, c


def whole_pieces(column, received):
    return [column] + received + [send(part, swap) for part in [column] + received]


def load_pieces(pieces, w_ref, stage_ref, sem):
    if len(pieces) == 1:
        copy = pltpu.make_async_copy(pieces[0], w_ref, sem.at[0])
        copy.start()
        copy.wait()
        return
    half = pieces[0].shape[-2]
    copies = [
        pltpu.make_async_copy(piece, stage_ref.at[index], sem.at[index])
        for index, piece in enumerate(pieces)
    ]
    for copy in copies:
        copy.start()
    lon, lat = lax.axis_index("lon"), lax.axis_index("lat")
    z, y, x = lon // 4, lon // 2 % 2, lon % 2
    by_x, by_y = y * 2 + 1 - x, (1 - y) * 2 + x
    parts = len(pieces) // 2
    for index, copy in enumerate(copies):
        core = lat if index < parts else 1 - lat
        squares = (
            y * 2 + x,
            jnp.where(core == 0, by_x, by_y),
            jnp.where(core == 0, by_y, by_x),
            (1 - y) * 2 + 1 - x,
        )
        held = squares[index % 4 : index % 4 + 1] if parts == 4 else squares[index % 2 * 2 :][:2]
        copy.wait()
        for step in range(pieces[0].shape[0]):
            shard = (z ^ Z_ORDER[step // len(held)]) * 4 + held[step % len(held)]
            row = pl.multiple_of((shard * 2 + core) * half, 16)
            w_ref[pl.ds(row, half), :] = stage_ref[index, step]


def load_scratch(pieces, rows, width):
    stage = (len(pieces),) + pieces[0].shape if len(pieces) > 1 else (1, 1, 16, 128)
    return [
        pltpu.VMEM((rows, width), jnp.bfloat16),
        pltpu.VMEM(stage, jnp.bfloat16),
        pltpu.SemaphoreType.DMA((len(pieces),)),
    ]


def rolled_window(place, row_windows, sides, ahead_ref, low_ref, ahead_low_ref):
    (left_0, right_0), (left_1, right_1) = sides
    first = place < row_windows
    row = place % row_windows
    following = jnp.minimum(row + 1, row_windows - 1)
    wide = lambda quarter: quarter.astype(jnp.float32)
    pick = lambda a, b: jnp.where(first, wide(a), wide(b))
    low = lambda quarter, value: jnp.where(row == row_windows - 1, quarter, value)
    quarters = [
        pick(right_0[row, 1], right_1[row, 1]),
        low(pick(low_ref[1], low_ref[3]), pick(right_0[following, 0], right_1[following, 0])),
        pick(left_1[row, 1], ahead_ref[row, 1]),
        low(pick(low_ref[2], ahead_low_ref[0]), pick(left_1[following, 0], ahead_ref[following, 0])),
    ]
    return jnp.concatenate(quarters, 0).astype(jnp.bfloat16)


def attend_kernel(shifted, row_windows, count, *refs):
    sources = 7 if shifted else 1
    x_refs, pieces = refs[:sources], refs[sources : sources + count]
    gain_ref, sharp_ref, ones_ref = refs[sources + count : sources + count + 3]
    allow_ref = refs[sources + count + 3] if shifted else None
    out_ref, w_ref, stage_ref, sem = refs[-4:]
    held, _, features = out_ref.shape

    @pl.when(pl.program_id(0) == 0)
    def _():
        load_pieces(pieces, w_ref, stage_ref, sem)

    if shifted:
        sides = (x_refs[0:2], x_refs[2:4])
        tokens = jnp.concatenate(
            [
                rolled_window(pl.program_id(0) * held + window, row_windows, sides, *x_refs[4:])
                for window in range(held)
            ],
            0,
        )
    else:
        tokens = x_refs[0][...].reshape(held * CELLS, features)
    channel = lax.broadcasted_iota(jnp.int32, (WIDE, WIDE), 0) // HEAD
    same_head = jnp.where(
        channel == lax.broadcasted_iota(jnp.int32, (WIDE, WIDE), 1) // HEAD, 1.0, 0.0
    ).astype(jnp.bfloat16)
    lane_head = lax.broadcasted_iota(jnp.int32, (1, WIDE), 1) // HEAD
    ones = lambda condition: jnp.where(condition, 1.0, 0.0).astype(jnp.bfloat16)
    pairs = [ones(lane_head % PART == head) for head in range(PART)]
    halves = [ones(lane_head // PART == part) for part in range(2)]
    masks = [ones(lane_head == head) for head in range(GROUP)]
    narrow = [ones(lane_head[:, :MAIN] == head) for head in range(PART)]

    def units(part):
        rounded = part.astype(jnp.bfloat16)
        length2 = dot(rounded * rounded, same_head)
        return part * lax.rsqrt(jnp.maximum(length2, 0.25 * HEAD))

    attended = [[] for _ in range(held)]
    for group in range(HEADS // GROUP):
        lanes = [slice(n * features + group * WIDE, n * features + (group + 1) * WIDE) for n in range(3)]
        queries = (units(dot(tokens, w_ref[:, lanes[0]])) * sharp_ref[:, lanes[0]]).astype(jnp.bfloat16)
        keys = units(dot(tokens, w_ref[:, lanes[1]])).astype(jnp.bfloat16)
        values = dot(tokens, w_ref[:, lanes[2]]).astype(jnp.bfloat16)
        for window in range(held):
            own = slice(window * CELLS, (window + 1) * CELLS)
            query, key, value = queries[own], keys[own], values[own]
            stacked = jnp.concatenate([query * pair for pair in pairs], 0)
            main_keys = jnp.concatenate([key[:MAIN] * half for half in halves], 0)
            main = jnp.exp2(dot(stacked, main_keys, NT)).astype(jnp.bfloat16)
            rest_keys = jnp.concatenate([key[MAIN:] * mask for mask in masks], 0)
            rest = jnp.exp2(dot(query, rest_keys, NT)).astype(jnp.bfloat16)
            if shifted:
                last = jnp.logical_and(
                    (pl.program_id(0) * held + window) % row_windows == row_windows - 1,
                    lax.axis_index("lat") == lax.axis_size("lat") - 1,
                )
                allow = jnp.where(last, allow_ref[...], 1.0).astype(jnp.bfloat16)
                rest = rest * allow[:, MAIN:]
            for part in range(2):
                lanes = slice(part * MAIN, (part + 1) * MAIN)
                parts = [main[head * CELLS : (head + 1) * CELLS, lanes] for head in range(PART)]
                if shifted:
                    parts = [one * allow[:, :MAIN] for one in parts]
                own_value = value[:, lanes]
                none = jnp.zeros((REST, MAIN), jnp.bfloat16)
                own_rest = [own_value[MAIN:] * mask for mask in narrow]
                other_rest = [none] * PART
                stacked = jnp.concatenate(
                    [own_value[:MAIN] * mask for mask in narrow]
                    + (own_rest + other_rest if part == 0 else other_rest + own_rest),
                    0,
                )
                both = jnp.concatenate([stacked, ones_ref[:, lanes]], 1)
                summed = dot(jnp.concatenate(parts + [rest], 1), both)
                attended[window].append(
                    (summed[:, :MAIN] / summed[:, MAIN:]).astype(jnp.bfloat16)
                )
    attended = jnp.concatenate([jnp.concatenate(parts, 1) for parts in attended], 0)
    projected = dot(attended, w_ref[:, 3 * features :])
    middle = tokens.astype(jnp.float32) + layer_norm(projected, gain_ref[...])
    out_ref[...] = middle.astype(jnp.bfloat16).reshape(out_ref.shape)


def allowed_pairs():
    side = np.arange(CELLS) // QUARTER % 2
    rest = np.tile(side[MAIN:], GROUP)
    return (side[:, None] == np.concatenate([side[:MAIN], rest])[None, :]).astype(np.float32)


def head_columns():
    halves = []
    for part in range(2):
        own = np.arange(part * PART, (part + 1) * PART)
        rows = np.concatenate([np.repeat(own, MAIN), np.repeat(np.arange(GROUP), REST)])
        halves.append(rows[:, None] == np.repeat(own, HEAD)[None, :])
    return np.concatenate(halves, 1).astype(np.float32)


def attend(sources, columns, pieces, gain, sharp, row_windows, after=(), held=2):
    shifted = len(sources) > 1
    features = sources[0].shape[-1]
    count = len(columns) * row_windows
    skipped = columns[0] * row_windows // held
    whole = lambda shape: pl.BlockSpec(shape, lambda i: (0,) * len(shape))
    block = pl.BlockSpec((held, CELLS, features), lambda i: (i, 0, 0))
    x_block = pl.BlockSpec((held, CELLS, features), lambda i: (i + skipped, 0, 0))
    ones = jnp.asarray(head_columns(), jnp.bfloat16)
    extra = (jnp.asarray(allowed_pairs()),) if shifted else ()
    return pl.pallas_call(
        functools.partial(attend_kernel, shifted, row_windows, len(pieces)),
        grid=(count // held,),
        out_shape=jax.ShapeDtypeStruct((count, CELLS, features), jnp.bfloat16),
        in_specs=([whole(source.shape) for source in sources] if shifted else [x_block])
        + [ANY] * len(pieces)
        + [whole((1, features))] * 2
        + [whole(ones.shape)]
        + [whole(e.shape) for e in extra]
        + [ANY] * len(after),
        out_specs=block,
        scratch_shapes=load_scratch(pieces, features, 4 * features),
        compiler_params=pltpu.CompilerParams(vmem_limit_bytes=24 * 2**20),
        cost_estimate=pl.CostEstimate(
            flops=count * 2_000_000_000, bytes_accessed=6_000_000, transcendentals=0
        ),
    )(*sources, *pieces, gain, sharp, ones, *extra, *after)


def feed_kernel(count, hidden_size, chunk, edge, *refs):
    x_ref, pieces, gain_ref = refs[0], refs[1 : 1 + count], refs[1 + count]
    left_ref, right_ref, edge_ref, w_ref, stage_ref, sem = refs[-6:]
    held, _, features = x_ref.shape

    @pl.when(pl.program_id(0) == 0)
    def _():
        load_pieces(pieces, w_ref, stage_ref, sem)

    tokens = x_ref[...].reshape(held * CELLS, features)
    total = jnp.zeros(tokens.shape, jnp.float32)
    for start in range(0, hidden_size, chunk):
        grown = dot(tokens, w_ref[:, start : start + chunk])
        slope = math.sqrt(2.0 / math.pi)
        bent = jnp.tanh(grown * (grown * grown * (0.044715 * slope) + slope))
        hidden = (grown + grown * bent).astype(jnp.bfloat16)
        total = total + dot(
            hidden, w_ref[:, hidden_size + start : hidden_size + start + chunk], NT
        )
    result = tokens.astype(jnp.float32) + layer_norm(0.5 * total, gain_ref[...])
    edge_window, edge_half = edge
    for window in range(held):
        for side, target in enumerate((left_ref, right_ref)):
            for half in range(2):
                start = window * CELLS + (side * 2 + half) * QUARTER
                quarter = result[start : start + QUARTER].astype(jnp.bfloat16)
                target[window, half] = quarter
                if half == edge_half and window == edge_window % held:

                    @pl.when(pl.program_id(0) == edge_window // held)
                    def _(quarter=quarter, side=side):
                        edge_ref[side] = quarter


def feed(windows, column, count, pieces, gain, hidden_size, edge, after=(), held=2):
    _, cells, features = windows.shape
    block = pl.BlockSpec((held, cells, features), lambda i: (i + column * count // held, 0, 0))
    side = pl.BlockSpec((held, 2, QUARTER, features), lambda i: (i, 0, 0, 0))
    return pl.pallas_call(
        functools.partial(feed_kernel, len(pieces), hidden_size, 512, edge),
        grid=(count // held,),
        out_shape=[jax.ShapeDtypeStruct((count, 2, QUARTER, features), jnp.bfloat16)] * 2
        + [jax.ShapeDtypeStruct((2, QUARTER, features), jnp.bfloat16)],
        in_specs=[block]
        + [ANY] * len(pieces)
        + [pl.BlockSpec((1, features), lambda i: (0, 0))]
        + [ANY] * len(after),
        out_specs=[side, side, pl.BlockSpec((2, QUARTER, features), lambda i: (0, 0, 0))],
        scratch_shapes=load_scratch(pieces, features, 2 * hidden_size),
        compiler_params=pltpu.CompilerParams(vmem_limit_bytes=24 * 2**20),
        cost_estimate=pl.CostEstimate(
            flops=8 * count * cells * features * hidden_size,
            bytes_accessed=8_000_000,
            transcendentals=0,
        ),
    )(windows, *pieces, gain, *after)


def shift_from(block, lon_step, lat_step):
    lons, lats = lax.axis_size("lon"), lax.axis_size("lat")
    pairs = []
    for lon in range(lons):
        for lat in range(lats):
            source = (lon + lon_step) % lons * lats + (lat + lat_step) % lats
            pairs.append((source, lon * lats + lat))
    return lax.ppermute(block, ("lon", "lat"), pairs)


def to_windows(cells):
    cols, rows, levels, features = cells.shape
    c, r = WLON // 2, WLAT // 2
    arranged = cells.reshape(cols // WLON, 2, c, rows // WLAT, 2, r, levels, features)
    arranged = arranged.transpose(0, 3, 1, 4, 2, 5, 6, 7)
    return arranged.reshape(-1, CELLS, features)


def strip(quarters):
    features = quarters.shape[-1]
    c, r = WLON // 2, WLAT // 2
    arranged = quarters.reshape(-1, c, r, LEVELS, features).transpose(1, 0, 2, 3, 4)
    return arranged.reshape(c, -1, LEVELS, features)


def back_in_place(sides, behind, above, high):
    features = behind.shape[-1]
    flat = lambda side: side.reshape(-1, QUARTER, features)[:-1]
    c, r = WLON // 2, WLAT // 2
    own = jnp.concatenate([strip(flat(side)) for side in sides], 0)
    tops = jnp.concatenate([strip(low[None]) for low in above], 0)
    first = jnp.concatenate([strip(high[None]), strip(flat(behind))], 1)
    return jnp.concatenate([first, jnp.concatenate([tops, own], 1)], 0)


def per_device(tokens, qkv_weight, out_weight, up_weight, down_weight, norm_gain, logit_scale):
    cols, rows, _, features = tokens.shape
    hidden_size = up_weight.shape[-1]
    row_windows = rows // WLAT
    weights = (qkv_weight, out_weight, up_weight, down_weight)
    relay = relayed(qkv_weight.shape[1], lax.axis_size("lon"), lax.axis_size("lat"))
    spread = np.arange(HEADS)[:, None] == np.arange(features)[None, :] // HEAD
    sharp = logit_scale[:, :, None] * jnp.asarray(spread * math.log2(math.e), jnp.float32)[None]
    sharp = jnp.sum(sharp, 1)
    windows = to_windows(tokens)

    def attention(block, sources, columns, pieces, after=()):
        gain, scale = norm_gain[block, :1], sharp[block : block + 1]
        return attend(sources, columns, pieces, gain, scale, row_windows, after)

    def forward(block, middle, column, pieces, edge, after=()):
        gain = norm_gain[block, 1:]
        return feed(middle, column, row_windows, pieces, gain, hidden_size, edge, after)

    low_edge, high_edge = (0, 0), (row_windows - 1, 1)
    if relay:
        (own,) = join([], [[(0, weight) for weight in weights[:2]]])
        feed_own, last_own = join(
            [], [[(0, weight) for weight in weights[2:]], [(1, weight) for weight in weights]]
        )
        widths = tuple(sum(weight.shape[2] for weight in pair) for pair in (weights[:2], weights[2:]))
        (pair,) = join([[own, across_z(own, 2)]], (), (windows,))
        (feed_pair,) = join([[feed_own, across_z(feed_own, 2)]])
        (last_pair,) = join([[last_own, send(last_own, beside)]])
        (column,) = join([[pair, across_z(pair, 1)]], (), (feed_pair, last_pair))
        pieces = whole_pieces(column, [send(column, way) for way in (beside, across, corner)])
        (last_four,) = join([[last_pair, across_z(last_pair, 2)]])
        (feed_column,) = join([[feed_pair, across_z(feed_pair, 1)]])
        received = [send(feed_column, way) for way in (beside, across)]
        last_other = across_z(last_four, 1)
        middle = attention(0, [windows], (0, 1), pieces, (feed_column, last_four))
        received.append(send(tied(received[0], middle), across))
        sent = [feed_column] + tied(received[:2], (middle, last_other)) + [tied(received[2], middle)]
        feed_pieces = [feed_column] + received + [send(part, swap) for part in sent]
        column, last_column = join([[last_four, last_other]], (), (middle,), widths)
        received = send(column, across)
        left_0, right_0, low_0 = forward(0, middle, 0, feed_pieces, low_edge, (column,))
        ahead, ahead_low = shift_from(left_0, 1, 0), shift_from(low_0, 1, 1)
        left_1, right_1, low_1 = forward(0, middle, 1, feed_pieces, low_edge, (low_0, received))
        pieces = [column, received]
        pieces += [send(column, swap), send(tied(received, low_1), swap)]
        last_received = send(tied(last_column, received), across)
    else:
        gathered = []
        for block in range(2):
            for pair in (weights[:2], weights[2:]):
                chunk = jnp.concatenate([weight[block] for weight in pair], 1)
                gathered.append([lax.all_gather(chunk, "lon", axis=0, tiled=True)])
        first_pieces, feed_pieces, pieces, last_pieces = gathered
        middle = attention(0, [windows], (0, 1), first_pieces)
        left_0, right_0, low_0 = forward(0, middle, 0, feed_pieces, low_edge)
        left_1, right_1, low_1 = forward(0, middle, 1, feed_pieces, low_edge)
        ahead, ahead_low = shift_from(left_0, 1, 0), shift_from(low_0, 1, 1)
    below = shift_from(tied(jnp.concatenate([low_0, low_1], 0), (ahead, ahead_low)), 0, 1)
    sources = [left_0, right_0, left_1, right_1, ahead, below, ahead_low]
    middle = attention(1, sources, (0, 1), pieces)
    if relay:
        last_pieces = [last_column, last_received]
        last_pieces += [send(last_column, swap), send(tied(last_received, middle), swap)]
    left_1, right_1, high_1 = forward(1, middle, 1, last_pieces, high_edge)
    behind = shift_from(right_1, -1, 0)
    behind_high = shift_from(high_1, -1, -1)
    left_0, right_0, high_0 = forward(1, middle, 0, last_pieces, high_edge, (high_1,))
    above = shift_from(tied(jnp.concatenate([high_0, high_1], 0), behind_high), 0, -1)
    sides, above, behind_high = tied(((left_0, right_0, left_1), above, behind_high), behind)
    return back_in_place(sides, behind, (above[0], above[1], above[2]), behind_high[1])


def solution(mesh):
    placed = (
        P("lon", "lat", None, None),
        P(None, "lon", None),
        P(None, "lon", None),
        P(None, "lon", None),
        P(None, "lon", None),
        P(),
        P(),
    )
    return jax.shard_map(
        per_device,
        mesh=mesh,
        in_specs=placed,
        out_specs=P("lon", "lat", None, None),
        check_vma=False,
    )
```

```python
import functools
import math

import numpy as np

import jax
import jax.numpy as jnp
from jax import lax
from jax.experimental import pallas as pl
from jax.experimental.pallas import tpu as pltpu
from jax.sharding import PartitionSpec as P

HEADS = 16
HEAD = 32
WLON = 12
WLAT = 6
LEVELS = 2
CELLS = WLON * WLAT * LEVELS
MAIN = 128
REST = CELLS - MAIN
QUARTER = CELLS // 4
GROUP = 8
PART = 4
WIDE = GROUP * HEAD
Z_ORDER = (0, 2, 1, 3)
ANY = pl.BlockSpec(memory_space=pl.ANY)
NT = (((1,), (1,)), ((), ()))


def dot(a, b, dims=(((1,), (0,)), ((), ()))):
    return lax.dot_general(a, b, dims, preferred_element_type=jnp.float32)


def layer_norm(value, gain_row):
    averaged = jnp.mean(value, -1, keepdims=True)
    centred = value - averaged
    variance = jnp.mean(centred * centred, -1, keepdims=True)
    return centred * lax.rsqrt(variance + 1e-05) * gain_row


def relayed(rows, lon_size, lat_size):
    return lat_size == 2 and rows % 32 == 0 and lon_size == 16


def join_kernel(columns, cuts, *refs):
    outs = refs[len(refs) - sum(len(widths) for _, widths in columns) - len(cuts) :]
    place, out = 0, 0
    for count, widths in columns:
        row = 0
        for piece in refs[place : place + count]:
            start = 0
            for target, width in zip(outs[out : out + len(widths)], widths):
                target[row : row + piece.shape[0]] = piece[:, :, start : start + width]
                start += width
            row += piece.shape[0]
        place, out = place + count, out + len(widths)
    for blocks, chunk_ref in zip(cuts, outs[out:]):
        half = chunk_ref.shape[1]
        first = pl.multiple_of(lax.axis_index("lat") * half, 16)
        start = 0
        for block, source in zip(blocks, refs[place : place + len(blocks)]):
            width = source.shape[2]
            chunk_ref[0, :, start : start + width] = source[block, pl.ds(first, half), :]
            start += width
        place += len(blocks)


def join(columns, cuts=(), after=(), widths=None):
    pieces = [piece for column in columns for piece in column]
    sources = [weight for cut in cuts for _, weight in cut]
    out_shape, sizes = [], []
    for column in columns:
        count, half, width = column[0].shape
        count = sum(piece.shape[0] for piece in column)
        sizes.append((len(column), widths or (width,)))
        for part in widths or (width,):
            out_shape.append(jax.ShapeDtypeStruct((count, half, part), jnp.bfloat16))
    for cut in cuts:
        width = sum(weight.shape[2] for _, weight in cut)
        out_shape.append(jax.ShapeDtypeStruct((1, cut[0][1].shape[1] // 2, width), jnp.bfloat16))
    held = pl.BlockSpec(memory_space=pltpu.VMEM)
    return pl.pallas_call(
        functools.partial(join_kernel, sizes, [[block for block, _ in cut] for cut in cuts]),
        out_shape=out_shape,
        in_specs=[held] * (len(pieces) + len(sources)) + [ANY] * len(after),
        compiler_params=pltpu.CompilerParams(vmem_limit_bytes=10 * 2**20),
    )(*pieces, *sources, *after)


def send(block, move):
    pairs = []
    for lon in range(lax.axis_size("lon")):
        for core in range(2):
            z, y, x, core_to = move(lon // 4, lon // 2 % 2, lon % 2, core)
            pairs.append((lon * 2 + core, (z * 4 + y * 2 + x) * 2 + core_to))
    return lax.ppermute(block, ("lon", "lat"), pairs)


def across_z(block, bit):
    return send(block, lambda z, y, x, c: (z ^ bit, y, x, c))


def swap(z, y, x, c):
    return z, y, x, 1 - c


def tied(array, after):
    return lax.optimization_barrier((array, after))[0]


def beside(z, y, x, c):
    return (z, y, 1 - x, c) if c == 0 else (z, 1 - y, x, c)


def across(z, y, x, c):
    return (z, 1 - y, x, c) if c == 0 else (z, y, 1 - x, c)


def corner(z, y, x, c):
    return z, 1 - y, 1 - x, c


def whole_pieces(column, received):
    return [column] + received + [send(part, swap) for part in [column] + received]


def load_pieces(pieces, w_ref, stage_ref, sem):
    if len(pieces) == 1:
        copy = pltpu.make_async_copy(pieces[0], w_ref, sem.at[0])
        copy.start()
        copy.wait()
        return
    half = pieces[0].shape[-2]
    copies = [
        pltpu.make_async_copy(piece, stage_ref.at[index], sem.at[index])
        for index, piece in enumerate(pieces)
    ]
    for copy in copies:
        copy.start()
    lon, lat = lax.axis_index("lon"), lax.axis_index("lat")
    z, y, x = lon // 4, lon // 2 % 2, lon % 2
    by_x, by_y = y * 2 + 1 - x, (1 - y) * 2 + x
    parts = len(pieces) // 2
    for index, copy in enumerate(copies):
        core = lat if index < parts else 1 - lat
        squares = (
            y * 2 + x,
            jnp.where(core == 0, by_x, by_y),
            jnp.where(core == 0, by_y, by_x),
            (1 - y) * 2 + 1 - x,
        )
        held = squares[index % 4 : index % 4 + 1] if parts == 4 else squares[index % 2 * 2 :][:2]
        copy.wait()
        for step in range(pieces[0].shape[0]):
            shard = (z ^ Z_ORDER[step // len(held)]) * 4 + held[step % len(held)]
            row = pl.multiple_of((shard * 2 + core) * half, 16)
            w_ref[pl.ds(row, half), :] = stage_ref[index, step]


def load_scratch(pieces, rows, width):
    stage = (len(pieces),) + pieces[0].shape if len(pieces) > 1 else (1, 1, 16, 128)
    return [
        pltpu.VMEM((rows, width), jnp.bfloat16),
        pltpu.VMEM(stage, jnp.bfloat16),
        pltpu.SemaphoreType.DMA((len(pieces),)),
    ]


def rolled_window(place, row_windows, sides, ahead_ref, low_ref, ahead_low_ref):
    (left_0, right_0), (left_1, right_1) = sides
    first = place < row_windows
    row = place % row_windows
    following = jnp.minimum(row + 1, row_windows - 1)
    wide = lambda quarter: quarter.astype(jnp.float32)
    pick = lambda a, b: jnp.where(first, wide(a), wide(b))
    low = lambda quarter, value: jnp.where(row == row_windows - 1, quarter, value)
    quarters = [
        pick(right_0[row, 1], right_1[row, 1]),
        low(pick(low_ref[1], low_ref[3]), pick(right_0[following, 0], right_1[following, 0])),
        pick(left_1[row, 1], ahead_ref[row, 1]),
        low(pick(low_ref[2], ahead_low_ref[0]), pick(left_1[following, 0], ahead_ref[following, 0])),
    ]
    return jnp.concatenate(quarters, 0).astype(jnp.bfloat16)


def attend_kernel(shifted, row_windows, skipped, count, *refs):
    sources = 7 if shifted else 1
    x_refs, pieces = refs[:sources], refs[sources : sources + count]
    gain_ref, sharp_ref, ones_ref = refs[sources + count : sources + count + 3]
    allow_ref = refs[sources + count + 3] if shifted else None
    out_ref, w_ref, stage_ref, sem = refs[-4:]
    held, _, features = out_ref.shape

    @pl.when(pl.program_id(0) == 0)
    def _():
        load_pieces(pieces, w_ref, stage_ref, sem)

    if shifted:
        sides = (x_refs[0:2], x_refs[2:4])
        tokens = jnp.concatenate(
            [
                rolled_window(
                    (pl.program_id(0) + skipped) * held + window, row_windows, sides, *x_refs[4:]
                )
                for window in range(held)
            ],
            0,
        )
    else:
        tokens = x_refs[0][...].reshape(held * CELLS, features)
    channel = lax.broadcasted_iota(jnp.int32, (WIDE, WIDE), 0) // HEAD
    same_head = jnp.where(
        channel == lax.broadcasted_iota(jnp.int32, (WIDE, WIDE), 1) // HEAD, 1.0, 0.0
    ).astype(jnp.bfloat16)
    lane_head = lax.broadcasted_iota(jnp.int32, (1, WIDE), 1) // HEAD
    ones = lambda condition: jnp.where(condition, 1.0, 0.0).astype(jnp.bfloat16)
    pairs = [ones(lane_head % PART == head) for head in range(PART)]
    halves = [ones(lane_head // PART == part) for part in range(2)]
    masks = [ones(lane_head == head) for head in range(GROUP)]
    narrow = [ones(lane_head[:, :MAIN] == head) for head in range(PART)]

    def units(part):
        rounded = part.astype(jnp.bfloat16)
        length2 = dot(rounded * rounded, same_head)
        return part * lax.rsqrt(jnp.maximum(length2, 0.25 * HEAD))

    attended = [[] for _ in range(held)]
    for group in range(HEADS // GROUP):
        lanes = [slice(n * features + group * WIDE, n * features + (group + 1) * WIDE) for n in range(3)]
        queries = (units(dot(tokens, w_ref[:, lanes[0]])) * sharp_ref[:, lanes[0]]).astype(jnp.bfloat16)
        keys = units(dot(tokens, w_ref[:, lanes[1]])).astype(jnp.bfloat16)
        values = dot(tokens, w_ref[:, lanes[2]]).astype(jnp.bfloat16)
        for window in range(held):
            own = slice(window * CELLS, (window + 1) * CELLS)
            query, key, value = queries[own], keys[own], values[own]
            stacked = jnp.concatenate([query * pair for pair in pairs], 0)
            main_keys = jnp.concatenate([key[:MAIN] * half for half in halves], 0)
            main = jnp.exp2(dot(stacked, main_keys, NT)).astype(jnp.bfloat16)
            rest_keys = jnp.concatenate([key[MAIN:] * mask for mask in masks], 0)
            rest = jnp.exp2(dot(query, rest_keys, NT)).astype(jnp.bfloat16)
            if shifted:
                last = jnp.logical_and(
                    ((pl.program_id(0) + skipped) * held + window) % row_windows == row_windows - 1,
                    lax.axis_index("lat") == lax.axis_size("lat") - 1,
                )
                allow = jnp.where(last, allow_ref[...], 1.0).astype(jnp.bfloat16)
                rest = rest * allow[:, MAIN:]
            for part in range(2):
                lanes = slice(part * MAIN, (part + 1) * MAIN)
                parts = [main[head * CELLS : (head + 1) * CELLS, lanes] for head in range(PART)]
                if shifted:
                    parts = [one * allow[:, :MAIN] for one in parts]
                own_value = value[:, lanes]
                none = jnp.zeros((REST, MAIN), jnp.bfloat16)
                own_rest = [own_value[MAIN:] * mask for mask in narrow]
                other_rest = [none] * PART
                stacked = jnp.concatenate(
                    [own_value[:MAIN] * mask for mask in narrow]
                    + (own_rest + other_rest if part == 0 else other_rest + own_rest),
                    0,
                )
                both = jnp.concatenate([stacked, ones_ref[:, lanes]], 1)
                summed = dot(jnp.concatenate(parts + [rest], 1), both)
                attended[window].append(
                    (summed[:, :MAIN] / summed[:, MAIN:]).astype(jnp.bfloat16)
                )
    attended = jnp.concatenate([jnp.concatenate(parts, 1) for parts in attended], 0)
    projected = dot(attended, w_ref[:, 3 * features :])
    middle = tokens.astype(jnp.float32) + layer_norm(projected, gain_ref[...])
    out_ref[...] = middle.astype(jnp.bfloat16).reshape(out_ref.shape)


def allowed_pairs():
    side = np.arange(CELLS) // QUARTER % 2
    rest = np.tile(side[MAIN:], GROUP)
    return (side[:, None] == np.concatenate([side[:MAIN], rest])[None, :]).astype(np.float32)


def head_columns():
    halves = []
    for part in range(2):
        own = np.arange(part * PART, (part + 1) * PART)
        rows = np.concatenate([np.repeat(own, MAIN), np.repeat(np.arange(GROUP), REST)])
        halves.append(rows[:, None] == np.repeat(own, HEAD)[None, :])
    return np.concatenate(halves, 1).astype(np.float32)


def attend(sources, columns, pieces, gain, sharp, row_windows, after=(), held=2):
    shifted = len(sources) > 1
    features = sources[0].shape[-1]
    count = len(columns) * row_windows
    skipped = columns[0] * row_windows // held
    whole = lambda shape: pl.BlockSpec(shape, lambda i: (0,) * len(shape))
    block = pl.BlockSpec((held, CELLS, features), lambda i: (i, 0, 0))
    x_block = pl.BlockSpec((held, CELLS, features), lambda i: (i + skipped, 0, 0))
    ones = jnp.asarray(head_columns(), jnp.bfloat16)
    extra = (jnp.asarray(allowed_pairs()),) if shifted else ()
    return pl.pallas_call(
        functools.partial(attend_kernel, shifted, row_windows, skipped, len(pieces)),
        grid=(count // held,),
        out_shape=jax.ShapeDtypeStruct((count, CELLS, features), jnp.bfloat16),
        in_specs=([whole(source.shape) for source in sources] if shifted else [x_block])
        + [ANY] * len(pieces)
        + [whole((1, features))] * 2
        + [whole(ones.shape)]
        + [whole(e.shape) for e in extra]
        + [ANY] * len(after),
        out_specs=block,
        scratch_shapes=load_scratch(pieces, features, 4 * features),
        compiler_params=pltpu.CompilerParams(vmem_limit_bytes=24 * 2**20),
        cost_estimate=pl.CostEstimate(
            flops=count * 2_000_000_000, bytes_accessed=6_000_000, transcendentals=0
        ),
    )(*sources, *pieces, gain, sharp, ones, *extra, *after)


def feed_kernel(count, hidden_size, chunk, edge, *refs):
    x_ref, pieces, gain_ref = refs[0], refs[1 : 1 + count], refs[1 + count]
    left_ref, right_ref, edge_ref, w_ref, stage_ref, sem = refs[-6:]
    held, _, features = x_ref.shape

    @pl.when(pl.program_id(0) == 0)
    def _():
        load_pieces(pieces, w_ref, stage_ref, sem)

    tokens = x_ref[...].reshape(held * CELLS, features)
    total = jnp.zeros(tokens.shape, jnp.float32)
    for start in range(0, hidden_size, chunk):
        grown = dot(tokens, w_ref[:, start : start + chunk])
        slope = math.sqrt(2.0 / math.pi)
        bent = jnp.tanh(grown * (grown * grown * (0.044715 * slope) + slope))
        hidden = (grown + grown * bent).astype(jnp.bfloat16)
        total = total + dot(
            hidden, w_ref[:, hidden_size + start : hidden_size + start + chunk], NT
        )
    result = tokens.astype(jnp.float32) + layer_norm(0.5 * total, gain_ref[...])
    edge_window, edge_half = edge
    for window in range(held):
        for side, target in enumerate((left_ref, right_ref)):
            for half in range(2):
                start = window * CELLS + (side * 2 + half) * QUARTER
                quarter = result[start : start + QUARTER].astype(jnp.bfloat16)
                target[window, half] = quarter
                if half == edge_half and window == edge_window % held:

                    @pl.when(pl.program_id(0) == edge_window // held)
                    def _(quarter=quarter, side=side):
                        edge_ref[side] = quarter


def feed(windows, column, count, pieces, gain, hidden_size, edge, after=(), held=2):
    _, cells, features = windows.shape
    block = pl.BlockSpec((held, cells, features), lambda i: (i + column * count // held, 0, 0))
    side = pl.BlockSpec((held, 2, QUARTER, features), lambda i: (i, 0, 0, 0))
    return pl.pallas_call(
        functools.partial(feed_kernel, len(pieces), hidden_size, 512, edge),
        grid=(count // held,),
        out_shape=[jax.ShapeDtypeStruct((count, 2, QUARTER, features), jnp.bfloat16)] * 2
        + [jax.ShapeDtypeStruct((2, QUARTER, features), jnp.bfloat16)],
        in_specs=[block]
        + [ANY] * len(pieces)
        + [pl.BlockSpec((1, features), lambda i: (0, 0))]
        + [ANY] * len(after),
        out_specs=[side, side, pl.BlockSpec((2, QUARTER, features), lambda i: (0, 0, 0))],
        scratch_shapes=load_scratch(pieces, features, 2 * hidden_size),
        compiler_params=pltpu.CompilerParams(vmem_limit_bytes=24 * 2**20),
        cost_estimate=pl.CostEstimate(
            flops=8 * count * cells * features * hidden_size,
            bytes_accessed=8_000_000,
            transcendentals=0,
        ),
    )(windows, *pieces, gain, *after)


def shift_from(block, lon_step, lat_step):
    lons, lats = lax.axis_size("lon"), lax.axis_size("lat")
    pairs = []
    for lon in range(lons):
        for lat in range(lats):
            source = (lon + lon_step) % lons * lats + (lat + lat_step) % lats
            pairs.append((source, lon * lats + lat))
    return lax.ppermute(block, ("lon", "lat"), pairs)


def to_windows(cells):
    cols, rows, levels, features = cells.shape
    c, r = WLON // 2, WLAT // 2
    arranged = cells.reshape(cols // WLON, 2, c, rows // WLAT, 2, r, levels, features)
    arranged = arranged.transpose(0, 3, 1, 4, 2, 5, 6, 7)
    return arranged.reshape(-1, CELLS, features)


def strip(quarters):
    features = quarters.shape[-1]
    c, r = WLON // 2, WLAT // 2
    arranged = quarters.reshape(-1, c, r, LEVELS, features).transpose(1, 0, 2, 3, 4)
    return arranged.reshape(c, -1, LEVELS, features)


def back_in_place(sides, behind, above, high):
    features = behind.shape[-1]
    flat = lambda side: side.reshape(-1, QUARTER, features)[:-1]
    c, r = WLON // 2, WLAT // 2
    own = jnp.concatenate([strip(flat(side)) for side in sides], 0)
    tops = jnp.concatenate([strip(low[None]) for low in above], 0)
    first = jnp.concatenate([strip(high[None]), strip(flat(behind))], 1)
    return jnp.concatenate([first, jnp.concatenate([tops, own], 1)], 0)


def per_device(tokens, qkv_weight, out_weight, up_weight, down_weight, norm_gain, logit_scale):
    cols, rows, _, features = tokens.shape
    hidden_size = up_weight.shape[-1]
    row_windows = rows // WLAT
    weights = (qkv_weight, out_weight, up_weight, down_weight)
    relay = relayed(qkv_weight.shape[1], lax.axis_size("lon"), lax.axis_size("lat"))
    spread = np.arange(HEADS)[:, None] == np.arange(features)[None, :] // HEAD
    sharp = logit_scale[:, :, None] * jnp.asarray(spread * math.log2(math.e), jnp.float32)[None]
    sharp = jnp.sum(sharp, 1)
    windows = to_windows(tokens)

    def attention(block, sources, columns, pieces, after=()):
        gain, scale = norm_gain[block, :1], sharp[block : block + 1]
        return attend(sources, columns, pieces, gain, scale, row_windows, after)

    def forward(block, middle, column, pieces, edge, after=()):
        gain = norm_gain[block, 1:]
        return feed(middle, column, row_windows, pieces, gain, hidden_size, edge, after)

    low_edge, high_edge = (0, 0), (row_windows - 1, 1)
    if relay:
        (own,) = join([], [[(0, weight) for weight in weights[:2]]])
        feed_own, last_own = join(
            [], [[(0, weight) for weight in weights[2:]], [(1, weight) for weight in weights]]
        )
        widths = tuple(sum(weight.shape[2] for weight in pair) for pair in (weights[:2], weights[2:]))
        (pair,) = join([[own, across_z(own, 2)]], (), (windows,))
        (feed_pair,) = join([[feed_own, across_z(feed_own, 2)]])
        last_pair, final_pair = join([[last_own, send(last_own, beside)]], widths=widths)
        (column,) = join([[pair, across_z(pair, 1)]], (), (feed_pair, last_pair))
        received = [send(column, way) for way in (beside, across, corner)]
        sent = [tied(column, received[0])] + received
        pieces = [column] + received + [send(part, swap) for part in sent]
        (feed_column,) = join([[feed_pair, across_z(feed_pair, 1)]])
        received = [send(feed_column, way) for way in (beside, across)]
        (last_four,) = join([[last_pair, across_z(last_pair, 2)]])
        (last_column,) = join([[last_four, across_z(last_four, 1)]])
        last_received = send(tied(last_column, feed_column), across)
        final_pair = tied(final_pair, last_four)
        final_other = across_z(final_pair, 2)
        middle = attention(0, [windows], (0, 1), pieces, (feed_column, last_column))
        received.append(send(tied(received[0], (middle, final_other, last_received)), across))
        swapped = [send(part, swap) for part in [feed_column] + tied(received[:2], middle)]
        swapped.append(send(tied(received[2], tuple(swapped)), swap))
        feed_pieces = [feed_column] + received + swapped
        (final_four,) = join([[final_pair, final_other]], (), (middle,))
        last_pieces = [last_column, last_received]
        last_pieces += [send(part, swap) for part in tied(last_pieces, middle)]
        left_0, right_0, low_0 = forward(0, middle, 0, feed_pieces, low_edge, (final_four,))
        ahead, ahead_low = shift_from(left_0, 1, 0), shift_from(low_0, 1, 1)
        left_1, right_1, low_1 = forward(0, middle, 1, feed_pieces, low_edge, (low_0, *last_pieces))
        (final_column,) = join([[final_four, across_z(final_four, 1)]], (), (low_1,))
        final_received = send(final_column, across)
        after = (final_column,)
    else:
        gathered = []
        for block in range(2):
            for pair in (weights[:2], weights[2:]):
                chunk = jnp.concatenate([weight[block] for weight in pair], 1)
                gathered.append([lax.all_gather(chunk, "lon", axis=0, tiled=True)])
        first_pieces, feed_pieces, last_pieces, final_pieces = gathered
        after = ()
        middle = attention(0, [windows], (0, 1), first_pieces)
        left_0, right_0, low_0 = forward(0, middle, 0, feed_pieces, low_edge)
        left_1, right_1, low_1 = forward(0, middle, 1, feed_pieces, low_edge)
        ahead, ahead_low = shift_from(left_0, 1, 0), shift_from(low_0, 1, 1)
    below = shift_from(tied(jnp.concatenate([low_0, low_1], 0), (ahead, ahead_low)), 0, 1)
    sides = [left_0, right_0, left_1, right_1]
    unused = [left_1, below, below]
    middle_0 = attention(1, sides + unused, (0,), last_pieces, after)
    middle_1 = attention(1, sides + [ahead, below, ahead_low], (1,), last_pieces, (middle_0,))
    if relay:
        final_pieces = [final_column, final_received]
        final_pieces += [send(final_column, swap), send(tied(final_received, middle_1), swap)]
    left_1, right_1, high_1 = forward(1, middle_1, 0, final_pieces, high_edge)
    behind = shift_from(right_1, -1, 0)
    behind_high = shift_from(high_1, -1, -1)
    left_0, right_0, high_0 = forward(1, middle_0, 0, final_pieces, high_edge, (high_1,))
    above = shift_from(tied(jnp.concatenate([high_0, high_1], 0), behind_high), 0, -1)
    sides, above, behind_high = tied(((left_0, right_0, left_1), above, behind_high), behind)
    return back_in_place(sides, behind, (above[0], above[1], above[2]), behind_high[1])


def solution(mesh):
    placed = (
        P("lon", "lat", None, None),
        P(None, "lon", None),
        P(None, "lon", None),
        P(None, "lon", None),
        P(None, "lon", None),
        P(),
        P(),
    )
    return jax.shard_map(
        per_device,
        mesh=mesh,
        in_specs=placed,
        out_specs=P("lon", "lat", None, None),
        check_vma=False,
    )
```

```python
import functools
import math

import numpy as np

import jax
import jax.numpy as jnp
from jax import lax
from jax.experimental import pallas as pl
from jax.experimental.pallas import tpu as pltpu
from jax.sharding import PartitionSpec as P

HEADS = 16
HEAD = 32
WLON = 12
WLAT = 6
LEVELS = 2
CELLS = WLON * WLAT * LEVELS
MAIN = 128
REST = CELLS - MAIN
QUARTER = CELLS // 4
GROUP = 8
PART = 4
WIDE = GROUP * HEAD
FEED_FLOPS, FEED_BYTES = 1_000_000, 100_000
Z_ORDER = (0, 2, 1, 3)
ANY = pl.BlockSpec(memory_space=pl.ANY)
NT = (((1,), (1,)), ((), ()))


def dot(a, b, dims=(((1,), (0,)), ((), ()))):
    return lax.dot_general(a, b, dims, preferred_element_type=jnp.float32)


def layer_norm(value, gain_row):
    averaged = jnp.mean(value, -1, keepdims=True)
    centred = value - averaged
    variance = jnp.mean(centred * centred, -1, keepdims=True)
    return centred * lax.rsqrt(variance + 1e-05) * gain_row


def relayed(rows, lon_size, lat_size):
    return lat_size == 2 and rows % 32 == 0 and lon_size == 16


def join_kernel(columns, cuts, *refs):
    outs = refs[len(refs) - sum(len(widths) for _, widths in columns) - len(cuts) :]
    place, out = 0, 0
    for count, widths in columns:
        row = 0
        for piece in refs[place : place + count]:
            start = 0
            for target, width in zip(outs[out : out + len(widths)], widths):
                target[row : row + piece.shape[0]] = piece[:, :, start : start + width]
                start += width
            row += piece.shape[0]
        place, out = place + count, out + len(widths)
    for blocks, chunk_ref in zip(cuts, outs[out:]):
        half = chunk_ref.shape[1]
        first = pl.multiple_of(lax.axis_index("lat") * half, 16)
        start = 0
        for block, source in zip(blocks, refs[place : place + len(blocks)]):
            width = source.shape[2]
            chunk_ref[0, :, start : start + width] = source[block, pl.ds(first, half), :]
            start += width
        place += len(blocks)


def join(columns, cuts=(), after=(), widths=None):
    pieces = [piece for column in columns for piece in column]
    sources = [weight for cut in cuts for _, weight in cut]
    out_shape, sizes = [], []
    for column in columns:
        count, half, width = column[0].shape
        count = sum(piece.shape[0] for piece in column)
        sizes.append((len(column), widths or (width,)))
        for part in widths or (width,):
            out_shape.append(jax.ShapeDtypeStruct((count, half, part), jnp.bfloat16))
    for cut in cuts:
        width = sum(weight.shape[2] for _, weight in cut)
        out_shape.append(jax.ShapeDtypeStruct((1, cut[0][1].shape[1] // 2, width), jnp.bfloat16))
    held = pl.BlockSpec(memory_space=pltpu.VMEM)
    return pl.pallas_call(
        functools.partial(join_kernel, sizes, [[block for block, _ in cut] for cut in cuts]),
        out_shape=out_shape,
        in_specs=[held] * (len(pieces) + len(sources)) + [ANY] * len(after),
        compiler_params=pltpu.CompilerParams(vmem_limit_bytes=10 * 2**20),
    )(*pieces, *sources, *after)


def send(block, move):
    pairs = []
    for lon in range(lax.axis_size("lon")):
        for core in range(2):
            z, y, x, core_to = move(lon // 4, lon // 2 % 2, lon % 2, core)
            pairs.append((lon * 2 + core, (z * 4 + y * 2 + x) * 2 + core_to))
    return lax.ppermute(block, ("lon", "lat"), pairs)


def across_z(block, bit):
    return send(block, lambda z, y, x, c: (z ^ bit, y, x, c))


def swap(z, y, x, c):
    return z, y, x, 1 - c


def tied(array, after):
    return lax.optimization_barrier((array, after))[0]


def beside(z, y, x, c):
    return (z, y, 1 - x, c) if c == 0 else (z, 1 - y, x, c)


def across(z, y, x, c):
    return (z, 1 - y, x, c) if c == 0 else (z, y, 1 - x, c)


def corner(z, y, x, c):
    return z, 1 - y, 1 - x, c


def whole_pieces(column, received):
    return [column] + received + [send(part, swap) for part in [column] + received]


def load_pieces(pieces, w_ref, stage_ref, sem):
    if len(pieces) == 1:
        copy = pltpu.make_async_copy(pieces[0], w_ref, sem.at[0])
        copy.start()
        copy.wait()
        return
    half = pieces[0].shape[-2]
    copies = [
        pltpu.make_async_copy(piece, stage_ref.at[index], sem.at[index])
        for index, piece in enumerate(pieces)
    ]
    for copy in copies:
        copy.start()
    lon, lat = lax.axis_index("lon"), lax.axis_index("lat")
    z, y, x = lon // 4, lon // 2 % 2, lon % 2
    by_x, by_y = y * 2 + 1 - x, (1 - y) * 2 + x
    parts = len(pieces) // 2
    for index, copy in enumerate(copies):
        core = lat if index < parts else 1 - lat
        squares = (
            y * 2 + x,
            jnp.where(core == 0, by_x, by_y),
            jnp.where(core == 0, by_y, by_x),
            (1 - y) * 2 + 1 - x,
        )
        held = squares[index % 4 : index % 4 + 1] if parts == 4 else squares[index % 2 * 2 :][:2]
        copy.wait()
        for step in range(pieces[0].shape[0]):
            shard = (z ^ Z_ORDER[step // len(held)]) * 4 + held[step % len(held)]
            row = pl.multiple_of((shard * 2 + core) * half, 16)
            w_ref[pl.ds(row, half), :] = stage_ref[index, step]


def load_scratch(pieces, rows, width):
    stage = (len(pieces),) + pieces[0].shape if len(pieces) > 1 else (1, 1, 16, 128)
    return [
        pltpu.VMEM((rows, width), jnp.bfloat16),
        pltpu.VMEM(stage, jnp.bfloat16),
        pltpu.SemaphoreType.DMA((len(pieces),)),
    ]


def attend_kernel(shifted, row_windows, count, *refs):
    sources = 2 if shifted else 1
    x_refs, pieces = refs[:sources], refs[sources : sources + count]
    gain_ref, sharp_ref, ones_ref = refs[sources + count : sources + count + 3]
    allow_ref = refs[sources + count + 3] if shifted else None
    out_ref, w_ref, stage_ref, sem = refs[-4:]
    held, _, features = out_ref.shape

    @pl.when(pl.program_id(0) == 0)
    def _():
        load_pieces(pieces, w_ref, stage_ref, sem)

    if shifted:
        quarters = []
        for window in range(held):
            for strip_ref in x_refs:
                quarters += [strip_ref[2 * window + half].astype(jnp.float32) for half in range(2)]
        tokens = jnp.concatenate(quarters, 0).astype(jnp.bfloat16)
    else:
        tokens = x_refs[0][...].reshape(held * CELLS, features)
    channel = lax.broadcasted_iota(jnp.int32, (WIDE, WIDE), 0) // HEAD
    same_head = jnp.where(
        channel == lax.broadcasted_iota(jnp.int32, (WIDE, WIDE), 1) // HEAD, 1.0, 0.0
    ).astype(jnp.bfloat16)
    lane_head = lax.broadcasted_iota(jnp.int32, (1, WIDE), 1) // HEAD
    ones = lambda condition: jnp.where(condition, 1.0, 0.0).astype(jnp.bfloat16)
    pairs = [ones(lane_head % PART == head) for head in range(PART)]
    halves = [ones(lane_head // PART == part) for part in range(2)]
    masks = [ones(lane_head == head) for head in range(GROUP)]
    narrow = [ones(lane_head[:, :MAIN] == head) for head in range(PART)]

    def units(part):
        rounded = part.astype(jnp.bfloat16)
        length2 = dot(rounded * rounded, same_head)
        return part * lax.rsqrt(jnp.maximum(length2, 0.25 * HEAD))

    attended = [[] for _ in range(held)]
    for group in range(HEADS // GROUP):
        lanes = [slice(n * features + group * WIDE, n * features + (group + 1) * WIDE) for n in range(3)]
        queries = (units(dot(tokens, w_ref[:, lanes[0]])) * sharp_ref[:, lanes[0]]).astype(jnp.bfloat16)
        keys = units(dot(tokens, w_ref[:, lanes[1]])).astype(jnp.bfloat16)
        values = dot(tokens, w_ref[:, lanes[2]]).astype(jnp.bfloat16)
        for window in range(held):
            own = slice(window * CELLS, (window + 1) * CELLS)
            query, key, value = queries[own], keys[own], values[own]
            stacked = jnp.concatenate([query * pair for pair in pairs], 0)
            main_keys = jnp.concatenate([key[:MAIN] * half for half in halves], 0)
            main = jnp.exp2(dot(stacked, main_keys, NT)).astype(jnp.bfloat16)
            rest_keys = jnp.concatenate([key[MAIN:] * mask for mask in masks], 0)
            rest = jnp.exp2(dot(query, rest_keys, NT)).astype(jnp.bfloat16)
            if shifted:
                last = jnp.logical_and(
                    (pl.program_id(0) * held + window) % row_windows == row_windows - 1,
                    lax.axis_index("lat") == lax.axis_size("lat") - 1,
                )
                allow = jnp.where(last, allow_ref[...], 1.0).astype(jnp.bfloat16)
                rest = rest * allow[:, MAIN:]
            for part in range(2):
                lanes = slice(part * MAIN, (part + 1) * MAIN)
                parts = [main[head * CELLS : (head + 1) * CELLS, lanes] for head in range(PART)]
                if shifted:
                    parts = [one * allow[:, :MAIN] for one in parts]
                own_value = value[:, lanes]
                none = jnp.zeros((REST, MAIN), jnp.bfloat16)
                own_rest = [own_value[MAIN:] * mask for mask in narrow]
                other_rest = [none] * PART
                stacked = jnp.concatenate(
                    [own_value[:MAIN] * mask for mask in narrow]
                    + (own_rest + other_rest if part == 0 else other_rest + own_rest),
                    0,
                )
                both = jnp.concatenate([stacked, ones_ref[:, lanes]], 1)
                summed = dot(jnp.concatenate(parts + [rest], 1), both)
                attended[window].append(
                    (summed[:, :MAIN] / summed[:, MAIN:]).astype(jnp.bfloat16)
                )
    attended = jnp.concatenate([jnp.concatenate(parts, 1) for parts in attended], 0)
    projected = dot(attended, w_ref[:, 3 * features :])
    middle = tokens.astype(jnp.float32) + layer_norm(projected, gain_ref[...])
    out_ref[...] = middle.astype(jnp.bfloat16).reshape(out_ref.shape)


def allowed_pairs():
    side = np.arange(CELLS) // QUARTER % 2
    rest = np.tile(side[MAIN:], GROUP)
    return (side[:, None] == np.concatenate([side[:MAIN], rest])[None, :]).astype(np.float32)


def head_columns():
    halves = []
    for part in range(2):
        own = np.arange(part * PART, (part + 1) * PART)
        rows = np.concatenate([np.repeat(own, MAIN), np.repeat(np.arange(GROUP), REST)])
        halves.append(rows[:, None] == np.repeat(own, HEAD)[None, :])
    return np.concatenate(halves, 1).astype(np.float32)


def attend(sources, columns, pieces, gain, sharp, row_windows, after=(), held=2):
    shifted = len(sources) > 1
    features = sources[0].shape[-1]
    count = len(columns) * row_windows
    skipped = columns[0] * row_windows // held
    whole = lambda shape: pl.BlockSpec(shape, lambda i: (0,) * len(shape))
    block = pl.BlockSpec((held, CELLS, features), lambda i: (i, 0, 0))
    strip_block = pl.BlockSpec((2 * held, QUARTER, features), lambda i: (i, 0, 0))
    x_block = pl.BlockSpec((held, CELLS, features), lambda i: (i + skipped, 0, 0))
    ones = jnp.asarray(head_columns(), jnp.bfloat16)
    extra = (jnp.asarray(allowed_pairs()),) if shifted else ()
    return pl.pallas_call(
        functools.partial(attend_kernel, shifted, row_windows, len(pieces)),
        grid=(count // held,),
        out_shape=jax.ShapeDtypeStruct((count, CELLS, features), jnp.bfloat16),
        in_specs=([strip_block] * 2 if shifted else [x_block])
        + [ANY] * len(pieces)
        + [whole((1, features))] * 2
        + [whole(ones.shape)]
        + [whole(e.shape) for e in extra]
        + [ANY] * len(after),
        out_specs=block,
        scratch_shapes=load_scratch(pieces, features, 4 * features),
        compiler_params=pltpu.CompilerParams(vmem_limit_bytes=24 * 2**20),
        cost_estimate=pl.CostEstimate(
            flops=count * 2_000_000_000, bytes_accessed=6_000_000, transcendentals=0
        ),
    )(*sources, *pieces, gain, sharp, ones, *extra, *after)


def feed_kernel(count, hidden_size, chunk, edge, *refs):
    x_ref, pieces, gain_ref = refs[0], refs[1 : 1 + count], refs[1 + count]
    left_ref, right_ref, edge_ref, w_ref, stage_ref, sem = refs[-6:]
    held, _, features = x_ref.shape

    @pl.when(pl.program_id(0) == 0)
    def _():
        load_pieces(pieces, w_ref, stage_ref, sem)

    tokens = x_ref[...].reshape(held * CELLS, features)
    total = jnp.zeros(tokens.shape, jnp.float32)
    for start in range(0, hidden_size, chunk):
        grown = dot(tokens, w_ref[:, start : start + chunk])
        slope = math.sqrt(2.0 / math.pi)
        bent = jnp.tanh(grown * (grown * grown * (0.044715 * slope) + slope))
        hidden = (grown + grown * bent).astype(jnp.bfloat16)
        total = total + dot(
            hidden, w_ref[:, hidden_size + start : hidden_size + start + chunk], NT
        )
    result = tokens.astype(jnp.float32) + layer_norm(0.5 * total, gain_ref[...])
    edge_window, edge_half = edge
    for window in range(held):
        for side, target in enumerate((left_ref, right_ref)):
            for half in range(2):
                start = window * CELLS + (side * 2 + half) * QUARTER
                quarter = result[start : start + QUARTER].astype(jnp.bfloat16)
                target[2 * window + half] = quarter
                if half == edge_half and window == edge_window % held:

                    @pl.when(pl.program_id(0) == edge_window // held)
                    def _(quarter=quarter, side=side):
                        edge_ref[side] = quarter


def feed(windows, column, count, pieces, gain, hidden_size, edge, after=(), held=2):
    _, cells, features = windows.shape
    block = pl.BlockSpec((held, cells, features), lambda i: (i + column * count // held, 0, 0))
    side = pl.BlockSpec((2 * held, QUARTER, features), lambda i: (i, 0, 0))
    return pl.pallas_call(
        functools.partial(feed_kernel, len(pieces), hidden_size, 512, edge),
        grid=(count // held,),
        out_shape=[jax.ShapeDtypeStruct((2 * count, QUARTER, features), jnp.bfloat16)] * 2
        + [jax.ShapeDtypeStruct((2, QUARTER, features), jnp.bfloat16)],
        in_specs=[block]
        + [ANY] * len(pieces)
        + [pl.BlockSpec((1, features), lambda i: (0, 0))]
        + [ANY] * len(after),
        out_specs=[side, side, pl.BlockSpec((2, QUARTER, features), lambda i: (0, 0, 0))],
        scratch_shapes=load_scratch(pieces, features, 2 * hidden_size),
        compiler_params=pltpu.CompilerParams(vmem_limit_bytes=24 * 2**20),
        cost_estimate=pl.CostEstimate(
            flops=FEED_FLOPS,
            bytes_accessed=FEED_BYTES,
            transcendentals=0,
        ),
    )(windows, *pieces, gain, *after)


def shift_from(block, lon_step, lat_step):
    lons, lats = lax.axis_size("lon"), lax.axis_size("lat")
    pairs = []
    for lon in range(lons):
        for lat in range(lats):
            source = (lon + lon_step) % lons * lats + (lat + lat_step) % lats
            pairs.append((source, lon * lats + lat))
    return lax.ppermute(block, ("lon", "lat"), pairs)


def to_windows(cells):
    cols, rows, levels, features = cells.shape
    c, r = WLON // 2, WLAT // 2
    arranged = cells.reshape(cols // WLON, 2, c, rows // WLAT, 2, r, levels, features)
    arranged = arranged.transpose(0, 3, 1, 4, 2, 5, 6, 7)
    return arranged.reshape(-1, CELLS, features)


def strips_kernel(picks, *refs):
    sources, outs = refs[: len(refs) - len(picks)], refs[len(refs) - len(picks) :]
    for pick, target in zip(picks, outs):
        place = 0
        for source, first, count in pick:
            target[place : place + count] = sources[source][first : first + count]
            place += count


def strips(sources, picks):
    shape = sources[0].shape[1:]
    held = pl.BlockSpec(memory_space=pltpu.VMEM)
    return pl.pallas_call(
        functools.partial(strips_kernel, picks),
        out_shape=[
            jax.ShapeDtypeStruct((sum(count for _, _, count in pick),) + shape, jnp.bfloat16)
            for pick in picks
        ],
        in_specs=[held] * len(sources),
        compiler_params=pltpu.CompilerParams(vmem_limit_bytes=10 * 2**20),
    )(*sources)


def from_strips(quarters, cols, rows):
    features = quarters.shape[-1]
    c, r = WLON // 2, WLAT // 2
    arranged = quarters.reshape(cols // c, rows // r, c, r, LEVELS, features)
    return arranged.transpose(0, 2, 1, 3, 4, 5).reshape(cols, rows, LEVELS, features)


def per_device(tokens, qkv_weight, out_weight, up_weight, down_weight, norm_gain, logit_scale):
    cols, rows, _, features = tokens.shape
    hidden_size = up_weight.shape[-1]
    row_windows = rows // WLAT
    weights = (qkv_weight, out_weight, up_weight, down_weight)
    relay = relayed(qkv_weight.shape[1], lax.axis_size("lon"), lax.axis_size("lat"))
    spread = np.arange(HEADS)[:, None] == np.arange(features)[None, :] // HEAD
    sharp = logit_scale[:, :, None] * jnp.asarray(spread * math.log2(math.e), jnp.float32)[None]
    sharp = jnp.sum(sharp, 1)
    windows = to_windows(tokens)

    def attention(block, sources, columns, pieces, after=()):
        gain, scale = norm_gain[block, :1], sharp[block : block + 1]
        return attend(sources, columns, pieces, gain, scale, row_windows, after)

    def forward(block, middle, column, pieces, edge, after=()):
        gain = norm_gain[block, 1:]
        return feed(middle, column, row_windows, pieces, gain, hidden_size, edge, after)

    low_edge, high_edge = (0, 0), (row_windows - 1, 1)
    if relay:
        (own,) = join([], [[(0, weight) for weight in weights[:2]]])
        feed_own, last_own = join(
            [], [[(0, weight) for weight in weights[2:]], [(1, weight) for weight in weights]]
        )
        widths = tuple(sum(weight.shape[2] for weight in pair) for pair in (weights[:2], weights[2:]))
        (pair,) = join([[own, across_z(own, 2)]], (), (windows,))
        (feed_pair,) = join([[feed_own, across_z(feed_own, 2)]])
        (last_pair,) = join([[last_own, send(last_own, beside)]])
        (column,) = join([[pair, across_z(pair, 1)]], (), (feed_pair, last_pair))
        received = [send(column, way) for way in (beside, across, corner)]
        sent = [tied(column, received[0])] + received
        pieces = [column] + received + [send(part, swap) for part in sent]
        (feed_column,) = join([[feed_pair, across_z(feed_pair, 1)]])
        received = [send(feed_column, way) for way in (beside, across)]
        last_other = across_z(last_pair, 2)
        middle_0 = attention(0, [windows], (0,), pieces, (feed_column,))
        received.append(send(tied(received[0], (middle_0, last_other)), across))
        (last_four,) = join([[last_pair, last_other]], (), (middle_0,))
        last_other = across_z(last_four, 1)
        middle_1 = attention(0, [windows], (1,), pieces, (middle_0, last_four))
        swapped = [send(part, swap) for part in [feed_column] + tied(received[:2], middle_0)]
        swapped.append(send(tied(received[2], (middle_1, *swapped)), swap))
        feed_pieces = [feed_column] + received + swapped
    else:
        gathered = []
        for block in range(2):
            for pair in (weights[:2], weights[2:]):
                chunk = jnp.concatenate([weight[block] for weight in pair], 1)
                gathered.append([lax.all_gather(chunk, "lon", axis=0, tiled=True)])
        pieces, feed_pieces, last_pieces, final_pieces = gathered
        middle_0 = attention(0, [windows], (0,), pieces)
        middle_1 = attention(0, [windows], (1,), pieces)
    left_0, right_0, low_0 = forward(0, middle_0, 0, feed_pieces, low_edge)
    below_0 = shift_from(low_0, 0, 1)
    size = left_0.shape[0]
    (ahead,) = strips([left_0, below_0], [[(0, 1, size - 1), (1, 0, 1)]])
    ahead = shift_from(ahead, 1, 0)
    after = (below_0,)
    if relay:
        last_column, final_column = join([[last_four, last_other]], (), (low_0,), widths)
        last_received = send(last_column, across)
        after += (last_column,)
    left_1, right_1, low_1 = forward(0, middle_1, 0, feed_pieces, low_edge, after)
    below_1 = shift_from(low_1, 0, 1)
    if relay:
        last_pieces = [last_column, last_received, send(last_column, swap)]
        last_pieces.append(send(tied(last_received, low_1), swap))
        final_received = send(tied(final_column, last_received), across)
    lefts = strips(
        [right_0, left_1, right_1, below_0, below_1],
        [
            [(0, 1, size - 1), (3, 1, 1)],
            [(1, 1, size - 1), (4, 0, 1)],
            [(2, 1, size - 1), (4, 1, 1)],
        ],
    )
    middle_0 = attention(1, lefts[:2], (0,), last_pieces)
    middle_1 = attention(1, [lefts[2], ahead], (1,), last_pieces, (middle_0,))
    if relay:
        final_pieces = [final_column, final_received, send(final_column, swap)]
        final_pieces.append(send(tied(final_received, middle_1), swap))
    left_1, right_1, high_1 = forward(1, middle_1, 0, final_pieces, high_edge)
    above_1 = shift_from(high_1, 0, -1)
    (behind,) = strips([above_1, right_1], [[(0, 1, 1), (1, 0, size - 1)]])
    behind = shift_from(behind, -1, 0)
    left_0, right_0, high_0 = forward(1, middle_0, 0, final_pieces, high_edge, (above_1,))
    above_0 = shift_from(high_0, 0, -1)
    picks = [(0, 0, size)]
    for place, (low, quarter) in enumerate(((4, 0), (4, 1), (5, 0))):
        picks += [(low, quarter, 1), (place + 1, 0, size - 1)]
    (mixed,) = strips([behind, left_0, right_0, left_1, above_0, above_1], [picks])
    return from_strips(mixed, cols, rows)


def solution(mesh):
    placed = (
        P("lon", "lat", None, None),
        P(None, "lon", None),
        P(None, "lon", None),
        P(None, "lon", None),
        P(None, "lon", None),
        P(),
        P(),
    )
    return jax.shard_map(
        per_device,
        mesh=mesh,
        in_specs=placed,
        out_specs=P("lon", "lat", None, None),
        check_vma=False,
    )
```

```python
import functools
import math

import numpy as np

import jax
import jax.numpy as jnp
from jax import lax
from jax.experimental import pallas as pl
from jax.experimental.pallas import tpu as pltpu
from jax.sharding import PartitionSpec as P

HEADS = 16
HEAD = 32
WLON = 12
WLAT = 6
LEVELS = 2
CELLS = WLON * WLAT * LEVELS
MAIN = 128
REST = CELLS - MAIN
QUARTER = CELLS // 4
GROUP = 8
PART = 4
WIDE = GROUP * HEAD
FEED_FLOPS, FEED_BYTES = 1_000_000, 100_000
Z_ORDER = (0, 2, 1, 3)
ANY = pl.BlockSpec(memory_space=pl.ANY)
NT = (((1,), (1,)), ((), ()))


def dot(a, b, dims=(((1,), (0,)), ((), ()))):
    return lax.dot_general(a, b, dims, preferred_element_type=jnp.float32)


def layer_norm(value, gain_row):
    averaged = jnp.mean(value, -1, keepdims=True)
    centred = value - averaged
    variance = jnp.mean(centred * centred, -1, keepdims=True)
    return centred * lax.rsqrt(variance + 1e-05) * gain_row


def relayed(rows, lon_size, lat_size):
    return lat_size == 2 and rows % 32 == 0 and lon_size == 16


def join_kernel(columns, cuts, *refs):
    outs = refs[len(refs) - sum(len(widths) for _, widths in columns) - len(cuts) :]
    place, out = 0, 0
    for count, widths in columns:
        row = 0
        for piece in refs[place : place + count]:
            start = 0
            for target, width in zip(outs[out : out + len(widths)], widths):
                target[row : row + piece.shape[0]] = piece[:, :, start : start + width]
                start += width
            row += piece.shape[0]
        place, out = place + count, out + len(widths)
    for blocks, chunk_ref in zip(cuts, outs[out:]):
        half = chunk_ref.shape[1]
        first = pl.multiple_of(lax.axis_index("lat") * half, 16)
        start = 0
        for block, source in zip(blocks, refs[place : place + len(blocks)]):
            width = source.shape[2]
            chunk_ref[0, :, start : start + width] = source[block, pl.ds(first, half), :]
            start += width
        place += len(blocks)


def join(columns, cuts=(), after=(), widths=None):
    pieces = [piece for column in columns for piece in column]
    sources = [weight for cut in cuts for _, weight in cut]
    out_shape, sizes = [], []
    for column in columns:
        count, half, width = column[0].shape
        count = sum(piece.shape[0] for piece in column)
        sizes.append((len(column), widths or (width,)))
        for part in widths or (width,):
            out_shape.append(jax.ShapeDtypeStruct((count, half, part), jnp.bfloat16))
    for cut in cuts:
        width = sum(weight.shape[2] for _, weight in cut)
        out_shape.append(jax.ShapeDtypeStruct((1, cut[0][1].shape[1] // 2, width), jnp.bfloat16))
    held = pl.BlockSpec(memory_space=pltpu.VMEM)
    return pl.pallas_call(
        functools.partial(join_kernel, sizes, [[block for block, _ in cut] for cut in cuts]),
        out_shape=out_shape,
        in_specs=[held] * (len(pieces) + len(sources)) + [ANY] * len(after),
        compiler_params=pltpu.CompilerParams(vmem_limit_bytes=10 * 2**20),
    )(*pieces, *sources, *after)


def send(block, move):
    pairs = []
    for lon in range(lax.axis_size("lon")):
        for core in range(2):
            z, y, x, core_to = move(lon // 4, lon // 2 % 2, lon % 2, core)
            pairs.append((lon * 2 + core, (z * 4 + y * 2 + x) * 2 + core_to))
    return lax.ppermute(block, ("lon", "lat"), pairs)


def across_z(block, bit):
    return send(block, lambda z, y, x, c: (z ^ bit, y, x, c))


def swap(z, y, x, c):
    return z, y, x, 1 - c


def tied(array, after):
    return lax.optimization_barrier((array, after))[0]


def beside(z, y, x, c):
    return (z, y, 1 - x, c) if c == 0 else (z, 1 - y, x, c)


def across(z, y, x, c):
    return (z, 1 - y, x, c) if c == 0 else (z, y, 1 - x, c)


def corner(z, y, x, c):
    return z, 1 - y, 1 - x, c


def whole_pieces(column, received):
    return [column] + received + [send(part, swap) for part in [column] + received]


def load_pieces(pieces, w_ref, stage_ref, sem):
    if len(pieces) == 1:
        copy = pltpu.make_async_copy(pieces[0], w_ref, sem.at[0])
        copy.start()
        copy.wait()
        return
    half = pieces[0].shape[-2]
    copies = [
        pltpu.make_async_copy(piece, stage_ref.at[index], sem.at[index])
        for index, piece in enumerate(pieces)
    ]
    for copy in copies:
        copy.start()
    lon, lat = lax.axis_index("lon"), lax.axis_index("lat")
    z, y, x = lon // 4, lon // 2 % 2, lon % 2
    by_x, by_y = y * 2 + 1 - x, (1 - y) * 2 + x
    parts = len(pieces) // 2
    for index, copy in enumerate(copies):
        core = lat if index < parts else 1 - lat
        squares = (
            y * 2 + x,
            jnp.where(core == 0, by_x, by_y),
            jnp.where(core == 0, by_y, by_x),
            (1 - y) * 2 + 1 - x,
        )
        copy.wait()
        for step in range(pieces[0].shape[0]):
            if parts == 4:
                square, along = squares[index % 4], Z_ORDER[step]
            else:
                square = squares[index % 2 * 2 + step // 2 % 2]
                along = Z_ORDER[step // 4 * 2 + step % 2]
            row = pl.multiple_of((((z ^ along) * 4 + square) * 2 + core) * half, 16)
            w_ref[pl.ds(row, half), :] = stage_ref[index, step]


def load_scratch(pieces, rows, width):
    stage = (len(pieces),) + pieces[0].shape if len(pieces) > 1 else (1, 1, 16, 128)
    return [
        pltpu.VMEM((rows, width), jnp.bfloat16),
        pltpu.VMEM(stage, jnp.bfloat16),
        pltpu.SemaphoreType.DMA((len(pieces),)),
    ]


def attend_kernel(shifted, row_windows, count, *refs):
    sources = 2 if shifted else 1
    x_refs, pieces = refs[:sources], refs[sources : sources + count]
    gain_ref, sharp_ref, ones_ref = refs[sources + count : sources + count + 3]
    allow_ref = refs[sources + count + 3] if shifted else None
    out_ref, w_ref, stage_ref, sem = refs[-4:]
    held, _, features = out_ref.shape

    @pl.when(pl.program_id(0) == 0)
    def _():
        load_pieces(pieces, w_ref, stage_ref, sem)

    if shifted:
        quarters = []
        for window in range(held):
            for strip_ref in x_refs:
                quarters += [strip_ref[2 * window + half].astype(jnp.float32) for half in range(2)]
        tokens = jnp.concatenate(quarters, 0).astype(jnp.bfloat16)
    else:
        tokens = x_refs[0][...].reshape(held * CELLS, features)
    channel = lax.broadcasted_iota(jnp.int32, (WIDE, WIDE), 0) // HEAD
    same_head = jnp.where(
        channel == lax.broadcasted_iota(jnp.int32, (WIDE, WIDE), 1) // HEAD, 1.0, 0.0
    ).astype(jnp.bfloat16)
    lane_head = lax.broadcasted_iota(jnp.int32, (1, WIDE), 1) // HEAD
    ones = lambda condition: jnp.where(condition, 1.0, 0.0).astype(jnp.bfloat16)
    pairs = [ones(lane_head % PART == head) for head in range(PART)]
    halves = [ones(lane_head // PART == part) for part in range(2)]
    masks = [ones(lane_head == head) for head in range(GROUP)]
    narrow = [ones(lane_head[:, :MAIN] == head) for head in range(PART)]

    def units(part):
        rounded = part.astype(jnp.bfloat16)
        length2 = dot(rounded * rounded, same_head)
        return part * lax.rsqrt(jnp.maximum(length2, 0.25 * HEAD))

    attended = [[] for _ in range(held)]
    for group in range(HEADS // GROUP):
        lanes = [slice(n * features + group * WIDE, n * features + (group + 1) * WIDE) for n in range(3)]
        queries = (units(dot(tokens, w_ref[:, lanes[0]])) * sharp_ref[:, lanes[0]]).astype(jnp.bfloat16)
        keys = units(dot(tokens, w_ref[:, lanes[1]])).astype(jnp.bfloat16)
        values = dot(tokens, w_ref[:, lanes[2]]).astype(jnp.bfloat16)
        for window in range(held):
            own = slice(window * CELLS, (window + 1) * CELLS)
            query, key, value = queries[own], keys[own], values[own]
            stacked = jnp.concatenate([query * pair for pair in pairs], 0)
            main_keys = jnp.concatenate([key[:MAIN] * half for half in halves], 0)
            main = jnp.exp2(dot(stacked, main_keys, NT)).astype(jnp.bfloat16)
            rest_keys = jnp.concatenate([key[MAIN:] * mask for mask in masks], 0)
            rest = jnp.exp2(dot(query, rest_keys, NT)).astype(jnp.bfloat16)
            if shifted:
                last = jnp.logical_and(
                    (pl.program_id(0) * held + window) % row_windows == row_windows - 1,
                    lax.axis_index("lat") == lax.axis_size("lat") - 1,
                )
                allow = jnp.where(last, allow_ref[...], 1.0).astype(jnp.bfloat16)
                rest = rest * allow[:, MAIN:]
            for part in range(2):
                lanes = slice(part * MAIN, (part + 1) * MAIN)
                parts = [main[head * CELLS : (head + 1) * CELLS, lanes] for head in range(PART)]
                if shifted:
                    parts = [one * allow[:, :MAIN] for one in parts]
                own_value = value[:, lanes]
                none = jnp.zeros((REST, MAIN), jnp.bfloat16)
                own_rest = [own_value[MAIN:] * mask for mask in narrow]
                other_rest = [none] * PART
                stacked = jnp.concatenate(
                    [own_value[:MAIN] * mask for mask in narrow]
                    + (own_rest + other_rest if part == 0 else other_rest + own_rest),
                    0,
                )
                both = jnp.concatenate([stacked, ones_ref[:, lanes]], 1)
                summed = dot(jnp.concatenate(parts + [rest], 1), both)
                attended[window].append(
                    (summed[:, :MAIN] / summed[:, MAIN:]).astype(jnp.bfloat16)
                )
    attended = jnp.concatenate([jnp.concatenate(parts, 1) for parts in attended], 0)
    projected = dot(attended, w_ref[:, 3 * features :])
    middle = tokens.astype(jnp.float32) + layer_norm(projected, gain_ref[...])
    out_ref[...] = middle.astype(jnp.bfloat16).reshape(out_ref.shape)


def allowed_pairs():
    side = np.arange(CELLS) // QUARTER % 2
    rest = np.tile(side[MAIN:], GROUP)
    return (side[:, None] == np.concatenate([side[:MAIN], rest])[None, :]).astype(np.float32)


def head_columns():
    halves = []
    for part in range(2):
        own = np.arange(part * PART, (part + 1) * PART)
        rows = np.concatenate([np.repeat(own, MAIN), np.repeat(np.arange(GROUP), REST)])
        halves.append(rows[:, None] == np.repeat(own, HEAD)[None, :])
    return np.concatenate(halves, 1).astype(np.float32)


def attend(sources, columns, pieces, gain, sharp, row_windows, after=(), held=2):
    shifted = len(sources) > 1
    features = sources[0].shape[-1]
    count = len(columns) * row_windows
    skipped = columns[0] * row_windows // held
    whole = lambda shape: pl.BlockSpec(shape, lambda i: (0,) * len(shape))
    block = pl.BlockSpec((held, CELLS, features), lambda i: (i, 0, 0))
    strip_block = pl.BlockSpec((2 * held, QUARTER, features), lambda i: (i, 0, 0))
    x_block = pl.BlockSpec((held, CELLS, features), lambda i: (i + skipped, 0, 0))
    ones = jnp.asarray(head_columns(), jnp.bfloat16)
    extra = (jnp.asarray(allowed_pairs()),) if shifted else ()
    return pl.pallas_call(
        functools.partial(attend_kernel, shifted, row_windows, len(pieces)),
        grid=(count // held,),
        out_shape=jax.ShapeDtypeStruct((count, CELLS, features), jnp.bfloat16),
        in_specs=([strip_block] * 2 if shifted else [x_block])
        + [ANY] * len(pieces)
        + [whole((1, features))] * 2
        + [whole(ones.shape)]
        + [whole(e.shape) for e in extra]
        + [ANY] * len(after),
        out_specs=block,
        scratch_shapes=load_scratch(pieces, features, 4 * features),
        compiler_params=pltpu.CompilerParams(vmem_limit_bytes=24 * 2**20),
        cost_estimate=pl.CostEstimate(
            flops=count * 2_000_000_000, bytes_accessed=6_000_000, transcendentals=0
        ),
    )(*sources, *pieces, gain, sharp, ones, *extra, *after)


def feed_kernel(count, hidden_size, chunk, edge, *refs):
    x_ref, pieces, gain_ref = refs[0], refs[1 : 1 + count], refs[1 + count]
    left_ref, right_ref, edge_ref, w_ref, stage_ref, sem = refs[-6:]
    held, _, features = x_ref.shape

    @pl.when(pl.program_id(0) == 0)
    def _():
        load_pieces(pieces, w_ref, stage_ref, sem)

    tokens = x_ref[...].reshape(held * CELLS, features)
    total = jnp.zeros(tokens.shape, jnp.float32)
    for start in range(0, hidden_size, chunk):
        grown = dot(tokens, w_ref[:, start : start + chunk])
        slope = math.sqrt(2.0 / math.pi)
        bent = jnp.tanh(grown * (grown * grown * (0.044715 * slope) + slope))
        hidden = (grown + grown * bent).astype(jnp.bfloat16)
        total = total + dot(
            hidden, w_ref[:, hidden_size + start : hidden_size + start + chunk], NT
        )
    result = tokens.astype(jnp.float32) + layer_norm(0.5 * total, gain_ref[...])
    edge_window, edge_half = edge
    for window in range(held):
        for side, target in enumerate((left_ref, right_ref)):
            for half in range(2):
                start = window * CELLS + (side * 2 + half) * QUARTER
                quarter = result[start : start + QUARTER].astype(jnp.bfloat16)
                target[2 * window + half] = quarter
                if half == edge_half and window == edge_window % held:

                    @pl.when(pl.program_id(0) == edge_window // held)
                    def _(quarter=quarter, side=side):
                        edge_ref[side] = quarter


def feed(windows, column, count, pieces, gain, hidden_size, edge, after=(), held=2):
    _, cells, features = windows.shape
    block = pl.BlockSpec((held, cells, features), lambda i: (i + column * count // held, 0, 0))
    side = pl.BlockSpec((2 * held, QUARTER, features), lambda i: (i, 0, 0))
    return pl.pallas_call(
        functools.partial(feed_kernel, len(pieces), hidden_size, 512, edge),
        grid=(count // held,),
        out_shape=[jax.ShapeDtypeStruct((2 * count, QUARTER, features), jnp.bfloat16)] * 2
        + [jax.ShapeDtypeStruct((2, QUARTER, features), jnp.bfloat16)],
        in_specs=[block]
        + [ANY] * len(pieces)
        + [pl.BlockSpec((1, features), lambda i: (0, 0))]
        + [ANY] * len(after),
        out_specs=[side, side, pl.BlockSpec((2, QUARTER, features), lambda i: (0, 0, 0))],
        scratch_shapes=load_scratch(pieces, features, 2 * hidden_size),
        compiler_params=pltpu.CompilerParams(vmem_limit_bytes=24 * 2**20),
        cost_estimate=pl.CostEstimate(
            flops=FEED_FLOPS,
            bytes_accessed=FEED_BYTES,
            transcendentals=0,
        ),
    )(windows, *pieces, gain, *after)


def shift_from(block, lon_step, lat_step):
    lons, lats = lax.axis_size("lon"), lax.axis_size("lat")
    pairs = []
    for lon in range(lons):
        for lat in range(lats):
            source = (lon + lon_step) % lons * lats + (lat + lat_step) % lats
            pairs.append((source, lon * lats + lat))
    return lax.ppermute(block, ("lon", "lat"), pairs)


def to_windows(cells):
    cols, rows, levels, features = cells.shape
    c, r = WLON // 2, WLAT // 2
    arranged = cells.reshape(cols // WLON, 2, c, rows // WLAT, 2, r, levels, features)
    arranged = arranged.transpose(0, 3, 1, 4, 2, 5, 6, 7)
    return arranged.reshape(-1, CELLS, features)


def strips_kernel(picks, *refs):
    sources, outs = refs[: len(refs) - len(picks)], refs[len(refs) - len(picks) :]
    for pick, target in zip(picks, outs):
        place = 0
        for source, first, count in pick:
            target[place : place + count] = sources[source][first : first + count]
            place += count


def strips(sources, picks):
    shape = sources[0].shape[1:]
    held = pl.BlockSpec(memory_space=pltpu.VMEM)
    return pl.pallas_call(
        functools.partial(strips_kernel, picks),
        out_shape=[
            jax.ShapeDtypeStruct((sum(count for _, _, count in pick),) + shape, jnp.bfloat16)
            for pick in picks
        ],
        in_specs=[held] * len(sources),
        compiler_params=pltpu.CompilerParams(vmem_limit_bytes=10 * 2**20),
    )(*sources)


def from_strips(quarters, cols, rows):
    features = quarters.shape[-1]
    c, r = WLON // 2, WLAT // 2
    arranged = quarters.reshape(cols // c, rows // r, c, r, LEVELS, features)
    return arranged.transpose(0, 2, 1, 3, 4, 5).reshape(cols, rows, LEVELS, features)


def per_device(tokens, qkv_weight, out_weight, up_weight, down_weight, norm_gain, logit_scale):
    cols, rows, _, features = tokens.shape
    hidden_size = up_weight.shape[-1]
    row_windows = rows // WLAT
    weights = (qkv_weight, out_weight, up_weight, down_weight)
    relay = relayed(qkv_weight.shape[1], lax.axis_size("lon"), lax.axis_size("lat"))
    spread = np.arange(HEADS)[:, None] == np.arange(features)[None, :] // HEAD
    sharp = logit_scale[:, :, None] * jnp.asarray(spread * math.log2(math.e), jnp.float32)[None]
    sharp = jnp.sum(sharp, 1)
    windows = to_windows(tokens)

    def attention(block, sources, columns, pieces, after=()):
        gain, scale = norm_gain[block, :1], sharp[block : block + 1]
        return attend(sources, columns, pieces, gain, scale, row_windows, after)

    def forward(block, middle, column, pieces, edge, after=()):
        gain = norm_gain[block, 1:]
        return feed(middle, column, row_windows, pieces, gain, hidden_size, edge, after)

    low_edge, high_edge = (0, 0), (row_windows - 1, 1)
    if relay:
        (own,) = join([], [[(0, weight) for weight in weights[:2]]])
        feed_own, last_own = join(
            [], [[(0, weight) for weight in weights[2:]], [(1, weight) for weight in weights]]
        )
        widths = tuple(sum(weight.shape[2] for weight in pair) for pair in (weights[:2], weights[2:]))
        (pair,) = join([[own, across_z(own, 2)]], (), (windows,))
        (feed_pair,) = join([[feed_own, across_z(feed_own, 2)]])
        (last_pair,) = join([[last_own, across_z(last_own, 2)]])
        (column,) = join([[pair, across_z(pair, 1)]], (), (feed_pair, last_pair))
        received = [send(column, way) for way in (beside, across, corner)]
        sent = [tied(column, received[0])] + received
        pieces = [column] + received + [send(part, swap) for part in sent]
        (last_four,) = join([[last_pair, send(last_pair, beside)]])
        (feed_column,) = join([[feed_pair, across_z(feed_pair, 1)]], (), (last_four,))
        received = [send(feed_column, way) for way in (beside, across)]
        last_other = across_z(last_four, 1)
        middle_0 = attention(0, [windows], (0,), pieces, (feed_column,))
        received.append(send(tied(received[0], middle_0), across))
        last_column, final_column = join([[last_four, last_other]], (), (middle_0,), widths)
        middle_1 = attention(0, [windows], (1,), pieces, (middle_0, last_column))
        swapped = [send(part, swap) for part in [feed_column] + tied(received[:2], middle_0)]
        swapped.append(send(tied(received[2], (middle_1, *swapped)), swap))
        feed_pieces = [feed_column] + received + swapped
    else:
        gathered = []
        for block in range(2):
            for pair in (weights[:2], weights[2:]):
                chunk = jnp.concatenate([weight[block] for weight in pair], 1)
                gathered.append([lax.all_gather(chunk, "lon", axis=0, tiled=True)])
        pieces, feed_pieces, last_pieces, final_pieces = gathered
        middle_0 = attention(0, [windows], (0,), pieces)
        middle_1 = attention(0, [windows], (1,), pieces)
    left_0, right_0, low_0 = forward(0, middle_0, 0, feed_pieces, low_edge)
    below_0 = shift_from(low_0, 0, 1)
    size = left_0.shape[0]
    (ahead,) = strips([left_0, below_0], [[(0, 1, size - 1), (1, 0, 1)]])
    ahead = shift_from(ahead, 1, 0)
    if relay:
        last_received = send(tied(last_column, middle_1), across)
    left_1, right_1, low_1 = forward(0, middle_1, 0, feed_pieces, low_edge, (below_0,))
    below_1 = shift_from(tied(low_1, ahead), 0, 1)
    if relay:
        last_pieces = [last_column, last_received, send(last_column, swap)]
        last_pieces.append(send(tied(last_received, low_1), swap))
        final_received = send(tied(final_column, (last_received, ahead)), across)
    lefts = strips(
        [right_0, left_1, right_1, below_0, below_1],
        [
            [(0, 1, size - 1), (3, 1, 1)],
            [(1, 1, size - 1), (4, 0, 1)],
            [(2, 1, size - 1), (4, 1, 1)],
        ],
    )
    middle_1 = attention(1, [lefts[2], ahead], (1,), last_pieces)
    if relay:
        final_pieces = [final_column, final_received, send(final_column, swap)]
        final_pieces.append(send(tied(final_received, middle_1), swap))
    left_1, right_1, high_1 = forward(1, middle_1, 0, final_pieces, high_edge)
    above_1 = shift_from(high_1, 0, -1)
    (behind,) = strips([above_1, right_1], [[(0, 1, 1), (1, 0, size - 1)]])
    behind = shift_from(behind, -1, 0)
    middle_0 = attention(1, lefts[:2], (0,), last_pieces, (above_1,))
    left_0, right_0, high_0 = forward(1, middle_0, 0, final_pieces, high_edge)
    above_0 = shift_from(high_0, 0, -1)
    picks = [(0, 0, size)]
    for place, (low, quarter) in enumerate(((4, 0), (4, 1), (5, 0))):
        picks += [(low, quarter, 1), (place + 1, 0, size - 1)]
    (mixed,) = strips([behind, left_0, right_0, left_1, above_0, above_1], [picks])
    return from_strips(mixed, cols, rows)


def solution(mesh):
    placed = (
        P("lon", "lat", None, None),
        P(None, "lon", None),
        P(None, "lon", None),
        P(None, "lon", None),
        P(None, "lon", None),
        P(),
        P(),
    )
    return jax.shard_map(
        per_device,
        mesh=mesh,
        in_specs=placed,
        out_specs=P("lon", "lat", None, None),
        check_vma=False,
    )
```

```python
import functools
import math

import numpy as np

import jax
import jax.numpy as jnp
from jax import lax
from jax.experimental import pallas as pl
from jax.experimental.pallas import tpu as pltpu
from jax.sharding import PartitionSpec as P

HEADS = 16
HEAD = 32
WLON = 12
WLAT = 6
LEVELS = 2
CELLS = WLON * WLAT * LEVELS
MAIN = 128
REST = CELLS - MAIN
QUARTER = CELLS // 4
GROUP = 8
PART = 4
WIDE = GROUP * HEAD
FEED_FLOPS, FEED_BYTES = 1_000_000, 100_000
Z_ORDER = (0, 2, 1, 3)
ANY = pl.BlockSpec(memory_space=pl.ANY)
NT = (((1,), (1,)), ((), ()))


def dot(a, b, dims=(((1,), (0,)), ((), ()))):
    return lax.dot_general(a, b, dims, preferred_element_type=jnp.float32)


def layer_norm(value, gain_row):
    averaged = jnp.mean(value, -1, keepdims=True)
    centred = value - averaged
    variance = jnp.mean(centred * centred, -1, keepdims=True)
    return centred * lax.rsqrt(variance + 1e-05) * gain_row


def relayed(rows, lon_size, lat_size):
    return lat_size == 2 and rows % 32 == 0 and lon_size == 16


def join_kernel(columns, cuts, *refs):
    outs = refs[len(refs) - sum(len(widths) for _, widths in columns) - len(cuts) :]
    place, out = 0, 0
    for count, widths in columns:
        row = 0
        for piece in refs[place : place + count]:
            start = 0
            for target, width in zip(outs[out : out + len(widths)], widths):
                target[row : row + piece.shape[0]] = piece[:, :, start : start + width]
                start += width
            row += piece.shape[0]
        place, out = place + count, out + len(widths)
    for blocks, chunk_ref in zip(cuts, outs[out:]):
        half = chunk_ref.shape[1]
        first = pl.multiple_of(lax.axis_index("lat") * half, 16)
        start = 0
        for block, source in zip(blocks, refs[place : place + len(blocks)]):
            width = source.shape[2]
            chunk_ref[0, :, start : start + width] = source[block, pl.ds(first, half), :]
            start += width
        place += len(blocks)


def join(columns, cuts=(), after=(), widths=None):
    pieces = [piece for column in columns for piece in column]
    sources = [weight for cut in cuts for _, weight in cut]
    out_shape, sizes = [], []
    for column in columns:
        count, half, width = column[0].shape
        count = sum(piece.shape[0] for piece in column)
        sizes.append((len(column), widths or (width,)))
        for part in widths or (width,):
            out_shape.append(jax.ShapeDtypeStruct((count, half, part), jnp.bfloat16))
    for cut in cuts:
        width = sum(weight.shape[2] for _, weight in cut)
        out_shape.append(jax.ShapeDtypeStruct((1, cut[0][1].shape[1] // 2, width), jnp.bfloat16))
    held = pl.BlockSpec(memory_space=pltpu.VMEM)
    return pl.pallas_call(
        functools.partial(join_kernel, sizes, [[block for block, _ in cut] for cut in cuts]),
        out_shape=out_shape,
        in_specs=[held] * (len(pieces) + len(sources)) + [ANY] * len(after),
        compiler_params=pltpu.CompilerParams(vmem_limit_bytes=10 * 2**20),
    )(*pieces, *sources, *after)


def halves_kernel(widths, here_ref, there_ref, *outs):
    start = 0
    for index, width in enumerate(widths):
        for half in range(2):
            rows, lanes = slice(2 * half, 2 * half + 2), slice(start, start + width)
            outs[2 * index + half][:2] = here_ref[rows, :, lanes]
            outs[2 * index + half][2:] = there_ref[rows, :, lanes]
        start += width


def halves(here, there, widths, after):
    held = pl.BlockSpec(memory_space=pltpu.VMEM)
    return pl.pallas_call(
        lambda *refs: halves_kernel(widths, refs[0], refs[1], *refs[2 + len(after) :]),
        out_shape=[
            jax.ShapeDtypeStruct((4, here.shape[1], width), jnp.bfloat16)
            for width in widths
            for _ in range(2)
        ],
        in_specs=[held] * 2 + [ANY] * len(after),
        compiler_params=pltpu.CompilerParams(vmem_limit_bytes=10 * 2**20),
    )(here, there, *after)


def send(block, move):
    pairs = []
    for lon in range(lax.axis_size("lon")):
        for core in range(2):
            z, y, x, core_to = move(lon // 4, lon // 2 % 2, lon % 2, core)
            pairs.append((lon * 2 + core, (z * 4 + y * 2 + x) * 2 + core_to))
    return lax.ppermute(block, ("lon", "lat"), pairs)


def across_z(block, bit):
    return send(block, lambda z, y, x, c: (z ^ bit, y, x, c))


def swap(z, y, x, c):
    return z, y, x, 1 - c


def tied(array, after):
    return lax.optimization_barrier((array, after))[0]


def beside(z, y, x, c):
    return (z, y, 1 - x, c) if c == 0 else (z, 1 - y, x, c)


def across(z, y, x, c):
    return (z, 1 - y, x, c) if c == 0 else (z, y, 1 - x, c)


def corner(z, y, x, c):
    return z, 1 - y, 1 - x, c


def whole_pieces(column, received):
    return [column] + received + [send(part, swap) for part in [column] + received]


def load_pieces(kind, pieces, w_ref, stage_ref, sem):
    copies = [
        pltpu.make_async_copy(piece, w_ref if kind == "rows" else stage_ref.at[index], sem.at[index])
        for index, piece in enumerate(pieces)
    ]
    for copy in copies:
        copy.start()
    if kind == "rows":
        copies[0].wait()
        return
    half = pieces[0].shape[-2]
    lon, lat = lax.axis_index("lon"), lax.axis_index("lat")
    z, y, x = lon // 4, lon // 2 % 2, lon % 2
    by_x, by_y = y * 2 + 1 - x, (1 - y) * 2 + x
    for index, copy in enumerate(copies):
        core = lat if index < 4 else 1 - lat
        own, opposite = y * 2 + x, (1 - y) * 2 + 1 - x
        one = jnp.where(core == 0, by_x, by_y)
        other = jnp.where(core == 0, by_y, by_x)
        copy.wait()
        for step in range(4):
            if kind == "columns":
                square, along = (own, one, other, opposite)[index % 4], Z_ORDER[step]
            else:
                pairs = ((own, one), (own, other), (other, opposite), (one, opposite))
                square, along = pairs[index % 4][step % 2], index % 2 * 2 + step // 2
            row = pl.multiple_of((((z ^ along) * 4 + square) * 2 + core) * half, 16)
            w_ref[pl.ds(row, half), :] = stage_ref[index, step]


def load_scratch(pieces, rows, width):
    stage = (len(pieces),) + pieces[0].shape if len(pieces) > 1 else (1, 1, 16, 128)
    return [
        pltpu.VMEM((rows, width), jnp.bfloat16),
        pltpu.VMEM(stage, jnp.bfloat16),
        pltpu.SemaphoreType.DMA((len(pieces),)),
    ]


def attend_kernel(shifted, row_windows, kind, count, *refs):
    sources = 2 if shifted else 1
    x_refs, pieces = refs[:sources], refs[sources : sources + count]
    gain_ref, sharp_ref, ones_ref = refs[sources + count : sources + count + 3]
    allow_ref = refs[sources + count + 3] if shifted else None
    out_ref, w_ref, stage_ref, sem = refs[-4:]
    held, _, features = out_ref.shape

    @pl.when(pl.program_id(0) == 0)
    def _():
        load_pieces(kind, pieces, w_ref, stage_ref, sem)

    if shifted:
        quarters = []
        for window in range(held):
            for strip_ref in x_refs:
                quarters += [strip_ref[2 * window + half].astype(jnp.float32) for half in range(2)]
        tokens = jnp.concatenate(quarters, 0).astype(jnp.bfloat16)
    else:
        tokens = x_refs[0][...].reshape(held * CELLS, features)
    channel = lax.broadcasted_iota(jnp.int32, (WIDE, WIDE), 0) // HEAD
    same_head = jnp.where(
        channel == lax.broadcasted_iota(jnp.int32, (WIDE, WIDE), 1) // HEAD, 1.0, 0.0
    ).astype(jnp.bfloat16)
    lane_head = lax.broadcasted_iota(jnp.int32, (1, WIDE), 1) // HEAD
    ones = lambda condition: jnp.where(condition, 1.0, 0.0).astype(jnp.bfloat16)
    pairs = [ones(lane_head % PART == head) for head in range(PART)]
    halves = [ones(lane_head // PART == part) for part in range(2)]
    masks = [ones(lane_head == head) for head in range(GROUP)]
    narrow = [ones(lane_head[:, :MAIN] == head) for head in range(PART)]

    def units(part):
        rounded = part.astype(jnp.bfloat16)
        length2 = dot(rounded * rounded, same_head)
        return part * lax.rsqrt(jnp.maximum(length2, 0.25 * HEAD))

    attended = [[] for _ in range(held)]
    for group in range(HEADS // GROUP):
        lanes = [slice(n * features + group * WIDE, n * features + (group + 1) * WIDE) for n in range(3)]
        queries = (units(dot(tokens, w_ref[:, lanes[0]])) * sharp_ref[:, lanes[0]]).astype(jnp.bfloat16)
        keys = units(dot(tokens, w_ref[:, lanes[1]])).astype(jnp.bfloat16)
        values = dot(tokens, w_ref[:, lanes[2]]).astype(jnp.bfloat16)
        for window in range(held):
            own = slice(window * CELLS, (window + 1) * CELLS)
            query, key, value = queries[own], keys[own], values[own]
            stacked = jnp.concatenate([query * pair for pair in pairs], 0)
            main_keys = jnp.concatenate([key[:MAIN] * half for half in halves], 0)
            main = jnp.exp2(dot(stacked, main_keys, NT)).astype(jnp.bfloat16)
            rest_keys = jnp.concatenate([key[MAIN:] * mask for mask in masks], 0)
            rest = jnp.exp2(dot(query, rest_keys, NT)).astype(jnp.bfloat16)
            if shifted:
                last = jnp.logical_and(
                    (pl.program_id(0) * held + window) % row_windows == row_windows - 1,
                    lax.axis_index("lat") == lax.axis_size("lat") - 1,
                )
                allow = jnp.where(last, allow_ref[...], 1.0).astype(jnp.bfloat16)
                rest = rest * allow[:, MAIN:]
            for part in range(2):
                lanes = slice(part * MAIN, (part + 1) * MAIN)
                parts = [main[head * CELLS : (head + 1) * CELLS, lanes] for head in range(PART)]
                if shifted:
                    parts = [one * allow[:, :MAIN] for one in parts]
                own_value = value[:, lanes]
                none = jnp.zeros((REST, MAIN), jnp.bfloat16)
                own_rest = [own_value[MAIN:] * mask for mask in narrow]
                other_rest = [none] * PART
                stacked = jnp.concatenate(
                    [own_value[:MAIN] * mask for mask in narrow]
                    + (own_rest + other_rest if part == 0 else other_rest + own_rest),
                    0,
                )
                both = jnp.concatenate([stacked, ones_ref[:, lanes]], 1)
                summed = dot(jnp.concatenate(parts + [rest], 1), both)
                attended[window].append(
                    (summed[:, :MAIN] / summed[:, MAIN:]).astype(jnp.bfloat16)
                )
    attended = jnp.concatenate([jnp.concatenate(parts, 1) for parts in attended], 0)
    projected = dot(attended, w_ref[:, 3 * features :])
    middle = tokens.astype(jnp.float32) + layer_norm(projected, gain_ref[...])
    out_ref[...] = middle.astype(jnp.bfloat16).reshape(out_ref.shape)


def allowed_pairs():
    side = np.arange(CELLS) // QUARTER % 2
    rest = np.tile(side[MAIN:], GROUP)
    return (side[:, None] == np.concatenate([side[:MAIN], rest])[None, :]).astype(np.float32)


def head_columns():
    halves = []
    for part in range(2):
        own = np.arange(part * PART, (part + 1) * PART)
        rows = np.concatenate([np.repeat(own, MAIN), np.repeat(np.arange(GROUP), REST)])
        halves.append(rows[:, None] == np.repeat(own, HEAD)[None, :])
    return np.concatenate(halves, 1).astype(np.float32)


def attend(sources, columns, pieces, gain, sharp, row_windows, after=(), held=2):
    shifted = len(sources) > 1
    kind, pieces = pieces
    features = sources[0].shape[-1]
    count = len(columns) * row_windows
    skipped = columns[0] * row_windows // held
    whole = lambda shape: pl.BlockSpec(shape, lambda i: (0,) * len(shape))
    block = pl.BlockSpec((held, CELLS, features), lambda i: (i, 0, 0))
    strip_block = pl.BlockSpec((2 * held, QUARTER, features), lambda i: (i, 0, 0))
    x_block = pl.BlockSpec((held, CELLS, features), lambda i: (i + skipped, 0, 0))
    ones = jnp.asarray(head_columns(), jnp.bfloat16)
    extra = (jnp.asarray(allowed_pairs()),) if shifted else ()
    return pl.pallas_call(
        functools.partial(attend_kernel, shifted, row_windows, kind, len(pieces)),
        grid=(count // held,),
        out_shape=jax.ShapeDtypeStruct((count, CELLS, features), jnp.bfloat16),
        in_specs=([strip_block] * 2 if shifted else [x_block])
        + [ANY] * len(pieces)
        + [whole((1, features))] * 2
        + [whole(ones.shape)]
        + [whole(e.shape) for e in extra]
        + [ANY] * len(after),
        out_specs=block,
        scratch_shapes=load_scratch(pieces, features, 4 * features),
        compiler_params=pltpu.CompilerParams(vmem_limit_bytes=24 * 2**20),
        cost_estimate=pl.CostEstimate(
            flops=count * 2_000_000_000, bytes_accessed=6_000_000, transcendentals=0
        ),
    )(*sources, *pieces, gain, sharp, ones, *extra, *after)


def feed_kernel(kind, count, hidden_size, chunk, edge, *refs):
    x_ref, pieces, gain_ref = refs[0], refs[1 : 1 + count], refs[1 + count]
    left_ref, right_ref, edge_ref, w_ref, stage_ref, sem = refs[-6:]
    held, _, features = x_ref.shape

    @pl.when(pl.program_id(0) == 0)
    def _():
        load_pieces(kind, pieces, w_ref, stage_ref, sem)

    tokens = x_ref[...].reshape(held * CELLS, features)
    total = jnp.zeros(tokens.shape, jnp.float32)
    for start in range(0, hidden_size, chunk):
        grown = dot(tokens, w_ref[:, start : start + chunk])
        slope = math.sqrt(2.0 / math.pi)
        bent = jnp.tanh(grown * (grown * grown * (0.044715 * slope) + slope))
        hidden = (grown + grown * bent).astype(jnp.bfloat16)
        total = total + dot(
            hidden, w_ref[:, hidden_size + start : hidden_size + start + chunk], NT
        )
    result = tokens.astype(jnp.float32) + layer_norm(0.5 * total, gain_ref[...])
    edge_window, edge_half = edge
    for window in range(held):
        for side, target in enumerate((left_ref, right_ref)):
            for half in range(2):
                start = window * CELLS + (side * 2 + half) * QUARTER
                quarter = result[start : start + QUARTER].astype(jnp.bfloat16)
                target[2 * window + half] = quarter
                if half == edge_half and window == edge_window % held:

                    @pl.when(pl.program_id(0) == edge_window // held)
                    def _(quarter=quarter, side=side):
                        edge_ref[side] = quarter


def feed(windows, column, count, pieces, gain, hidden_size, edge, after=(), held=2):
    _, cells, features = windows.shape
    kind, pieces = pieces
    block = pl.BlockSpec((held, cells, features), lambda i: (i + column * count // held, 0, 0))
    side = pl.BlockSpec((2 * held, QUARTER, features), lambda i: (i, 0, 0))
    return pl.pallas_call(
        functools.partial(feed_kernel, kind, len(pieces), hidden_size, 512, edge),
        grid=(count // held,),
        out_shape=[jax.ShapeDtypeStruct((2 * count, QUARTER, features), jnp.bfloat16)] * 2
        + [jax.ShapeDtypeStruct((2, QUARTER, features), jnp.bfloat16)],
        in_specs=[block]
        + [ANY] * len(pieces)
        + [pl.BlockSpec((1, features), lambda i: (0, 0))]
        + [ANY] * len(after),
        out_specs=[side, side, pl.BlockSpec((2, QUARTER, features), lambda i: (0, 0, 0))],
        scratch_shapes=load_scratch(pieces, features, 2 * hidden_size),
        compiler_params=pltpu.CompilerParams(vmem_limit_bytes=24 * 2**20),
        cost_estimate=pl.CostEstimate(
            flops=FEED_FLOPS,
            bytes_accessed=FEED_BYTES,
            transcendentals=0,
        ),
    )(windows, *pieces, gain, *after)


def shift_from(block, lon_step, lat_step):
    lons, lats = lax.axis_size("lon"), lax.axis_size("lat")
    pairs = []
    for lon in range(lons):
        for lat in range(lats):
            source = (lon + lon_step) % lons * lats + (lat + lat_step) % lats
            pairs.append((source, lon * lats + lat))
    return lax.ppermute(block, ("lon", "lat"), pairs)


def to_windows(cells):
    cols, rows, levels, features = cells.shape
    c, r = WLON // 2, WLAT // 2
    arranged = cells.reshape(cols // WLON, 2, c, rows // WLAT, 2, r, levels, features)
    arranged = arranged.transpose(0, 3, 1, 4, 2, 5, 6, 7)
    return arranged.reshape(-1, CELLS, features)


def strips_kernel(picks, *refs):
    sources, outs = refs[: len(refs) - len(picks)], refs[len(refs) - len(picks) :]
    for pick, target in zip(picks, outs):
        place = 0
        for source, first, count in pick:
            target[place : place + count] = sources[source][first : first + count]
            place += count


def strips(sources, picks):
    shape = sources[0].shape[1:]
    held = pl.BlockSpec(memory_space=pltpu.VMEM)
    return pl.pallas_call(
        functools.partial(strips_kernel, picks),
        out_shape=[
            jax.ShapeDtypeStruct((sum(count for _, _, count in pick),) + shape, jnp.bfloat16)
            for pick in picks
        ],
        in_specs=[held] * len(sources),
        compiler_params=pltpu.CompilerParams(vmem_limit_bytes=10 * 2**20),
    )(*sources)


def from_strips(quarters, cols, rows):
    features = quarters.shape[-1]
    c, r = WLON // 2, WLAT // 2
    arranged = quarters.reshape(cols // c, rows // r, c, r, LEVELS, features)
    return arranged.transpose(0, 2, 1, 3, 4, 5).reshape(cols, rows, LEVELS, features)


def per_device(tokens, qkv_weight, out_weight, up_weight, down_weight, norm_gain, logit_scale):
    cols, rows, _, features = tokens.shape
    hidden_size = up_weight.shape[-1]
    row_windows = rows // WLAT
    weights = (qkv_weight, out_weight, up_weight, down_weight)
    relay = relayed(qkv_weight.shape[1], lax.axis_size("lon"), lax.axis_size("lat"))
    spread = np.arange(HEADS)[:, None] == np.arange(features)[None, :] // HEAD
    sharp = logit_scale[:, :, None] * jnp.asarray(spread * math.log2(math.e), jnp.float32)[None]
    sharp = jnp.sum(sharp, 1)
    windows = to_windows(tokens)

    def attention(block, sources, columns, pieces, after=()):
        gain, scale = norm_gain[block, :1], sharp[block : block + 1]
        return attend(sources, columns, pieces, gain, scale, row_windows, after)

    def forward(block, middle, column, pieces, edge, after=()):
        gain = norm_gain[block, 1:]
        return feed(middle, column, row_windows, pieces, gain, hidden_size, edge, after)

    low_edge, high_edge = (0, 0), (row_windows - 1, 1)
    if relay:
        (own,) = join([], [[(0, weight) for weight in weights[:2]]])
        feed_own, last_own = join(
            [],
            [[(0, weight) for weight in weights[2:]], [(1, weight) for weight in weights]],
            (own,),
        )
        widths = tuple(sum(weight.shape[2] for weight in pair) for pair in (weights[:2], weights[2:]))
        (pair,) = join([[own, across_z(own, 2)]], (), (windows,))
        (feed_pair,) = join([[feed_own, across_z(feed_own, 2)]])
        (column,) = join([[pair, across_z(pair, 1)]], (), (feed_pair,))
        received = [send(column, way) for way in (beside, across, corner)]
        sent = [tied(column, received[0])] + received
        pieces = "columns", [column] + received + [send(part, swap) for part in sent]
        last_own = tied(last_own, pair)
        last_other = across_z(last_own, 2)
        (last_four,) = join(
            [[last_own, send(last_own, beside), last_other, send(last_other, across)]]
        )
        (feed_column,) = join([[feed_pair, across_z(feed_pair, 1)]], (), (last_four,))
        received = [send(feed_column, way) for way in (beside, across)]
        last_other = across_z(last_four, 1)
        middle_0 = attention(0, [windows], (0,), pieces, (feed_column,))
        first, second = tied((received[0][:2], received[1][2:]), middle_0)
        corners = [send(first, across), send(second, beside)]
        *last_columns, final_one, final_other = halves(last_four, last_other, widths, (middle_0,))
        middle_1 = attention(0, [windows], (1,), pieces, (middle_0, last_columns[0]))
        swapped = [send(part, swap) for part in [feed_column] + tied(received, middle_0)]
        received += join([tied(corners, (middle_1, *swapped))])
        feed_pieces = "columns", [feed_column] + received + swapped + [send(received[2], swap)]
    else:
        gathered = []
        for block in range(2):
            for pair in (weights[:2], weights[2:]):
                chunk = jnp.concatenate([weight[block] for weight in pair], 1)
                gathered.append(lax.all_gather(chunk, "lon", axis=0, tiled=True))
        pieces, feed_pieces, last_pieces, final_pieces = (("rows", [rows]) for rows in gathered)
        middle_0 = attention(0, [windows], (0,), pieces)
        middle_1 = attention(0, [windows], (1,), pieces)
    left_0, right_0, low_0 = forward(0, middle_0, 0, feed_pieces, low_edge)
    below_0 = shift_from(low_0, 0, 1)
    size = left_0.shape[0]
    (ahead,) = strips([left_0, below_0], [[(0, 1, size - 1), (1, 0, 1)]])
    ahead = shift_from(ahead, 1, 0)
    if relay:
        last_received = [
            send(part, way) for part, way in zip(tied(last_columns, middle_1), (across, beside))
        ]
    left_1, right_1, low_1 = forward(0, middle_1, 0, feed_pieces, low_edge, (below_0,))
    below_1 = shift_from(tied(low_1, ahead), 0, 1)
    if relay:
        last_pieces = last_columns + last_received
        last_pieces += [send(part, swap) for part in last_columns + tied(last_received, low_1)]
        last_pieces = "halves", last_pieces
        final_columns = [final_one, final_other]
        final_received = [
            send(part, way)
            for part, way in zip(tied(final_columns, (last_received, ahead)), (across, beside))
        ]
    lefts = strips(
        [right_0, left_1, right_1, below_0, below_1],
        [
            [(0, 1, size - 1), (3, 1, 1)],
            [(1, 1, size - 1), (4, 0, 1)],
            [(2, 1, size - 1), (4, 1, 1)],
        ],
    )
    middle_1 = attention(1, [lefts[2], ahead], (1,), last_pieces)
    if relay:
        final_pieces = final_columns + final_received
        final_pieces += [send(part, swap) for part in final_columns + tied(final_received, middle_1)]
        final_pieces = "halves", final_pieces
    left_1, right_1, high_1 = forward(1, middle_1, 0, final_pieces, high_edge)
    above_1 = shift_from(high_1, 0, -1)
    (behind,) = strips([above_1, right_1], [[(0, 1, 1), (1, 0, size - 1)]])
    behind = shift_from(behind, -1, 0)
    middle_0 = attention(1, lefts[:2], (0,), last_pieces, (above_1,))
    left_0, right_0, high_0 = forward(1, middle_0, 0, final_pieces, high_edge)
    above_0 = shift_from(high_0, 0, -1)
    picks = [(0, 0, size)]
    for place, (low, quarter) in enumerate(((4, 0), (4, 1), (5, 0))):
        picks += [(low, quarter, 1), (place + 1, 0, size - 1)]
    (mixed,) = strips([behind, left_0, right_0, left_1, above_0, above_1], [picks])
    return from_strips(mixed, cols, rows)


def solution(mesh):
    placed = (
        P("lon", "lat", None, None),
        P(None, "lon", None),
        P(None, "lon", None),
        P(None, "lon", None),
        P(None, "lon", None),
        P(),
        P(),
    )
    return jax.shard_map(
        per_device,
        mesh=mesh,
        in_specs=placed,
        out_specs=P("lon", "lat", None, None),
        check_vma=False,
    )
```

```python
import functools
import math

import numpy as np

import jax
import jax.numpy as jnp
from jax import lax
from jax.experimental import pallas as pl
from jax.experimental.pallas import tpu as pltpu
from jax.sharding import PartitionSpec as P

HEADS = 16
HEAD = 32
WLON = 12
WLAT = 6
LEVELS = 2
CELLS = WLON * WLAT * LEVELS
MAIN = 128
REST = CELLS - MAIN
QUARTER = CELLS // 4
GROUP = 8
PART = 4
WIDE = GROUP * HEAD
FEED_FLOPS, FEED_BYTES = 1_000_000, 100_000
Z_ORDER = (0, 2, 1, 3)
ANY = pl.BlockSpec(memory_space=pl.ANY)
NT = (((1,), (1,)), ((), ()))


def dot(a, b, dims=(((1,), (0,)), ((), ()))):
    return lax.dot_general(a, b, dims, preferred_element_type=jnp.float32)


def layer_norm(value, gain_row):
    averaged = jnp.mean(value, -1, keepdims=True)
    centred = value - averaged
    variance = jnp.mean(centred * centred, -1, keepdims=True)
    return centred * lax.rsqrt(variance + 1e-05) * gain_row


def relayed(rows, lon_size, lat_size):
    return lat_size == 2 and rows % 32 == 0 and lon_size == 16


def join_kernel(columns, cuts, *refs):
    outs = refs[len(refs) - sum(len(widths) for _, widths in columns) - len(cuts) :]
    place, out = 0, 0
    for count, widths in columns:
        row = 0
        for piece in refs[place : place + count]:
            start = 0
            for target, width in zip(outs[out : out + len(widths)], widths):
                target[row : row + piece.shape[0]] = piece[:, :, start : start + width]
                start += width
            row += piece.shape[0]
        place, out = place + count, out + len(widths)
    for blocks, chunk_ref in zip(cuts, outs[out:]):
        half = chunk_ref.shape[1]
        first = pl.multiple_of(lax.axis_index("lat") * half, 16)
        start = 0
        for block, source in zip(blocks, refs[place : place + len(blocks)]):
            width = source.shape[2]
            chunk_ref[0, :, start : start + width] = source[block, pl.ds(first, half), :]
            start += width
        place += len(blocks)


def join(columns, cuts=(), after=(), widths=None):
    pieces = [piece for column in columns for piece in column]
    sources = [weight for cut in cuts for _, weight in cut]
    out_shape, sizes = [], []
    for column in columns:
        count, half, width = column[0].shape
        count = sum(piece.shape[0] for piece in column)
        sizes.append((len(column), widths or (width,)))
        for part in widths or (width,):
            out_shape.append(jax.ShapeDtypeStruct((count, half, part), jnp.bfloat16))
    for cut in cuts:
        width = sum(weight.shape[2] for _, weight in cut)
        out_shape.append(jax.ShapeDtypeStruct((1, cut[0][1].shape[1] // 2, width), jnp.bfloat16))
    held = pl.BlockSpec(memory_space=pltpu.VMEM)
    return pl.pallas_call(
        functools.partial(join_kernel, sizes, [[block for block, _ in cut] for cut in cuts]),
        out_shape=out_shape,
        in_specs=[held] * (len(pieces) + len(sources)) + [ANY] * len(after),
        compiler_params=pltpu.CompilerParams(vmem_limit_bytes=10 * 2**20),
    )(*pieces, *sources, *after)


def halves_kernel(widths, here_ref, there_ref, *outs):
    start = 0
    for index, width in enumerate(widths):
        for half in range(2):
            rows, lanes = slice(2 * half, 2 * half + 2), slice(start, start + width)
            outs[2 * index + half][:2] = here_ref[rows, :, lanes]
            outs[2 * index + half][2:] = there_ref[rows, :, lanes]
        start += width


def halves(here, there, widths, after):
    held = pl.BlockSpec(memory_space=pltpu.VMEM)
    return pl.pallas_call(
        lambda *refs: halves_kernel(widths, refs[0], refs[1], *refs[2 + len(after) :]),
        out_shape=[
            jax.ShapeDtypeStruct((4, here.shape[1], width), jnp.bfloat16)
            for width in widths
            for _ in range(2)
        ],
        in_specs=[held] * 2 + [ANY] * len(after),
        compiler_params=pltpu.CompilerParams(vmem_limit_bytes=10 * 2**20),
    )(here, there, *after)


def send(block, move):
    pairs = []
    for lon in range(lax.axis_size("lon")):
        for core in range(2):
            z, y, x, core_to = move(lon // 4, lon // 2 % 2, lon % 2, core)
            pairs.append((lon * 2 + core, (z * 4 + y * 2 + x) * 2 + core_to))
    return lax.ppermute(block, ("lon", "lat"), pairs)


def across_z(block, bit):
    return send(block, lambda z, y, x, c: (z ^ bit, y, x, c))


def swap(z, y, x, c):
    return z, y, x, 1 - c


def tied(array, after):
    return lax.optimization_barrier((array, after))[0]


def beside(z, y, x, c):
    return (z, y, 1 - x, c) if c == 0 else (z, 1 - y, x, c)


def across(z, y, x, c):
    return (z, 1 - y, x, c) if c == 0 else (z, y, 1 - x, c)


def corner(z, y, x, c):
    return z, 1 - y, 1 - x, c


def whole_pieces(column, received):
    return [column] + received + [send(part, swap) for part in [column] + received]


def load_pieces(kind, pieces, w_ref, stage_ref, sem):
    copies = [
        pltpu.make_async_copy(piece, w_ref if kind == "rows" else stage_ref.at[index], sem.at[index])
        for index, piece in enumerate(pieces)
    ]
    for copy in copies:
        copy.start()
    if kind == "rows":
        copies[0].wait()
        return
    half = pieces[0].shape[-2]
    lon, lat = lax.axis_index("lon"), lax.axis_index("lat")
    z, y, x = lon // 4, lon // 2 % 2, lon % 2
    by_x, by_y = y * 2 + 1 - x, (1 - y) * 2 + x
    for index, copy in enumerate(copies):
        core = lat if index < 4 else 1 - lat
        own, opposite = y * 2 + x, (1 - y) * 2 + 1 - x
        one = jnp.where(core == 0, by_x, by_y)
        other = jnp.where(core == 0, by_y, by_x)
        copy.wait()
        for step in range(4):
            if kind == "columns":
                square, along = (own, one, other, opposite)[index % 4], Z_ORDER[step]
            else:
                pairs = ((own, one), (own, other), (other, opposite), (one, opposite))
                square, along = pairs[index % 4][step % 2], index % 2 * 2 + step // 2
            row = pl.multiple_of((((z ^ along) * 4 + square) * 2 + core) * half, 16)
            w_ref[pl.ds(row, half), :] = stage_ref[index, step]


def load_scratch(pieces, rows, width):
    stage = (len(pieces),) + pieces[0].shape if len(pieces) > 1 else (1, 1, 16, 128)
    return [
        pltpu.VMEM((rows, width), jnp.bfloat16),
        pltpu.VMEM(stage, jnp.bfloat16),
        pltpu.SemaphoreType.DMA((len(pieces),)),
    ]


def attend_kernel(shifted, row_windows, kind, count, *refs):
    sources = 2 if shifted else 1
    x_refs, pieces = refs[:sources], refs[sources : sources + count]
    gain_ref, sharp_ref, ones_ref = refs[sources + count : sources + count + 3]
    allow_ref = refs[sources + count + 3] if shifted else None
    out_ref, w_ref, stage_ref, sem = refs[-4:]
    held, _, features = out_ref.shape

    @pl.when(pl.program_id(0) == 0)
    def _():
        load_pieces(kind, pieces, w_ref, stage_ref, sem)

    if shifted:
        quarters = []
        for window in range(held):
            for strip_ref in x_refs:
                quarters += [strip_ref[2 * window + half].astype(jnp.float32) for half in range(2)]
        tokens = jnp.concatenate(quarters, 0).astype(jnp.bfloat16)
    else:
        tokens = x_refs[0][...].reshape(held * CELLS, features)
    channel = lax.broadcasted_iota(jnp.int32, (WIDE, WIDE), 0) // HEAD
    same_head = jnp.where(
        channel == lax.broadcasted_iota(jnp.int32, (WIDE, WIDE), 1) // HEAD, 1.0, 0.0
    ).astype(jnp.bfloat16)
    lane_head = lax.broadcasted_iota(jnp.int32, (1, WIDE), 1) // HEAD
    ones = lambda condition: jnp.where(condition, 1.0, 0.0).astype(jnp.bfloat16)
    pairs = [ones(lane_head % PART == head) for head in range(PART)]
    halves = [ones(lane_head // PART == part) for part in range(2)]
    masks = [ones(lane_head == head) for head in range(GROUP)]
    narrow = [ones(lane_head[:, :MAIN] == head) for head in range(PART)]

    def units(part):
        rounded = part.astype(jnp.bfloat16)
        length2 = dot(rounded * rounded, same_head)
        return part * lax.rsqrt(jnp.maximum(length2, 0.25 * HEAD))

    attended = [[] for _ in range(held)]
    for group in range(HEADS // GROUP):
        lanes = [slice(n * features + group * WIDE, n * features + (group + 1) * WIDE) for n in range(3)]
        queries = (units(dot(tokens, w_ref[:, lanes[0]])) * sharp_ref[:, lanes[0]]).astype(jnp.bfloat16)
        keys = units(dot(tokens, w_ref[:, lanes[1]])).astype(jnp.bfloat16)
        values = dot(tokens, w_ref[:, lanes[2]]).astype(jnp.bfloat16)
        for window in range(held):
            own = slice(window * CELLS, (window + 1) * CELLS)
            query, key, value = queries[own], keys[own], values[own]
            stacked = jnp.concatenate([query * pair for pair in pairs], 0)
            main_keys = jnp.concatenate([key[:MAIN] * half for half in halves], 0)
            main = jnp.exp2(dot(stacked, main_keys, NT)).astype(jnp.bfloat16)
            rest_keys = jnp.concatenate([key[MAIN:] * mask for mask in masks], 0)
            rest = jnp.exp2(dot(query, rest_keys, NT)).astype(jnp.bfloat16)
            if shifted:
                last = jnp.logical_and(
                    (pl.program_id(0) * held + window) % row_windows == row_windows - 1,
                    lax.axis_index("lat") == lax.axis_size("lat") - 1,
                )
                allow = jnp.where(last, allow_ref[...], 1.0).astype(jnp.bfloat16)
                rest = rest * allow[:, MAIN:]
            for part in range(2):
                lanes = slice(part * MAIN, (part + 1) * MAIN)
                parts = [main[head * CELLS : (head + 1) * CELLS, lanes] for head in range(PART)]
                if shifted:
                    parts = [one * allow[:, :MAIN] for one in parts]
                own_value = value[:, lanes]
                none = jnp.zeros((REST, MAIN), jnp.bfloat16)
                own_rest = [own_value[MAIN:] * mask for mask in narrow]
                other_rest = [none] * PART
                stacked = jnp.concatenate(
                    [own_value[:MAIN] * mask for mask in narrow]
                    + (own_rest + other_rest if part == 0 else other_rest + own_rest),
                    0,
                )
                both = jnp.concatenate([stacked, ones_ref[:, lanes]], 1)
                summed = dot(jnp.concatenate(parts + [rest], 1), both)
                attended[window].append(
                    (summed[:, :MAIN] / summed[:, MAIN:]).astype(jnp.bfloat16)
                )
    attended = jnp.concatenate([jnp.concatenate(parts, 1) for parts in attended], 0)
    projected = dot(attended, w_ref[:, 3 * features :])
    middle = tokens.astype(jnp.float32) + layer_norm(projected, gain_ref[...])
    out_ref[...] = middle.astype(jnp.bfloat16).reshape(out_ref.shape)


def allowed_pairs():
    side = np.arange(CELLS) // QUARTER % 2
    rest = np.tile(side[MAIN:], GROUP)
    return (side[:, None] == np.concatenate([side[:MAIN], rest])[None, :]).astype(np.float32)


def head_columns():
    halves = []
    for part in range(2):
        own = np.arange(part * PART, (part + 1) * PART)
        rows = np.concatenate([np.repeat(own, MAIN), np.repeat(np.arange(GROUP), REST)])
        halves.append(rows[:, None] == np.repeat(own, HEAD)[None, :])
    return np.concatenate(halves, 1).astype(np.float32)


def attend(sources, columns, pieces, gain, sharp, row_windows, after=(), held=2):
    shifted = len(sources) > 1
    kind, pieces = pieces
    features = sources[0].shape[-1]
    count = len(columns) * row_windows
    skipped = columns[0] * row_windows // held
    whole = lambda shape: pl.BlockSpec(shape, lambda i: (0,) * len(shape))
    block = pl.BlockSpec((held, CELLS, features), lambda i: (i, 0, 0))
    strip_block = pl.BlockSpec((2 * held, QUARTER, features), lambda i: (i, 0, 0))
    x_block = pl.BlockSpec((held, CELLS, features), lambda i: (i + skipped, 0, 0))
    ones = jnp.asarray(head_columns(), jnp.bfloat16)
    extra = (jnp.asarray(allowed_pairs()),) if shifted else ()
    return pl.pallas_call(
        functools.partial(attend_kernel, shifted, row_windows, kind, len(pieces)),
        grid=(count // held,),
        out_shape=jax.ShapeDtypeStruct((count, CELLS, features), jnp.bfloat16),
        in_specs=([strip_block] * 2 if shifted else [x_block])
        + [ANY] * len(pieces)
        + [whole((1, features))] * 2
        + [whole(ones.shape)]
        + [whole(e.shape) for e in extra]
        + [ANY] * len(after),
        out_specs=block,
        scratch_shapes=load_scratch(pieces, features, 4 * features),
        compiler_params=pltpu.CompilerParams(vmem_limit_bytes=24 * 2**20),
        cost_estimate=pl.CostEstimate(
            flops=count * 2_000_000_000, bytes_accessed=6_000_000, transcendentals=0
        ),
    )(*sources, *pieces, gain, sharp, ones, *extra, *after)


def feed_kernel(kind, count, hidden_size, chunk, edge, *refs):
    x_ref, pieces, gain_ref = refs[0], refs[1 : 1 + count], refs[1 + count]
    left_ref, right_ref, edge_ref, w_ref, stage_ref, sem = refs[-6:]
    held, _, features = x_ref.shape

    @pl.when(pl.program_id(0) == 0)
    def _():
        load_pieces(kind, pieces, w_ref, stage_ref, sem)

    tokens = x_ref[...].reshape(held * CELLS, features)
    total = jnp.zeros(tokens.shape, jnp.float32)
    for start in range(0, hidden_size, chunk):
        grown = dot(tokens, w_ref[:, start : start + chunk])
        slope = math.sqrt(2.0 / math.pi)
        bent = jnp.tanh(grown * (grown * grown * (0.044715 * slope) + slope))
        hidden = (grown + grown * bent).astype(jnp.bfloat16)
        total = total + dot(
            hidden, w_ref[:, hidden_size + start : hidden_size + start + chunk], NT
        )
    result = tokens.astype(jnp.float32) + layer_norm(0.5 * total, gain_ref[...])
    edge_window, edge_half = edge
    for window in range(held):
        for side, target in enumerate((left_ref, right_ref)):
            for half in range(2):
                start = window * CELLS + (side * 2 + half) * QUARTER
                quarter = result[start : start + QUARTER].astype(jnp.bfloat16)
                target[2 * window + half] = quarter
                if half == edge_half and window == edge_window % held:

                    @pl.when(pl.program_id(0) == edge_window // held)
                    def _(quarter=quarter, side=side):
                        edge_ref[side] = quarter


def feed(windows, column, count, pieces, gain, hidden_size, edge, after=(), held=2):
    _, cells, features = windows.shape
    kind, pieces = pieces
    block = pl.BlockSpec((held, cells, features), lambda i: (i + column * count // held, 0, 0))
    side = pl.BlockSpec((2 * held, QUARTER, features), lambda i: (i, 0, 0))
    return pl.pallas_call(
        functools.partial(feed_kernel, kind, len(pieces), hidden_size, 512, edge),
        grid=(count // held,),
        out_shape=[jax.ShapeDtypeStruct((2 * count, QUARTER, features), jnp.bfloat16)] * 2
        + [jax.ShapeDtypeStruct((2, QUARTER, features), jnp.bfloat16)],
        in_specs=[block]
        + [ANY] * len(pieces)
        + [pl.BlockSpec((1, features), lambda i: (0, 0))]
        + [ANY] * len(after),
        out_specs=[side, side, pl.BlockSpec((2, QUARTER, features), lambda i: (0, 0, 0))],
        scratch_shapes=load_scratch(pieces, features, 2 * hidden_size),
        compiler_params=pltpu.CompilerParams(vmem_limit_bytes=24 * 2**20),
        cost_estimate=pl.CostEstimate(
            flops=FEED_FLOPS,
            bytes_accessed=FEED_BYTES,
            transcendentals=0,
        ),
    )(windows, *pieces, gain, *after)


def shift_from(block, lon_step, lat_step):
    lons, lats = lax.axis_size("lon"), lax.axis_size("lat")
    pairs = []
    for lon in range(lons):
        for lat in range(lats):
            source = (lon + lon_step) % lons * lats + (lat + lat_step) % lats
            pairs.append((source, lon * lats + lat))
    return lax.ppermute(block, ("lon", "lat"), pairs)


def to_windows(cells):
    cols, rows, levels, features = cells.shape
    c, r = WLON // 2, WLAT // 2
    arranged = cells.reshape(cols // WLON, 2, c, rows // WLAT, 2, r, levels, features)
    arranged = arranged.transpose(0, 3, 1, 4, 2, 5, 6, 7)
    return arranged.reshape(-1, CELLS, features)


def strips_kernel(picks, *refs):
    sources, outs = refs[: len(refs) - len(picks)], refs[len(refs) - len(picks) :]
    for pick, target in zip(picks, outs):
        place = 0
        for source, first, count in pick:
            target[place : place + count] = sources[source][first : first + count]
            place += count


def strips(sources, picks):
    shape = sources[0].shape[1:]
    held = pl.BlockSpec(memory_space=pltpu.VMEM)
    return pl.pallas_call(
        functools.partial(strips_kernel, picks),
        out_shape=[
            jax.ShapeDtypeStruct((sum(count for _, _, count in pick),) + shape, jnp.bfloat16)
            for pick in picks
        ],
        in_specs=[held] * len(sources),
        compiler_params=pltpu.CompilerParams(vmem_limit_bytes=10 * 2**20),
    )(*sources)


def from_strips(quarters, cols, rows):
    features = quarters.shape[-1]
    c, r = WLON // 2, WLAT // 2
    arranged = quarters.reshape(cols // c, rows // r, c, r, LEVELS, features)
    return arranged.transpose(0, 2, 1, 3, 4, 5).reshape(cols, rows, LEVELS, features)


def per_device(tokens, qkv_weight, out_weight, up_weight, down_weight, norm_gain, logit_scale):
    cols, rows, _, features = tokens.shape
    hidden_size = up_weight.shape[-1]
    row_windows = rows // WLAT
    weights = (qkv_weight, out_weight, up_weight, down_weight)
    relay = relayed(qkv_weight.shape[1], lax.axis_size("lon"), lax.axis_size("lat"))
    spread = np.arange(HEADS)[:, None] == np.arange(features)[None, :] // HEAD
    sharp = logit_scale[:, :, None] * jnp.asarray(spread * math.log2(math.e), jnp.float32)[None]
    sharp = jnp.sum(sharp, 1)
    windows = to_windows(tokens)

    def attention(block, sources, columns, pieces, after=()):
        gain, scale = norm_gain[block, :1], sharp[block : block + 1]
        return attend(sources, columns, pieces, gain, scale, row_windows, after)

    def forward(block, middle, column, pieces, edge, after=()):
        gain = norm_gain[block, 1:]
        return feed(middle, column, row_windows, pieces, gain, hidden_size, edge, after)

    low_edge, high_edge = (0, 0), (row_windows - 1, 1)
    if relay:
        (own,) = join([], [[(0, weight) for weight in weights[:2]]])
        feed_own, last_own = join(
            [],
            [[(0, weight) for weight in weights[2:]], [(1, weight) for weight in weights]],
            (own,),
        )
        widths = tuple(sum(weight.shape[2] for weight in pair) for pair in (weights[:2], weights[2:]))
        (pair,) = join([[own, across_z(own, 2)]], (), (windows,))
        (feed_pair,) = join([[feed_own, across_z(feed_own, 2)]])
        last_beside = send(last_own, beside)
        (column,) = join([[pair, across_z(pair, 1)]], (), (feed_pair, last_beside))
        received = [send(column, way) for way in (beside, across, corner)]
        sent = [tied(column, received[0])] + received
        pieces = "columns", [column] + received + [send(part, swap) for part in sent]
        last_other = across_z(tied(last_own, feed_pair), 2)
        (last_four,) = join([[last_own, last_beside, last_other, send(last_other, across)]])
        (feed_column,) = join([[feed_pair, across_z(feed_pair, 1)]])
        received = [send(feed_column, way) for way in (beside, across)]
        last_other = across_z(last_four, 1)
        middle_0 = attention(0, [windows], (0,), pieces, (feed_column,))
        first, second = tied((received[0][:2], received[1][2:]), middle_0)
        corners = [send(first, across), send(second, beside)]
        *last_columns, final_one, final_other = halves(last_four, last_other, widths, (middle_0,))
        middle_1 = attention(0, [windows], (1,), pieces, (middle_0, last_columns[0]))
        swapped = [send(part, swap) for part in [feed_column] + tied(received, middle_0)]
        received += join([tied(corners, (middle_1, *swapped))])
        feed_pieces = "columns", [feed_column] + received + swapped + [send(received[2], swap)]
    else:
        gathered = []
        for block in range(2):
            for pair in (weights[:2], weights[2:]):
                chunk = jnp.concatenate([weight[block] for weight in pair], 1)
                gathered.append(lax.all_gather(chunk, "lon", axis=0, tiled=True))
        pieces, feed_pieces, last_pieces, final_pieces = (("rows", [rows]) for rows in gathered)
        middle_0 = attention(0, [windows], (0,), pieces)
        middle_1 = attention(0, [windows], (1,), pieces)
    left_0, right_0, low_0 = forward(0, middle_0, 0, feed_pieces, low_edge)
    below_0 = shift_from(low_0, 0, 1)
    size = left_0.shape[0]
    (ahead,) = strips([left_0, below_0], [[(0, 1, size - 1), (1, 0, 1)]])
    ahead = shift_from(ahead, 1, 0)
    if relay:
        last_received = [
            send(part, way) for part, way in zip(tied(last_columns, middle_1), (across, beside))
        ]
    left_1, right_1, low_1 = forward(0, middle_1, 0, feed_pieces, low_edge, (below_0,))
    below_1 = shift_from(tied(low_1, ahead), 0, 1)
    if relay:
        last_pieces = last_columns + last_received
        last_pieces += [send(part, swap) for part in last_columns + tied(last_received, low_1)]
        last_pieces = "halves", last_pieces
        final_columns = [final_one, final_other]
        final_received = [
            send(part, way)
            for part, way in zip(tied(final_columns, last_received), (across, beside))
        ]
    lefts = strips(
        [right_0, left_1, right_1, below_0, below_1],
        [
            [(0, 1, size - 1), (3, 1, 1)],
            [(1, 1, size - 1), (4, 0, 1)],
            [(2, 1, size - 1), (4, 1, 1)],
        ],
    )
    middle_1 = attention(1, [lefts[2], ahead], (1,), last_pieces)
    if relay:
        final_pieces = final_columns + final_received
        final_pieces += [send(part, swap) for part in final_columns + tied(final_received, middle_1)]
        final_pieces = "halves", final_pieces
    left_1, right_1, high_1 = forward(1, middle_1, 0, final_pieces, high_edge)
    above_1 = shift_from(high_1, 0, -1)
    (behind,) = strips([above_1, right_1], [[(0, 1, 1), (1, 0, size - 1)]])
    behind = shift_from(behind, -1, 0)
    middle_0 = attention(1, lefts[:2], (0,), last_pieces, (above_1,))
    left_0, right_0, high_0 = forward(1, middle_0, 0, final_pieces, high_edge)
    above_0 = shift_from(high_0, 0, -1)
    picks = [(0, 0, size)]
    for place, (low, quarter) in enumerate(((4, 0), (4, 1), (5, 0))):
        picks += [(low, quarter, 1), (place + 1, 0, size - 1)]
    (mixed,) = strips([behind, left_0, right_0, left_1, above_0, above_1], [picks])
    return from_strips(mixed, cols, rows)


def solution(mesh):
    placed = (
        P("lon", "lat", None, None),
        P(None, "lon", None),
        P(None, "lon", None),
        P(None, "lon", None),
        P(None, "lon", None),
        P(),
        P(),
    )
    return jax.shard_map(
        per_device,
        mesh=mesh,
        in_specs=placed,
        out_specs=P("lon", "lat", None, None),
        check_vma=False,
    )
```

```python
import functools
import math

import numpy as np

import jax
import jax.numpy as jnp
from jax import lax
from jax.experimental import pallas as pl
from jax.experimental.pallas import tpu as pltpu
from jax.sharding import PartitionSpec as P

HEADS = 16
HEAD = 32
WLON = 12
WLAT = 6
LEVELS = 2
CELLS = WLON * WLAT * LEVELS
MAIN = 128
REST = CELLS - MAIN
QUARTER = CELLS // 4
GROUP = 8
PART = 4
WIDE = GROUP * HEAD
FEED_FLOPS, FEED_BYTES = 1_000_000, 100_000
Z_ORDER = (0, 2, 1, 3)
ANY = pl.BlockSpec(memory_space=pl.ANY)
NT = (((1,), (1,)), ((), ()))


def dot(a, b, dims=(((1,), (0,)), ((), ()))):
    return lax.dot_general(a, b, dims, preferred_element_type=jnp.float32)


def layer_norm(value, gain_row):
    averaged = jnp.mean(value, -1, keepdims=True)
    centred = value - averaged
    variance = jnp.mean(centred * centred, -1, keepdims=True)
    return centred * lax.rsqrt(variance + 1e-05) * gain_row


def relayed(rows, lon_size, lat_size):
    return lat_size == 2 and rows % 32 == 0 and lon_size == 16


def join_kernel(columns, cuts, *refs):
    outs = refs[len(refs) - sum(len(widths) for _, widths in columns) - len(cuts) :]
    place, out = 0, 0
    for count, widths in columns:
        row = 0
        for piece in refs[place : place + count]:
            start = 0
            for target, width in zip(outs[out : out + len(widths)], widths):
                target[row : row + piece.shape[0]] = piece[:, :, start : start + width]
                start += width
            row += piece.shape[0]
        place, out = place + count, out + len(widths)
    for blocks, chunk_ref in zip(cuts, outs[out:]):
        half = chunk_ref.shape[1]
        first = pl.multiple_of(lax.axis_index("lat") * half, 16)
        start = 0
        for block, source in zip(blocks, refs[place : place + len(blocks)]):
            width = source.shape[2]
            chunk_ref[0, :, start : start + width] = source[block, pl.ds(first, half), :]
            start += width
        place += len(blocks)


def join(columns, cuts=(), after=(), widths=None):
    pieces = [piece for column in columns for piece in column]
    sources = [weight for cut in cuts for _, weight in cut]
    out_shape, sizes = [], []
    for column in columns:
        count, half, width = column[0].shape
        count = sum(piece.shape[0] for piece in column)
        sizes.append((len(column), widths or (width,)))
        for part in widths or (width,):
            out_shape.append(jax.ShapeDtypeStruct((count, half, part), jnp.bfloat16))
    for cut in cuts:
        width = sum(weight.shape[2] for _, weight in cut)
        out_shape.append(jax.ShapeDtypeStruct((1, cut[0][1].shape[1] // 2, width), jnp.bfloat16))
    held = pl.BlockSpec(memory_space=pltpu.VMEM)
    return pl.pallas_call(
        functools.partial(join_kernel, sizes, [[block for block, _ in cut] for cut in cuts]),
        out_shape=out_shape,
        in_specs=[held] * (len(pieces) + len(sources)) + [ANY] * len(after),
        compiler_params=pltpu.CompilerParams(vmem_limit_bytes=10 * 2**20),
    )(*pieces, *sources, *after)


def halves_kernel(widths, here_ref, there_ref, *outs):
    start = 0
    for index, width in enumerate(widths):
        for half in range(2):
            rows, lanes = slice(2 * half, 2 * half + 2), slice(start, start + width)
            outs[2 * index + half][:2] = here_ref[rows, :, lanes]
            outs[2 * index + half][2:] = there_ref[rows, :, lanes]
        start += width


def halves(here, there, widths, after):
    held = pl.BlockSpec(memory_space=pltpu.VMEM)
    return pl.pallas_call(
        lambda *refs: halves_kernel(widths, refs[0], refs[1], *refs[2 + len(after) :]),
        out_shape=[
            jax.ShapeDtypeStruct((4, here.shape[1], width), jnp.bfloat16)
            for width in widths
            for _ in range(2)
        ],
        in_specs=[held] * 2 + [ANY] * len(after),
        compiler_params=pltpu.CompilerParams(vmem_limit_bytes=10 * 2**20),
    )(here, there, *after)


def send(block, move):
    pairs = []
    for lon in range(lax.axis_size("lon")):
        for core in range(2):
            z, y, x, core_to = move(lon // 4, lon // 2 % 2, lon % 2, core)
            pairs.append((lon * 2 + core, (z * 4 + y * 2 + x) * 2 + core_to))
    return lax.ppermute(block, ("lon", "lat"), pairs)


def across_z(block, bit):
    return send(block, lambda z, y, x, c: (z ^ bit, y, x, c))


def swap(z, y, x, c):
    return z, y, x, 1 - c


def tied(array, after):
    return lax.optimization_barrier((array, after))[0]


def beside(z, y, x, c):
    return (z, y, 1 - x, c) if c == 0 else (z, 1 - y, x, c)


def across(z, y, x, c):
    return (z, 1 - y, x, c) if c == 0 else (z, y, 1 - x, c)


def corner(z, y, x, c):
    return z, 1 - y, 1 - x, c


def whole_pieces(column, received):
    return [column] + received + [send(part, swap) for part in [column] + received]


def load_pieces(kind, pieces, w_ref, stage_ref, sem):
    copies = [
        pltpu.make_async_copy(piece, w_ref if kind == "rows" else stage_ref.at[index], sem.at[index])
        for index, piece in enumerate(pieces)
    ]
    for copy in copies:
        copy.start()
    if kind == "rows":
        copies[0].wait()
        return
    half = pieces[0].shape[-2]
    lon, lat = lax.axis_index("lon"), lax.axis_index("lat")
    z, y, x = lon // 4, lon // 2 % 2, lon % 2
    by_x, by_y = y * 2 + 1 - x, (1 - y) * 2 + x
    for index, copy in enumerate(copies):
        core = lat if index < 4 else 1 - lat
        own, opposite = y * 2 + x, (1 - y) * 2 + 1 - x
        one = jnp.where(core == 0, by_x, by_y)
        other = jnp.where(core == 0, by_y, by_x)
        copy.wait()
        for step in range(4):
            if kind == "columns":
                square, along = (own, one, other, opposite)[index % 4], Z_ORDER[step]
            else:
                pairs = ((own, one), (own, other), (other, opposite), (one, opposite))
                square, along = pairs[index % 4][step % 2], index % 2 * 2 + step // 2
            row = pl.multiple_of((((z ^ along) * 4 + square) * 2 + core) * half, 16)
            w_ref[pl.ds(row, half), :] = stage_ref[index, step]


def load_scratch(pieces, rows, width):
    stage = (len(pieces),) + pieces[0].shape if len(pieces) > 1 else (1, 1, 16, 128)
    return [
        pltpu.VMEM((rows, width), jnp.bfloat16),
        pltpu.VMEM(stage, jnp.bfloat16),
        pltpu.SemaphoreType.DMA((len(pieces),)),
    ]


def attend_kernel(shifted, row_windows, kind, count, *refs):
    sources = 2 if shifted else 1
    x_refs, pieces = refs[:sources], refs[sources : sources + count]
    gain_ref, sharp_ref, ones_ref = refs[sources + count : sources + count + 3]
    allow_ref = refs[sources + count + 3] if shifted else None
    out_ref, w_ref, stage_ref, sem = refs[-4:]
    held, _, features = out_ref.shape

    @pl.when(pl.program_id(0) == 0)
    def _():
        load_pieces(kind, pieces, w_ref, stage_ref, sem)

    if shifted:
        quarters = []
        for window in range(held):
            for strip_ref in x_refs:
                quarters += [strip_ref[2 * window + half].astype(jnp.float32) for half in range(2)]
        tokens = jnp.concatenate(quarters, 0).astype(jnp.bfloat16)
    else:
        tokens = x_refs[0][...].reshape(held * CELLS, features)
    channel = lax.broadcasted_iota(jnp.int32, (WIDE, WIDE), 0) // HEAD
    same_head = jnp.where(
        channel == lax.broadcasted_iota(jnp.int32, (WIDE, WIDE), 1) // HEAD, 1.0, 0.0
    ).astype(jnp.bfloat16)
    lane_head = lax.broadcasted_iota(jnp.int32, (1, WIDE), 1) // HEAD
    ones = lambda condition: jnp.where(condition, 1.0, 0.0).astype(jnp.bfloat16)
    pairs = [ones(lane_head % PART == head) for head in range(PART)]
    halves = [ones(lane_head // PART == part) for part in range(2)]
    masks = [ones(lane_head == head) for head in range(GROUP)]
    narrow = [ones(lane_head[:, :MAIN] == head) for head in range(PART)]

    def units(part):
        rounded = part.astype(jnp.bfloat16)
        length2 = dot(rounded * rounded, same_head)
        return part * lax.rsqrt(jnp.maximum(length2, 0.25 * HEAD))

    attended = [[] for _ in range(held)]
    for group in range(HEADS // GROUP):
        lanes = [slice(n * features + group * WIDE, n * features + (group + 1) * WIDE) for n in range(3)]
        queries = (units(dot(tokens, w_ref[:, lanes[0]])) * sharp_ref[:, lanes[0]]).astype(jnp.bfloat16)
        keys = units(dot(tokens, w_ref[:, lanes[1]])).astype(jnp.bfloat16)
        values = dot(tokens, w_ref[:, lanes[2]]).astype(jnp.bfloat16)
        for window in range(held):
            own = slice(window * CELLS, (window + 1) * CELLS)
            query, key, value = queries[own], keys[own], values[own]
            stacked = jnp.concatenate([query * pair for pair in pairs], 0)
            main_keys = jnp.concatenate([key[:MAIN] * half for half in halves], 0)
            main = jnp.exp2(dot(stacked, main_keys, NT)).astype(jnp.bfloat16)
            rest_keys = jnp.concatenate([key[MAIN:] * mask for mask in masks], 0)
            rest = jnp.exp2(dot(query, rest_keys, NT)).astype(jnp.bfloat16)
            if shifted:
                last = jnp.logical_and(
                    (pl.program_id(0) * held + window) % row_windows == row_windows - 1,
                    lax.axis_index("lat") == lax.axis_size("lat") - 1,
                )
                allow = jnp.where(last, allow_ref[...], 1.0).astype(jnp.bfloat16)
                rest = rest * allow[:, MAIN:]
            for part in range(2):
                lanes = slice(part * MAIN, (part + 1) * MAIN)
                parts = [main[head * CELLS : (head + 1) * CELLS, lanes] for head in range(PART)]
                if shifted:
                    parts = [one * allow[:, :MAIN] for one in parts]
                own_value = value[:, lanes]
                none = jnp.zeros((REST, MAIN), jnp.bfloat16)
                own_rest = [own_value[MAIN:] * mask for mask in narrow]
                other_rest = [none] * PART
                stacked = jnp.concatenate(
                    [own_value[:MAIN] * mask for mask in narrow]
                    + (own_rest + other_rest if part == 0 else other_rest + own_rest),
                    0,
                )
                both = jnp.concatenate([stacked, ones_ref[:, lanes]], 1)
                summed = dot(jnp.concatenate(parts + [rest], 1), both)
                attended[window].append(
                    (summed[:, :MAIN] / summed[:, MAIN:]).astype(jnp.bfloat16)
                )
    attended = jnp.concatenate([jnp.concatenate(parts, 1) for parts in attended], 0)
    projected = dot(attended, w_ref[:, 3 * features :])
    middle = tokens.astype(jnp.float32) + layer_norm(projected, gain_ref[...])
    out_ref[...] = middle.astype(jnp.bfloat16).reshape(out_ref.shape)


def allowed_pairs():
    side = np.arange(CELLS) // QUARTER % 2
    rest = np.tile(side[MAIN:], GROUP)
    return (side[:, None] == np.concatenate([side[:MAIN], rest])[None, :]).astype(np.float32)


def head_columns():
    halves = []
    for part in range(2):
        own = np.arange(part * PART, (part + 1) * PART)
        rows = np.concatenate([np.repeat(own, MAIN), np.repeat(np.arange(GROUP), REST)])
        halves.append(rows[:, None] == np.repeat(own, HEAD)[None, :])
    return np.concatenate(halves, 1).astype(np.float32)


def attend(sources, columns, pieces, gain, sharp, row_windows, after=(), held=2):
    shifted = len(sources) > 1
    kind, pieces = pieces
    features = sources[0].shape[-1]
    count = len(columns) * row_windows
    skipped = columns[0] * row_windows // held
    whole = lambda shape: pl.BlockSpec(shape, lambda i: (0,) * len(shape))
    block = pl.BlockSpec((held, CELLS, features), lambda i: (i, 0, 0))
    strip_block = pl.BlockSpec((2 * held, QUARTER, features), lambda i: (i, 0, 0))
    x_block = pl.BlockSpec((held, CELLS, features), lambda i: (i + skipped, 0, 0))
    ones = jnp.asarray(head_columns(), jnp.bfloat16)
    extra = (jnp.asarray(allowed_pairs()),) if shifted else ()
    return pl.pallas_call(
        functools.partial(attend_kernel, shifted, row_windows, kind, len(pieces)),
        grid=(count // held,),
        out_shape=jax.ShapeDtypeStruct((count, CELLS, features), jnp.bfloat16),
        in_specs=([strip_block] * 2 if shifted else [x_block])
        + [ANY] * len(pieces)
        + [whole((1, features))] * 2
        + [whole(ones.shape)]
        + [whole(e.shape) for e in extra]
        + [ANY] * len(after),
        out_specs=block,
        scratch_shapes=load_scratch(pieces, features, 4 * features),
        compiler_params=pltpu.CompilerParams(vmem_limit_bytes=24 * 2**20),
        cost_estimate=pl.CostEstimate(
            flops=count * 2_000_000_000, bytes_accessed=6_000_000, transcendentals=0
        ),
    )(*sources, *pieces, gain, sharp, ones, *extra, *after)


def feed_kernel(kind, count, hidden_size, chunk, edge, *refs):
    x_ref, pieces, gain_ref = refs[0], refs[1 : 1 + count], refs[1 + count]
    left_ref, right_ref, edge_ref, w_ref, stage_ref, sem = refs[-6:]
    held, _, features = x_ref.shape

    @pl.when(pl.program_id(0) == 0)
    def _():
        load_pieces(kind, pieces, w_ref, stage_ref, sem)

    tokens = x_ref[...].reshape(held * CELLS, features)
    total = jnp.zeros(tokens.shape, jnp.float32)
    for start in range(0, hidden_size, chunk):
        grown = dot(tokens, w_ref[:, start : start + chunk])
        slope = math.sqrt(2.0 / math.pi)
        bent = jnp.tanh(grown * (grown * grown * (0.044715 * slope) + slope))
        hidden = (grown + grown * bent).astype(jnp.bfloat16)
        total = total + dot(
            hidden, w_ref[:, hidden_size + start : hidden_size + start + chunk], NT
        )
    result = tokens.astype(jnp.float32) + layer_norm(0.5 * total, gain_ref[...])
    edge_window, edge_half = edge
    for window in range(held):
        for side, target in enumerate((left_ref, right_ref)):
            for half in range(2):
                start = window * CELLS + (side * 2 + half) * QUARTER
                quarter = result[start : start + QUARTER].astype(jnp.bfloat16)
                target[2 * window + half] = quarter
                if half == edge_half and window == edge_window % held:

                    @pl.when(pl.program_id(0) == edge_window // held)
                    def _(quarter=quarter, side=side):
                        edge_ref[side] = quarter


def feed(windows, column, count, pieces, gain, hidden_size, edge, after=(), held=2):
    _, cells, features = windows.shape
    kind, pieces = pieces
    block = pl.BlockSpec((held, cells, features), lambda i: (i + column * count // held, 0, 0))
    side = pl.BlockSpec((2 * held, QUARTER, features), lambda i: (i, 0, 0))
    return pl.pallas_call(
        functools.partial(feed_kernel, kind, len(pieces), hidden_size, 512, edge),
        grid=(count // held,),
        out_shape=[jax.ShapeDtypeStruct((2 * count, QUARTER, features), jnp.bfloat16)] * 2
        + [jax.ShapeDtypeStruct((2, QUARTER, features), jnp.bfloat16)],
        in_specs=[block]
        + [ANY] * len(pieces)
        + [pl.BlockSpec((1, features), lambda i: (0, 0))]
        + [ANY] * len(after),
        out_specs=[side, side, pl.BlockSpec((2, QUARTER, features), lambda i: (0, 0, 0))],
        scratch_shapes=load_scratch(pieces, features, 2 * hidden_size),
        compiler_params=pltpu.CompilerParams(vmem_limit_bytes=24 * 2**20),
        cost_estimate=pl.CostEstimate(
            flops=FEED_FLOPS,
            bytes_accessed=FEED_BYTES,
            transcendentals=0,
        ),
    )(windows, *pieces, gain, *after)


def shift_from(block, lon_step, lat_step):
    lons, lats = lax.axis_size("lon"), lax.axis_size("lat")
    pairs = []
    for lon in range(lons):
        for lat in range(lats):
            source = (lon + lon_step) % lons * lats + (lat + lat_step) % lats
            pairs.append((source, lon * lats + lat))
    return lax.ppermute(block, ("lon", "lat"), pairs)


def to_windows(cells):
    cols, rows, levels, features = cells.shape
    c, r = WLON // 2, WLAT // 2
    arranged = cells.reshape(cols // WLON, 2, c, rows // WLAT, 2, r, levels, features)
    arranged = arranged.transpose(0, 3, 1, 4, 2, 5, 6, 7)
    return arranged.reshape(-1, CELLS, features)


def strips_kernel(picks, *refs):
    sources, outs = refs[: len(refs) - len(picks)], refs[len(refs) - len(picks) :]
    for pick, target in zip(picks, outs):
        place = 0
        for source, first, count in pick:
            target[place : place + count] = sources[source][first : first + count]
            place += count


def strips(sources, picks):
    shape = sources[0].shape[1:]
    held = pl.BlockSpec(memory_space=pltpu.VMEM)
    return pl.pallas_call(
        functools.partial(strips_kernel, picks),
        out_shape=[
            jax.ShapeDtypeStruct((sum(count for _, _, count in pick),) + shape, jnp.bfloat16)
            for pick in picks
        ],
        in_specs=[held] * len(sources),
        compiler_params=pltpu.CompilerParams(vmem_limit_bytes=10 * 2**20),
    )(*sources)


def from_strips(quarters, cols, rows):
    features = quarters.shape[-1]
    c, r = WLON // 2, WLAT // 2
    arranged = quarters.reshape(cols // c, rows // r, c, r, LEVELS, features)
    return arranged.transpose(0, 2, 1, 3, 4, 5).reshape(cols, rows, LEVELS, features)


def per_device(tokens, qkv_weight, out_weight, up_weight, down_weight, norm_gain, logit_scale):
    cols, rows, _, features = tokens.shape
    hidden_size = up_weight.shape[-1]
    row_windows = rows // WLAT
    weights = (qkv_weight, out_weight, up_weight, down_weight)
    relay = relayed(qkv_weight.shape[1], lax.axis_size("lon"), lax.axis_size("lat"))
    spread = np.arange(HEADS)[:, None] == np.arange(features)[None, :] // HEAD
    sharp = logit_scale[:, :, None] * jnp.asarray(spread * math.log2(math.e), jnp.float32)[None]
    sharp = jnp.sum(sharp, 1)
    windows = to_windows(tokens)

    def attention(block, sources, columns, pieces, after=()):
        gain, scale = norm_gain[block, :1], sharp[block : block + 1]
        return attend(sources, columns, pieces, gain, scale, row_windows, after)

    def forward(block, middle, column, pieces, edge, after=()):
        gain = norm_gain[block, 1:]
        return feed(middle, column, row_windows, pieces, gain, hidden_size, edge, after)

    low_edge, high_edge = (0, 0), (row_windows - 1, 1)
    if relay:
        (own,) = join([], [[(0, weight) for weight in weights[:2]]])
        feed_own, last_own = join(
            [],
            [[(0, weight) for weight in weights[2:]], [(1, weight) for weight in weights]],
            (own,),
        )
        widths = tuple(sum(weight.shape[2] for weight in pair) for pair in (weights[:2], weights[2:]))
        (pair,) = join([[own, across_z(own, 2)]], (), (windows,))
        (feed_pair,) = join([[feed_own, across_z(feed_own, 2)]])
        last_beside = send(last_own, beside)
        (column,) = join([[pair, across_z(pair, 1)]], (), (feed_pair, last_beside))
        received = [send(column, way) for way in (beside, across, corner)]
        sent = [tied(column, received[0])] + received
        pieces = "columns", [column] + received + [send(part, swap) for part in sent]
        last_other = across_z(tied(last_own, column), 2)
        last_across = send(tied(last_other, received[0]), across)
        last_four, final_four = join(
            [[last_own, last_beside, last_other, last_across]], widths=widths
        )
        (feed_column,) = join([[feed_pair, across_z(feed_pair, 1)]])
        received = [send(feed_column, way) for way in (beside, across)]
        last_other = across_z(last_four, 1)
        middle_0 = attention(0, [windows], (0,), pieces, (feed_column,))
        first, second = tied((received[0][:2], received[1][2:]), middle_0)
        corners = [send(first, across), send(second, beside)]
        last_columns = list(halves(last_four, last_other, widths[:1], (middle_0,)))
        final_other = across_z(tied(final_four, middle_0), 1)
        middle_1 = attention(0, [windows], (1,), pieces, (middle_0, last_columns[0]))
        swapped = [send(part, swap) for part in [feed_column] + tied(received, middle_0)]
        received += join([tied(corners, (middle_1, *swapped))])
        feed_pieces = "columns", [feed_column] + received + swapped + [send(received[2], swap)]
    else:
        gathered = []
        for block in range(2):
            for pair in (weights[:2], weights[2:]):
                chunk = jnp.concatenate([weight[block] for weight in pair], 1)
                gathered.append(lax.all_gather(chunk, "lon", axis=0, tiled=True))
        pieces, feed_pieces, last_pieces, final_pieces = (("rows", [rows]) for rows in gathered)
        middle_0 = attention(0, [windows], (0,), pieces)
        middle_1 = attention(0, [windows], (1,), pieces)
    left_0, right_0, low_0 = forward(0, middle_0, 0, feed_pieces, low_edge)
    below_0 = shift_from(low_0, 0, 1)
    size = left_0.shape[0]
    (ahead,) = strips([left_0, below_0], [[(0, 1, size - 1), (1, 0, 1)]])
    ahead = shift_from(ahead, 1, 0)
    after = (below_0,)
    if relay:
        last_received = [
            send(part, way) for part, way in zip(tied(last_columns, middle_1), (across, beside))
        ]
        final_columns = list(halves(final_four, final_other, widths[1:], (low_0,)))
        after += (final_columns[0],)
    left_1, right_1, low_1 = forward(0, middle_1, 0, feed_pieces, low_edge, after)
    below_1 = shift_from(tied(low_1, ahead), 0, 1)
    if relay:
        last_pieces = last_columns + last_received
        last_pieces += [send(part, swap) for part in last_columns + tied(last_received, low_1)]
        last_pieces = "halves", last_pieces
        final_received = [
            send(part, way)
            for part, way in zip(tied(final_columns, last_received), (across, beside))
        ]
    lefts = strips(
        [right_0, left_1, right_1, below_0, below_1],
        [
            [(0, 1, size - 1), (3, 1, 1)],
            [(1, 1, size - 1), (4, 0, 1)],
            [(2, 1, size - 1), (4, 1, 1)],
        ],
    )
    middle_1 = attention(1, [lefts[2], ahead], (1,), last_pieces)
    if relay:
        final_pieces = final_columns + final_received
        final_pieces += [send(part, swap) for part in final_columns + tied(final_received, middle_1)]
        final_pieces = "halves", final_pieces
    left_1, right_1, high_1 = forward(1, middle_1, 0, final_pieces, high_edge)
    above_1 = shift_from(high_1, 0, -1)
    (behind,) = strips([above_1, right_1], [[(0, 1, 1), (1, 0, size - 1)]])
    behind = shift_from(behind, -1, 0)
    middle_0 = attention(1, lefts[:2], (0,), last_pieces, (above_1,))
    left_0, right_0, high_0 = forward(1, middle_0, 0, final_pieces, high_edge)
    above_0 = shift_from(high_0, 0, -1)
    picks = [(0, 0, size)]
    for place, (low, quarter) in enumerate(((4, 0), (4, 1), (5, 0))):
        picks += [(low, quarter, 1), (place + 1, 0, size - 1)]
    (mixed,) = strips([behind, left_0, right_0, left_1, above_0, above_1], [picks])
    return from_strips(mixed, cols, rows)


def solution(mesh):
    placed = (
        P("lon", "lat", None, None),
        P(None, "lon", None),
        P(None, "lon", None),
        P(None, "lon", None),
        P(None, "lon", None),
        P(),
        P(),
    )
    return jax.shard_map(
        per_device,
        mesh=mesh,
        in_specs=placed,
        out_specs=P("lon", "lat", None, None),
        check_vma=False,
    )
```

```python
import functools
import math

import numpy as np

import jax
import jax.numpy as jnp
from jax import lax
from jax.experimental import pallas as pl
from jax.experimental.pallas import tpu as pltpu
from jax.sharding import PartitionSpec as P

HEADS = 16
HEAD = 32
WLON = 12
WLAT = 6
LEVELS = 2
CELLS = WLON * WLAT * LEVELS
MAIN = 128
REST = CELLS - MAIN
QUARTER = CELLS // 4
GROUP = 8
PART = 4
WIDE = GROUP * HEAD
FEED_FLOPS, FEED_BYTES = 1_000_000, 100_000
Z_ORDER = (0, 2, 1, 3)
ANY = pl.BlockSpec(memory_space=pl.ANY)
NT = (((1,), (1,)), ((), ()))


def dot(a, b, dims=(((1,), (0,)), ((), ()))):
    return lax.dot_general(a, b, dims, preferred_element_type=jnp.float32)


def layer_norm(value, gain_row):
    averaged = jnp.mean(value, -1, keepdims=True)
    centred = value - averaged
    variance = jnp.mean(centred * centred, -1, keepdims=True)
    return centred * lax.rsqrt(variance + 1e-05) * gain_row


def relayed(rows, lon_size, lat_size):
    return lat_size == 2 and rows % 32 == 0 and lon_size == 16


def join_kernel(columns, cuts, *refs):
    outs = refs[len(refs) - sum(len(widths) for _, widths in columns) - len(cuts) :]
    place, out = 0, 0
    for count, widths in columns:
        row = 0
        for piece in refs[place : place + count]:
            start = 0
            for target, width in zip(outs[out : out + len(widths)], widths):
                target[row : row + piece.shape[0]] = piece[:, :, start : start + width]
                start += width
            row += piece.shape[0]
        place, out = place + count, out + len(widths)
    for blocks, chunk_ref in zip(cuts, outs[out:]):
        half = chunk_ref.shape[1]
        first = pl.multiple_of(lax.axis_index("lat") * half, 16)
        start = 0
        for block, source in zip(blocks, refs[place : place + len(blocks)]):
            width = source.shape[2]
            chunk_ref[0, :, start : start + width] = source[block, pl.ds(first, half), :]
            start += width
        place += len(blocks)


def join(columns, cuts=(), after=(), widths=None):
    pieces = [piece for column in columns for piece in column]
    sources = [weight for cut in cuts for _, weight in cut]
    out_shape, sizes = [], []
    for column in columns:
        count, half, width = column[0].shape
        count = sum(piece.shape[0] for piece in column)
        sizes.append((len(column), widths or (width,)))
        for part in widths or (width,):
            out_shape.append(jax.ShapeDtypeStruct((count, half, part), jnp.bfloat16))
    for cut in cuts:
        width = sum(weight.shape[2] for _, weight in cut)
        out_shape.append(jax.ShapeDtypeStruct((1, cut[0][1].shape[1] // 2, width), jnp.bfloat16))
    held = pl.BlockSpec(memory_space=pltpu.VMEM)
    return pl.pallas_call(
        functools.partial(join_kernel, sizes, [[block for block, _ in cut] for cut in cuts]),
        out_shape=out_shape,
        in_specs=[held] * (len(pieces) + len(sources)) + [ANY] * len(after),
        compiler_params=pltpu.CompilerParams(vmem_limit_bytes=10 * 2**20),
    )(*pieces, *sources, *after)


def halves_kernel(widths, here_ref, there_ref, *outs):
    start = 0
    for index, width in enumerate(widths):
        for half in range(2):
            rows, lanes = slice(2 * half, 2 * half + 2), slice(start, start + width)
            outs[2 * index + half][:2] = here_ref[rows, :, lanes]
            outs[2 * index + half][2:] = there_ref[rows, :, lanes]
        start += width


def halves(here, there, widths, after):
    held = pl.BlockSpec(memory_space=pltpu.VMEM)
    return pl.pallas_call(
        lambda *refs: halves_kernel(widths, refs[0], refs[1], *refs[2 + len(after) :]),
        out_shape=[
            jax.ShapeDtypeStruct((4, here.shape[1], width), jnp.bfloat16)
            for width in widths
            for _ in range(2)
        ],
        in_specs=[held] * 2 + [ANY] * len(after),
        compiler_params=pltpu.CompilerParams(vmem_limit_bytes=10 * 2**20),
    )(here, there, *after)


def send(block, move):
    pairs = []
    for lon in range(lax.axis_size("lon")):
        for core in range(2):
            z, y, x, core_to = move(lon // 4, lon // 2 % 2, lon % 2, core)
            pairs.append((lon * 2 + core, (z * 4 + y * 2 + x) * 2 + core_to))
    return lax.ppermute(block, ("lon", "lat"), pairs)


def across_z(block, bit):
    return send(block, lambda z, y, x, c: (z ^ bit, y, x, c))


def swap(z, y, x, c):
    return z, y, x, 1 - c


def tied(array, after):
    return lax.optimization_barrier((array, after))[0]


def beside(z, y, x, c):
    return (z, y, 1 - x, c) if c == 0 else (z, 1 - y, x, c)


def across(z, y, x, c):
    return (z, 1 - y, x, c) if c == 0 else (z, y, 1 - x, c)


def corner(z, y, x, c):
    return z, 1 - y, 1 - x, c


def whole_pieces(column, received):
    return [column] + received + [send(part, swap) for part in [column] + received]


def load_pieces(kind, pieces, w_ref, stage_ref, sem):
    copies = [
        pltpu.make_async_copy(piece, w_ref if kind == "rows" else stage_ref.at[index], sem.at[index])
        for index, piece in enumerate(pieces)
    ]
    for copy in copies:
        copy.start()
    if kind == "rows":
        copies[0].wait()
        return
    half = pieces[0].shape[-2]
    lon, lat = lax.axis_index("lon"), lax.axis_index("lat")
    z, y, x = lon // 4, lon // 2 % 2, lon % 2
    by_x, by_y = y * 2 + 1 - x, (1 - y) * 2 + x
    for index, copy in enumerate(copies):
        core = lat if index < 4 else 1 - lat
        own, opposite = y * 2 + x, (1 - y) * 2 + 1 - x
        one = jnp.where(core == 0, by_x, by_y)
        other = jnp.where(core == 0, by_y, by_x)
        copy.wait()
        for step in range(4):
            if kind == "columns":
                square, along = (own, one, other, opposite)[index % 4], Z_ORDER[step]
            else:
                pairs = ((own, one), (own, other), (other, opposite), (one, opposite))
                square, along = pairs[index % 4][step % 2], index % 2 * 2 + step // 2
            row = pl.multiple_of((((z ^ along) * 4 + square) * 2 + core) * half, 16)
            w_ref[pl.ds(row, half), :] = stage_ref[index, step]


def load_scratch(pieces, rows, width):
    stage = (len(pieces),) + pieces[0].shape if len(pieces) > 1 else (1, 1, 16, 128)
    return [
        pltpu.VMEM((rows, width), jnp.bfloat16),
        pltpu.VMEM(stage, jnp.bfloat16),
        pltpu.SemaphoreType.DMA((len(pieces),)),
    ]


def attend_kernel(shifted, row_windows, kind, count, *refs):
    sources = 2 if shifted else 1
    x_refs, pieces = refs[:sources], refs[sources : sources + count]
    gain_ref, sharp_ref, ones_ref = refs[sources + count : sources + count + 3]
    allow_ref = refs[sources + count + 3] if shifted else None
    out_ref, w_ref, stage_ref, sem = refs[-4:]
    held, _, features = out_ref.shape

    @pl.when(pl.program_id(0) == 0)
    def _():
        load_pieces(kind, pieces, w_ref, stage_ref, sem)

    if shifted:
        quarters = []
        for window in range(held):
            for strip_ref in x_refs:
                quarters += [strip_ref[2 * window + half].astype(jnp.float32) for half in range(2)]
        tokens = jnp.concatenate(quarters, 0).astype(jnp.bfloat16)
    else:
        tokens = x_refs[0][...].reshape(held * CELLS, features)
    channel = lax.broadcasted_iota(jnp.int32, (WIDE, WIDE), 0) // HEAD
    same_head = jnp.where(
        channel == lax.broadcasted_iota(jnp.int32, (WIDE, WIDE), 1) // HEAD, 1.0, 0.0
    ).astype(jnp.bfloat16)
    lane_head = lax.broadcasted_iota(jnp.int32, (1, WIDE), 1) // HEAD
    ones = lambda condition: jnp.where(condition, 1.0, 0.0).astype(jnp.bfloat16)
    pairs = [ones(lane_head % PART == head) for head in range(PART)]
    halves = [ones(lane_head // PART == part) for part in range(2)]
    masks = [ones(lane_head == head) for head in range(GROUP)]
    narrow = [ones(lane_head[:, :MAIN] == head) for head in range(PART)]

    def units(part):
        rounded = part.astype(jnp.bfloat16)
        length2 = dot(rounded * rounded, same_head)
        return part * lax.rsqrt(jnp.maximum(length2, 0.25 * HEAD))

    attended = [[] for _ in range(held)]
    for group in range(HEADS // GROUP):
        lanes = [slice(n * features + group * WIDE, n * features + (group + 1) * WIDE) for n in range(3)]
        queries = (units(dot(tokens, w_ref[:, lanes[0]])) * sharp_ref[:, lanes[0]]).astype(jnp.bfloat16)
        keys = units(dot(tokens, w_ref[:, lanes[1]])).astype(jnp.bfloat16)
        values = dot(tokens, w_ref[:, lanes[2]]).astype(jnp.bfloat16)
        for window in range(held):
            own = slice(window * CELLS, (window + 1) * CELLS)
            query, key, value = queries[own], keys[own], values[own]
            stacked = jnp.concatenate([query * pair for pair in pairs], 0)
            main_keys = jnp.concatenate([key[:MAIN] * half for half in halves], 0)
            main = jnp.exp2(dot(stacked, main_keys, NT)).astype(jnp.bfloat16)
            rest_keys = jnp.concatenate([key[MAIN:] * mask for mask in masks], 0)
            rest = jnp.exp2(dot(query, rest_keys, NT)).astype(jnp.bfloat16)
            if shifted:
                last = jnp.logical_and(
                    (pl.program_id(0) * held + window) % row_windows == row_windows - 1,
                    lax.axis_index("lat") == lax.axis_size("lat") - 1,
                )
                allow = jnp.where(last, allow_ref[...], 1.0).astype(jnp.bfloat16)
                rest = rest * allow[:, MAIN:]
            for part in range(2):
                lanes = slice(part * MAIN, (part + 1) * MAIN)
                parts = [main[head * CELLS : (head + 1) * CELLS, lanes] for head in range(PART)]
                if shifted:
                    parts = [one * allow[:, :MAIN] for one in parts]
                own_value = value[:, lanes]
                none = jnp.zeros((REST, MAIN), jnp.bfloat16)
                own_rest = [own_value[MAIN:] * mask for mask in narrow]
                other_rest = [none] * PART
                stacked = jnp.concatenate(
                    [own_value[:MAIN] * mask for mask in narrow]
                    + (own_rest + other_rest if part == 0 else other_rest + own_rest),
                    0,
                )
                both = jnp.concatenate([stacked, ones_ref[:, lanes]], 1)
                summed = dot(jnp.concatenate(parts + [rest], 1), both)
                attended[window].append(
                    (summed[:, :MAIN] / summed[:, MAIN:]).astype(jnp.bfloat16)
                )
    attended = jnp.concatenate([jnp.concatenate(parts, 1) for parts in attended], 0)
    projected = dot(attended, w_ref[:, 3 * features :])
    middle = tokens.astype(jnp.float32) + layer_norm(projected, gain_ref[...])
    out_ref[...] = middle.astype(jnp.bfloat16).reshape(out_ref.shape)


def allowed_pairs():
    side = np.arange(CELLS) // QUARTER % 2
    rest = np.tile(side[MAIN:], GROUP)
    return (side[:, None] == np.concatenate([side[:MAIN], rest])[None, :]).astype(np.float32)


def head_columns():
    halves = []
    for part in range(2):
        own = np.arange(part * PART, (part + 1) * PART)
        rows = np.concatenate([np.repeat(own, MAIN), np.repeat(np.arange(GROUP), REST)])
        halves.append(rows[:, None] == np.repeat(own, HEAD)[None, :])
    return np.concatenate(halves, 1).astype(np.float32)


def attend(sources, columns, pieces, gain, sharp, row_windows, after=(), held=2):
    shifted = len(sources) > 1
    kind, pieces = pieces
    features = sources[0].shape[-1]
    count = len(columns) * row_windows
    skipped = columns[0] * row_windows // held
    whole = lambda shape: pl.BlockSpec(shape, lambda i: (0,) * len(shape))
    block = pl.BlockSpec((held, CELLS, features), lambda i: (i, 0, 0))
    strip_block = pl.BlockSpec((2 * held, QUARTER, features), lambda i: (i, 0, 0))
    x_block = pl.BlockSpec((held, CELLS, features), lambda i: (i + skipped, 0, 0))
    ones = jnp.asarray(head_columns(), jnp.bfloat16)
    extra = (jnp.asarray(allowed_pairs()),) if shifted else ()
    return pl.pallas_call(
        functools.partial(attend_kernel, shifted, row_windows, kind, len(pieces)),
        grid=(count // held,),
        out_shape=jax.ShapeDtypeStruct((count, CELLS, features), jnp.bfloat16),
        in_specs=([strip_block] * 2 if shifted else [x_block])
        + [ANY] * len(pieces)
        + [whole((1, features))] * 2
        + [whole(ones.shape)]
        + [whole(e.shape) for e in extra]
        + [ANY] * len(after),
        out_specs=block,
        scratch_shapes=load_scratch(pieces, features, 4 * features),
        compiler_params=pltpu.CompilerParams(vmem_limit_bytes=24 * 2**20),
        cost_estimate=pl.CostEstimate(
            flops=count * 2_000_000_000, bytes_accessed=6_000_000, transcendentals=0
        ),
    )(*sources, *pieces, gain, sharp, ones, *extra, *after)


def feed_kernel(kind, count, hidden_size, chunk, edge, *refs):
    x_ref, pieces, gain_ref = refs[0], refs[1 : 1 + count], refs[1 + count]
    left_ref, right_ref, edge_ref, w_ref, stage_ref, sem = refs[-6:]
    held, _, features = x_ref.shape

    @pl.when(pl.program_id(0) == 0)
    def _():
        load_pieces(kind, pieces, w_ref, stage_ref, sem)

    tokens = x_ref[...].reshape(held * CELLS, features)
    total = jnp.zeros(tokens.shape, jnp.float32)
    for start in range(0, hidden_size, chunk):
        grown = dot(tokens, w_ref[:, start : start + chunk])
        slope = math.sqrt(2.0 / math.pi)
        bent = jnp.tanh(grown * (grown * grown * (0.044715 * slope) + slope))
        hidden = (grown + grown * bent).astype(jnp.bfloat16)
        total = total + dot(
            hidden, w_ref[:, hidden_size + start : hidden_size + start + chunk], NT
        )
    result = tokens.astype(jnp.float32) + layer_norm(0.5 * total, gain_ref[...])
    edge_window, edge_half = edge
    for window in range(held):
        for side, target in enumerate((left_ref, right_ref)):
            for half in range(2):
                start = window * CELLS + (side * 2 + half) * QUARTER
                quarter = result[start : start + QUARTER].astype(jnp.bfloat16)
                target[2 * window + half] = quarter
                if half == edge_half and window == edge_window % held:

                    @pl.when(pl.program_id(0) == edge_window // held)
                    def _(quarter=quarter, side=side):
                        edge_ref[side] = quarter


def feed(windows, column, count, pieces, gain, hidden_size, edge, after=(), held=2):
    _, cells, features = windows.shape
    kind, pieces = pieces
    block = pl.BlockSpec((held, cells, features), lambda i: (i + column * count // held, 0, 0))
    side = pl.BlockSpec((2 * held, QUARTER, features), lambda i: (i, 0, 0))
    return pl.pallas_call(
        functools.partial(feed_kernel, kind, len(pieces), hidden_size, 512, edge),
        grid=(count // held,),
        out_shape=[jax.ShapeDtypeStruct((2 * count, QUARTER, features), jnp.bfloat16)] * 2
        + [jax.ShapeDtypeStruct((2, QUARTER, features), jnp.bfloat16)],
        in_specs=[block]
        + [ANY] * len(pieces)
        + [pl.BlockSpec((1, features), lambda i: (0, 0))]
        + [ANY] * len(after),
        out_specs=[side, side, pl.BlockSpec((2, QUARTER, features), lambda i: (0, 0, 0))],
        scratch_shapes=load_scratch(pieces, features, 2 * hidden_size),
        compiler_params=pltpu.CompilerParams(vmem_limit_bytes=24 * 2**20),
        cost_estimate=pl.CostEstimate(
            flops=FEED_FLOPS,
            bytes_accessed=FEED_BYTES,
            transcendentals=0,
        ),
    )(windows, *pieces, gain, *after)


def shift_from(block, lon_step, lat_step):
    lons, lats = lax.axis_size("lon"), lax.axis_size("lat")
    pairs = []
    for lon in range(lons):
        for lat in range(lats):
            source = (lon + lon_step) % lons * lats + (lat + lat_step) % lats
            pairs.append((source, lon * lats + lat))
    return lax.ppermute(block, ("lon", "lat"), pairs)


def to_windows(cells):
    cols, rows, levels, features = cells.shape
    c, r = WLON // 2, WLAT // 2
    arranged = cells.reshape(cols // WLON, 2, c, rows // WLAT, 2, r, levels, features)
    arranged = arranged.transpose(0, 3, 1, 4, 2, 5, 6, 7)
    return arranged.reshape(-1, CELLS, features)


def strips_kernel(picks, *refs):
    sources, outs = refs[: len(refs) - len(picks)], refs[len(refs) - len(picks) :]
    for pick, target in zip(picks, outs):
        place = 0
        for source, first, count in pick:
            target[place : place + count] = sources[source][first : first + count]
            place += count


def strips(sources, picks):
    shape = sources[0].shape[1:]
    held = pl.BlockSpec(memory_space=pltpu.VMEM)
    return pl.pallas_call(
        functools.partial(strips_kernel, picks),
        out_shape=[
            jax.ShapeDtypeStruct((sum(count for _, _, count in pick),) + shape, jnp.bfloat16)
            for pick in picks
        ],
        in_specs=[held] * len(sources),
        compiler_params=pltpu.CompilerParams(vmem_limit_bytes=10 * 2**20),
    )(*sources)


def from_strips(quarters, cols, rows):
    features = quarters.shape[-1]
    c, r = WLON // 2, WLAT // 2
    arranged = quarters.reshape(cols // c, rows // r, c, r, LEVELS, features)
    return arranged.transpose(0, 2, 1, 3, 4, 5).reshape(cols, rows, LEVELS, features)


def per_device(tokens, qkv_weight, out_weight, up_weight, down_weight, norm_gain, logit_scale):
    cols, rows, _, features = tokens.shape
    hidden_size = up_weight.shape[-1]
    row_windows = rows // WLAT
    weights = (qkv_weight, out_weight, up_weight, down_weight)
    relay = relayed(qkv_weight.shape[1], lax.axis_size("lon"), lax.axis_size("lat"))
    spread = np.arange(HEADS)[:, None] == np.arange(features)[None, :] // HEAD
    sharp = logit_scale[:, :, None] * jnp.asarray(spread * math.log2(math.e), jnp.float32)[None]
    sharp = jnp.sum(sharp, 1)
    windows = to_windows(tokens)

    def attention(block, sources, columns, pieces, after=()):
        gain, scale = norm_gain[block, :1], sharp[block : block + 1]
        return attend(sources, columns, pieces, gain, scale, row_windows, after)

    def forward(block, middle, column, pieces, edge, after=()):
        gain = norm_gain[block, 1:]
        return feed(middle, column, row_windows, pieces, gain, hidden_size, edge, after)

    low_edge, high_edge = (0, 0), (row_windows - 1, 1)
    if relay:
        (own,) = join([], [[(0, weight) for weight in weights[:2]]])
        feed_own, last_own = join(
            [],
            [[(0, weight) for weight in weights[2:]], [(1, weight) for weight in weights]],
            (own,),
        )
        widths = tuple(sum(weight.shape[2] for weight in pair) for pair in (weights[:2], weights[2:]))
        (pair,) = join([[own, across_z(own, 2)]], (), (windows,))
        (feed_pair,) = join([[feed_own, across_z(feed_own, 2)]])
        last_beside = send(last_own, beside)
        (column,) = join([[pair, across_z(pair, 1)]], (), (feed_pair, last_beside))
        received = [send(column, way) for way in (beside, across, corner)]
        last_other = across_z(tied(last_own, column), 2)
        sent = [tied(column, (received[0], last_other))] + received
        pieces = "columns", [column] + received + [send(part, swap) for part in sent]
        last_across = send(tied(last_other, received[0]), across)
        (feed_column,) = join([[feed_pair, across_z(feed_pair, 1)]])
        received = [send(feed_column, way) for way in (beside, across)]
        middle_0 = attention(0, [windows], (0,), pieces, (feed_column,))
        first, second = tied((received[0][:2], received[1][2:]), (middle_0, last_across))
        corners = [send(first, across), send(second, beside)]
        (last_four,) = join([[last_own, last_beside, last_other, last_across]], (), (middle_0,))
        middle_1 = attention(0, [windows], (1,), pieces, (middle_0, last_four))
        last_other = across_z(last_four, 1)
        swapped = [send(part, swap) for part in [feed_column] + tied(received, middle_0)]
        received += join([tied(corners, (middle_1, *swapped))])
        feed_pieces = "columns", [feed_column] + received + swapped + [send(received[2], swap)]
    else:
        gathered = []
        for block in range(2):
            for pair in (weights[:2], weights[2:]):
                chunk = jnp.concatenate([weight[block] for weight in pair], 1)
                gathered.append(lax.all_gather(chunk, "lon", axis=0, tiled=True))
        pieces, feed_pieces, last_pieces, final_pieces = (("rows", [rows]) for rows in gathered)
        middle_0 = attention(0, [windows], (0,), pieces)
        middle_1 = attention(0, [windows], (1,), pieces)
    left_0, right_0, low_0 = forward(0, middle_0, 0, feed_pieces, low_edge)
    below_0 = shift_from(low_0, 0, 1)
    size = left_0.shape[0]
    (ahead,) = strips([left_0, below_0], [[(0, 1, size - 1), (1, 0, 1)]])
    ahead = shift_from(ahead, 1, 0)
    after = (below_0,)
    if relay:
        columns = halves(last_four, last_other, widths, (low_0,))
        last_columns, final_columns = list(columns[:2]), list(columns[2:])
        last_received = [send(part, way) for part, way in zip(last_columns, (across, beside))]
        after += (last_columns[0],)
    left_1, right_1, low_1 = forward(0, middle_1, 0, feed_pieces, low_edge, after)
    below_1 = shift_from(tied(low_1, ahead), 0, 1)
    if relay:
        last_pieces = last_columns + last_received
        last_pieces += [send(part, swap) for part in last_columns + tied(last_received, low_1)]
        last_pieces = "halves", last_pieces
        final_received = [
            send(part, way)
            for part, way in zip(tied(final_columns, last_received), (across, beside))
        ]
    lefts = strips(
        [right_0, left_1, right_1, below_0, below_1],
        [
            [(0, 1, size - 1), (3, 1, 1)],
            [(1, 1, size - 1), (4, 0, 1)],
            [(2, 1, size - 1), (4, 1, 1)],
        ],
    )
    middle_1 = attention(1, [lefts[2], ahead], (1,), last_pieces)
    if relay:
        final_pieces = final_columns + final_received
        final_pieces += [send(part, swap) for part in final_columns + tied(final_received, middle_1)]
        final_pieces = "halves", final_pieces
    left_1, right_1, high_1 = forward(1, middle_1, 0, final_pieces, high_edge)
    above_1 = shift_from(high_1, 0, -1)
    (behind,) = strips([above_1, right_1], [[(0, 1, 1), (1, 0, size - 1)]])
    behind = shift_from(behind, -1, 0)
    middle_0 = attention(1, lefts[:2], (0,), last_pieces, (above_1,))
    left_0, right_0, high_0 = forward(1, middle_0, 0, final_pieces, high_edge)
    above_0 = shift_from(high_0, 0, -1)
    picks = [(0, 0, size)]
    for place, (low, quarter) in enumerate(((4, 0), (4, 1), (5, 0))):
        picks += [(low, quarter, 1), (place + 1, 0, size - 1)]
    (mixed,) = strips([behind, left_0, right_0, left_1, above_0, above_1], [picks])
    return from_strips(mixed, cols, rows)


def solution(mesh):
    placed = (
        P("lon", "lat", None, None),
        P(None, "lon", None),
        P(None, "lon", None),
        P(None, "lon", None),
        P(None, "lon", None),
        P(),
        P(),
    )
    return jax.shard_map(
        per_device,
        mesh=mesh,
        in_specs=placed,
        out_specs=P("lon", "lat", None, None),
        check_vma=False,
    )
```

```python
import functools
import math

import numpy as np

import jax
import jax.numpy as jnp
from jax import lax
from jax.experimental import pallas as pl
from jax.experimental.pallas import tpu as pltpu
from jax.sharding import PartitionSpec as P

HEADS = 16
HEAD = 32
WLON = 12
WLAT = 6
LEVELS = 2
CELLS = WLON * WLAT * LEVELS
MAIN = 128
REST = CELLS - MAIN
QUARTER = CELLS // 4
GROUP = 8
PART = 4
WIDE = GROUP * HEAD
FEED_FLOPS, FEED_BYTES = 1_000_000, 100_000
Z_ORDER = (0, 2, 1, 3)
ANY = pl.BlockSpec(memory_space=pl.ANY)
NT = (((1,), (1,)), ((), ()))


def dot(a, b, dims=(((1,), (0,)), ((), ()))):
    return lax.dot_general(a, b, dims, preferred_element_type=jnp.float32)


def layer_norm(value, gain_row):
    averaged = jnp.mean(value, -1, keepdims=True)
    centred = value - averaged
    variance = jnp.mean(centred * centred, -1, keepdims=True)
    return centred * lax.rsqrt(variance + 1e-05) * gain_row


def relayed(rows, lon_size, lat_size):
    return lat_size == 2 and rows % 32 == 0 and lon_size == 16


def join_kernel(columns, cuts, *refs):
    outs = refs[len(refs) - sum(len(widths) for _, widths in columns) - len(cuts) :]
    place, out = 0, 0
    for count, widths in columns:
        row = 0
        for piece in refs[place : place + count]:
            start = 0
            for target, width in zip(outs[out : out + len(widths)], widths):
                target[row : row + piece.shape[0]] = piece[:, :, start : start + width]
                start += width
            row += piece.shape[0]
        place, out = place + count, out + len(widths)
    for blocks, chunk_ref in zip(cuts, outs[out:]):
        half = chunk_ref.shape[1]
        first = pl.multiple_of(lax.axis_index("lat") * half, 16)
        start = 0
        for block, source in zip(blocks, refs[place : place + len(blocks)]):
            width = source.shape[2]
            chunk_ref[0, :, start : start + width] = source[block, pl.ds(first, half), :]
            start += width
        place += len(blocks)


def join(columns, cuts=(), after=(), widths=None):
    pieces = [piece for column in columns for piece in column]
    sources = [weight for cut in cuts for _, weight in cut]
    out_shape, sizes = [], []
    for column in columns:
        count, half, width = column[0].shape
        count = sum(piece.shape[0] for piece in column)
        sizes.append((len(column), widths or (width,)))
        for part in widths or (width,):
            out_shape.append(jax.ShapeDtypeStruct((count, half, part), jnp.bfloat16))
    for cut in cuts:
        width = sum(weight.shape[2] for _, weight in cut)
        out_shape.append(jax.ShapeDtypeStruct((1, cut[0][1].shape[1] // 2, width), jnp.bfloat16))
    held = pl.BlockSpec(memory_space=pltpu.VMEM)
    return pl.pallas_call(
        functools.partial(join_kernel, sizes, [[block for block, _ in cut] for cut in cuts]),
        out_shape=out_shape,
        in_specs=[held] * (len(pieces) + len(sources)) + [ANY] * len(after),
        compiler_params=pltpu.CompilerParams(vmem_limit_bytes=10 * 2**20),
    )(*pieces, *sources, *after)


def halves_kernel(widths, here_ref, there_ref, *outs):
    start = 0
    for index, width in enumerate(widths):
        for half in range(2):
            rows, lanes = slice(2 * half, 2 * half + 2), slice(start, start + width)
            outs[2 * index + half][:2] = here_ref[rows, :, lanes]
            outs[2 * index + half][2:] = there_ref[rows, :, lanes]
        start += width


def halves(here, there, widths, after):
    held = pl.BlockSpec(memory_space=pltpu.VMEM)
    return pl.pallas_call(
        lambda *refs: halves_kernel(widths, refs[0], refs[1], *refs[2 + len(after) :]),
        out_shape=[
            jax.ShapeDtypeStruct((4, here.shape[1], width), jnp.bfloat16)
            for width in widths
            for _ in range(2)
        ],
        in_specs=[held] * 2 + [ANY] * len(after),
        compiler_params=pltpu.CompilerParams(vmem_limit_bytes=10 * 2**20),
    )(here, there, *after)


def send(block, move):
    pairs = []
    for lon in range(lax.axis_size("lon")):
        for core in range(2):
            z, y, x, core_to = move(lon // 4, lon // 2 % 2, lon % 2, core)
            pairs.append((lon * 2 + core, (z * 4 + y * 2 + x) * 2 + core_to))
    return lax.ppermute(block, ("lon", "lat"), pairs)


def across_z(block, bit):
    return send(block, lambda z, y, x, c: (z ^ bit, y, x, c))


def swap(z, y, x, c):
    return z, y, x, 1 - c


def tied(array, after):
    return lax.optimization_barrier((array, after))[0]


def beside(z, y, x, c):
    return (z, y, 1 - x, c) if c == 0 else (z, 1 - y, x, c)


def across(z, y, x, c):
    return (z, 1 - y, x, c) if c == 0 else (z, y, 1 - x, c)


def corner(z, y, x, c):
    return z, 1 - y, 1 - x, c


def whole_pieces(column, received):
    return [column] + received + [send(part, swap) for part in [column] + received]


def load_pieces(kind, first, pieces, w_ref, stage_ref, sem):
    if kind == "halves":
        pieces = [piece.at[:, :, pl.ds(first, w_ref.shape[1])] for piece in pieces]
    copies = [
        pltpu.make_async_copy(piece, w_ref if kind == "rows" else stage_ref.at[index], sem.at[index])
        for index, piece in enumerate(pieces)
    ]
    for copy in copies:
        copy.start()
    if kind == "rows":
        copies[0].wait()
        return
    half = pieces[0].shape[-2]
    lon, lat = lax.axis_index("lon"), lax.axis_index("lat")
    z, y, x = lon // 4, lon // 2 % 2, lon % 2
    by_x, by_y = y * 2 + 1 - x, (1 - y) * 2 + x
    for index, copy in enumerate(copies):
        core = lat if index < 4 else 1 - lat
        own, opposite = y * 2 + x, (1 - y) * 2 + 1 - x
        one = jnp.where(core == 0, by_x, by_y)
        other = jnp.where(core == 0, by_y, by_x)
        copy.wait()
        for step in range(4):
            if kind == "columns":
                square, along = (own, one, other, opposite)[index % 4], Z_ORDER[step]
            else:
                pairs = ((own, one), (own, other), (other, opposite), (one, opposite))
                square, along = pairs[index % 4][step % 2], index % 2 * 2 + step // 2
            row = pl.multiple_of((((z ^ along) * 4 + square) * 2 + core) * half, 16)
            w_ref[pl.ds(row, half), :] = stage_ref[index, step]


def load_scratch(pieces, rows, width):
    stage = (len(pieces),) + pieces[0].shape[:2] + (width,) if len(pieces) > 1 else (1, 1, 16, 128)
    return [
        pltpu.VMEM((rows, width), jnp.bfloat16),
        pltpu.VMEM(stage, jnp.bfloat16),
        pltpu.SemaphoreType.DMA((len(pieces),)),
    ]


def attend_kernel(shifted, row_windows, kind, count, *refs):
    sources = 2 if shifted else 1
    x_refs, pieces = refs[:sources], refs[sources : sources + count]
    gain_ref, sharp_ref, ones_ref = refs[sources + count : sources + count + 3]
    allow_ref = refs[sources + count + 3] if shifted else None
    out_ref, w_ref, stage_ref, sem = refs[-4:]
    held, _, features = out_ref.shape

    @pl.when(pl.program_id(0) == 0)
    def _():
        load_pieces(kind, 0, pieces, w_ref, stage_ref, sem)

    if shifted:
        quarters = []
        for window in range(held):
            for strip_ref in x_refs:
                quarters += [strip_ref[2 * window + half].astype(jnp.float32) for half in range(2)]
        tokens = jnp.concatenate(quarters, 0).astype(jnp.bfloat16)
    else:
        tokens = x_refs[0][...].reshape(held * CELLS, features)
    channel = lax.broadcasted_iota(jnp.int32, (WIDE, WIDE), 0) // HEAD
    same_head = jnp.where(
        channel == lax.broadcasted_iota(jnp.int32, (WIDE, WIDE), 1) // HEAD, 1.0, 0.0
    ).astype(jnp.bfloat16)
    lane_head = lax.broadcasted_iota(jnp.int32, (1, WIDE), 1) // HEAD
    ones = lambda condition: jnp.where(condition, 1.0, 0.0).astype(jnp.bfloat16)
    pairs = [ones(lane_head % PART == head) for head in range(PART)]
    halves = [ones(lane_head // PART == part) for part in range(2)]
    masks = [ones(lane_head == head) for head in range(GROUP)]
    narrow = [ones(lane_head[:, :MAIN] == head) for head in range(PART)]

    def units(part):
        rounded = part.astype(jnp.bfloat16)
        length2 = dot(rounded * rounded, same_head)
        return part * lax.rsqrt(jnp.maximum(length2, 0.25 * HEAD))

    attended = [[] for _ in range(held)]
    for group in range(HEADS // GROUP):
        lanes = [slice(n * features + group * WIDE, n * features + (group + 1) * WIDE) for n in range(3)]
        queries = (units(dot(tokens, w_ref[:, lanes[0]])) * sharp_ref[:, lanes[0]]).astype(jnp.bfloat16)
        keys = units(dot(tokens, w_ref[:, lanes[1]])).astype(jnp.bfloat16)
        values = dot(tokens, w_ref[:, lanes[2]]).astype(jnp.bfloat16)
        for window in range(held):
            own = slice(window * CELLS, (window + 1) * CELLS)
            query, key, value = queries[own], keys[own], values[own]
            stacked = jnp.concatenate([query * pair for pair in pairs], 0)
            main_keys = jnp.concatenate([key[:MAIN] * half for half in halves], 0)
            main = jnp.exp2(dot(stacked, main_keys, NT)).astype(jnp.bfloat16)
            rest_keys = jnp.concatenate([key[MAIN:] * mask for mask in masks], 0)
            rest = jnp.exp2(dot(query, rest_keys, NT)).astype(jnp.bfloat16)
            if shifted:
                last = jnp.logical_and(
                    (pl.program_id(0) * held + window) % row_windows == row_windows - 1,
                    lax.axis_index("lat") == lax.axis_size("lat") - 1,
                )
                allow = jnp.where(last, allow_ref[...], 1.0).astype(jnp.bfloat16)
                rest = rest * allow[:, MAIN:]
            for part in range(2):
                lanes = slice(part * MAIN, (part + 1) * MAIN)
                parts = [main[head * CELLS : (head + 1) * CELLS, lanes] for head in range(PART)]
                if shifted:
                    parts = [one * allow[:, :MAIN] for one in parts]
                own_value = value[:, lanes]
                none = jnp.zeros((REST, MAIN), jnp.bfloat16)
                own_rest = [own_value[MAIN:] * mask for mask in narrow]
                other_rest = [none] * PART
                stacked = jnp.concatenate(
                    [own_value[:MAIN] * mask for mask in narrow]
                    + (own_rest + other_rest if part == 0 else other_rest + own_rest),
                    0,
                )
                both = jnp.concatenate([stacked, ones_ref[:, lanes]], 1)
                summed = dot(jnp.concatenate(parts + [rest], 1), both)
                attended[window].append(
                    (summed[:, :MAIN] / summed[:, MAIN:]).astype(jnp.bfloat16)
                )
    attended = jnp.concatenate([jnp.concatenate(parts, 1) for parts in attended], 0)
    projected = dot(attended, w_ref[:, 3 * features :])
    middle = tokens.astype(jnp.float32) + layer_norm(projected, gain_ref[...])
    out_ref[...] = middle.astype(jnp.bfloat16).reshape(out_ref.shape)


def allowed_pairs():
    side = np.arange(CELLS) // QUARTER % 2
    rest = np.tile(side[MAIN:], GROUP)
    return (side[:, None] == np.concatenate([side[:MAIN], rest])[None, :]).astype(np.float32)


def head_columns():
    halves = []
    for part in range(2):
        own = np.arange(part * PART, (part + 1) * PART)
        rows = np.concatenate([np.repeat(own, MAIN), np.repeat(np.arange(GROUP), REST)])
        halves.append(rows[:, None] == np.repeat(own, HEAD)[None, :])
    return np.concatenate(halves, 1).astype(np.float32)


def attend(sources, columns, pieces, gain, sharp, row_windows, after=(), held=2):
    shifted = len(sources) > 1
    kind, pieces = pieces
    features = sources[0].shape[-1]
    count = len(columns) * row_windows
    skipped = columns[0] * row_windows // held
    whole = lambda shape: pl.BlockSpec(shape, lambda i: (0,) * len(shape))
    block = pl.BlockSpec((held, CELLS, features), lambda i: (i, 0, 0))
    strip_block = pl.BlockSpec((2 * held, QUARTER, features), lambda i: (i, 0, 0))
    x_block = pl.BlockSpec((held, CELLS, features), lambda i: (i + skipped, 0, 0))
    ones = jnp.asarray(head_columns(), jnp.bfloat16)
    extra = (jnp.asarray(allowed_pairs()),) if shifted else ()
    return pl.pallas_call(
        functools.partial(attend_kernel, shifted, row_windows, kind, len(pieces)),
        grid=(count // held,),
        out_shape=jax.ShapeDtypeStruct((count, CELLS, features), jnp.bfloat16),
        in_specs=([strip_block] * 2 if shifted else [x_block])
        + [ANY] * len(pieces)
        + [whole((1, features))] * 2
        + [whole(ones.shape)]
        + [whole(e.shape) for e in extra]
        + [ANY] * len(after),
        out_specs=block,
        scratch_shapes=load_scratch(pieces, features, 4 * features),
        compiler_params=pltpu.CompilerParams(vmem_limit_bytes=24 * 2**20),
        cost_estimate=pl.CostEstimate(
            flops=count * 300_000_000, bytes_accessed=1_000_000, transcendentals=0
        ),
    )(*sources, *pieces, gain, sharp, ones, *extra, *after)


def feed_kernel(kind, count, hidden_size, chunk, edge, *refs):
    x_ref, pieces, gain_ref = refs[0], refs[1 : 1 + count], refs[1 + count]
    left_ref, right_ref, edge_ref, w_ref, stage_ref, sem = refs[-6:]
    held, _, features = x_ref.shape

    @pl.when(pl.program_id(0) == 0)
    def _():
        load_pieces(kind, 4 * x_ref.shape[-1], pieces, w_ref, stage_ref, sem)

    tokens = x_ref[...].reshape(held * CELLS, features)
    total = jnp.zeros(tokens.shape, jnp.float32)
    for start in range(0, hidden_size, chunk):
        grown = dot(tokens, w_ref[:, start : start + chunk])
        slope = math.sqrt(2.0 / math.pi)
        bent = jnp.tanh(grown * (grown * grown * (0.044715 * slope) + slope))
        hidden = (grown + grown * bent).astype(jnp.bfloat16)
        total = total + dot(
            hidden, w_ref[:, hidden_size + start : hidden_size + start + chunk], NT
        )
    result = tokens.astype(jnp.float32) + layer_norm(0.5 * total, gain_ref[...])
    edge_window, edge_half = edge
    for window in range(held):
        for side, target in enumerate((left_ref, right_ref)):
            for half in range(2):
                start = window * CELLS + (side * 2 + half) * QUARTER
                quarter = result[start : start + QUARTER].astype(jnp.bfloat16)
                target[2 * window + half] = quarter
                if half == edge_half and window == edge_window % held:

                    @pl.when(pl.program_id(0) == edge_window // held)
                    def _(quarter=quarter, side=side):
                        edge_ref[side] = quarter


def feed(windows, column, count, pieces, gain, hidden_size, edge, after=(), held=2):
    _, cells, features = windows.shape
    kind, pieces = pieces
    block = pl.BlockSpec((held, cells, features), lambda i: (i + column * count // held, 0, 0))
    side = pl.BlockSpec((2 * held, QUARTER, features), lambda i: (i, 0, 0))
    return pl.pallas_call(
        functools.partial(feed_kernel, kind, len(pieces), hidden_size, 512, edge),
        grid=(count // held,),
        out_shape=[jax.ShapeDtypeStruct((2 * count, QUARTER, features), jnp.bfloat16)] * 2
        + [jax.ShapeDtypeStruct((2, QUARTER, features), jnp.bfloat16)],
        in_specs=[block]
        + [ANY] * len(pieces)
        + [pl.BlockSpec((1, features), lambda i: (0, 0))]
        + [ANY] * len(after),
        out_specs=[side, side, pl.BlockSpec((2, QUARTER, features), lambda i: (0, 0, 0))],
        scratch_shapes=load_scratch(pieces, features, 2 * hidden_size),
        compiler_params=pltpu.CompilerParams(vmem_limit_bytes=24 * 2**20),
        cost_estimate=pl.CostEstimate(
            flops=FEED_FLOPS,
            bytes_accessed=FEED_BYTES,
            transcendentals=0,
        ),
    )(windows, *pieces, gain, *after)


def shift_from(block, lon_step, lat_step):
    lons, lats = lax.axis_size("lon"), lax.axis_size("lat")
    pairs = []
    for lon in range(lons):
        for lat in range(lats):
            source = (lon + lon_step) % lons * lats + (lat + lat_step) % lats
            pairs.append((source, lon * lats + lat))
    return lax.ppermute(block, ("lon", "lat"), pairs)


def to_windows(cells):
    cols, rows, levels, features = cells.shape
    c, r = WLON // 2, WLAT // 2
    arranged = cells.reshape(cols // WLON, 2, c, rows // WLAT, 2, r, levels, features)
    arranged = arranged.transpose(0, 3, 1, 4, 2, 5, 6, 7)
    return arranged.reshape(-1, CELLS, features)


def strips_kernel(picks, *refs):
    sources, outs = refs[: len(refs) - len(picks)], refs[len(refs) - len(picks) :]
    for pick, target in zip(picks, outs):
        place = 0
        for source, first, count in pick:
            target[place : place + count] = sources[source][first : first + count]
            place += count


def strips(sources, picks):
    shape = sources[0].shape[1:]
    held = pl.BlockSpec(memory_space=pltpu.VMEM)
    return pl.pallas_call(
        functools.partial(strips_kernel, picks),
        out_shape=[
            jax.ShapeDtypeStruct((sum(count for _, _, count in pick),) + shape, jnp.bfloat16)
            for pick in picks
        ],
        in_specs=[held] * len(sources),
        compiler_params=pltpu.CompilerParams(vmem_limit_bytes=10 * 2**20),
    )(*sources)


def from_strips(quarters, cols, rows):
    features = quarters.shape[-1]
    c, r = WLON // 2, WLAT // 2
    arranged = quarters.reshape(cols // c, rows // r, c, r, LEVELS, features)
    return arranged.transpose(0, 2, 1, 3, 4, 5).reshape(cols, rows, LEVELS, features)


def per_device(tokens, qkv_weight, out_weight, up_weight, down_weight, norm_gain, logit_scale):
    cols, rows, _, features = tokens.shape
    hidden_size = up_weight.shape[-1]
    row_windows = rows // WLAT
    weights = (qkv_weight, out_weight, up_weight, down_weight)
    relay = relayed(qkv_weight.shape[1], lax.axis_size("lon"), lax.axis_size("lat"))
    spread = np.arange(HEADS)[:, None] == np.arange(features)[None, :] // HEAD
    sharp = logit_scale[:, :, None] * jnp.asarray(spread * math.log2(math.e), jnp.float32)[None]
    sharp = jnp.sum(sharp, 1)
    windows = to_windows(tokens)

    def attention(block, sources, columns, pieces, after=()):
        gain, scale = norm_gain[block, :1], sharp[block : block + 1]
        return attend(sources, columns, pieces, gain, scale, row_windows, after)

    def forward(block, middle, column, pieces, edge, after=()):
        gain = norm_gain[block, 1:]
        return feed(middle, column, row_windows, pieces, gain, hidden_size, edge, after)

    low_edge, high_edge = (0, 0), (row_windows - 1, 1)
    if relay:
        (own,) = join([], [[(0, weight) for weight in weights[:2]]])
        feed_own, last_own = join(
            [],
            [[(0, weight) for weight in weights[2:]], [(1, weight) for weight in weights]],
            (own,),
        )
        (pair,) = join([[own, across_z(own, 2)]], (), (windows,))
        (feed_pair,) = join([[feed_own, across_z(feed_own, 2)]])
        last_beside, last_across = send(last_own, beside), send(last_own, across)
        (last_pair,) = join([[last_own, last_across]])
        (column,) = join([[pair, across_z(pair, 1)]], (), (feed_pair, last_beside, last_pair))
        received = [send(column, way) for way in (beside, across, corner)]
        last_other = across_z(tied(last_pair, column), 2)
        sent = [tied(column, (received[0], last_other))] + received
        pieces = "columns", [column] + received + [send(part, swap) for part in sent]
        (feed_column,) = join([[feed_pair, across_z(feed_pair, 1)]])
        (last_four,) = join([[last_own, last_beside, last_other]])
        received = [send(feed_column, way) for way in (beside, across)]
        middle_0 = attention(0, [windows], (0,), pieces, (feed_column,))
        first, second = tied((received[0][:2], received[1][2:]), middle_0)
        corners = [send(first, across), send(second, beside)]
        middle_1 = attention(0, [windows], (1,), pieces, (middle_0, last_four))
        last_other = across_z(last_four, 1)
        swapped = [send(part, swap) for part in [feed_column] + tied(received, middle_0)]
        received += join([tied(corners, (middle_1, *swapped))])
        feed_pieces = "columns", [feed_column] + received + swapped + [send(received[2], swap)]
    else:
        gathered = []
        for block in range(2):
            for pair in (weights[:2], weights[2:]):
                chunk = jnp.concatenate([weight[block] for weight in pair], 1)
                gathered.append(lax.all_gather(chunk, "lon", axis=0, tiled=True))
        pieces, feed_pieces, last_pieces, final_pieces = (("rows", [rows]) for rows in gathered)
        middle_0 = attention(0, [windows], (0,), pieces)
        middle_1 = attention(0, [windows], (1,), pieces)
    left_0, right_0, low_0 = forward(0, middle_0, 0, feed_pieces, low_edge)
    below_0 = shift_from(low_0, 0, 1)
    size = left_0.shape[0]
    (ahead,) = strips([left_0, below_0], [[(0, 1, size - 1), (1, 0, 1)]])
    ahead = shift_from(ahead, 1, 0)
    if relay:
        last_columns = list(halves(last_four, last_other, (last_four.shape[2],), (low_0,)))
        last_received = [send(part, way) for part, way in zip(last_columns, (across, beside))]
    left_1, right_1, low_1 = forward(0, middle_1, 0, feed_pieces, low_edge, (below_0,))
    below_1 = shift_from(tied(low_1, ahead), 0, 1)
    if relay:
        last_pieces = last_columns + last_received
        swapped = [send(tied(last_columns[0], low_0), swap)]
        swapped.append(send(tied(last_columns[1], swapped[0]), swap))
        last_received = tied(last_received, (low_1, ahead, *swapped))
        last_pieces += swapped + [send(part, swap) for part in last_received]
        last_pieces = final_pieces = "halves", last_pieces
    lefts = strips(
        [right_0, left_1, right_1, below_0, below_1],
        [
            [(0, 1, size - 1), (3, 1, 1)],
            [(1, 1, size - 1), (4, 0, 1)],
            [(2, 1, size - 1), (4, 1, 1)],
        ],
    )
    middle_1 = attention(1, [lefts[2], ahead], (1,), last_pieces)
    left_1, right_1, high_1 = forward(1, middle_1, 0, final_pieces, high_edge)
    above_1 = shift_from(high_1, 0, -1)
    (behind,) = strips([above_1, right_1], [[(0, 1, 1), (1, 0, size - 1)]])
    behind = shift_from(behind, -1, 0)
    middle_0 = attention(1, lefts[:2], (0,), last_pieces, (above_1,))
    left_0, right_0, high_0 = forward(1, middle_0, 0, final_pieces, high_edge)
    above_0 = shift_from(high_0, 0, -1)
    picks = [(0, 0, size)]
    for place, (low, quarter) in enumerate(((4, 0), (4, 1), (5, 0))):
        picks += [(low, quarter, 1), (place + 1, 0, size - 1)]
    (mixed,) = strips([behind, left_0, right_0, left_1, above_0, above_1], [picks])
    return from_strips(mixed, cols, rows)


def solution(mesh):
    placed = (
        P("lon", "lat", None, None),
        P(None, "lon", None),
        P(None, "lon", None),
        P(None, "lon", None),
        P(None, "lon", None),
        P(),
        P(),
    )
    return jax.shard_map(
        per_device,
        mesh=mesh,
        in_specs=placed,
        out_specs=P("lon", "lat", None, None),
        check_vma=False,
    )
```

```python
import functools
import math

import numpy as np

import jax
import jax.numpy as jnp
from jax import lax
from jax.experimental import pallas as pl
from jax.experimental.pallas import tpu as pltpu
from jax.sharding import PartitionSpec as P

HEADS = 16
HEAD = 32
WLON = 12
WLAT = 6
LEVELS = 2
CELLS = WLON * WLAT * LEVELS
MAIN = 128
REST = CELLS - MAIN
QUARTER = CELLS // 4
GROUP = 8
PART = 4
WIDE = GROUP * HEAD
FEED_FLOPS, FEED_BYTES = 1_000_000, 100_000
Z_ORDER = (0, 2, 1, 3)
ANY = pl.BlockSpec(memory_space=pl.ANY)
NT = (((1,), (1,)), ((), ()))


def dot(a, b, dims=(((1,), (0,)), ((), ()))):
    return lax.dot_general(a, b, dims, preferred_element_type=jnp.float32)


def layer_norm(value, gain_row):
    averaged = jnp.mean(value, -1, keepdims=True)
    centred = value - averaged
    variance = jnp.mean(centred * centred, -1, keepdims=True)
    return centred * lax.rsqrt(variance + 1e-05) * gain_row


def relayed(rows, lon_size, lat_size):
    return lat_size == 2 and rows % 32 == 0 and lon_size == 16


def join_kernel(columns, cuts, *refs):
    outs = refs[len(refs) - sum(len(widths) for _, widths in columns) - len(cuts) :]
    place, out = 0, 0
    for count, widths in columns:
        row = 0
        for piece in refs[place : place + count]:
            start = 0
            for target, width in zip(outs[out : out + len(widths)], widths):
                target[row : row + piece.shape[0]] = piece[:, :, start : start + width]
                start += width
            row += piece.shape[0]
        place, out = place + count, out + len(widths)
    for blocks, chunk_ref in zip(cuts, outs[out:]):
        half = chunk_ref.shape[1]
        first = pl.multiple_of(lax.axis_index("lat") * half, 16)
        start = 0
        for block, source in zip(blocks, refs[place : place + len(blocks)]):
            width = source.shape[2]
            chunk_ref[0, :, start : start + width] = source[block, pl.ds(first, half), :]
            start += width
        place += len(blocks)


def join(columns, cuts=(), after=(), widths=None):
    pieces = [piece for column in columns for piece in column]
    sources = [weight for cut in cuts for _, weight in cut]
    out_shape, sizes = [], []
    for column in columns:
        count, half, width = column[0].shape
        count = sum(piece.shape[0] for piece in column)
        sizes.append((len(column), widths or (width,)))
        for part in widths or (width,):
            out_shape.append(jax.ShapeDtypeStruct((count, half, part), jnp.bfloat16))
    for cut in cuts:
        width = sum(weight.shape[2] for _, weight in cut)
        out_shape.append(jax.ShapeDtypeStruct((1, cut[0][1].shape[1] // 2, width), jnp.bfloat16))
    held = pl.BlockSpec(memory_space=pltpu.VMEM)
    return pl.pallas_call(
        functools.partial(join_kernel, sizes, [[block for block, _ in cut] for cut in cuts]),
        out_shape=out_shape,
        in_specs=[held] * (len(pieces) + len(sources)) + [ANY] * len(after),
        compiler_params=pltpu.CompilerParams(vmem_limit_bytes=10 * 2**20),
    )(*pieces, *sources, *after)


def halves_kernel(widths, here_ref, there_ref, *outs):
    start = 0
    for index, width in enumerate(widths):
        for half in range(2):
            rows, lanes = slice(2 * half, 2 * half + 2), slice(start, start + width)
            outs[2 * index + half][:2] = here_ref[rows, :, lanes]
            outs[2 * index + half][2:] = there_ref[rows, :, lanes]
        start += width


def halves(here, there, widths, after):
    held = pl.BlockSpec(memory_space=pltpu.VMEM)
    return pl.pallas_call(
        lambda *refs: halves_kernel(widths, refs[0], refs[1], *refs[2 + len(after) :]),
        out_shape=[
            jax.ShapeDtypeStruct((4, here.shape[1], width), jnp.bfloat16)
            for width in widths
            for _ in range(2)
        ],
        in_specs=[held] * 2 + [ANY] * len(after),
        compiler_params=pltpu.CompilerParams(vmem_limit_bytes=10 * 2**20),
    )(here, there, *after)


def send(block, move):
    pairs = []
    for lon in range(lax.axis_size("lon")):
        for core in range(2):
            z, y, x, core_to = move(lon // 4, lon // 2 % 2, lon % 2, core)
            pairs.append((lon * 2 + core, (z * 4 + y * 2 + x) * 2 + core_to))
    return lax.ppermute(block, ("lon", "lat"), pairs)


def across_z(block, bit):
    return send(block, lambda z, y, x, c: (z ^ bit, y, x, c))


def swap(z, y, x, c):
    return z, y, x, 1 - c


def tied(array, after):
    return lax.optimization_barrier((array, after))[0]


def beside(z, y, x, c):
    return (z, y, 1 - x, c) if c == 0 else (z, 1 - y, x, c)


def across(z, y, x, c):
    return (z, 1 - y, x, c) if c == 0 else (z, y, 1 - x, c)


def corner(z, y, x, c):
    return z, 1 - y, 1 - x, c


def whole_pieces(column, received):
    return [column] + received + [send(part, swap) for part in [column] + received]


def load_pieces(kind, pieces, w_ref, stage_ref, sem):
    copies = [
        pltpu.make_async_copy(piece, w_ref if kind == "rows" else stage_ref.at[index], sem.at[index])
        for index, piece in enumerate(pieces)
    ]
    for copy in copies:
        copy.start()
    if kind == "rows":
        copies[0].wait()
        return
    half = pieces[0].shape[-2]
    lon, lat = lax.axis_index("lon"), lax.axis_index("lat")
    z, y, x = lon // 4, lon // 2 % 2, lon % 2
    by_x, by_y = y * 2 + 1 - x, (1 - y) * 2 + x
    for index, copy in enumerate(copies):
        core = lat if index < 4 else 1 - lat
        own, opposite = y * 2 + x, (1 - y) * 2 + 1 - x
        one = jnp.where(core == 0, by_x, by_y)
        other = jnp.where(core == 0, by_y, by_x)
        copy.wait()
        for step in range(4):
            if kind == "columns":
                square, along = (own, one, other, opposite)[index % 4], Z_ORDER[step]
            else:
                pairs = ((own, one), (own, other), (other, opposite), (one, opposite))
                square, along = pairs[index % 4][step % 2], index % 2 * 2 + step // 2
            row = pl.multiple_of((((z ^ along) * 4 + square) * 2 + core) * half, 16)
            w_ref[pl.ds(row, half), :] = stage_ref[index, step]


def load_scratch(pieces, rows, width):
    stage = (len(pieces),) + pieces[0].shape if len(pieces) > 1 else (1, 1, 16, 128)
    return [
        pltpu.VMEM((rows, width), jnp.bfloat16),
        pltpu.VMEM(stage, jnp.bfloat16),
        pltpu.SemaphoreType.DMA((len(pieces),)),
    ]


def attend_kernel(shifted, row_windows, kind, count, *refs):
    sources = 2 if shifted else 1
    x_refs, pieces = refs[:sources], refs[sources : sources + count]
    gain_ref, sharp_ref, ones_ref = refs[sources + count : sources + count + 3]
    allow_ref = refs[sources + count + 3] if shifted else None
    out_ref, w_ref, stage_ref, sem = refs[-4:]
    held, _, features = out_ref.shape

    @pl.when(pl.program_id(0) == 0)
    def _():
        load_pieces(kind, pieces, w_ref, stage_ref, sem)

    if shifted:
        quarters = []
        for window in range(held):
            for strip_ref in x_refs:
                quarters += [strip_ref[2 * window + half].astype(jnp.float32) for half in range(2)]
        tokens = jnp.concatenate(quarters, 0).astype(jnp.bfloat16)
    else:
        tokens = x_refs[0][...].reshape(held * CELLS, features)
    channel = lax.broadcasted_iota(jnp.int32, (WIDE, WIDE), 0) // HEAD
    same_head = jnp.where(
        channel == lax.broadcasted_iota(jnp.int32, (WIDE, WIDE), 1) // HEAD, 1.0, 0.0
    ).astype(jnp.bfloat16)
    lane_head = lax.broadcasted_iota(jnp.int32, (1, WIDE), 1) // HEAD
    ones = lambda condition: jnp.where(condition, 1.0, 0.0).astype(jnp.bfloat16)
    pairs = [ones(lane_head % PART == head) for head in range(PART)]
    halves = [ones(lane_head // PART == part) for part in range(2)]
    masks = [ones(lane_head == head) for head in range(GROUP)]
    narrow = [ones(lane_head[:, :MAIN] == head) for head in range(PART)]

    def units(part):
        rounded = part.astype(jnp.bfloat16)
        length2 = dot(rounded * rounded, same_head)
        return part * lax.rsqrt(jnp.maximum(length2, 0.25 * HEAD))

    attended = [[] for _ in range(held)]
    for group in range(HEADS // GROUP):
        lanes = [slice(n * features + group * WIDE, n * features + (group + 1) * WIDE) for n in range(3)]
        queries = (units(dot(tokens, w_ref[:, lanes[0]])) * sharp_ref[:, lanes[0]]).astype(jnp.bfloat16)
        keys = units(dot(tokens, w_ref[:, lanes[1]])).astype(jnp.bfloat16)
        values = dot(tokens, w_ref[:, lanes[2]]).astype(jnp.bfloat16)
        for window in range(held):
            own = slice(window * CELLS, (window + 1) * CELLS)
            query, key, value = queries[own], keys[own], values[own]
            stacked = jnp.concatenate([query * pair for pair in pairs], 0)
            main_keys = jnp.concatenate([key[:MAIN] * half for half in halves], 0)
            main = jnp.exp2(dot(stacked, main_keys, NT)).astype(jnp.bfloat16)
            rest_keys = jnp.concatenate([key[MAIN:] * mask for mask in masks], 0)
            rest = jnp.exp2(dot(query, rest_keys, NT)).astype(jnp.bfloat16)
            if shifted:
                last = jnp.logical_and(
                    (pl.program_id(0) * held + window) % row_windows == row_windows - 1,
                    lax.axis_index("lat") == lax.axis_size("lat") - 1,
                )
                allow = jnp.where(last, allow_ref[...], 1.0).astype(jnp.bfloat16)
                rest = rest * allow[:, MAIN:]
            for part in range(2):
                lanes = slice(part * MAIN, (part + 1) * MAIN)
                parts = [main[head * CELLS : (head + 1) * CELLS, lanes] for head in range(PART)]
                if shifted:
                    parts = [one * allow[:, :MAIN] for one in parts]
                own_value = value[:, lanes]
                none = jnp.zeros((REST, MAIN), jnp.bfloat16)
                own_rest = [own_value[MAIN:] * mask for mask in narrow]
                other_rest = [none] * PART
                stacked = jnp.concatenate(
                    [own_value[:MAIN] * mask for mask in narrow]
                    + (own_rest + other_rest if part == 0 else other_rest + own_rest),
                    0,
                )
                both = jnp.concatenate([stacked, ones_ref[:, lanes]], 1)
                summed = dot(jnp.concatenate(parts + [rest], 1), both)
                attended[window].append(
                    (summed[:, :MAIN] / summed[:, MAIN:]).astype(jnp.bfloat16)
                )
    attended = jnp.concatenate([jnp.concatenate(parts, 1) for parts in attended], 0)
    projected = dot(attended, w_ref[:, 3 * features :])
    middle = tokens.astype(jnp.float32) + layer_norm(projected, gain_ref[...])
    out_ref[...] = middle.astype(jnp.bfloat16).reshape(out_ref.shape)


def allowed_pairs():
    side = np.arange(CELLS) // QUARTER % 2
    rest = np.tile(side[MAIN:], GROUP)
    return (side[:, None] == np.concatenate([side[:MAIN], rest])[None, :]).astype(np.float32)


def head_columns():
    halves = []
    for part in range(2):
        own = np.arange(part * PART, (part + 1) * PART)
        rows = np.concatenate([np.repeat(own, MAIN), np.repeat(np.arange(GROUP), REST)])
        halves.append(rows[:, None] == np.repeat(own, HEAD)[None, :])
    return np.concatenate(halves, 1).astype(np.float32)


def attend(sources, columns, pieces, gain, sharp, row_windows, after=(), held=2):
    shifted = len(sources) > 1
    kind, pieces = pieces
    features = sources[0].shape[-1]
    count = len(columns) * row_windows
    skipped = columns[0] * row_windows // held
    whole = lambda shape: pl.BlockSpec(shape, lambda i: (0,) * len(shape))
    block = pl.BlockSpec((held, CELLS, features), lambda i: (i, 0, 0))
    strip_block = pl.BlockSpec((2 * held, QUARTER, features), lambda i: (i, 0, 0))
    x_block = pl.BlockSpec((held, CELLS, features), lambda i: (i + skipped, 0, 0))
    ones = jnp.asarray(head_columns(), jnp.bfloat16)
    extra = (jnp.asarray(allowed_pairs()),) if shifted else ()
    return pl.pallas_call(
        functools.partial(attend_kernel, shifted, row_windows, kind, len(pieces)),
        grid=(count // held,),
        out_shape=jax.ShapeDtypeStruct((count, CELLS, features), jnp.bfloat16),
        in_specs=([strip_block] * 2 if shifted else [x_block])
        + [ANY] * len(pieces)
        + [whole((1, features))] * 2
        + [whole(ones.shape)]
        + [whole(e.shape) for e in extra]
        + [ANY] * len(after),
        out_specs=block,
        scratch_shapes=load_scratch(pieces, features, 4 * features),
        compiler_params=pltpu.CompilerParams(vmem_limit_bytes=24 * 2**20),
        cost_estimate=pl.CostEstimate(
            flops=count * 2_000_000_000, bytes_accessed=6_000_000, transcendentals=0
        ),
    )(*sources, *pieces, gain, sharp, ones, *extra, *after)


def feed_kernel(kind, count, hidden_size, chunk, edge, *refs):
    x_ref, pieces, gain_ref = refs[0], refs[1 : 1 + count], refs[1 + count]
    left_ref, right_ref, edge_ref, w_ref, stage_ref, sem = refs[-6:]
    held, _, features = x_ref.shape

    @pl.when(pl.program_id(0) == 0)
    def _():
        load_pieces(kind, pieces, w_ref, stage_ref, sem)

    tokens = x_ref[...].reshape(held * CELLS, features)
    total = jnp.zeros(tokens.shape, jnp.float32)
    for start in range(0, hidden_size, chunk):
        grown = dot(tokens, w_ref[:, start : start + chunk])
        slope = math.sqrt(2.0 / math.pi)
        bent = jnp.tanh(grown * (grown * grown * (0.044715 * slope) + slope))
        hidden = (grown + grown * bent).astype(jnp.bfloat16)
        total = total + dot(
            hidden, w_ref[:, hidden_size + start : hidden_size + start + chunk], NT
        )
    result = tokens.astype(jnp.float32) + layer_norm(0.5 * total, gain_ref[...])
    edge_window, edge_half = edge
    for window in range(held):
        for side, target in enumerate((left_ref, right_ref)):
            for half in range(2):
                start = window * CELLS + (side * 2 + half) * QUARTER
                quarter = result[start : start + QUARTER].astype(jnp.bfloat16)
                target[2 * window + half] = quarter
                if half == edge_half and window == edge_window % held:

                    @pl.when(pl.program_id(0) == edge_window // held)
                    def _(quarter=quarter, side=side):
                        edge_ref[side] = quarter


def feed(windows, column, count, pieces, gain, hidden_size, edge, after=(), held=2):
    _, cells, features = windows.shape
    kind, pieces = pieces
    block = pl.BlockSpec((held, cells, features), lambda i: (i + column * count // held, 0, 0))
    side = pl.BlockSpec((2 * held, QUARTER, features), lambda i: (i, 0, 0))
    return pl.pallas_call(
        functools.partial(feed_kernel, kind, len(pieces), hidden_size, 512, edge),
        grid=(count // held,),
        out_shape=[jax.ShapeDtypeStruct((2 * count, QUARTER, features), jnp.bfloat16)] * 2
        + [jax.ShapeDtypeStruct((2, QUARTER, features), jnp.bfloat16)],
        in_specs=[block]
        + [ANY] * len(pieces)
        + [pl.BlockSpec((1, features), lambda i: (0, 0))]
        + [ANY] * len(after),
        out_specs=[side, side, pl.BlockSpec((2, QUARTER, features), lambda i: (0, 0, 0))],
        scratch_shapes=load_scratch(pieces, features, 2 * hidden_size),
        compiler_params=pltpu.CompilerParams(vmem_limit_bytes=24 * 2**20),
        cost_estimate=pl.CostEstimate(
            flops=FEED_FLOPS,
            bytes_accessed=FEED_BYTES,
            transcendentals=0,
        ),
    )(windows, *pieces, gain, *after)


def shift_from(block, lon_step, lat_step):
    lons, lats = lax.axis_size("lon"), lax.axis_size("lat")
    pairs = []
    for lon in range(lons):
        for lat in range(lats):
            source = (lon + lon_step) % lons * lats + (lat + lat_step) % lats
            pairs.append((source, lon * lats + lat))
    return lax.ppermute(block, ("lon", "lat"), pairs)


def to_windows(cells):
    cols, rows, levels, features = cells.shape
    c, r = WLON // 2, WLAT // 2
    arranged = cells.reshape(cols // WLON, 2, c, rows // WLAT, 2, r, levels, features)
    arranged = arranged.transpose(0, 3, 1, 4, 2, 5, 6, 7)
    return arranged.reshape(-1, CELLS, features)


def strips_kernel(picks, *refs):
    sources, outs = refs[: len(refs) - len(picks)], refs[len(refs) - len(picks) :]
    for pick, target in zip(picks, outs):
        place = 0
        for source, first, count in pick:
            target[place : place + count] = sources[source][first : first + count]
            place += count


def strips(sources, picks):
    shape = sources[0].shape[1:]
    held = pl.BlockSpec(memory_space=pltpu.VMEM)
    return pl.pallas_call(
        functools.partial(strips_kernel, picks),
        out_shape=[
            jax.ShapeDtypeStruct((sum(count for _, _, count in pick),) + shape, jnp.bfloat16)
            for pick in picks
        ],
        in_specs=[held] * len(sources),
        compiler_params=pltpu.CompilerParams(vmem_limit_bytes=10 * 2**20),
    )(*sources)


def from_strips(quarters, cols, rows):
    features = quarters.shape[-1]
    c, r = WLON // 2, WLAT // 2
    arranged = quarters.reshape(cols // c, rows // r, c, r, LEVELS, features)
    return arranged.transpose(0, 2, 1, 3, 4, 5).reshape(cols, rows, LEVELS, features)


def per_device(tokens, qkv_weight, out_weight, up_weight, down_weight, norm_gain, logit_scale):
    cols, rows, _, features = tokens.shape
    hidden_size = up_weight.shape[-1]
    row_windows = rows // WLAT
    weights = (qkv_weight, out_weight, up_weight, down_weight)
    relay = relayed(qkv_weight.shape[1], lax.axis_size("lon"), lax.axis_size("lat"))
    spread = np.arange(HEADS)[:, None] == np.arange(features)[None, :] // HEAD
    sharp = logit_scale[:, :, None] * jnp.asarray(spread * math.log2(math.e), jnp.float32)[None]
    sharp = jnp.sum(sharp, 1)
    windows = to_windows(tokens)

    def attention(block, sources, columns, pieces, after=()):
        gain, scale = norm_gain[block, :1], sharp[block : block + 1]
        return attend(sources, columns, pieces, gain, scale, row_windows, after)

    def forward(block, middle, column, pieces, edge, after=()):
        gain = norm_gain[block, 1:]
        return feed(middle, column, row_windows, pieces, gain, hidden_size, edge, after)

    low_edge, high_edge = (0, 0), (row_windows - 1, 1)
    if relay:
        (own,) = join([], [[(0, weight) for weight in weights[:2]]])
        feed_own, last_own = join(
            [],
            [[(0, weight) for weight in weights[2:]], [(1, weight) for weight in weights]],
            (own,),
        )
        widths = tuple(sum(weight.shape[2] for weight in pair) for pair in (weights[:2], weights[2:]))
        (pair,) = join([[own, across_z(own, 2)]], (), (windows,))
        (feed_pair,) = join([[feed_own, across_z(feed_own, 2)]])
        last_beside = send(last_own, beside)
        (column,) = join([[pair, across_z(pair, 1)]], (), (feed_pair, last_beside))
        received = [send(column, way) for way in (beside, across, corner)]
        last_other = across_z(tied(last_own, column), 2)
        sent = [tied(column, (received[0], last_other))] + received
        pieces = "columns", [column] + received + [send(part, swap) for part in sent]
        last_across = send(tied(last_other, received[0]), across)
        (feed_column,) = join([[feed_pair, across_z(feed_pair, 1)]])
        received = [send(feed_column, way) for way in (beside, across)]
        middle_0 = attention(0, [windows], (0,), pieces, (feed_column,))
        first, second = tied((received[0][:2], received[1][2:]), (middle_0, last_across))
        corners = [send(first, across), send(second, beside)]
        last_four, final_four = join(
            [[last_own, last_beside, last_other, last_across]], (), (middle_0,), widths
        )
        middle_1 = attention(0, [windows], (1,), pieces, (middle_0, last_four))
        last_other, final_other = across_z(last_four, 1), across_z(final_four, 1)
        last_columns = list(halves(last_four, last_other, widths[:1], (middle_1,)))
        last_received = [send(part, way) for part, way in zip(last_columns, (across, beside))]
        swapped = [send(part, swap) for part in [feed_column] + tied(received, middle_0)]
        received += join([tied(corners, (middle_1, last_other, *swapped))])
        feed_pieces = "columns", [feed_column] + received + swapped + [send(received[2], swap)]
    else:
        gathered = []
        for block in range(2):
            for pair in (weights[:2], weights[2:]):
                chunk = jnp.concatenate([weight[block] for weight in pair], 1)
                gathered.append(lax.all_gather(chunk, "lon", axis=0, tiled=True))
        pieces, feed_pieces, last_pieces, final_pieces = (("rows", [rows]) for rows in gathered)
        last_columns = ()
        middle_0 = attention(0, [windows], (0,), pieces)
        middle_1 = attention(0, [windows], (1,), pieces)
    left_0, right_0, low_0 = forward(0, middle_0, 0, feed_pieces, low_edge, last_columns)
    below_0 = shift_from(low_0, 0, 1)
    size = left_0.shape[0]
    (ahead,) = strips([left_0, below_0], [[(0, 1, size - 1), (1, 0, 1)]])
    ahead = shift_from(ahead, 1, 0)
    after = (below_0,)
    if relay:
        final_columns = list(halves(final_four, final_other, widths[1:], (low_0,)))
    left_1, right_1, low_1 = forward(0, middle_1, 0, feed_pieces, low_edge, after)
    below_1 = shift_from(tied(low_1, ahead), 0, 1)
    if relay:
        last_pieces = last_columns + last_received
        last_pieces += [send(part, swap) for part in last_columns + tied(last_received, low_1)]
        last_pieces = "halves", last_pieces
        final_received = [
            send(part, way)
            for part, way in zip(tied(final_columns, ahead), (across, beside))
        ]
    lefts = strips(
        [right_0, left_1, right_1, below_0, below_1],
        [
            [(0, 1, size - 1), (3, 1, 1)],
            [(1, 1, size - 1), (4, 0, 1)],
            [(2, 1, size - 1), (4, 1, 1)],
        ],
    )
    middle_1 = attention(1, [lefts[2], ahead], (1,), last_pieces)
    if relay:
        final_pieces = final_columns + final_received
        final_pieces += [send(part, swap) for part in final_columns + tied(final_received, middle_1)]
        final_pieces = "halves", final_pieces
    left_1, right_1, high_1 = forward(1, middle_1, 0, final_pieces, high_edge)
    above_1 = shift_from(high_1, 0, -1)
    (behind,) = strips([above_1, right_1], [[(0, 1, 1), (1, 0, size - 1)]])
    behind = shift_from(behind, -1, 0)
    middle_0 = attention(1, lefts[:2], (0,), last_pieces, (above_1,))
    left_0, right_0, high_0 = forward(1, middle_0, 0, final_pieces, high_edge)
    above_0 = shift_from(high_0, 0, -1)
    picks = [(0, 0, size)]
    for place, (low, quarter) in enumerate(((4, 0), (4, 1), (5, 0))):
        picks += [(low, quarter, 1), (place + 1, 0, size - 1)]
    (mixed,) = strips([behind, left_0, right_0, left_1, above_0, above_1], [picks])
    return from_strips(mixed, cols, rows)


def solution(mesh):
    placed = (
        P("lon", "lat", None, None),
        P(None, "lon", None),
        P(None, "lon", None),
        P(None, "lon", None),
        P(None, "lon", None),
        P(),
        P(),
    )
    return jax.shard_map(
        per_device,
        mesh=mesh,
        in_specs=placed,
        out_specs=P("lon", "lat", None, None),
        check_vma=False,
    )
```

```python
import functools
import math

import numpy as np

import jax
import jax.numpy as jnp
from jax import lax
from jax.experimental import pallas as pl
from jax.experimental.pallas import tpu as pltpu
from jax.sharding import PartitionSpec as P

HEADS = 16
HEAD = 32
WLON = 12
WLAT = 6
LEVELS = 2
CELLS = WLON * WLAT * LEVELS
MAIN = 128
REST = CELLS - MAIN
QUARTER = CELLS // 4
GROUP = 8
PART = 4
WIDE = GROUP * HEAD
FEED_FLOPS, FEED_BYTES = 1_000_000, 100_000
Z_ORDER = (0, 2, 1, 3)
ANY = pl.BlockSpec(memory_space=pl.ANY)
NT = (((1,), (1,)), ((), ()))


def dot(a, b, dims=(((1,), (0,)), ((), ()))):
    return lax.dot_general(a, b, dims, preferred_element_type=jnp.float32)


def layer_norm(value, gain_row):
    averaged = jnp.mean(value, -1, keepdims=True)
    centred = value - averaged
    variance = jnp.mean(centred * centred, -1, keepdims=True)
    return centred * lax.rsqrt(variance + 1e-05) * gain_row


def relayed(rows, lon_size, lat_size):
    return lat_size == 2 and rows % 32 == 0 and lon_size == 16


def join_kernel(columns, cuts, *refs):
    outs = refs[len(refs) - sum(len(widths) for _, widths in columns) - len(cuts) :]
    place, out = 0, 0
    for count, widths in columns:
        row = 0
        for piece in refs[place : place + count]:
            start = 0
            for target, width in zip(outs[out : out + len(widths)], widths):
                target[row : row + piece.shape[0]] = piece[:, :, start : start + width]
                start += width
            row += piece.shape[0]
        place, out = place + count, out + len(widths)
    for blocks, chunk_ref in zip(cuts, outs[out:]):
        half = chunk_ref.shape[1]
        first = pl.multiple_of(lax.axis_index("lat") * half, 16)
        start = 0
        for block, source in zip(blocks, refs[place : place + len(blocks)]):
            width = source.shape[2]
            chunk_ref[0, :, start : start + width] = source[block, pl.ds(first, half), :]
            start += width
        place += len(blocks)


def join(columns, cuts=(), after=(), widths=None):
    pieces = [piece for column in columns for piece in column]
    sources = [weight for cut in cuts for _, weight in cut]
    out_shape, sizes = [], []
    for column in columns:
        count, half, width = column[0].shape
        count = sum(piece.shape[0] for piece in column)
        sizes.append((len(column), widths or (width,)))
        for part in widths or (width,):
            out_shape.append(jax.ShapeDtypeStruct((count, half, part), jnp.bfloat16))
    for cut in cuts:
        width = sum(weight.shape[2] for _, weight in cut)
        out_shape.append(jax.ShapeDtypeStruct((1, cut[0][1].shape[1] // 2, width), jnp.bfloat16))
    held = pl.BlockSpec(memory_space=pltpu.VMEM)
    return pl.pallas_call(
        functools.partial(join_kernel, sizes, [[block for block, _ in cut] for cut in cuts]),
        out_shape=out_shape,
        in_specs=[held] * (len(pieces) + len(sources)) + [ANY] * len(after),
        compiler_params=pltpu.CompilerParams(vmem_limit_bytes=10 * 2**20),
    )(*pieces, *sources, *after)


def halves_kernel(widths, here_ref, there_ref, *outs):
    start = 0
    for index, width in enumerate(widths):
        for half in range(2):
            rows, lanes = slice(2 * half, 2 * half + 2), slice(start, start + width)
            outs[2 * index + half][:2] = here_ref[rows, :, lanes]
            outs[2 * index + half][2:] = there_ref[rows, :, lanes]
        start += width


def halves(here, there, widths, after):
    held = pl.BlockSpec(memory_space=pltpu.VMEM)
    return pl.pallas_call(
        lambda *refs: halves_kernel(widths, refs[0], refs[1], *refs[2 + len(after) :]),
        out_shape=[
            jax.ShapeDtypeStruct((4, here.shape[1], width), jnp.bfloat16)
            for width in widths
            for _ in range(2)
        ],
        in_specs=[held] * 2 + [ANY] * len(after),
        compiler_params=pltpu.CompilerParams(vmem_limit_bytes=10 * 2**20),
    )(here, there, *after)


def send(block, move):
    pairs = []
    for lon in range(lax.axis_size("lon")):
        for core in range(2):
            z, y, x, core_to = move(lon // 4, lon // 2 % 2, lon % 2, core)
            pairs.append((lon * 2 + core, (z * 4 + y * 2 + x) * 2 + core_to))
    return lax.ppermute(block, ("lon", "lat"), pairs)


def across_z(block, bit):
    return send(block, lambda z, y, x, c: (z ^ bit, y, x, c))


def swap(z, y, x, c):
    return z, y, x, 1 - c


def tied(array, after):
    return lax.optimization_barrier((array, after))[0]


def beside(z, y, x, c):
    return (z, y, 1 - x, c) if c == 0 else (z, 1 - y, x, c)


def across(z, y, x, c):
    return (z, 1 - y, x, c) if c == 0 else (z, y, 1 - x, c)


def corner(z, y, x, c):
    return z, 1 - y, 1 - x, c


def whole_pieces(column, received):
    return [column] + received + [send(part, swap) for part in [column] + received]


def load_pieces(kind, pieces, w_ref, stage_ref, sem):
    copies = [
        pltpu.make_async_copy(piece, w_ref if kind == "rows" else stage_ref.at[index], sem.at[index])
        for index, piece in enumerate(pieces)
    ]
    for copy in copies:
        copy.start()
    if kind == "rows":
        copies[0].wait()
        return
    half = pieces[0].shape[-2]
    lon, lat = lax.axis_index("lon"), lax.axis_index("lat")
    z, y, x = lon // 4, lon // 2 % 2, lon % 2
    by_x, by_y = y * 2 + 1 - x, (1 - y) * 2 + x
    for index, copy in enumerate(copies):
        core = lat if index < 4 else 1 - lat
        own, opposite = y * 2 + x, (1 - y) * 2 + 1 - x
        one = jnp.where(core == 0, by_x, by_y)
        other = jnp.where(core == 0, by_y, by_x)
        copy.wait()
        for step in range(4):
            if kind == "columns":
                square, along = (own, one, other, opposite)[index % 4], Z_ORDER[step]
            else:
                pairs = ((own, one), (own, other), (other, opposite), (one, opposite))
                square, along = pairs[index % 4][step % 2], index % 2 * 2 + step // 2
            row = pl.multiple_of((((z ^ along) * 4 + square) * 2 + core) * half, 16)
            w_ref[pl.ds(row, half), :] = stage_ref[index, step]


def load_scratch(pieces, rows, width):
    stage = (len(pieces),) + pieces[0].shape if len(pieces) > 1 else (1, 1, 16, 128)
    return [
        pltpu.VMEM((rows, width), jnp.bfloat16),
        pltpu.VMEM(stage, jnp.bfloat16),
        pltpu.SemaphoreType.DMA((len(pieces),)),
    ]


def attend_kernel(shifted, row_windows, kind, count, *refs):
    sources = 2 if shifted else 1
    x_refs, pieces = refs[:sources], refs[sources : sources + count]
    gain_ref, sharp_ref, ones_ref = refs[sources + count : sources + count + 3]
    allow_ref = refs[sources + count + 3] if shifted else None
    out_ref, w_ref, stage_ref, sem = refs[-4:]
    held, _, features = out_ref.shape

    @pl.when(pl.program_id(0) == 0)
    def _():
        load_pieces(kind, pieces, w_ref, stage_ref, sem)

    if shifted:
        quarters = []
        for window in range(held):
            for strip_ref in x_refs:
                quarters += [strip_ref[2 * window + half].astype(jnp.float32) for half in range(2)]
        tokens = jnp.concatenate(quarters, 0).astype(jnp.bfloat16)
    else:
        tokens = x_refs[0][...].reshape(held * CELLS, features)
    channel = lax.broadcasted_iota(jnp.int32, (WIDE, WIDE), 0) // HEAD
    same_head = jnp.where(
        channel == lax.broadcasted_iota(jnp.int32, (WIDE, WIDE), 1) // HEAD, 1.0, 0.0
    ).astype(jnp.bfloat16)
    lane_head = lax.broadcasted_iota(jnp.int32, (1, WIDE), 1) // HEAD
    ones = lambda condition: jnp.where(condition, 1.0, 0.0).astype(jnp.bfloat16)
    pairs = [ones(lane_head % PART == head) for head in range(PART)]
    halves = [ones(lane_head // PART == part) for part in range(2)]
    masks = [ones(lane_head == head) for head in range(GROUP)]
    narrow = [ones(lane_head[:, :MAIN] == head) for head in range(PART)]

    def units(part):
        rounded = part.astype(jnp.bfloat16)
        length2 = dot(rounded * rounded, same_head)
        return part * lax.rsqrt(jnp.maximum(length2, 0.25 * HEAD))

    attended = [[] for _ in range(held)]
    for group in range(HEADS // GROUP):
        lanes = [slice(n * features + group * WIDE, n * features + (group + 1) * WIDE) for n in range(3)]
        queries = (units(dot(tokens, w_ref[:, lanes[0]])) * sharp_ref[:, lanes[0]]).astype(jnp.bfloat16)
        keys = units(dot(tokens, w_ref[:, lanes[1]])).astype(jnp.bfloat16)
        values = dot(tokens, w_ref[:, lanes[2]]).astype(jnp.bfloat16)
        for window in range(held):
            own = slice(window * CELLS, (window + 1) * CELLS)
            query, key, value = queries[own], keys[own], values[own]
            stacked = jnp.concatenate([query * pair for pair in pairs], 0)
            main_keys = jnp.concatenate([key[:MAIN] * half for half in halves], 0)
            main = jnp.exp2(dot(stacked, main_keys, NT)).astype(jnp.bfloat16)
            rest_keys = jnp.concatenate([key[MAIN:] * mask for mask in masks], 0)
            rest = jnp.exp2(dot(query, rest_keys, NT)).astype(jnp.bfloat16)
            if shifted:
                last = jnp.logical_and(
                    (pl.program_id(0) * held + window) % row_windows == row_windows - 1,
                    lax.axis_index("lat") == lax.axis_size("lat") - 1,
                )
                allow = jnp.where(last, allow_ref[...], 1.0).astype(jnp.bfloat16)
                rest = rest * allow[:, MAIN:]
            for part in range(2):
                lanes = slice(part * MAIN, (part + 1) * MAIN)
                parts = [main[head * CELLS : (head + 1) * CELLS, lanes] for head in range(PART)]
                if shifted:
                    parts = [one * allow[:, :MAIN] for one in parts]
                own_value = value[:, lanes]
                none = jnp.zeros((REST, MAIN), jnp.bfloat16)
                own_rest = [own_value[MAIN:] * mask for mask in narrow]
                other_rest = [none] * PART
                stacked = jnp.concatenate(
                    [own_value[:MAIN] * mask for mask in narrow]
                    + (own_rest + other_rest if part == 0 else other_rest + own_rest),
                    0,
                )
                both = jnp.concatenate([stacked, ones_ref[:, lanes]], 1)
                summed = dot(jnp.concatenate(parts + [rest], 1), both)
                attended[window].append(
                    (summed[:, :MAIN] / summed[:, MAIN:]).astype(jnp.bfloat16)
                )
    attended = jnp.concatenate([jnp.concatenate(parts, 1) for parts in attended], 0)
    projected = dot(attended, w_ref[:, 3 * features :])
    middle = tokens.astype(jnp.float32) + layer_norm(projected, gain_ref[...])
    out_ref[...] = middle.astype(jnp.bfloat16).reshape(out_ref.shape)


def allowed_pairs():
    side = np.arange(CELLS) // QUARTER % 2
    rest = np.tile(side[MAIN:], GROUP)
    return (side[:, None] == np.concatenate([side[:MAIN], rest])[None, :]).astype(np.float32)


def head_columns():
    halves = []
    for part in range(2):
        own = np.arange(part * PART, (part + 1) * PART)
        rows = np.concatenate([np.repeat(own, MAIN), np.repeat(np.arange(GROUP), REST)])
        halves.append(rows[:, None] == np.repeat(own, HEAD)[None, :])
    return np.concatenate(halves, 1).astype(np.float32)


def attend(sources, columns, pieces, gain, sharp, row_windows, after=(), held=4):
    shifted = len(sources) > 1
    kind, pieces = pieces
    features = sources[0].shape[-1]
    count = len(columns) * row_windows
    skipped = columns[0] * row_windows // held
    whole = lambda shape: pl.BlockSpec(shape, lambda i: (0,) * len(shape))
    block = pl.BlockSpec((held, CELLS, features), lambda i: (i, 0, 0))
    strip_block = pl.BlockSpec((2 * held, QUARTER, features), lambda i: (i, 0, 0))
    x_block = pl.BlockSpec((held, CELLS, features), lambda i: (i + skipped, 0, 0))
    ones = jnp.asarray(head_columns(), jnp.bfloat16)
    extra = (jnp.asarray(allowed_pairs()),) if shifted else ()
    return pl.pallas_call(
        functools.partial(attend_kernel, shifted, row_windows, kind, len(pieces)),
        grid=(count // held,),
        out_shape=jax.ShapeDtypeStruct((count, CELLS, features), jnp.bfloat16),
        in_specs=([strip_block] * 2 if shifted else [x_block])
        + [ANY] * len(pieces)
        + [whole((1, features))] * 2
        + [whole(ones.shape)]
        + [whole(e.shape) for e in extra]
        + [ANY] * len(after),
        out_specs=block,
        scratch_shapes=load_scratch(pieces, features, 4 * features),
        compiler_params=pltpu.CompilerParams(vmem_limit_bytes=24 * 2**20),
        cost_estimate=pl.CostEstimate(
            flops=count * 2_000_000_000, bytes_accessed=6_000_000, transcendentals=0
        ),
    )(*sources, *pieces, gain, sharp, ones, *extra, *after)


def feed_kernel(kind, count, hidden_size, chunk, edge, *refs):
    x_ref, pieces, gain_ref = refs[0], refs[1 : 1 + count], refs[1 + count]
    left_ref, right_ref, edge_ref, w_ref, stage_ref, sem = refs[-6:]
    held, _, features = x_ref.shape

    @pl.when(pl.program_id(0) == 0)
    def _():
        load_pieces(kind, pieces, w_ref, stage_ref, sem)

    tokens = x_ref[...].reshape(held * CELLS, features)
    total = jnp.zeros(tokens.shape, jnp.float32)
    for start in range(0, hidden_size, chunk):
        grown = dot(tokens, w_ref[:, start : start + chunk])
        slope = math.sqrt(2.0 / math.pi)
        bent = jnp.tanh(grown * (grown * grown * (0.044715 * slope) + slope))
        hidden = (grown + grown * bent).astype(jnp.bfloat16)
        total = total + dot(
            hidden, w_ref[:, hidden_size + start : hidden_size + start + chunk], NT
        )
    result = tokens.astype(jnp.float32) + layer_norm(0.5 * total, gain_ref[...])
    edge_window, edge_half = edge
    for window in range(held):
        for side, target in enumerate((left_ref, right_ref)):
            for half in range(2):
                start = window * CELLS + (side * 2 + half) * QUARTER
                quarter = result[start : start + QUARTER].astype(jnp.bfloat16)
                target[2 * window + half] = quarter
                if half == edge_half and window == edge_window % held:

                    @pl.when(pl.program_id(0) == edge_window // held)
                    def _(quarter=quarter, side=side):
                        edge_ref[side] = quarter


def feed(windows, column, count, pieces, gain, hidden_size, edge, after=(), held=4):
    _, cells, features = windows.shape
    kind, pieces = pieces
    block = pl.BlockSpec((held, cells, features), lambda i: (i + column * count // held, 0, 0))
    side = pl.BlockSpec((2 * held, QUARTER, features), lambda i: (i, 0, 0))
    return pl.pallas_call(
        functools.partial(feed_kernel, kind, len(pieces), hidden_size, 512, edge),
        grid=(count // held,),
        out_shape=[jax.ShapeDtypeStruct((2 * count, QUARTER, features), jnp.bfloat16)] * 2
        + [jax.ShapeDtypeStruct((2, QUARTER, features), jnp.bfloat16)],
        in_specs=[block]
        + [ANY] * len(pieces)
        + [pl.BlockSpec((1, features), lambda i: (0, 0))]
        + [ANY] * len(after),
        out_specs=[side, side, pl.BlockSpec((2, QUARTER, features), lambda i: (0, 0, 0))],
        scratch_shapes=load_scratch(pieces, features, 2 * hidden_size),
        compiler_params=pltpu.CompilerParams(vmem_limit_bytes=24 * 2**20),
        cost_estimate=pl.CostEstimate(
            flops=FEED_FLOPS,
            bytes_accessed=FEED_BYTES,
            transcendentals=0,
        ),
    )(windows, *pieces, gain, *after)


def shift_from(block, lon_step, lat_step):
    lons, lats = lax.axis_size("lon"), lax.axis_size("lat")
    pairs = []
    for lon in range(lons):
        for lat in range(lats):
            source = (lon + lon_step) % lons * lats + (lat + lat_step) % lats
            pairs.append((source, lon * lats + lat))
    return lax.ppermute(block, ("lon", "lat"), pairs)


def to_windows(cells):
    cols, rows, levels, features = cells.shape
    c, r = WLON // 2, WLAT // 2
    arranged = cells.reshape(cols // WLON, 2, c, rows // WLAT, 2, r, levels, features)
    arranged = arranged.transpose(0, 3, 1, 4, 2, 5, 6, 7)
    return arranged.reshape(-1, CELLS, features)


def strips_kernel(picks, *refs):
    sources, outs = refs[: len(refs) - len(picks)], refs[len(refs) - len(picks) :]
    for pick, target in zip(picks, outs):
        place = 0
        for source, first, count in pick:
            target[place : place + count] = sources[source][first : first + count]
            place += count


def strips(sources, picks):
    shape = sources[0].shape[1:]
    held = pl.BlockSpec(memory_space=pltpu.VMEM)
    return pl.pallas_call(
        functools.partial(strips_kernel, picks),
        out_shape=[
            jax.ShapeDtypeStruct((sum(count for _, _, count in pick),) + shape, jnp.bfloat16)
            for pick in picks
        ],
        in_specs=[held] * len(sources),
        compiler_params=pltpu.CompilerParams(vmem_limit_bytes=10 * 2**20),
    )(*sources)


def from_strips(quarters, cols, rows):
    features = quarters.shape[-1]
    c, r = WLON // 2, WLAT // 2
    arranged = quarters.reshape(cols // c, rows // r, c, r, LEVELS, features)
    return arranged.transpose(0, 2, 1, 3, 4, 5).reshape(cols, rows, LEVELS, features)


def per_device(tokens, qkv_weight, out_weight, up_weight, down_weight, norm_gain, logit_scale):
    cols, rows, _, features = tokens.shape
    hidden_size = up_weight.shape[-1]
    row_windows = rows // WLAT
    weights = (qkv_weight, out_weight, up_weight, down_weight)
    relay = relayed(qkv_weight.shape[1], lax.axis_size("lon"), lax.axis_size("lat"))
    spread = np.arange(HEADS)[:, None] == np.arange(features)[None, :] // HEAD
    sharp = logit_scale[:, :, None] * jnp.asarray(spread * math.log2(math.e), jnp.float32)[None]
    sharp = jnp.sum(sharp, 1)
    windows = to_windows(tokens)

    def attention(block, sources, columns, pieces, after=()):
        gain, scale = norm_gain[block, :1], sharp[block : block + 1]
        return attend(sources, columns, pieces, gain, scale, row_windows, after)

    def forward(block, middle, column, pieces, edge, after=()):
        gain = norm_gain[block, 1:]
        return feed(middle, column, row_windows, pieces, gain, hidden_size, edge, after)

    low_edge, high_edge = (0, 0), (row_windows - 1, 1)
    if relay:
        (own,) = join([], [[(0, weight) for weight in weights[:2]]])
        feed_own, last_own = join(
            [],
            [[(0, weight) for weight in weights[2:]], [(1, weight) for weight in weights]],
            (own,),
        )
        widths = tuple(sum(weight.shape[2] for weight in pair) for pair in (weights[:2], weights[2:]))
        (pair,) = join([[own, across_z(own, 2)]], (), (windows,))
        (feed_pair,) = join([[feed_own, across_z(feed_own, 2)]])
        (column,) = join([[pair, across_z(pair, 1)]], (), (feed_pair,))
        received = [send(column, way) for way in (beside, across, corner)]
        sent = [tied(column, received[0])] + received
        pieces = "columns", [column] + received + [send(part, swap) for part in sent]
        last_own = tied(last_own, pair)
        last_other = across_z(last_own, 2)
        (last_four,) = join(
            [[last_own, send(last_own, beside), last_other, send(last_other, across)]]
        )
        (feed_column,) = join([[feed_pair, across_z(feed_pair, 1)]], (), (last_four,))
        received = [send(feed_column, way) for way in (beside, across)]
        last_other = across_z(last_four, 1)
        middle_0 = attention(0, [windows], (0,), pieces, (feed_column,))
        first, second = tied((received[0][:2], received[1][2:]), middle_0)
        corners = [send(first, across), send(second, beside)]
        *last_columns, final_one, final_other = halves(last_four, last_other, widths, (middle_0,))
        middle_1 = attention(0, [windows], (1,), pieces, (middle_0, last_columns[0]))
        swapped = [send(part, swap) for part in [feed_column] + tied(received, middle_0)]
        received += join([tied(corners, (middle_1, *swapped))])
        feed_pieces = "columns", [feed_column] + received + swapped + [send(received[2], swap)]
    else:
        gathered = []
        for block in range(2):
            for pair in (weights[:2], weights[2:]):
                chunk = jnp.concatenate([weight[block] for weight in pair], 1)
                gathered.append(lax.all_gather(chunk, "lon", axis=0, tiled=True))
        pieces, feed_pieces, last_pieces, final_pieces = (("rows", [rows]) for rows in gathered)
        middle_0 = attention(0, [windows], (0,), pieces)
        middle_1 = attention(0, [windows], (1,), pieces)
    left_0, right_0, low_0 = forward(0, middle_0, 0, feed_pieces, low_edge)
    below_0 = shift_from(low_0, 0, 1)
    size = left_0.shape[0]
    (ahead,) = strips([left_0, below_0], [[(0, 1, size - 1), (1, 0, 1)]])
    ahead = shift_from(ahead, 1, 0)
    if relay:
        last_received = [
            send(part, way) for part, way in zip(tied(last_columns, middle_1), (across, beside))
        ]
    left_1, right_1, low_1 = forward(0, middle_1, 0, feed_pieces, low_edge, (below_0,))
    below_1 = shift_from(tied(low_1, ahead), 0, 1)
    if relay:
        last_pieces = last_columns + last_received
        last_pieces += [send(part, swap) for part in last_columns + tied(last_received, low_1)]
        last_pieces = "halves", last_pieces
        final_columns = [final_one, final_other]
        final_received = [
            send(part, way)
            for part, way in zip(tied(final_columns, last_received), (across, beside))
        ]
    lefts = strips(
        [right_0, left_1, right_1, below_0, below_1],
        [
            [(0, 1, size - 1), (3, 1, 1)],
            [(1, 1, size - 1), (4, 0, 1)],
            [(2, 1, size - 1), (4, 1, 1)],
        ],
    )
    middle_1 = attention(1, [lefts[2], ahead], (1,), last_pieces)
    if relay:
        final_pieces = final_columns + final_received
        final_pieces += [send(part, swap) for part in final_columns + tied(final_received, middle_1)]
        final_pieces = "halves", final_pieces
    left_1, right_1, high_1 = forward(1, middle_1, 0, final_pieces, high_edge)
    above_1 = shift_from(high_1, 0, -1)
    (behind,) = strips([above_1, right_1], [[(0, 1, 1), (1, 0, size - 1)]])
    behind = shift_from(behind, -1, 0)
    middle_0 = attention(1, lefts[:2], (0,), last_pieces, (above_1,))
    left_0, right_0, high_0 = forward(1, middle_0, 0, final_pieces, high_edge)
    above_0 = shift_from(high_0, 0, -1)
    picks = [(0, 0, size)]
    for place, (low, quarter) in enumerate(((4, 0), (4, 1), (5, 0))):
        picks += [(low, quarter, 1), (place + 1, 0, size - 1)]
    (mixed,) = strips([behind, left_0, right_0, left_1, above_0, above_1], [picks])
    return from_strips(mixed, cols, rows)


def solution(mesh):
    placed = (
        P("lon", "lat", None, None),
        P(None, "lon", None),
        P(None, "lon", None),
        P(None, "lon", None),
        P(None, "lon", None),
        P(),
        P(),
    )
    return jax.shard_map(
        per_device,
        mesh=mesh,
        in_specs=placed,
        out_specs=P("lon", "lat", None, None),
        check_vma=False,
    )
```

```python
import functools
import math

import numpy as np

import jax
import jax.numpy as jnp
from jax import lax
from jax.experimental import pallas as pl
from jax.experimental.pallas import tpu as pltpu
from jax.sharding import PartitionSpec as P

HEADS = 16
HEAD = 32
WLON = 12
WLAT = 6
LEVELS = 2
CELLS = WLON * WLAT * LEVELS
MAIN = 128
REST = CELLS - MAIN
QUARTER = CELLS // 4
GROUP = 8
PART = 4
WIDE = GROUP * HEAD
FEED_FLOPS, FEED_BYTES = 1_000_000, 100_000
Z_ORDER = (0, 2, 1, 3)
ANY = pl.BlockSpec(memory_space=pl.ANY)
NT = (((1,), (1,)), ((), ()))


def dot(a, b, dims=(((1,), (0,)), ((), ()))):
    return lax.dot_general(a, b, dims, preferred_element_type=jnp.float32)


def layer_norm(value, gain_row):
    averaged = jnp.mean(value, -1, keepdims=True)
    centred = value - averaged
    variance = jnp.mean(centred * centred, -1, keepdims=True)
    return centred * lax.rsqrt(variance + 1e-05) * gain_row


def relayed(rows, lon_size, lat_size):
    return lat_size == 2 and rows % 32 == 0 and lon_size == 16


def join_kernel(columns, cuts, *refs):
    outs = refs[len(refs) - sum(len(widths) for _, widths in columns) - len(cuts) :]
    place, out = 0, 0
    for count, widths in columns:
        row = 0
        for piece in refs[place : place + count]:
            start = 0
            for target, width in zip(outs[out : out + len(widths)], widths):
                target[row : row + piece.shape[0]] = piece[:, :, start : start + width]
                start += width
            row += piece.shape[0]
        place, out = place + count, out + len(widths)
    for blocks, chunk_ref in zip(cuts, outs[out:]):
        half = chunk_ref.shape[1]
        first = pl.multiple_of(lax.axis_index("lat") * half, 16)
        start = 0
        for block, source in zip(blocks, refs[place : place + len(blocks)]):
            width = source.shape[2]
            chunk_ref[0, :, start : start + width] = source[block, pl.ds(first, half), :]
            start += width
        place += len(blocks)


def join(columns, cuts=(), after=(), widths=None):
    pieces = [piece for column in columns for piece in column]
    sources = [weight for cut in cuts for _, weight in cut]
    out_shape, sizes = [], []
    for column in columns:
        count, half, width = column[0].shape
        count = sum(piece.shape[0] for piece in column)
        sizes.append((len(column), widths or (width,)))
        for part in widths or (width,):
            out_shape.append(jax.ShapeDtypeStruct((count, half, part), jnp.bfloat16))
    for cut in cuts:
        width = sum(weight.shape[2] for _, weight in cut)
        out_shape.append(jax.ShapeDtypeStruct((1, cut[0][1].shape[1] // 2, width), jnp.bfloat16))
    held = pl.BlockSpec(memory_space=pltpu.VMEM)
    return pl.pallas_call(
        functools.partial(join_kernel, sizes, [[block for block, _ in cut] for cut in cuts]),
        out_shape=out_shape,
        in_specs=[held] * (len(pieces) + len(sources)) + [ANY] * len(after),
        compiler_params=pltpu.CompilerParams(vmem_limit_bytes=10 * 2**20),
    )(*pieces, *sources, *after)


def halves_kernel(widths, here_ref, there_ref, *outs):
    start = 0
    for index, width in enumerate(widths):
        for half in range(2):
            rows, lanes = slice(2 * half, 2 * half + 2), slice(start, start + width)
            outs[2 * index + half][:2] = here_ref[rows, :, lanes]
            outs[2 * index + half][2:] = there_ref[rows, :, lanes]
        start += width


def halves(here, there, widths, after):
    held = pl.BlockSpec(memory_space=pltpu.VMEM)
    return pl.pallas_call(
        lambda *refs: halves_kernel(widths, refs[0], refs[1], *refs[2 + len(after) :]),
        out_shape=[
            jax.ShapeDtypeStruct((4, here.shape[1], width), jnp.bfloat16)
            for width in widths
            for _ in range(2)
        ],
        in_specs=[held] * 2 + [ANY] * len(after),
        compiler_params=pltpu.CompilerParams(vmem_limit_bytes=10 * 2**20),
    )(here, there, *after)


def send(block, move):
    pairs = []
    for lon in range(lax.axis_size("lon")):
        for core in range(2):
            z, y, x, core_to = move(lon // 4, lon // 2 % 2, lon % 2, core)
            pairs.append((lon * 2 + core, (z * 4 + y * 2 + x) * 2 + core_to))
    return lax.ppermute(block, ("lon", "lat"), pairs)


def across_z(block, bit):
    return send(block, lambda z, y, x, c: (z ^ bit, y, x, c))


def swap(z, y, x, c):
    return z, y, x, 1 - c


def tied(array, after):
    return lax.optimization_barrier((array, after))[0]


def beside(z, y, x, c):
    return (z, y, 1 - x, c) if c == 0 else (z, 1 - y, x, c)


def across(z, y, x, c):
    return (z, 1 - y, x, c) if c == 0 else (z, y, 1 - x, c)


def corner(z, y, x, c):
    return z, 1 - y, 1 - x, c


def whole_pieces(column, received):
    return [column] + received + [send(part, swap) for part in [column] + received]


def load_pieces(kind, pieces, w_ref, stage_ref, sem):
    copies = [
        pltpu.make_async_copy(piece, w_ref if kind == "rows" else stage_ref.at[index], sem.at[index])
        for index, piece in enumerate(pieces)
    ]
    for copy in copies:
        copy.start()
    if kind == "rows":
        copies[0].wait()
        return
    half = pieces[0].shape[-2]
    lon, lat = lax.axis_index("lon"), lax.axis_index("lat")
    z, y, x = lon // 4, lon // 2 % 2, lon % 2
    by_x, by_y = y * 2 + 1 - x, (1 - y) * 2 + x
    for index, copy in enumerate(copies):
        core = lat if index < 4 else 1 - lat
        own, opposite = y * 2 + x, (1 - y) * 2 + 1 - x
        one = jnp.where(core == 0, by_x, by_y)
        other = jnp.where(core == 0, by_y, by_x)
        copy.wait()
        for step in range(4):
            if kind == "columns":
                square, along = (own, one, other, opposite)[index % 4], Z_ORDER[step]
            else:
                pairs = ((own, one), (own, other), (other, opposite), (one, opposite))
                square, along = pairs[index % 4][step % 2], index % 2 * 2 + step // 2
            row = pl.multiple_of((((z ^ along) * 4 + square) * 2 + core) * half, 16)
            w_ref[pl.ds(row, half), :] = stage_ref[index, step]


def load_scratch(pieces, rows, width):
    stage = (len(pieces),) + pieces[0].shape if len(pieces) > 1 else (1, 1, 16, 128)
    return [
        pltpu.VMEM((rows, width), jnp.bfloat16),
        pltpu.VMEM(stage, jnp.bfloat16),
        pltpu.SemaphoreType.DMA((len(pieces),)),
    ]


def attend_kernel(shifted, row_windows, kind, count, *refs):
    sources = 2 if shifted else 1
    x_refs, pieces = refs[:sources], refs[sources : sources + count]
    gain_ref, sharp_ref, ones_ref = refs[sources + count : sources + count + 3]
    allow_ref = refs[sources + count + 3] if shifted else None
    out_ref, w_ref, stage_ref, sem = refs[-4:]
    held, _, features = out_ref.shape

    @pl.when(pl.program_id(0) == 0)
    def _():
        load_pieces(kind, pieces, w_ref, stage_ref, sem)

    if shifted:
        quarters = []
        for window in range(held):
            for strip_ref in x_refs:
                quarters += [strip_ref[2 * window + half].astype(jnp.float32) for half in range(2)]
        tokens = jnp.concatenate(quarters, 0).astype(jnp.bfloat16)
    else:
        tokens = x_refs[0][...].reshape(held * CELLS, features)
    channel = lax.broadcasted_iota(jnp.int32, (WIDE, WIDE), 0) // HEAD
    same_head = jnp.where(
        channel == lax.broadcasted_iota(jnp.int32, (WIDE, WIDE), 1) // HEAD, 1.0, 0.0
    ).astype(jnp.bfloat16)
    lane_head = lax.broadcasted_iota(jnp.int32, (1, WIDE), 1) // HEAD
    ones = lambda condition: jnp.where(condition, 1.0, 0.0).astype(jnp.bfloat16)
    pairs = [ones(lane_head % PART == head) for head in range(PART)]
    halves = [ones(lane_head // PART == part) for part in range(2)]
    masks = [ones(lane_head == head) for head in range(GROUP)]
    narrow = [ones(lane_head[:, :MAIN] == head) for head in range(PART)]

    def units(part):
        rounded = part.astype(jnp.bfloat16)
        length2 = dot(rounded * rounded, same_head)
        return part * lax.rsqrt(jnp.maximum(length2, 0.25 * HEAD))

    attended = [[] for _ in range(held)]
    for group in range(HEADS // GROUP):
        lanes = [slice(n * features + group * WIDE, n * features + (group + 1) * WIDE) for n in range(3)]
        queries = (units(dot(tokens, w_ref[:, lanes[0]])) * sharp_ref[:, lanes[0]]).astype(jnp.bfloat16)
        keys = units(dot(tokens, w_ref[:, lanes[1]])).astype(jnp.bfloat16)
        values = dot(tokens, w_ref[:, lanes[2]]).astype(jnp.bfloat16)
        for window in range(held):
            own = slice(window * CELLS, (window + 1) * CELLS)
            query, key, value = queries[own], keys[own], values[own]
            stacked = jnp.concatenate([query * pair for pair in pairs], 0)
            main_keys = jnp.concatenate([key[:MAIN] * half for half in halves], 0)
            main = jnp.exp2(dot(stacked, main_keys, NT)).astype(jnp.bfloat16)
            rest_keys = jnp.concatenate([key[MAIN:] * mask for mask in masks], 0)
            rest = jnp.exp2(dot(query, rest_keys, NT)).astype(jnp.bfloat16)
            if shifted:
                last = jnp.logical_and(
                    (pl.program_id(0) * held + window) % row_windows == row_windows - 1,
                    lax.axis_index("lat") == lax.axis_size("lat") - 1,
                )
                allow = jnp.where(last, allow_ref[...], 1.0).astype(jnp.bfloat16)
                rest = rest * allow[:, MAIN:]
            for part in range(2):
                lanes = slice(part * MAIN, (part + 1) * MAIN)
                parts = [main[head * CELLS : (head + 1) * CELLS, lanes] for head in range(PART)]
                if shifted:
                    parts = [one * allow[:, :MAIN] for one in parts]
                own_value = value[:, lanes]
                none = jnp.zeros((REST, MAIN), jnp.bfloat16)
                own_rest = [own_value[MAIN:] * mask for mask in narrow]
                other_rest = [none] * PART
                stacked = jnp.concatenate(
                    [own_value[:MAIN] * mask for mask in narrow]
                    + (own_rest + other_rest if part == 0 else other_rest + own_rest),
                    0,
                )
                both = jnp.concatenate([stacked, ones_ref[:, lanes]], 1)
                summed = dot(jnp.concatenate(parts + [rest], 1), both)
                attended[window].append(
                    (summed[:, :MAIN] / summed[:, MAIN:]).astype(jnp.bfloat16)
                )
    attended = jnp.concatenate([jnp.concatenate(parts, 1) for parts in attended], 0)
    projected = dot(attended, w_ref[:, 3 * features :])
    middle = tokens.astype(jnp.float32) + layer_norm(projected, gain_ref[...])
    out_ref[...] = middle.astype(jnp.bfloat16).reshape(out_ref.shape)


def allowed_pairs():
    side = np.arange(CELLS) // QUARTER % 2
    rest = np.tile(side[MAIN:], GROUP)
    return (side[:, None] == np.concatenate([side[:MAIN], rest])[None, :]).astype(np.float32)


def head_columns():
    halves = []
    for part in range(2):
        own = np.arange(part * PART, (part + 1) * PART)
        rows = np.concatenate([np.repeat(own, MAIN), np.repeat(np.arange(GROUP), REST)])
        halves.append(rows[:, None] == np.repeat(own, HEAD)[None, :])
    return np.concatenate(halves, 1).astype(np.float32)


def attend(sources, columns, pieces, gain, sharp, row_windows, after=(), held=4):
    shifted = len(sources) > 1
    kind, pieces = pieces
    features = sources[0].shape[-1]
    count = len(columns) * row_windows
    skipped = columns[0] * row_windows // held
    whole = lambda shape: pl.BlockSpec(shape, lambda i: (0,) * len(shape))
    block = pl.BlockSpec((held, CELLS, features), lambda i: (i, 0, 0))
    strip_block = pl.BlockSpec((2 * held, QUARTER, features), lambda i: (i, 0, 0))
    x_block = pl.BlockSpec((held, CELLS, features), lambda i: (i + skipped, 0, 0))
    ones = jnp.asarray(head_columns(), jnp.bfloat16)
    extra = (jnp.asarray(allowed_pairs()),) if shifted else ()
    return pl.pallas_call(
        functools.partial(attend_kernel, shifted, row_windows, kind, len(pieces)),
        grid=(count // held,),
        out_shape=jax.ShapeDtypeStruct((count, CELLS, features), jnp.bfloat16),
        in_specs=([strip_block] * 2 if shifted else [x_block])
        + [ANY] * len(pieces)
        + [whole((1, features))] * 2
        + [whole(ones.shape)]
        + [whole(e.shape) for e in extra]
        + [ANY] * len(after),
        out_specs=block,
        scratch_shapes=load_scratch(pieces, features, 4 * features),
        compiler_params=pltpu.CompilerParams(vmem_limit_bytes=24 * 2**20),
        cost_estimate=pl.CostEstimate(
            flops=count * 2_000_000_000, bytes_accessed=6_000_000, transcendentals=0
        ),
    )(*sources, *pieces, gain, sharp, ones, *extra, *after)


def feed_kernel(kind, count, hidden_size, chunk, edge, *refs):
    x_ref, pieces, gain_ref = refs[0], refs[1 : 1 + count], refs[1 + count]
    left_ref, right_ref, edge_ref, w_ref, stage_ref, sem = refs[-6:]
    held, _, features = x_ref.shape

    @pl.when(pl.program_id(0) == 0)
    def _():
        load_pieces(kind, pieces, w_ref, stage_ref, sem)

    tokens = x_ref[...].reshape(held * CELLS, features)
    total = jnp.zeros(tokens.shape, jnp.float32)
    for start in range(0, hidden_size, chunk):
        grown = dot(tokens, w_ref[:, start : start + chunk])
        slope = math.sqrt(2.0 / math.pi)
        bent = jnp.tanh(grown * (grown * grown * (0.044715 * slope) + slope))
        hidden = (grown + grown * bent).astype(jnp.bfloat16)
        total = total + dot(
            hidden, w_ref[:, hidden_size + start : hidden_size + start + chunk], NT
        )
    result = tokens.astype(jnp.float32) + layer_norm(0.5 * total, gain_ref[...])
    edge_window, edge_half = edge
    for window in range(held):
        for side, target in enumerate((left_ref, right_ref)):
            for half in range(2):
                start = window * CELLS + (side * 2 + half) * QUARTER
                quarter = result[start : start + QUARTER].astype(jnp.bfloat16)
                target[2 * window + half] = quarter
                if half == edge_half and window == edge_window % held:

                    @pl.when(pl.program_id(0) == edge_window // held)
                    def _(quarter=quarter, side=side):
                        edge_ref[side] = quarter


def feed(windows, column, count, pieces, gain, hidden_size, edge, after=(), held=4):
    _, cells, features = windows.shape
    kind, pieces = pieces
    block = pl.BlockSpec((held, cells, features), lambda i: (i + column * count // held, 0, 0))
    side = pl.BlockSpec((2 * held, QUARTER, features), lambda i: (i, 0, 0))
    return pl.pallas_call(
        functools.partial(feed_kernel, kind, len(pieces), hidden_size, 512, edge),
        grid=(count // held,),
        out_shape=[jax.ShapeDtypeStruct((2 * count, QUARTER, features), jnp.bfloat16)] * 2
        + [jax.ShapeDtypeStruct((2, QUARTER, features), jnp.bfloat16)],
        in_specs=[block]
        + [ANY] * len(pieces)
        + [pl.BlockSpec((1, features), lambda i: (0, 0))]
        + [ANY] * len(after),
        out_specs=[side, side, pl.BlockSpec((2, QUARTER, features), lambda i: (0, 0, 0))],
        scratch_shapes=load_scratch(pieces, features, 2 * hidden_size),
        compiler_params=pltpu.CompilerParams(vmem_limit_bytes=24 * 2**20),
        cost_estimate=pl.CostEstimate(
            flops=FEED_FLOPS,
            bytes_accessed=FEED_BYTES,
            transcendentals=0,
        ),
    )(windows, *pieces, gain, *after)


def shift_from(block, lon_step, lat_step):
    lons, lats = lax.axis_size("lon"), lax.axis_size("lat")
    pairs = []
    for lon in range(lons):
        for lat in range(lats):
            source = (lon + lon_step) % lons * lats + (lat + lat_step) % lats
            pairs.append((source, lon * lats + lat))
    return lax.ppermute(block, ("lon", "lat"), pairs)


def to_windows(cells):
    cols, rows, levels, features = cells.shape
    c, r = WLON // 2, WLAT // 2
    arranged = cells.reshape(cols // WLON, 2, c, rows // WLAT, 2, r, levels, features)
    arranged = arranged.transpose(0, 3, 1, 4, 2, 5, 6, 7)
    return arranged.reshape(-1, CELLS, features)


def strips_kernel(picks, *refs):
    sources, outs = refs[: len(refs) - len(picks)], refs[len(refs) - len(picks) :]
    for pick, target in zip(picks, outs):
        place = 0
        for source, first, count in pick:
            target[place : place + count] = sources[source][first : first + count]
            place += count


def strips(sources, picks):
    shape = sources[0].shape[1:]
    held = pl.BlockSpec(memory_space=pltpu.VMEM)
    return pl.pallas_call(
        functools.partial(strips_kernel, picks),
        out_shape=[
            jax.ShapeDtypeStruct((sum(count for _, _, count in pick),) + shape, jnp.bfloat16)
            for pick in picks
        ],
        in_specs=[held] * len(sources),
        compiler_params=pltpu.CompilerParams(vmem_limit_bytes=10 * 2**20),
    )(*sources)


def from_strips(quarters, cols, rows):
    features = quarters.shape[-1]
    c, r = WLON // 2, WLAT // 2
    arranged = quarters.reshape(cols // c, rows // r, c, r, LEVELS, features)
    return arranged.transpose(0, 2, 1, 3, 4, 5).reshape(cols, rows, LEVELS, features)


def per_device(tokens, qkv_weight, out_weight, up_weight, down_weight, norm_gain, logit_scale):
    cols, rows, _, features = tokens.shape
    hidden_size = up_weight.shape[-1]
    row_windows = rows // WLAT
    weights = (qkv_weight, out_weight, up_weight, down_weight)
    relay = relayed(qkv_weight.shape[1], lax.axis_size("lon"), lax.axis_size("lat"))
    spread = np.arange(HEADS)[:, None] == np.arange(features)[None, :] // HEAD
    sharp = logit_scale[:, :, None] * jnp.asarray(spread * math.log2(math.e), jnp.float32)[None]
    sharp = jnp.sum(sharp, 1)
    windows = to_windows(tokens)

    def attention(block, sources, columns, pieces, after=()):
        gain, scale = norm_gain[block, :1], sharp[block : block + 1]
        return attend(sources, columns, pieces, gain, scale, row_windows, after)

    def forward(block, middle, column, pieces, edge, after=()):
        gain = norm_gain[block, 1:]
        return feed(middle, column, row_windows, pieces, gain, hidden_size, edge, after)

    low_edge, high_edge = (0, 0), (row_windows - 1, 1)
    if relay:
        (own,) = join([], [[(0, weight) for weight in weights[:2]]])
        feed_own, last_own = join(
            [],
            [[(0, weight) for weight in weights[2:]], [(1, weight) for weight in weights]],
            (own,),
        )
        widths = tuple(sum(weight.shape[2] for weight in pair) for pair in (weights[:2], weights[2:]))
        (pair,) = join([[own, across_z(own, 2)]], (), (windows,))
        (feed_pair,) = join([[feed_own, across_z(feed_own, 2)]])
        (column,) = join([[pair, across_z(pair, 1)]], (), (feed_pair,))
        received = [send(column, way) for way in (beside, across, corner)]
        sent = [tied(column, received[0])] + received
        pieces = "columns", [column] + received + [send(part, swap) for part in sent]
        last_own = tied(last_own, pair)
        last_other = across_z(last_own, 2)
        (last_four,) = join(
            [[last_own, send(last_own, beside), last_other, send(last_other, across)]]
        )
        (feed_column,) = join([[feed_pair, across_z(feed_pair, 1)]], (), (last_four,))
        received = [send(feed_column, way) for way in (beside, across)]
        last_other = across_z(last_four, 1)
        middle_0 = attention(0, [windows], (0,), pieces, (feed_column,))
        first, second = tied((received[0][:2], received[1][2:]), middle_0)
        corners = [send(first, across), send(second, beside)]
        *last_columns, final_one, final_other = halves(last_four, last_other, widths, (middle_0,))
        middle_1 = attention(0, [windows], (1,), pieces, (middle_0, last_columns[0]))
        swapped = [send(part, swap) for part in [feed_column] + tied(received, middle_0)]
        received += join([tied(corners, (middle_1, *swapped))])
        feed_pieces = "columns", [feed_column] + received + swapped + [send(received[2], swap)]
    else:
        gathered = []
        for block in range(2):
            for pair in (weights[:2], weights[2:]):
                chunk = jnp.concatenate([weight[block] for weight in pair], 1)
                gathered.append(lax.all_gather(chunk, "lon", axis=0, tiled=True))
        pieces, feed_pieces, last_pieces, final_pieces = (("rows", [rows]) for rows in gathered)
        middle_0 = attention(0, [windows], (0,), pieces)
        middle_1 = attention(0, [windows], (1,), pieces)
    left_0, right_0, low_0 = forward(0, middle_0, 0, feed_pieces, low_edge)
    below_0 = shift_from(low_0, 0, 1)
    size = left_0.shape[0]
    (ahead,) = strips([left_0, below_0], [[(0, 1, size - 1), (1, 0, 1)]])
    ahead = shift_from(ahead, 1, 0)
    if relay:
        last_received = [
            send(part, way) for part, way in zip(tied(last_columns, middle_1), (across, beside))
        ]
    left_1, right_1, low_1 = forward(0, middle_1, 0, feed_pieces, low_edge, (below_0,))
    below_1 = shift_from(tied(low_1, ahead), 0, 1)
    if relay:
        last_pieces = last_columns + last_received
        last_pieces += [send(part, swap) for part in last_columns + tied(last_received, low_1)]
        last_pieces = "halves", last_pieces
        final_columns = [final_one, final_other]
        final_received = [
            send(part, way)
            for part, way in zip(tied(final_columns, (last_received, ahead)), (across, beside))
        ]
    lefts = strips(
        [right_0, left_1, right_1, below_0, below_1],
        [
            [(0, 1, size - 1), (3, 1, 1)],
            [(1, 1, size - 1), (4, 0, 1)],
            [(2, 1, size - 1), (4, 1, 1)],
        ],
    )
    middle_1 = attention(1, [lefts[2], ahead], (1,), last_pieces)
    if relay:
        final_pieces = final_columns + final_received
        final_pieces += [send(part, swap) for part in final_columns + tied(final_received, middle_1)]
        final_pieces = "halves", final_pieces
    left_1, right_1, high_1 = forward(1, middle_1, 0, final_pieces, high_edge)
    above_1 = shift_from(high_1, 0, -1)
    (behind,) = strips([above_1, right_1], [[(0, 1, 1), (1, 0, size - 1)]])
    behind = shift_from(behind, -1, 0)
    middle_0 = attention(1, lefts[:2], (0,), last_pieces, (above_1,))
    left_0, right_0, high_0 = forward(1, middle_0, 0, final_pieces, high_edge)
    above_0 = shift_from(high_0, 0, -1)
    picks = [(0, 0, size)]
    for place, (low, quarter) in enumerate(((4, 0), (4, 1), (5, 0))):
        picks += [(low, quarter, 1), (place + 1, 0, size - 1)]
    (mixed,) = strips([behind, left_0, right_0, left_1, above_0, above_1], [picks])
    return from_strips(mixed, cols, rows)


def solution(mesh):
    placed = (
        P("lon", "lat", None, None),
        P(None, "lon", None),
        P(None, "lon", None),
        P(None, "lon", None),
        P(None, "lon", None),
        P(),
        P(),
    )
    return jax.shard_map(
        per_device,
        mesh=mesh,
        in_specs=placed,
        out_specs=P("lon", "lat", None, None),
        check_vma=False,
    )
```
